32 devices in a mesh: parts: 2 (over y), seq: 16 (over z, x, core).
Axes of the slice: x: 2, y: 2, z: 4, core: 2. Of those that a mesh axis runs over, the one named last changes fastest.
Arguments:
- points: bfloat16 [8192, 128], P(('parts', 'seq')), parts along dimension 0, may hold values from -6 to 6
- route: int32 [2, 256], P(None, ('parts', 'seq')), parts along dimension 1, may hold values from 0 to 15, as said below
- owned: int32 [32], P(('parts', 'seq')), parts along dimension 0, may hold values from 0 to 16, as said below
- cotangent: bfloat16 [8192, 128], P(('parts', 'seq')), parts along dimension 0, may hold values from -6 to 6
- gain: float32 [128], replicated, may hold values from 0.1 to 1.9
- w_qkv: bfloat16 [128, 384], replicated, may hold values from -0.5 to 0.5
- b_qkv: float32 [384], replicated, may hold values from -3 to 3
- w_out: bfloat16 [128, 128], replicated, may hold values from -0.5 to 0.5
- b_out: float32 [128], replicated, may hold values from -3 to 3
Outputs:
- mixed: bfloat16 [8192, 128], P(('parts', 'seq')), parts along dimension 0
- grad_points: bfloat16 [8192, 128], P(('parts', 'seq')), parts along dimension 0
- grad_gain: float32 [256], P('parts'), parts along dimension 0
- grad_w_qkv: float32 [256, 384], P('parts'), parts along dimension 0
- grad_b_qkv: float32 [768], P('parts'), parts along dimension 0
- grad_w_out: float32 [256, 128], P('parts'), parts along dimension 0
- grad_b_out: float32 [256], P('parts'), parts along dimension 0
The draws below stay inside these ranges and needn't reach their ends.
There are 2 independent parts, one for each index of `parts`. The reference program is written for one: setup_inputs(seed, part) draws one part's arguments, and reference() takes and returns one part's arrays. A program takes and returns all parts, laid end to end along the dimension named above; an argument that names none is the same for every part. Nothing has to cross between parts.
Inputs may be any that keep to these rules, and one draw needn't show every extreme that they name: `route`: row 0 names each block's owner, row 1 its slot there. Every slot below owned[o] of every owner o receives exactly one block, slots are numbered in Hilbert order of the owner's range; no device's Z-order blocks name the same owner twice. `owned`: the counts sum to 128; some device holds exactly 16 blocks and some none.
All inputs are finite; a program needn't handle non-finite values.
Results may differ from the reference program's by a relative error of at most 0.0095.
Values may be sent and summed in bfloat16 or wider, within the bound.
No kernel may reach another device: no remote copies, remote signals or barrier semaphores. Data moves between devices by JAX's collectives and lax.ppermute only.
A program may use at most 64 MiB of HBM per device.

```python
import jax
import jax.numpy as jnp
from jax import lax

C = 128
HEADS = 8
PATCH = 512
BLK_DEV = 8
BLOCK = 32
OWN_MAX = 16
BLOCKS = 128
POINTS = 4096
N_SEQ = 16


def owner_counts(key):
    first, second = jax.random.split(key)
    order = jax.random.permutation(first, N_SEQ)
    lift = jax.random.randint(second, (N_SEQ // 2,), 0, BLK_DEV + 1).astype(jnp.int32)
    lift = lift.at[0].set(BLK_DEV)
    counts = jnp.full((N_SEQ,), BLK_DEV, jnp.int32)
    counts = counts.at[order[:N_SEQ // 2]].add(lift)
    counts = counts.at[order[N_SEQ // 2:]].add(-lift)
    return counts.astype(jnp.int32)


def draw_owned(key, part):
    counts = owner_counts(key)
    return counts


def draw_route(key, part):
    counts = owner_counts(key)
    key = jax.random.fold_in(key, 7)
    key_dev, key_blk = jax.random.split(key)
    total = N_SEQ * BLK_DEV
    ends = jnp.cumsum(counts).astype(jnp.int32)
    starts = ends - counts
    place = jnp.arange(total, dtype=jnp.int32)
    owner = jnp.sum((ends[None, :] <= place[:, None]).astype(jnp.int32), axis=1).astype(jnp.int32)
    slot = place - starts[owner]
    devices = jax.random.permutation(key_dev, N_SEQ).astype(jnp.int32)
    source = devices[place % N_SEQ]
    orders = jax.vmap(lambda k: jax.random.permutation(k, BLK_DEV))(jax.random.split(key_blk, N_SEQ)).astype(jnp.int32)
    within = orders[source, place // N_SEQ]
    flat = source * BLK_DEV + within
    dest_row = jnp.zeros((total,), jnp.int32).at[flat].set(owner)
    slot_row = jnp.zeros((total,), jnp.int32).at[flat].set(slot)
    return jnp.stack([dest_row, slot_row]).astype(jnp.int32)


def level_of(key, shape, cuts, smallest, top_value):
    level, own = 1.0, jax.random.fold_in(key, 6)
    for axis_at, shards_of in cuts:
        draws = jnp.exp(jax.random.uniform(jax.random.fold_in(own, axis_at), (shards_of,), jnp.float32, smallest / len(cuts), top_value / len(cuts)))
        level = level * jnp.repeat(draws, shape[axis_at] // shards_of).reshape([-1 if axis == axis_at else 1 for axis in range(len(shape))])
    return level


def noise(rng, shape, scale, limit, shards=(), kind=jnp.bfloat16):
    entries = jax.random.normal(rng, shape, jnp.float32) * scale
    if len(shards) > 0:
        entries = level_of(rng, shape, shards, -0.22, 0.18) * entries
    return jnp.clip(entries, min=-limit, max=limit).astype(kind)


def setup_inputs(seed: int = 0, part: int = 0) -> dict:
    streams_of = jax.random.split(jax.random.key(seed), 10)
    own_keys = jax.random.split(jax.random.fold_in(streams_of[9], part), 10)
    return {
        "points": noise(own_keys[0], (POINTS, C), 1.0, 6.0, ((0, 16),)),
        "route": draw_route(jax.random.fold_in(jax.random.fold_in(streams_of[9], part), 71), part),
        "owned": draw_owned(jax.random.fold_in(jax.random.fold_in(streams_of[9], part), 71), part),
        "cotangent": noise(own_keys[3], (POINTS, C), 1.0, 6.0, ((0, 16),)),
        "gain": jnp.clip(1.0 + 0.18 * jax.random.normal(streams_of[4], (C,), jnp.float32), 0.1, 1.9),
        "w_qkv": noise(streams_of[5], (C, 3 * C), C ** -0.5, 0.5),
        "b_qkv": noise(streams_of[6], (3 * C,), 0.5, 3.0, (), jnp.float32),
        "w_out": noise(streams_of[7], (C, C), C ** -0.5, 0.5),
        "b_out": noise(streams_of[8], (C,), 0.5, 3.0, (), jnp.float32),
    }


EPS = 1e-05

def mult(form, left, right):
    return jnp.einsum(form, left.astype(jnp.float32), right.astype(jnp.float32))

def row_norms(local_rows, gain):
    values = local_rows.astype(jnp.float32)
    centered_rows = values - lax.optimization_barrier(jnp.mean(values, axis=-1, keepdims=True))
    inverse_deviation = lax.rsqrt(lax.optimization_barrier(jnp.mean(centered_rows * centered_rows, axis=-1, keepdims=True)) + EPS)
    standardized_input = centered_rows * inverse_deviation
    return ((standardized_input * gain).astype(jnp.bfloat16), standardized_input, inverse_deviation)

def group_parts(qkv_patch, group, width):
    cols = qkv_patch.shape[1] // 3
    lo = group * width
    query = qkv_patch[:, lo:lo + width].reshape(-1, 2, width // 2)
    keys = qkv_patch[:, cols + lo:cols + lo + width].reshape(-1, 2, width // 2)
    values = qkv_patch[:, 2 * cols + lo:2 * cols + lo + width].reshape(-1, 2, width // 2)
    return (query, keys, values)

def patch_probs(query, keys, keep, scale):
    scores = mult('qhd,khd->hqk', query, keys) * scale
    scores = jnp.where(keep[None, None, :], scores, -1e+30)
    top = lax.optimization_barrier(jnp.max(scores, axis=-1, keepdims=True))
    expo = jnp.exp(scores - top)
    return expo / lax.optimization_barrier(jnp.sum(expo, axis=-1, keepdims=True))

def patch_forward(qkv_patch, keep):
    cols = qkv_patch.shape[1] // 3
    width = 2 * (cols // HEADS)
    scale = (cols // HEADS) ** (-0.5)
    outs = []
    for group in range(HEADS // 2):
        query, keys, values = group_parts(qkv_patch, group, width)
        probs_b = patch_probs(query, keys, keep, scale).astype(jnp.bfloat16)
        outs.append(mult('hqk,khd->qhd', probs_b, values).reshape(-1, width))
    return jnp.concatenate(outs, axis=1).astype(jnp.bfloat16)

def patch_backward(qkv_patch, keep, d_attn):
    cols = qkv_patch.shape[1] // 3
    width = 2 * (cols // HEADS)
    scale = (cols // HEADS) ** (-0.5)
    grad_q, grad_k, grad_v = ([], [], [])
    for group in range(HEADS // 2):
        query, keys, values = group_parts(qkv_patch, group, width)
        probs = patch_probs(query, keys, keep, scale)
        probs_b = probs.astype(jnp.bfloat16)
        upper = d_attn[:, group * width:(group + 1) * width].reshape(-1, 2, width // 2)
        dprobs = mult('qhd,khd->hqk', upper, values)
        grad_v.append(mult('hqk,qhd->khd', probs_b, upper).reshape(-1, width))
        dscore = (probs * (dprobs - lax.optimization_barrier(jnp.sum(dprobs * probs, axis=-1, keepdims=True))) * scale).astype(jnp.bfloat16)
        grad_q.append(mult('hqk,khd->qhd', dscore, keys).reshape(-1, width))
        grad_k.append(mult('hqk,qhd->khd', dscore, query).reshape(-1, width))
    return jnp.concatenate(grad_q + grad_k + grad_v, axis=1).astype(jnp.bfloat16)

def owner_forward(local_rows, keep, gain, w_qkv, b_qkv, w_out, b_out):
    normalized_input, standardized_input, inverse_deviation = row_norms(local_rows, gain)
    query_key_value = (jnp.dot(normalized_input, w_qkv, preferred_element_type=jnp.float32) + b_qkv).astype(jnp.bfloat16)
    patches = query_key_value.reshape(-1, PATCH, query_key_value.shape[1])
    keeps = keep.reshape(-1, PATCH)
    attention_output = lax.map(lambda pair: patch_forward(pair[0], pair[1]), (patches, keeps)).reshape(local_rows.shape)
    out = jnp.dot(attention_output, w_out, preferred_element_type=jnp.float32) + b_out
    mixed = (local_rows.astype(jnp.float32) + out).astype(jnp.bfloat16)
    return (mixed, (normalized_input, standardized_input, inverse_deviation, query_key_value, attention_output))

def owner_out_grads(saved_residuals, cot_held, w_out):
    attention_output = saved_residuals[4]
    grad_w = lax.dot_general(attention_output, cot_held, (((0,), (0,)), ((), ())), preferred_element_type=jnp.float32)
    grad_b = lax.optimization_barrier(jnp.sum(cot_held.astype(jnp.float32), axis=0))
    d_attn = lax.dot_general(cot_held, w_out, (((1,), (1,)), ((), ())), preferred_element_type=jnp.float32)
    return (grad_w, grad_b, d_attn.astype(jnp.bfloat16))

def owner_in_grads(saved_residuals, keep, cot_held, d_attn, gain, w_qkv):
    normalized_input, standardized_input, inverse_deviation, query_key_value, attention_output = saved_residuals
    patches = query_key_value.reshape(-1, PATCH, query_key_value.shape[1])
    keeps = keep.reshape(-1, PATCH)
    uppers = d_attn.reshape(-1, PATCH, d_attn.shape[1])
    dqkv = lax.map(lambda trio: patch_backward(trio[0], trio[1], trio[2]), (patches, keeps, uppers))
    dqkv = dqkv.reshape(query_key_value.shape)
    normalized_gradient = lax.dot_general(dqkv, w_qkv, (((1,), (1,)), ((), ())), preferred_element_type=jnp.float32)
    grad_w = lax.dot_general(normalized_input, dqkv, (((0,), (0,)), ((), ())), preferred_element_type=jnp.float32)
    grad_b = lax.optimization_barrier(jnp.sum(dqkv.astype(jnp.float32), axis=0))
    gain_gradient = lax.optimization_barrier(jnp.sum(normalized_gradient * standardized_input, axis=0))
    standardized_gradient = normalized_gradient * gain
    inner_product = standardized_gradient - lax.optimization_barrier(jnp.mean(standardized_gradient, axis=-1, keepdims=True)) - standardized_input * lax.optimization_barrier(jnp.mean(standardized_gradient * standardized_input, axis=-1, keepdims=True))
    grad_rows = (cot_held.astype(jnp.float32) + inverse_deviation * inner_product).astype(jnp.bfloat16)
    return (grad_rows, gain_gradient, grad_w, grad_b)

def reference(points, route, owned, cotangent, gain, w_qkv, b_qkv, w_out, b_out):
    width = points.shape[1]
    dest = route[0]
    slot = route[1]
    empty = jnp.zeros((N_SEQ, OWN_MAX, BLOCK, width), jnp.bfloat16)
    held_all = empty.at[dest, slot].set(points.reshape(BLOCKS, BLOCK, width)).reshape(N_SEQ, OWN_MAX * BLOCK, width)
    cot_all = empty.at[dest, slot].set(cotangent.reshape(BLOCKS, BLOCK, width)).reshape(N_SEQ, OWN_MAX * BLOCK, width)
    row_slot = jnp.arange(OWN_MAX * BLOCK, dtype=jnp.int32) // BLOCK
    keep_all = row_slot[None, :] < owned[:, None]

    def per_owner(item):
        local_rows, cot_held, keep = item
        mixed, saved_residuals = owner_forward(local_rows, keep, gain, w_qkv, b_qkv, w_out, b_out)
        grad_wo, grad_bo, d_attn = owner_out_grads(saved_residuals, cot_held, w_out)
        grad_rows, gain_gradient, grad_wq, grad_bq = owner_in_grads(saved_residuals, keep, cot_held, d_attn, gain, w_qkv)
        return (mixed, grad_rows, gain_gradient, grad_wq, grad_bq, grad_wo, grad_bo)
    result = lax.map(per_owner, (held_all, cot_all, keep_all))
    mixed_all = result[0].reshape(N_SEQ, OWN_MAX, BLOCK, width)
    grad_all = result[1].reshape(N_SEQ, OWN_MAX, BLOCK, width)
    mixed = mixed_all[dest, slot].reshape(BLOCKS * BLOCK, width)
    grad_points = grad_all[dest, slot].reshape(BLOCKS * BLOCK, width)
    return (mixed, grad_points, lax.optimization_barrier(jnp.sum(result[2], axis=0)), lax.optimization_barrier(jnp.sum(result[3], axis=0)), lax.optimization_barrier(jnp.sum(result[4], axis=0)), lax.optimization_barrier(jnp.sum(result[5], axis=0)), lax.optimization_barrier(jnp.sum(result[6], axis=0)))
```

```python
import functools

import jax
import jax.numpy as jnp
from jax import lax
from jax.experimental import pallas as pl
from jax.experimental.pallas import tpu as pltpu
from jax.sharding import PartitionSpec as P

HEADS = 8
EPS = 1e-05
EMPTY = 64.0
MASKED = -1e30

F32 = jnp.float32
BF16 = jnp.bfloat16

VMEM = pl.BlockSpec(memory_space=pltpu.VMEM)
SMEM = pl.BlockSpec(memory_space=pltpu.SMEM)
PARAMS = pltpu.CompilerParams(vmem_limit_bytes=48 * 1024 * 1024)


def matmul(left, right, dims=((1,), (0,))):
    return lax.dot_general(left, right, (dims, ((), ())), preferred_element_type=F32)


def send_rows(route_ref, shape, axis, block_rows):
    place = lax.broadcasted_iota(jnp.int32, shape, axis)
    target = jnp.zeros(shape, jnp.int32)
    for block in range(shape[axis] // block_rows):
        first = block * block_rows
        moved = route_ref[0, block] * block_rows + place - first
        target = jnp.where(place >= first, moved, target)
    return target


def scatter_kernel(block_rows, route_ref, points_ref, cot_ref, out_ref):
    rows, width = points_ref.shape
    target = send_rows(route_ref, (1, rows), 1, block_rows)
    index = lax.broadcasted_iota(jnp.int32, (out_ref.shape[0], rows), 0)
    pick = jnp.where(index == target, 1.0, 0.0).astype(BF16)
    ones = jnp.ones((rows, width), BF16)
    moved = matmul(pick, jnp.concatenate([points_ref[...], ones], axis=1))
    empty = (1.0 - moved[:, width:]) * EMPTY
    out_ref[:, :width] = (moved[:, :width] + empty).astype(BF16)
    out_ref[:, width:] = matmul(pick, cot_ref[...]).astype(BF16)


def owner_kernel(layout, got_ref, gain_ref, w_qkv_ref, b_qkv_ref, w_out_ref, b_out_ref, *outs):
    rows = got_ref.shape[0]
    width = got_ref.shape[1] // 2
    head = width // HEADS
    scale = head ** (-0.5)
    gain = gain_ref[...]
    w_qkv = w_qkv_ref[...]
    w_out = w_out_ref[...]

    points = got_ref[:, :width].astype(F32)
    cot = got_ref[:, width:]
    centered = points - jnp.mean(points, axis=-1, keepdims=True)
    rstd = lax.rsqrt(jnp.mean(centered * centered, axis=-1, keepdims=True) + EPS)
    xhat = centered * rstd
    normed = (xhat * gain).astype(BF16)
    qkv = (matmul(normed, w_qkv) + b_qkv_ref[...]).astype(BF16)
    query, keys, values = qkv[:, :width], qkv[:, width : 2 * width], qkv[:, 2 * width :]
    d_attn = matmul(cot, w_out, ((1,), (1,))).astype(BF16)
    d_attn_t = matmul(w_out, cot, ((1,), (1,))).astype(BF16)
    d_attn_s = (d_attn.astype(F32) * scale).astype(BF16)

    keys_t = keys.T
    values_t = values.T
    keys_s = (keys.astype(F32) * scale).astype(BF16)
    lane = lax.broadcasted_iota(jnp.int32, (rows, width), 1)
    hidden = jnp.where(points > EMPTY / 2, MASKED, 0.0).astype(BF16)
    query_x = jnp.concatenate([query, jnp.where(lane == 0, 1.0, 0.0).astype(BF16)], axis=1)

    attn_t, dq_t = [], []
    d_keys = jnp.zeros((rows, width), F32)
    d_values = jnp.zeros((rows, width), F32)
    for h in range(HEADS):
        lo, hi = h * head, (h + 1) * head
        mine = (lane >= lo) & (lane < hi)
        keys_h = jnp.concatenate([jnp.where(mine, keys_s, 0), hidden], axis=1)
        scores = matmul(keys_h, query_x, ((1,), (1,)))
        expo = jnp.exp(scores - jnp.max(scores, axis=0, keepdims=True))
        probs = expo * (1.0 / jnp.sum(expo, axis=0, keepdims=True))
        probs_b = probs.astype(BF16)
        out_t = matmul(values_t[lo:hi, :], probs_b)
        attn_t.append(out_t)
        inner = jnp.sum(out_t * d_attn_t[lo:hi, :].astype(F32), axis=0, keepdims=True) * scale
        d_probs = matmul(jnp.where(mine, values, 0), d_attn_s, ((1,), (1,)))
        d_score = (probs * (d_probs - inner)).astype(BF16)
        dq_t.append(matmul(keys_t[lo:hi, :], d_score))
        d_values = jnp.where(mine, matmul(probs_b, d_attn), d_values)
        d_keys = jnp.where(mine, matmul(d_score, query), d_keys)

    attn_t = jnp.concatenate(attn_t, axis=0)
    attn = attn_t.T.astype(BF16)
    mixed = points + (matmul(attn, w_out) + b_out_ref[...])
    grad_w_out = matmul(attn_t.astype(BF16), cot)
    grad_b_out = jnp.sum(cot.astype(F32), axis=0, keepdims=True)

    d_query = jnp.concatenate(dq_t, axis=0).T
    d_qkv = jnp.concatenate([d_query, d_keys, d_values], axis=1).astype(BF16)
    d_normed = matmul(d_qkv, w_qkv, ((1,), (1,)))
    grad_w_qkv = matmul(normed, d_qkv, ((0,), (0,)))
    grad_b_qkv = jnp.sum(d_qkv.astype(F32), axis=0, keepdims=True)
    grad_gain = jnp.sum(d_normed * xhat, axis=0, keepdims=True)
    d_xhat = d_normed * gain
    inner = (
        d_xhat
        - jnp.mean(d_xhat, axis=-1, keepdims=True)
        - xhat * jnp.mean(d_xhat * xhat, axis=-1, keepdims=True)
    )
    grad_rows = cot.astype(F32) + rstd * inner

    back = jnp.concatenate([mixed.astype(BF16), grad_rows.astype(BF16)], axis=1)
    sums = jnp.concatenate(
        [
            grad_b_qkv[:, : 2 * width],
            jnp.concatenate([grad_b_qkv[:, 2 * width :], grad_b_out], axis=1),
            jnp.concatenate([grad_gain, jnp.zeros_like(grad_gain)], axis=1),
            jnp.zeros((5, 2 * width), F32),
        ],
        axis=0,
    )
    left = grad_w_qkv[:, : 2 * width]
    right = jnp.concatenate([grad_w_qkv[:, 2 * width :], grad_w_out], axis=1)
    if layout is None:
        back_ref, left_ref, right_ref, sums_ref = outs
        back_ref[...] = back
        left_ref[...] = left.astype(BF16)
        right_ref[...] = right.astype(BF16)
        sums_ref[...] = sums.astype(BF16)
        return
    devs, block_rows, share = layout
    (message_ref,) = outs
    sums16 = jnp.concatenate([sums, jnp.zeros_like(sums)], axis=0).astype(BF16)
    for dev in range(devs):
        message_ref[dev, :block_rows] = back[dev * block_rows : (dev + 1) * block_rows]
        message_ref[dev, block_rows : block_rows + 2 * share] = jnp.concatenate(
            [left[dev * share : (dev + 1) * share], right[dev * share : (dev + 1) * share]], axis=0
        ).astype(BF16)
        message_ref[dev, block_rows + 2 * share :] = sums16


def share_kernel(block_rows, share, message_ref, out_ref, sums_ref):
    devs = message_ref.shape[0]
    total = message_ref[0, block_rows:].astype(F32)
    for dev in range(1, devs):
        total = total + message_ref[dev, block_rows:].astype(F32)
    mine = total[: 2 * share].astype(BF16)
    for dev in range(devs):
        out_ref[dev] = mine
    sums_ref[...] = total[2 * share : 2 * share + 8]


def return_kernel(block_rows, route_ref, message_ref, mixed_ref, grad_ref):
    rows, width = mixed_ref.shape
    target = send_rows(route_ref, (rows, 1), 0, block_rows)
    if len(message_ref.shape) == 3:
        back = jnp.concatenate(
            [message_ref[dev, :block_rows] for dev in range(message_ref.shape[0])], axis=0
        )
    else:
        back = message_ref[...]
    index = lax.broadcasted_iota(jnp.int32, (rows, back.shape[0]), 1)
    pick = jnp.where(index == target, 1.0, 0.0).astype(BF16)
    moved = matmul(pick, back).astype(BF16)
    mixed_ref[...] = moved[:, :width]
    grad_ref[...] = moved[:, width:]


def weights_kernel(share, got_ref, w_qkv_ref, w_out_ref):
    width = w_out_ref.shape[1]
    for dev in range(got_ref.shape[0]):
        both = got_ref[dev].astype(F32)
        rows = slice(dev * share, (dev + 1) * share)
        w_qkv_ref[rows, : 2 * width] = both[:share]
        w_qkv_ref[rows, 2 * width :] = both[share:, :width]
        w_out_ref[rows, :] = both[share:, width:]


def exchange(message):
    return lax.all_to_all(message, "seq", split_axis=0, concat_axis=0, tiled=True)


def local(points, route, owned, cotangent, gain, w_qkv, b_qkv, w_out, b_out):
    devs = lax.axis_size("seq")
    rows, width = points.shape
    block_rows = rows // route.shape[1]
    held = devs * block_rows
    share = width // devs
    aligned = block_rows % 16 == 0 and share % 8 == 0

    def shape(*dims, dtype=BF16):
        return jax.ShapeDtypeStruct(dims, dtype)

    sent = pl.pallas_call(
        functools.partial(scatter_kernel, block_rows),
        out_shape=shape(held, 2 * width),
        in_specs=[SMEM, VMEM, VMEM],
        out_specs=VMEM,
        compiler_params=PARAMS,
    )(route, points, cotangent)
    got = exchange(sent.reshape(devs, block_rows, 2 * width)).reshape(held, 2 * width)

    weights = (gain[None, :], w_qkv, b_qkv[None, :], w_out, b_out[None, :])
    if aligned:
        message = pl.pallas_call(
            functools.partial(owner_kernel, (devs, block_rows, share)),
            out_shape=shape(devs, block_rows + 2 * share + 16, 2 * width),
            in_specs=[VMEM] * 6,
            out_specs=VMEM,
            compiler_params=PARAMS,
        )(got, *weights)
        message = exchange(message)
        mine, sums = pl.pallas_call(
            functools.partial(share_kernel, block_rows, share),
            out_shape=(shape(devs, 2 * share, 2 * width), shape(8, 2 * width, dtype=F32)),
            in_specs=[VMEM],
            out_specs=(VMEM, VMEM),
            compiler_params=PARAMS,
        )(message)
        back = message
    else:
        back, left, right, sums = pl.pallas_call(
            functools.partial(owner_kernel, None),
            out_shape=(
                shape(held, 2 * width),
                shape(width, 2 * width),
                shape(width, 2 * width),
                shape(8, 2 * width),
            ),
            in_specs=[VMEM] * 6,
            out_specs=(VMEM,) * 4,
            compiler_params=PARAMS,
        )(got, *weights)
        message = jnp.concatenate(
            [
                back.reshape(devs, block_rows, 2 * width),
                left.reshape(devs, share, 2 * width),
                right.reshape(devs, share, 2 * width),
                jnp.broadcast_to(sums[None], (devs, 8, 2 * width)),
            ],
            axis=1,
        )
        message = exchange(message)
        total = jnp.sum(message[:, block_rows:].astype(F32), axis=0)
        mine = jnp.broadcast_to(total[None, : 2 * share].astype(BF16), (devs, 2 * share, 2 * width))
        sums = total[2 * share :]
        back = message[:, :block_rows].reshape(held, 2 * width)

    got_weights = exchange(mine)
    mixed, grad_points = pl.pallas_call(
        functools.partial(return_kernel, block_rows),
        out_shape=(shape(rows, width), shape(rows, width)),
        in_specs=[SMEM, VMEM],
        out_specs=(VMEM, VMEM),
        compiler_params=PARAMS,
    )(route, back)
    if aligned:
        grad_wq, grad_wo = pl.pallas_call(
            functools.partial(weights_kernel, share),
            out_shape=(shape(width, 3 * width, dtype=F32), shape(width, width, dtype=F32)),
            in_specs=[VMEM],
            out_specs=(VMEM, VMEM),
            compiler_params=PARAMS,
        )(got_weights)
    else:
        both = got_weights.astype(F32)
        left = both[:, :share].reshape(width, 2 * width)
        right = both[:, share:].reshape(width, 2 * width)
        grad_wq = jnp.concatenate([left, right[:, :width]], axis=1)
        grad_wo = right[:, width:]
    flat = sums[:3].reshape(-1)
    return (
        mixed,
        grad_points,
        flat[4 * width : 5 * width],
        grad_wq,
        flat[: 3 * width],
        grad_wo,
        flat[3 * width : 4 * width],
    )


def solution(mesh):
    placed = (
        P(("parts", "seq"), None),
        P(None, ("parts", "seq")),
        P(("parts", "seq")),
        P(("parts", "seq"), None),
        P(),
        P(),
        P(),
        P(),
        P(),
    )
    return jax.shard_map(
        local,
        mesh=mesh,
        in_specs=placed,
        out_specs=(
            P(("parts", "seq"), None),
            P(("parts", "seq"), None),
            P("parts"),
            P("parts", None),
            P("parts"),
            P("parts", None),
            P("parts"),
        ),
        check_vma=False,
    )
```

```python
import functools

import jax
import jax.numpy as jnp
from jax import lax
from jax.experimental import pallas as pl
from jax.experimental.pallas import tpu as pltpu
from jax.sharding import PartitionSpec as P

HEADS = 8
EPS = 1e-05
EMPTY = 64.0
MASKED = -1e30

F32 = jnp.float32
BF16 = jnp.bfloat16

VMEM = pl.BlockSpec(memory_space=pltpu.VMEM)
ANY = pl.BlockSpec(memory_space=pl.ANY)
SMEM = pl.BlockSpec(memory_space=pltpu.SMEM)
PARAMS = pltpu.CompilerParams(vmem_limit_bytes=48 * 1024 * 1024)


def matmul(left, right, dims=((1,), (0,))):
    return lax.dot_general(left, right, (dims, ((), ())), preferred_element_type=F32)


def send_rows(route_ref, shape, axis, block_rows):
    place = lax.broadcasted_iota(jnp.int32, shape, axis)
    target = jnp.zeros(shape, jnp.int32)
    for block in range(shape[axis] // block_rows):
        first = block * block_rows
        moved = route_ref[0, block] * block_rows + place - first
        target = jnp.where(place >= first, moved, target)
    return target


def scatter_kernel(block_rows, route_hbm, points_hbm, cot_hbm, out_ref, route_ref, points_ref, cot_ref, sems):
    copies = [
        pltpu.make_async_copy(source, target, sems.at[at])
        for at, (source, target) in enumerate(
            ((route_hbm, route_ref), (points_hbm, points_ref), (cot_hbm, cot_ref))
        )
    ]
    for copy in copies:
        copy.start()
    for copy in copies:
        copy.wait()
    rows, width = points_ref.shape
    target = send_rows(route_ref, (1, rows), 1, block_rows)
    index = lax.broadcasted_iota(jnp.int32, (out_ref.shape[0], rows), 0)
    pick = jnp.where(index == target, 1.0, 0.0).astype(BF16)
    ones = jnp.ones((rows, width), BF16)
    moved = matmul(pick, jnp.concatenate([points_ref[...], ones], axis=1))
    empty = (1.0 - moved[:, width:]) * EMPTY
    out_ref[:, :width] = (moved[:, :width] + empty).astype(BF16)
    out_ref[:, width:] = matmul(pick, cot_ref[...]).astype(BF16)


def owner_kernel(layout, got_ref, gain_ref, w_qkv_ref, b_qkv_ref, w_out_ref, b_out_ref, *outs):
    rows = got_ref.shape[0]
    width = got_ref.shape[1] // 2
    head = width // HEADS
    scale = head ** (-0.5)
    gain = gain_ref[...]
    w_qkv = w_qkv_ref[...]
    w_out = w_out_ref[...]

    points = got_ref[:, :width].astype(F32)
    cot = got_ref[:, width:]
    centered = points - jnp.mean(points, axis=-1, keepdims=True)
    rstd = lax.rsqrt(jnp.mean(centered * centered, axis=-1, keepdims=True) + EPS)
    xhat = centered * rstd
    normed = (xhat * gain).astype(BF16)
    qkv = (matmul(normed, w_qkv) + b_qkv_ref[...]).astype(BF16)
    query, keys, values = qkv[:, :width], qkv[:, width : 2 * width], qkv[:, 2 * width :]
    d_attn = matmul(cot, w_out, ((1,), (1,))).astype(BF16)
    d_attn_t = matmul(w_out, cot, ((1,), (1,))).astype(BF16)
    d_attn_s = (d_attn.astype(F32) * scale).astype(BF16)

    keys_t = keys.T
    values_t = values.T
    keys_s = (keys.astype(F32) * scale).astype(BF16)
    lane = lax.broadcasted_iota(jnp.int32, (rows, width), 1)
    hidden = jnp.where(points > EMPTY / 2, MASKED, 0.0).astype(BF16)
    query_x = jnp.concatenate([query, jnp.where(lane == 0, 1.0, 0.0).astype(BF16)], axis=1)

    attn_t, dq_t = [], []
    d_keys = jnp.zeros((rows, width), F32)
    d_values = jnp.zeros((rows, width), F32)
    for h in range(HEADS):
        lo, hi = h * head, (h + 1) * head
        mine = (lane >= lo) & (lane < hi)
        keys_h = jnp.concatenate([jnp.where(mine, keys_s, 0), hidden], axis=1)
        scores = matmul(keys_h, query_x, ((1,), (1,)))
        expo = jnp.exp(scores - jnp.max(scores, axis=0, keepdims=True))
        probs = expo * (1.0 / jnp.sum(expo, axis=0, keepdims=True))
        probs_b = probs.astype(BF16)
        out_t = matmul(values_t[lo:hi, :], probs_b)
        attn_t.append(out_t)
        inner = jnp.sum(out_t * d_attn_t[lo:hi, :].astype(F32), axis=0, keepdims=True) * scale
        d_probs = matmul(jnp.where(mine, values, 0), d_attn_s, ((1,), (1,)))
        d_score = (probs * (d_probs - inner)).astype(BF16)
        dq_t.append(matmul(keys_t[lo:hi, :], d_score))
        d_values = jnp.where(mine, matmul(probs_b, d_attn), d_values)
        d_keys = jnp.where(mine, matmul(d_score, query), d_keys)

    attn_t = jnp.concatenate(attn_t, axis=0)
    attn = attn_t.T.astype(BF16)
    mixed = points + (matmul(attn, w_out) + b_out_ref[...])
    grad_w_out = matmul(attn_t.astype(BF16), cot)
    grad_b_out = jnp.sum(cot.astype(F32), axis=0, keepdims=True)

    d_query = jnp.concatenate(dq_t, axis=0).T
    d_qkv = jnp.concatenate([d_query, d_keys, d_values], axis=1).astype(BF16)
    d_normed = matmul(d_qkv, w_qkv, ((1,), (1,)))
    grad_w_qkv = matmul(normed, d_qkv, ((0,), (0,)))
    grad_b_qkv = jnp.sum(d_qkv.astype(F32), axis=0, keepdims=True)
    grad_gain = jnp.sum(d_normed * xhat, axis=0, keepdims=True)
    d_xhat = d_normed * gain
    inner = (
        d_xhat
        - jnp.mean(d_xhat, axis=-1, keepdims=True)
        - xhat * jnp.mean(d_xhat * xhat, axis=-1, keepdims=True)
    )
    grad_rows = cot.astype(F32) + rstd * inner

    back = jnp.concatenate([mixed.astype(BF16), grad_rows.astype(BF16)], axis=1)
    sums = jnp.concatenate(
        [
            grad_b_qkv[:, : 2 * width],
            jnp.concatenate([grad_b_qkv[:, 2 * width :], grad_b_out], axis=1),
            jnp.concatenate([grad_gain, jnp.zeros_like(grad_gain)], axis=1),
            jnp.zeros((5, 2 * width), F32),
        ],
        axis=0,
    )
    left = grad_w_qkv[:, : 2 * width]
    right = jnp.concatenate([grad_w_qkv[:, 2 * width :], grad_w_out], axis=1)
    if layout is None:
        back_ref, left_ref, right_ref, sums_ref = outs
        back_ref[...] = back
        left_ref[...] = left.astype(BF16)
        right_ref[...] = right.astype(BF16)
        sums_ref[...] = sums.astype(BF16)
        return
    devs, block_rows, share = layout
    (message_ref,) = outs
    for dev in range(devs):
        message_ref[dev, :block_rows] = back[dev * block_rows : (dev + 1) * block_rows]
        message_ref[dev, block_rows : block_rows + 2 * share] = jnp.concatenate(
            [left[dev * share : (dev + 1) * share], right[dev * share : (dev + 1) * share]], axis=0
        ).astype(BF16)
        message_ref[dev, block_rows + 2 * share :] = sums.astype(BF16)


def share_kernel(block_rows, share, message_ref, out_ref, sums_ref):
    devs = message_ref.shape[0]
    total = message_ref[0, block_rows:].astype(F32)
    for dev in range(1, devs):
        total = total + message_ref[dev, block_rows:].astype(F32)
    mine = total[: 2 * share].astype(BF16)
    out_ref[...] = mine
    sums_ref[...] = total[2 * share : 2 * share + 8]


def return_kernel(block_rows, route_ref, message_ref, mixed_ref, grad_ref):
    rows, width = mixed_ref.shape
    target = send_rows(route_ref, (rows, 1), 0, block_rows)
    if len(message_ref.shape) == 3:
        back = jnp.concatenate(
            [message_ref[dev, :block_rows] for dev in range(message_ref.shape[0])], axis=0
        )
    else:
        back = message_ref[...]
    index = lax.broadcasted_iota(jnp.int32, (rows, back.shape[0]), 1)
    pick = jnp.where(index == target, 1.0, 0.0).astype(BF16)
    moved = matmul(pick, back).astype(BF16)
    mixed_ref[...] = moved[:, :width]
    grad_ref[...] = moved[:, width:]


def weights_kernel(share, place_ref, *refs):
    *got_refs, w_qkv_ref, w_out_ref = refs
    width = w_out_ref.shape[1]
    near = len(got_refs)
    far = w_out_ref.shape[0] // share // near
    me = place_ref[0]
    for low, got_ref in enumerate(got_refs):
        for high in range(far):
            both = got_ref[2 * share * high : 2 * share * (high + 1)].astype(F32)
            source = lax.rem(me // near - high + far, far) * near + (lax.rem(me, near) ^ low)
            rows = pl.ds(pl.multiple_of(source * share, share), share)
            w_qkv_ref[rows, : 2 * width] = both[:share]
            w_qkv_ref[rows, 2 * width :] = both[share:, :width]
            w_out_ref[rows, :] = both[share:, width:]


def exchange(message):
    return lax.all_to_all(message, "seq", split_axis=0, concat_axis=0, tiled=True)


def gather_far(piece, devs, near):
    pieces = [piece]
    for step in range(1, devs // near):
        pairs = [(dev, (dev + step * near) % devs) for dev in range(devs)]
        pieces.append(lax.ppermute(piece, "seq", pairs))
    return jnp.concatenate(pieces, axis=0)


def gather_near(piece, devs, near):
    pieces = [piece]
    for low in range(1, near):
        pieces.append(lax.ppermute(piece, "seq", [(dev, dev ^ low) for dev in range(devs)]))
    return pieces


def local(points, route, owned, cotangent, gain, w_qkv, b_qkv, w_out, b_out):
    devs = lax.axis_size("seq")
    rows, width = points.shape
    block_rows = rows // route.shape[1]
    held = devs * block_rows
    share = width // devs
    aligned = block_rows % 16 == 0 and share % 8 == 0

    def shape(*dims, dtype=BF16):
        return jax.ShapeDtypeStruct(dims, dtype)

    sent = pl.pallas_call(
        functools.partial(scatter_kernel, block_rows),
        out_shape=shape(held, 2 * width),
        in_specs=[ANY] * 3,
        out_specs=VMEM,
        scratch_shapes=[
            pltpu.SMEM(route.shape, route.dtype),
            pltpu.VMEM(points.shape, points.dtype),
            pltpu.VMEM(cotangent.shape, cotangent.dtype),
            pltpu.SemaphoreType.DMA((3,)),
        ],
        compiler_params=PARAMS,
    )(route, points, cotangent)
    got = exchange(sent.reshape(devs, block_rows, 2 * width)).reshape(held, 2 * width)

    weights = (gain[None, :], w_qkv, b_qkv[None, :], w_out, b_out[None, :])
    if aligned:
        message = pl.pallas_call(
            functools.partial(owner_kernel, (devs, block_rows, share)),
            out_shape=shape(devs, block_rows + 2 * share + 8, 2 * width),
            in_specs=[VMEM] * 6,
            out_specs=VMEM,
            compiler_params=PARAMS,
        )(got, *weights)
        message = exchange(message)
        mine, sums = pl.pallas_call(
            functools.partial(share_kernel, block_rows, share),
            out_shape=(shape(2 * share, 2 * width), shape(8, 2 * width, dtype=F32)),
            in_specs=[VMEM],
            out_specs=(VMEM, VMEM),
            compiler_params=PARAMS,
        )(message)
        back = message
    else:
        back, left, right, sums = pl.pallas_call(
            functools.partial(owner_kernel, None),
            out_shape=(
                shape(held, 2 * width),
                shape(width, 2 * width),
                shape(width, 2 * width),
                shape(8, 2 * width),
            ),
            in_specs=[VMEM] * 6,
            out_specs=(VMEM,) * 4,
            compiler_params=PARAMS,
        )(got, *weights)
        message = jnp.concatenate(
            [
                back.reshape(devs, block_rows, 2 * width),
                left.reshape(devs, share, 2 * width),
                right.reshape(devs, share, 2 * width),
                jnp.broadcast_to(sums[None], (devs, 8, 2 * width)),
            ],
            axis=1,
        )
        message = exchange(message)
        total = jnp.sum(message[:, block_rows:].astype(F32), axis=0)
        mine = total[: 2 * share].astype(BF16)
        sums = total[2 * share :]
        back = message[:, :block_rows].reshape(held, 2 * width)

    near = 4
    pieces = gather_near(gather_far(mine, devs, near), devs, near)
    me = lax.axis_index("seq").astype(jnp.int32)
    mixed, grad_points = pl.pallas_call(
        functools.partial(return_kernel, block_rows),
        out_shape=(shape(rows, width), shape(rows, width)),
        in_specs=[SMEM, VMEM],
        out_specs=(VMEM, VMEM),
        compiler_params=PARAMS,
    )(route, back)
    if aligned:
        grad_wq, grad_wo = pl.pallas_call(
            functools.partial(weights_kernel, share),
            out_shape=(shape(width, 3 * width, dtype=F32), shape(width, width, dtype=F32)),
            in_specs=[SMEM] + [VMEM] * near,
            out_specs=(VMEM, VMEM),
            compiler_params=PARAMS,
        )(me[None], *pieces)
    else:
        far = devs // near
        by_low = jnp.stack(pieces).reshape(near, far, 2 * share, 2 * width).astype(F32)
        low = lax.rem(me, near) ^ jnp.arange(near, dtype=jnp.int32)
        high = lax.rem(me // near + far - jnp.arange(far, dtype=jnp.int32), far)
        both = by_low[low][:, high].transpose(1, 0, 2, 3).reshape(devs, 2 * share, 2 * width)
        left = both[:, :share].reshape(width, 2 * width)
        right = both[:, share:].reshape(width, 2 * width)
        grad_wq = jnp.concatenate([left, right[:, :width]], axis=1)
        grad_wo = right[:, width:]
    flat = sums[:3].reshape(-1)
    return (
        mixed,
        grad_points,
        flat[4 * width : 5 * width],
        grad_wq,
        flat[: 3 * width],
        grad_wo,
        flat[3 * width : 4 * width],
    )


def solution(mesh):
    placed = (
        P(("parts", "seq"), None),
        P(None, ("parts", "seq")),
        P(("parts", "seq")),
        P(("parts", "seq"), None),
        P(),
        P(),
        P(),
        P(),
        P(),
    )
    return jax.shard_map(
        local,
        mesh=mesh,
        in_specs=placed,
        out_specs=(
            P(("parts", "seq"), None),
            P(("parts", "seq"), None),
            P("parts"),
            P("parts", None),
            P("parts"),
            P("parts", None),
            P("parts"),
        ),
        check_vma=False,
    )
```

```python
import functools

import jax
import jax.numpy as jnp
from jax import lax
from jax.experimental import pallas as pl
from jax.experimental.pallas import tpu as pltpu
from jax.sharding import PartitionSpec as P

HEADS = 8
EPS = 1e-05
EMPTY = 64.0
MASKED = -1e30

F32 = jnp.float32
BF16 = jnp.bfloat16

VMEM = pl.BlockSpec(memory_space=pltpu.VMEM)
ANY = pl.BlockSpec(memory_space=pl.ANY)
SMEM = pl.BlockSpec(memory_space=pltpu.SMEM)
PARAMS = pltpu.CompilerParams(vmem_limit_bytes=48 * 1024 * 1024)


def matmul(left, right, dims=((1,), (0,))):
    return lax.dot_general(left, right, (dims, ((), ())), preferred_element_type=F32)


def send_rows(route_ref, shape, axis, block_rows, pieces):
    me = lax.axis_index("seq") if pieces > 1 else 0
    place = lax.broadcasted_iota(jnp.int32, shape, axis)
    target = jnp.zeros(shape, jnp.int32)
    for block in range(shape[axis] // block_rows):
        first = block * block_rows
        moved = (route_ref[0, block] ^ me) * block_rows + place - first
        target = jnp.where(place >= first, moved, target)
    return target


def scatter_kernel(block_rows, route_hbm, points_hbm, cot_hbm, *refs):
    *outs, route_ref, points_ref, cot_ref, sems = refs
    copies = [
        pltpu.make_async_copy(source, target, sems.at[at])
        for at, (source, target) in enumerate(
            ((route_hbm, route_ref), (points_hbm, points_ref), (cot_hbm, cot_ref))
        )
    ]
    for copy in copies:
        copy.start()
    for copy in copies:
        copy.wait()
    rows, width = points_ref.shape
    held = outs[0].shape[0] * len(outs)
    target = send_rows(route_ref, (1, rows), 1, block_rows, len(outs))
    index = lax.broadcasted_iota(jnp.int32, (held, rows), 0)
    pick = jnp.where(index == target, 1.0, 0.0).astype(BF16)
    ones = jnp.ones((rows, width), BF16)
    moved = matmul(pick, jnp.concatenate([points_ref[...], ones], axis=1))
    empty = (1.0 - moved[:, width:]) * EMPTY
    points = (moved[:, :width] + empty).astype(BF16)
    cot = matmul(pick, cot_ref[...]).astype(BF16)
    for at, out_ref in enumerate(outs):
        span = slice(at * out_ref.shape[0], (at + 1) * out_ref.shape[0])
        out_ref[:, :width] = points[span]
        out_ref[:, width:] = cot[span]


def owner_kernel(pieces, *refs):
    got_refs, refs = refs[:pieces], refs[pieces:]
    gain_ref, w_qkv_ref, b_qkv_ref, w_out_ref, b_out_ref, *outs = refs
    got = jnp.concatenate([got_ref[...] for got_ref in got_refs], axis=0)
    rows, width = got.shape[0], got.shape[1] // 2
    head = width // HEADS
    scale = head ** (-0.5)
    gain = gain_ref[...]
    w_qkv = w_qkv_ref[...]
    w_out = w_out_ref[...]

    points = got[:, :width].astype(F32)
    cot = got[:, width:]
    centered = points - jnp.mean(points, axis=-1, keepdims=True)
    rstd = lax.rsqrt(jnp.mean(centered * centered, axis=-1, keepdims=True) + EPS)
    xhat = centered * rstd
    normed = (xhat * gain).astype(BF16)
    qkv = (matmul(normed, w_qkv) + b_qkv_ref[...]).astype(BF16)
    query, keys, values = qkv[:, :width], qkv[:, width : 2 * width], qkv[:, 2 * width :]
    d_attn = matmul(cot, w_out, ((1,), (1,))).astype(BF16)
    d_attn_t = matmul(w_out, cot, ((1,), (1,))).astype(BF16)
    d_attn_s = (d_attn.astype(F32) * scale).astype(BF16)

    keys_t = keys.T
    values_t = values.T
    keys_s = (keys.astype(F32) * scale).astype(BF16)
    lane = lax.broadcasted_iota(jnp.int32, (rows, width), 1)
    hidden = jnp.where(points > EMPTY / 2, MASKED, 0.0).astype(BF16)
    query_x = jnp.concatenate([query, jnp.where(lane == 0, 1.0, 0.0).astype(BF16)], axis=1)

    attn_t, dq_t = [], []
    d_keys = jnp.zeros((rows, width), F32)
    d_values = jnp.zeros((rows, width), F32)
    for h in range(HEADS):
        lo, hi = h * head, (h + 1) * head
        mine = (lane >= lo) & (lane < hi)
        keys_h = jnp.concatenate([jnp.where(mine, keys_s, 0), hidden], axis=1)
        scores = matmul(keys_h, query_x, ((1,), (1,)))
        expo = jnp.exp(scores - jnp.max(scores, axis=0, keepdims=True))
        probs = expo * (1.0 / jnp.sum(expo, axis=0, keepdims=True))
        probs_b = probs.astype(BF16)
        out_t = matmul(values_t[lo:hi, :], probs_b)
        attn_t.append(out_t)
        inner = jnp.sum(out_t * d_attn_t[lo:hi, :].astype(F32), axis=0, keepdims=True) * scale
        d_probs = matmul(jnp.where(mine, values, 0), d_attn_s, ((1,), (1,)))
        d_score = (probs * (d_probs - inner)).astype(BF16)
        dq_t.append(matmul(keys_t[lo:hi, :], d_score))
        d_values = jnp.where(mine, matmul(probs_b, d_attn), d_values)
        d_keys = jnp.where(mine, matmul(d_score, query), d_keys)

    attn_t = jnp.concatenate(attn_t, axis=0)
    attn = attn_t.T.astype(BF16)
    mixed = points + (matmul(attn, w_out) + b_out_ref[...])
    grad_w_out = matmul(attn_t.astype(BF16), cot)
    grad_b_out = jnp.sum(cot.astype(F32), axis=0, keepdims=True)

    d_query = jnp.concatenate(dq_t, axis=0).T
    d_qkv = jnp.concatenate([d_query, d_keys, d_values], axis=1).astype(BF16)
    d_normed = matmul(d_qkv, w_qkv, ((1,), (1,)))
    grad_w_qkv = matmul(normed, d_qkv, ((0,), (0,)))
    grad_b_qkv = jnp.sum(d_qkv.astype(F32), axis=0, keepdims=True)
    grad_gain = jnp.sum(d_normed * xhat, axis=0, keepdims=True)
    d_xhat = d_normed * gain
    inner = (
        d_xhat
        - jnp.mean(d_xhat, axis=-1, keepdims=True)
        - xhat * jnp.mean(d_xhat * xhat, axis=-1, keepdims=True)
    )
    grad_rows = cot.astype(F32) + rstd * inner

    back = jnp.concatenate([mixed.astype(BF16), grad_rows.astype(BF16)], axis=1)
    sums = jnp.concatenate(
        [
            grad_b_qkv[:, : 2 * width],
            jnp.concatenate([grad_b_qkv[:, 2 * width :], grad_b_out], axis=1),
            jnp.concatenate([grad_gain, jnp.zeros_like(grad_gain)], axis=1),
            jnp.zeros((5, 2 * width), F32),
        ],
        axis=0,
    )
    left = grad_w_qkv[:, : 2 * width]
    right = jnp.concatenate([grad_w_qkv[:, 2 * width :], grad_w_out], axis=1)
    if pieces == 1:
        back_ref, left_ref, right_ref, sums_ref = outs
        back_ref[...] = back
        left_ref[...] = left.astype(BF16)
        right_ref[...] = right.astype(BF16)
        sums_ref[...] = sums.astype(BF16)
        return
    *message_refs, left_ref, right_ref = outs
    left_ref[...] = left
    right_ref[...] = right
    block_rows, share = rows // pieces, width // pieces
    me = lax.axis_index("seq")
    for at, message_ref in enumerate(message_refs):
        theirs = pl.ds(pl.multiple_of((me ^ at) * share, share), share)
        message_ref[:block_rows] = back[at * block_rows : (at + 1) * block_rows]
        message_ref[block_rows : block_rows + 2 * share] = jnp.concatenate(
            [left_ref[theirs], right_ref[theirs]], axis=0
        ).astype(BF16)
        message_ref[block_rows + 2 * share :] = sums.astype(BF16)


def share_kernel(block_rows, share, *refs):
    *message_refs, out_ref, sums_ref = refs
    total = message_refs[0][block_rows:].astype(F32)
    for message_ref in message_refs[1:]:
        total = total + message_ref[block_rows:].astype(F32)
    out_ref[...] = total[: 2 * share].astype(BF16)
    sums_ref[...] = total[2 * share :]


def return_kernel(block_rows, route_ref, *refs):
    *back_refs, mixed_ref, grad_ref = refs
    rows, width = mixed_ref.shape
    target = send_rows(route_ref, (rows, 1), 0, block_rows, len(back_refs))
    if len(back_refs) > 1:
        back = jnp.concatenate([back_ref[:block_rows] for back_ref in back_refs], axis=0)
    else:
        back = back_refs[0][...]
    index = lax.broadcasted_iota(jnp.int32, (rows, back.shape[0]), 1)
    pick = jnp.where(index == target, 1.0, 0.0).astype(BF16)
    moved = matmul(pick, back).astype(BF16)
    mixed_ref[...] = moved[:, :width]
    grad_ref[...] = moved[:, width:]


def weights_kernel(share, *refs):
    *got_refs, w_qkv_ref, w_out_ref = refs
    width = w_out_ref.shape[1]
    me = lax.axis_index("seq")
    for at, got_ref in enumerate(got_refs):
        both = got_ref[...].astype(F32)
        rows = pl.ds(pl.multiple_of((me ^ at) * share, share), share)
        w_qkv_ref[rows, : 2 * width] = both[:share]
        w_qkv_ref[rows, 2 * width :] = both[share:, :width]
        w_out_ref[rows, :] = both[share:, width:]


def exchange(message):
    return lax.all_to_all(message, "seq", split_axis=0, concat_axis=0, tiled=True)


def swap(pieces):
    devs = len(pieces)
    got = {0: pieces[0]}
    for step in reversed(range(1, devs)):
        got[step] = lax.ppermute(pieces[step], "seq", [(dev, dev ^ step) for dev in range(devs)])
    return [got[step] for step in range(devs)]


def local(points, route, owned, cotangent, gain, w_qkv, b_qkv, w_out, b_out):
    devs = lax.axis_size("seq")
    rows, width = points.shape
    block_rows = rows // route.shape[1]
    held = devs * block_rows
    share = width // devs
    direct = block_rows % 16 == 0 and share % 8 == 0
    pieces = devs if direct else 1

    def shape(*dims, dtype=BF16):
        return jax.ShapeDtypeStruct(dims, dtype)

    sent = pl.pallas_call(
        functools.partial(scatter_kernel, block_rows),
        out_shape=(shape(held // pieces, 2 * width),) * pieces,
        in_specs=[ANY] * 3,
        out_specs=(VMEM,) * pieces,
        scratch_shapes=[
            pltpu.SMEM(route.shape, route.dtype),
            pltpu.VMEM(points.shape, points.dtype),
            pltpu.VMEM(cotangent.shape, cotangent.dtype),
            pltpu.SemaphoreType.DMA((3,)),
        ],
    )(route, points, cotangent)

    weights = (gain[None, :], w_qkv, b_qkv[None, :], w_out, b_out[None, :])
    if direct:
        got = swap(sent)
        messages = pl.pallas_call(
            functools.partial(owner_kernel, pieces),
            out_shape=(shape(block_rows + 2 * share + 8, 2 * width),) * pieces,
            in_specs=[VMEM] * (pieces + 5),
            out_specs=(VMEM,) * pieces,
            scratch_shapes=[pltpu.VMEM((width, 2 * width), F32)] * 2,
            compiler_params=PARAMS,
        )(*got, *weights)
        back = swap(messages)
        mine, sums = pl.pallas_call(
            functools.partial(share_kernel, block_rows, share),
            out_shape=(shape(2 * share, 2 * width), shape(8, 2 * width, dtype=F32)),
            in_specs=[VMEM] * pieces,
            out_specs=(VMEM, VMEM),
            compiler_params=PARAMS,
        )(*back)
        shares = swap([mine] * devs)
    else:
        got = exchange(sent[0].reshape(devs, block_rows, 2 * width)).reshape(held, 2 * width)
        back, left, right, sums = pl.pallas_call(
            functools.partial(owner_kernel, pieces),
            out_shape=(
                shape(held, 2 * width),
                shape(width, 2 * width),
                shape(width, 2 * width),
                shape(8, 2 * width),
            ),
            in_specs=[VMEM] * 6,
            out_specs=(VMEM,) * 4,
            compiler_params=PARAMS,
        )(got, *weights)
        message = jnp.concatenate(
            [
                back.reshape(devs, block_rows, 2 * width),
                left.reshape(devs, share, 2 * width),
                right.reshape(devs, share, 2 * width),
                jnp.broadcast_to(sums[None], (devs, 8, 2 * width)),
            ],
            axis=1,
        )
        message = exchange(message)
        total = jnp.sum(message[:, block_rows:].astype(F32), axis=0)
        mine = total[: 2 * share].astype(BF16)
        both = exchange(jnp.broadcast_to(mine[None], (devs, 2 * share, 2 * width)))
        sums = total[2 * share :]
        back = [message[:, :block_rows].reshape(held, 2 * width)]

    mixed, grad_points = pl.pallas_call(
        functools.partial(return_kernel, block_rows),
        out_shape=(shape(rows, width), shape(rows, width)),
        in_specs=[SMEM] + [VMEM] * pieces,
        out_specs=(VMEM, VMEM),
        compiler_params=PARAMS,
    )(route, *back)
    if direct:
        grad_wq, grad_wo = pl.pallas_call(
            functools.partial(weights_kernel, share),
            out_shape=(shape(width, 3 * width, dtype=F32), shape(width, width, dtype=F32)),
            in_specs=[VMEM] * pieces,
            out_specs=(VMEM, VMEM),
            compiler_params=PARAMS,
        )(*shares)
    else:
        both = both.astype(F32)
        left = both[:, :share].reshape(width, 2 * width)
        right = both[:, share:].reshape(width, 2 * width)
        grad_wq = jnp.concatenate([left, right[:, :width]], axis=1)
        grad_wo = right[:, width:]
    flat = sums[:3].reshape(-1)
    return (
        mixed,
        grad_points,
        flat[4 * width : 5 * width],
        grad_wq,
        flat[: 3 * width],
        grad_wo,
        flat[3 * width : 4 * width],
    )


def solution(mesh):
    placed = (
        P(("parts", "seq"), None),
        P(None, ("parts", "seq")),
        P(("parts", "seq")),
        P(("parts", "seq"), None),
        P(),
        P(),
        P(),
        P(),
        P(),
    )
    return jax.shard_map(
        local,
        mesh=mesh,
        in_specs=placed,
        out_specs=(
            P(("parts", "seq"), None),
            P(("parts", "seq"), None),
            P("parts"),
            P("parts", None),
            P("parts"),
            P("parts", None),
            P("parts"),
        ),
        check_vma=False,
    )
```

```python
import functools

import jax
import jax.numpy as jnp
from jax import lax
from jax.experimental import pallas as pl
from jax.experimental.pallas import tpu as pltpu
from jax.sharding import PartitionSpec as P

HEADS = 8
EPS = 1e-05
EMPTY = 64.0
MASKED = -1e30

F32 = jnp.float32
BF16 = jnp.bfloat16

VMEM = pl.BlockSpec(memory_space=pltpu.VMEM)
ANY = pl.BlockSpec(memory_space=pl.ANY)
SMEM = pl.BlockSpec(memory_space=pltpu.SMEM)
PARAMS = pltpu.CompilerParams(vmem_limit_bytes=48 * 1024 * 1024)


def matmul(left, right, dims=((1,), (0,))):
    return lax.dot_general(left, right, (dims, ((), ())), preferred_element_type=F32)


def send_rows(route_ref, shape, axis, block_rows):
    place = lax.broadcasted_iota(jnp.int32, shape, axis)
    target = jnp.zeros(shape, jnp.int32)
    for block in range(shape[axis] // block_rows):
        first = block * block_rows
        moved = route_ref[0, block] * block_rows + place - first
        target = jnp.where(place >= first, moved, target)
    return target


def scatter_kernel(block_rows, route_hbm, points_hbm, cot_hbm, out_ref, route_ref, points_ref, cot_ref, sems):
    copies = [
        pltpu.make_async_copy(source, target, sems.at[at])
        for at, (source, target) in enumerate(
            ((route_hbm, route_ref), (points_hbm, points_ref), (cot_hbm, cot_ref))
        )
    ]
    for copy in copies:
        copy.start()
    for copy in copies:
        copy.wait()
    rows, width = points_ref.shape
    target = send_rows(route_ref, (1, rows), 1, block_rows)
    index = lax.broadcasted_iota(jnp.int32, (out_ref.shape[0], rows), 0)
    pick = jnp.where(index == target, 1.0, 0.0).astype(BF16)
    ones = jnp.ones((rows, width), BF16)
    moved = matmul(pick, jnp.concatenate([points_ref[...], ones], axis=1))
    empty = (1.0 - moved[:, width:]) * EMPTY
    out_ref[:, :width] = (moved[:, :width] + empty).astype(BF16)
    out_ref[:, width:] = matmul(pick, cot_ref[...]).astype(BF16)


def owner_kernel(layout, got_ref, gain_ref, w_qkv_ref, b_qkv_ref, w_out_ref, b_out_ref, *outs):
    rows = got_ref.shape[0]
    width = got_ref.shape[1] // 2
    head = width // HEADS
    scale = head ** (-0.5)
    gain = gain_ref[...]
    w_qkv = w_qkv_ref[...]
    w_out = w_out_ref[...]

    points = got_ref[:, :width].astype(F32)
    cot = got_ref[:, width:]
    centered = points - jnp.mean(points, axis=-1, keepdims=True)
    rstd = lax.rsqrt(jnp.mean(centered * centered, axis=-1, keepdims=True) + EPS)
    xhat = centered * rstd
    normed = (xhat * gain).astype(BF16)
    qkv = (matmul(normed, w_qkv) + b_qkv_ref[...]).astype(BF16)
    query, keys, values = qkv[:, :width], qkv[:, width : 2 * width], qkv[:, 2 * width :]
    d_attn = matmul(cot, w_out, ((1,), (1,))).astype(BF16)
    d_attn_t = matmul(w_out, cot, ((1,), (1,))).astype(BF16)
    d_attn_s = (d_attn.astype(F32) * scale).astype(BF16)

    keys_t = keys.T
    values_t = values.T
    keys_s = (keys.astype(F32) * scale).astype(BF16)
    lane = lax.broadcasted_iota(jnp.int32, (rows, width), 1)
    hidden = jnp.where(points > EMPTY / 2, MASKED, 0.0).astype(BF16)
    query_x = jnp.concatenate([query, jnp.where(lane == 0, 1.0, 0.0).astype(BF16)], axis=1)

    attn_t, dq_t = [], []
    d_keys = jnp.zeros((rows, width), F32)
    d_values = jnp.zeros((rows, width), F32)
    for h in range(HEADS):
        lo, hi = h * head, (h + 1) * head
        mine = (lane >= lo) & (lane < hi)
        keys_h = jnp.concatenate([jnp.where(mine, keys_s, 0), hidden], axis=1)
        scores = matmul(keys_h, query_x, ((1,), (1,)))
        expo = jnp.exp(scores - jnp.max(scores, axis=0, keepdims=True))
        probs = expo * (1.0 / jnp.sum(expo, axis=0, keepdims=True))
        probs_b = probs.astype(BF16)
        out_t = matmul(values_t[lo:hi, :], probs_b)
        attn_t.append(out_t)
        inner = jnp.sum(out_t * d_attn_t[lo:hi, :].astype(F32), axis=0, keepdims=True) * scale
        d_probs = matmul(jnp.where(mine, values, 0), d_attn_s, ((1,), (1,)))
        d_score = (probs * (d_probs - inner)).astype(BF16)
        dq_t.append(matmul(keys_t[lo:hi, :], d_score))
        d_values = jnp.where(mine, matmul(probs_b, d_attn), d_values)
        d_keys = jnp.where(mine, matmul(d_score, query), d_keys)

    attn_t = jnp.concatenate(attn_t, axis=0)
    attn = attn_t.T.astype(BF16)
    mixed = points + (matmul(attn, w_out) + b_out_ref[...])
    grad_w_out = matmul(attn_t.astype(BF16), cot)
    grad_b_out = jnp.sum(cot.astype(F32), axis=0, keepdims=True)

    d_query = jnp.concatenate(dq_t, axis=0).T
    d_qkv = jnp.concatenate([d_query, d_keys, d_values], axis=1).astype(BF16)
    d_normed = matmul(d_qkv, w_qkv, ((1,), (1,)))
    grad_w_qkv = matmul(normed, d_qkv, ((0,), (0,)))
    grad_b_qkv = jnp.sum(d_qkv.astype(F32), axis=0, keepdims=True)
    grad_gain = jnp.sum(d_normed * xhat, axis=0, keepdims=True)
    d_xhat = d_normed * gain
    inner = (
        d_xhat
        - jnp.mean(d_xhat, axis=-1, keepdims=True)
        - xhat * jnp.mean(d_xhat * xhat, axis=-1, keepdims=True)
    )
    grad_rows = cot.astype(F32) + rstd * inner

    back = jnp.concatenate([mixed.astype(BF16), grad_rows.astype(BF16)], axis=1)
    sums = jnp.concatenate(
        [
            grad_b_qkv[:, : 2 * width],
            jnp.concatenate([grad_b_qkv[:, 2 * width :], grad_b_out], axis=1),
            jnp.concatenate([grad_gain, jnp.zeros_like(grad_gain)], axis=1),
            jnp.zeros((5, 2 * width), F32),
        ],
        axis=0,
    )
    left = grad_w_qkv[:, : 2 * width]
    right = jnp.concatenate([grad_w_qkv[:, 2 * width :], grad_w_out], axis=1)
    if layout is None:
        back_ref, left_ref, right_ref, sums_ref = outs
        back_ref[...] = back
        left_ref[...] = left.astype(BF16)
        right_ref[...] = right.astype(BF16)
        sums_ref[...] = sums.astype(BF16)
        return
    devs, block_rows, share = layout
    (message_ref,) = outs
    for dev in range(devs):
        message_ref[dev, :block_rows] = back[dev * block_rows : (dev + 1) * block_rows]
        message_ref[dev, block_rows : block_rows + 2 * share] = jnp.concatenate(
            [left[dev * share : (dev + 1) * share], right[dev * share : (dev + 1) * share]], axis=0
        ).astype(BF16)
        message_ref[dev, block_rows + 2 * share :] = sums.astype(BF16)


def share_kernel(block_rows, share, message_ref, out_ref, sums_ref):
    devs = message_ref.shape[0]
    total = message_ref[0, block_rows:].astype(F32)
    for dev in range(1, devs):
        total = total + message_ref[dev, block_rows:].astype(F32)
    mine = total[: 2 * share].astype(BF16)
    out_ref[...] = mine
    sums_ref[...] = total[2 * share : 2 * share + 8]


def return_kernel(block_rows, route_ref, message_ref, mixed_ref, grad_ref):
    rows, width = mixed_ref.shape
    target = send_rows(route_ref, (rows, 1), 0, block_rows)
    if len(message_ref.shape) == 3:
        back = jnp.concatenate(
            [message_ref[dev, :block_rows] for dev in range(message_ref.shape[0])], axis=0
        )
    else:
        back = message_ref[...]
    index = lax.broadcasted_iota(jnp.int32, (rows, back.shape[0]), 1)
    pick = jnp.where(index == target, 1.0, 0.0).astype(BF16)
    moved = matmul(pick, back).astype(BF16)
    mixed_ref[...] = moved[:, :width]
    grad_ref[...] = moved[:, width:]


def weights_kernel(share, near, got_ref, w_qkv_ref, w_out_ref):
    width = w_out_ref.shape[1]
    far = width // share // near
    for dev in range(near * far):
        place = (dev % near * far + dev // near) * 2 * share
        both = got_ref[place : place + 2 * share].astype(F32)
        rows = slice(dev * share, (dev + 1) * share)
        w_qkv_ref[rows, : 2 * width] = both[:share]
        w_qkv_ref[rows, 2 * width :] = both[share:, :width]
        w_out_ref[rows, :] = both[share:, width:]


def exchange(message):
    return lax.all_to_all(message, "seq", split_axis=0, concat_axis=0, tiled=True)


def gather(piece, groups):
    sent = jnp.broadcast_to(piece[None], (len(groups[0]), *piece.shape))
    got = lax.all_to_all(
        sent, "seq", split_axis=0, concat_axis=0, axis_index_groups=groups, tiled=True
    )
    return got.reshape(-1, piece.shape[1])


def local(points, route, owned, cotangent, gain, w_qkv, b_qkv, w_out, b_out):
    devs = lax.axis_size("seq")
    rows, width = points.shape
    block_rows = rows // route.shape[1]
    held = devs * block_rows
    share = width // devs
    aligned = block_rows % 16 == 0 and share % 8 == 0

    def shape(*dims, dtype=BF16):
        return jax.ShapeDtypeStruct(dims, dtype)

    sent = pl.pallas_call(
        functools.partial(scatter_kernel, block_rows),
        out_shape=shape(held, 2 * width),
        in_specs=[ANY] * 3,
        out_specs=VMEM,
        scratch_shapes=[
            pltpu.SMEM(route.shape, route.dtype),
            pltpu.VMEM(points.shape, points.dtype),
            pltpu.VMEM(cotangent.shape, cotangent.dtype),
            pltpu.SemaphoreType.DMA((3,)),
        ],
    )(route, points, cotangent)
    got = exchange(sent.reshape(devs, block_rows, 2 * width)).reshape(held, 2 * width)

    weights = (gain[None, :], w_qkv, b_qkv[None, :], w_out, b_out[None, :])
    if aligned:
        message = pl.pallas_call(
            functools.partial(owner_kernel, (devs, block_rows, share)),
            out_shape=shape(devs, block_rows + 2 * share + 8, 2 * width),
            in_specs=[VMEM] * 6,
            out_specs=VMEM,
            compiler_params=PARAMS,
        )(got, *weights)
        message = exchange(message)
        mine, sums = pl.pallas_call(
            functools.partial(share_kernel, block_rows, share),
            out_shape=(shape(2 * share, 2 * width), shape(8, 2 * width, dtype=F32)),
            in_specs=[VMEM],
            out_specs=(VMEM, VMEM),
            compiler_params=PARAMS,
        )(message)
        back = message
    else:
        back, left, right, sums = pl.pallas_call(
            functools.partial(owner_kernel, None),
            out_shape=(
                shape(held, 2 * width),
                shape(width, 2 * width),
                shape(width, 2 * width),
                shape(8, 2 * width),
            ),
            in_specs=[VMEM] * 6,
            out_specs=(VMEM,) * 4,
            compiler_params=PARAMS,
        )(got, *weights)
        message = jnp.concatenate(
            [
                back.reshape(devs, block_rows, 2 * width),
                left.reshape(devs, share, 2 * width),
                right.reshape(devs, share, 2 * width),
                jnp.broadcast_to(sums[None], (devs, 8, 2 * width)),
            ],
            axis=1,
        )
        message = exchange(message)
        total = jnp.sum(message[:, block_rows:].astype(F32), axis=0)
        mine = total[: 2 * share].astype(BF16)
        sums = total[2 * share :]
        back = message[:, :block_rows].reshape(held, 2 * width)

    near = 4
    far_groups = [[dev for dev in range(devs) if dev % near == low] for low in range(near)]
    near_groups = [list(range(dev, dev + near)) for dev in range(0, devs, near)]
    pieces = gather(gather(mine, far_groups), near_groups)
    mixed, grad_points = pl.pallas_call(
        functools.partial(return_kernel, block_rows),
        out_shape=(shape(rows, width), shape(rows, width)),
        in_specs=[SMEM, VMEM],
        out_specs=(VMEM, VMEM),
        compiler_params=PARAMS,
    )(route, back)
    if aligned:
        grad_wq, grad_wo = pl.pallas_call(
            functools.partial(weights_kernel, share, near),
            out_shape=(shape(width, 3 * width, dtype=F32), shape(width, width, dtype=F32)),
            in_specs=[VMEM],
            out_specs=(VMEM, VMEM),
            compiler_params=PARAMS,
        )(pieces)
    else:
        both = pieces.reshape(near, devs // near, 2 * share, 2 * width).astype(F32)
        both = both.transpose(1, 0, 2, 3).reshape(devs, 2 * share, 2 * width)
        left = both[:, :share].reshape(width, 2 * width)
        right = both[:, share:].reshape(width, 2 * width)
        grad_wq = jnp.concatenate([left, right[:, :width]], axis=1)
        grad_wo = right[:, width:]
    flat = sums[:3].reshape(-1)
    return (
        mixed,
        grad_points,
        flat[4 * width : 5 * width],
        grad_wq,
        flat[: 3 * width],
        grad_wo,
        flat[3 * width : 4 * width],
    )


def solution(mesh):
    placed = (
        P(("parts", "seq"), None),
        P(None, ("parts", "seq")),
        P(("parts", "seq")),
        P(("parts", "seq"), None),
        P(),
        P(),
        P(),
        P(),
        P(),
    )
    return jax.shard_map(
        local,
        mesh=mesh,
        in_specs=placed,
        out_specs=(
            P(("parts", "seq"), None),
            P(("parts", "seq"), None),
            P("parts"),
            P("parts", None),
            P("parts"),
            P("parts", None),
            P("parts"),
        ),
        check_vma=False,
    )
```

```python
import functools

import jax
import jax.numpy as jnp
from jax import lax
from jax.experimental import pallas as pl
from jax.experimental.pallas import tpu as pltpu
from jax.sharding import PartitionSpec as P

HEADS = 8
EPS = 1e-05
EMPTY = 64.0
MASKED = -1e30

F32 = jnp.float32
BF16 = jnp.bfloat16

VMEM = pl.BlockSpec(memory_space=pltpu.VMEM)
ANY = pl.BlockSpec(memory_space=pl.ANY)
SMEM = pl.BlockSpec(memory_space=pltpu.SMEM)
PARAMS = pltpu.CompilerParams(vmem_limit_bytes=48 * 1024 * 1024)


def matmul(left, right, dims=((1,), (0,))):
    return lax.dot_general(left, right, (dims, ((), ())), preferred_element_type=F32)


def send_rows(route_ref, shape, axis, block_rows):
    place = lax.broadcasted_iota(jnp.int32, shape, axis)
    target = jnp.zeros(shape, jnp.int32)
    for block in range(shape[axis] // block_rows):
        first = block * block_rows
        moved = route_ref[0, block] * block_rows + place - first
        target = jnp.where(place >= first, moved, target)
    return target


def scatter_kernel(block_rows, route_hbm, points_hbm, cot_hbm, out_ref, route_ref, points_ref, cot_ref, sems):
    copies = [
        pltpu.make_async_copy(source, target, sems.at[at])
        for at, (source, target) in enumerate(
            ((route_hbm, route_ref), (points_hbm, points_ref), (cot_hbm, cot_ref))
        )
    ]
    for copy in copies:
        copy.start()
    for copy in copies:
        copy.wait()
    rows, width = points_ref.shape
    target = send_rows(route_ref, (1, rows), 1, block_rows)
    index = lax.broadcasted_iota(jnp.int32, (out_ref.shape[0], rows), 0)
    pick = jnp.where(index == target, 1.0, 0.0).astype(BF16)
    ones = jnp.ones((rows, width), BF16)
    moved = matmul(pick, jnp.concatenate([points_ref[...], ones], axis=1))
    empty = (1.0 - moved[:, width:]) * EMPTY
    out_ref[:, :width] = (moved[:, :width] + empty).astype(BF16)
    out_ref[:, width:] = matmul(pick, cot_ref[...]).astype(BF16)


def owner_kernel(near, got_ref, gain_ref, w_qkv_ref, b_qkv_ref, w_out_ref, b_out_ref, back_ref, *outs):
    rows = got_ref.shape[0]
    width = got_ref.shape[1] // 2
    head = width // HEADS
    scale = head ** (-0.5)
    gain = gain_ref[...]
    w_qkv = w_qkv_ref[...]
    w_out = w_out_ref[...]

    points = got_ref[:, :width].astype(F32)
    cot = got_ref[:, width:]
    centered = points - jnp.mean(points, axis=-1, keepdims=True)
    rstd = lax.rsqrt(jnp.mean(centered * centered, axis=-1, keepdims=True) + EPS)
    xhat = centered * rstd
    normed = (xhat * gain).astype(BF16)
    qkv = (matmul(normed, w_qkv) + b_qkv_ref[...]).astype(BF16)
    query, keys, values = qkv[:, :width], qkv[:, width : 2 * width], qkv[:, 2 * width :]
    d_attn = matmul(cot, w_out, ((1,), (1,))).astype(BF16)
    d_attn_t = matmul(w_out, cot, ((1,), (1,))).astype(BF16)
    d_attn_s = (d_attn.astype(F32) * scale).astype(BF16)

    keys_t = keys.T
    values_t = values.T
    keys_s = (keys.astype(F32) * scale).astype(BF16)
    lane = lax.broadcasted_iota(jnp.int32, (rows, width), 1)
    hidden = jnp.where(points > EMPTY / 2, MASKED, 0.0).astype(BF16)
    query_x = jnp.concatenate([query, jnp.where(lane == 0, 1.0, 0.0).astype(BF16)], axis=1)

    attn_t, dq_t = [], []
    d_keys = jnp.zeros((rows, width), F32)
    d_values = jnp.zeros((rows, width), F32)
    for h in range(HEADS):
        lo, hi = h * head, (h + 1) * head
        mine = (lane >= lo) & (lane < hi)
        keys_h = jnp.concatenate([jnp.where(mine, keys_s, 0), hidden], axis=1)
        scores = matmul(keys_h, query_x, ((1,), (1,)))
        expo = jnp.exp(scores - jnp.max(scores, axis=0, keepdims=True))
        probs = expo * (1.0 / jnp.sum(expo, axis=0, keepdims=True))
        probs_b = probs.astype(BF16)
        out_t = matmul(values_t[lo:hi, :], probs_b)
        attn_t.append(out_t)
        inner = jnp.sum(out_t * d_attn_t[lo:hi, :].astype(F32), axis=0, keepdims=True) * scale
        d_probs = matmul(jnp.where(mine, values, 0), d_attn_s, ((1,), (1,)))
        d_score = (probs * (d_probs - inner)).astype(BF16)
        dq_t.append(matmul(keys_t[lo:hi, :], d_score))
        d_values = jnp.where(mine, matmul(probs_b, d_attn), d_values)
        d_keys = jnp.where(mine, matmul(d_score, query), d_keys)

    attn_t = jnp.concatenate(attn_t, axis=0)
    attn = attn_t.T.astype(BF16)
    mixed = points + (matmul(attn, w_out) + b_out_ref[...])
    grad_w_out = matmul(attn_t.astype(BF16), cot)
    grad_b_out = jnp.sum(cot.astype(F32), axis=0, keepdims=True)

    d_query = jnp.concatenate(dq_t, axis=0).T
    d_qkv = jnp.concatenate([d_query, d_keys, d_values], axis=1).astype(BF16)
    d_normed = matmul(d_qkv, w_qkv, ((1,), (1,)))
    grad_w_qkv = matmul(normed, d_qkv, ((0,), (0,)))
    grad_b_qkv = jnp.sum(d_qkv.astype(F32), axis=0, keepdims=True)
    grad_gain = jnp.sum(d_normed * xhat, axis=0, keepdims=True)
    d_xhat = d_normed * gain
    inner = (
        d_xhat
        - jnp.mean(d_xhat, axis=-1, keepdims=True)
        - xhat * jnp.mean(d_xhat * xhat, axis=-1, keepdims=True)
    )
    grad_rows = cot.astype(F32) + rstd * inner

    back = jnp.concatenate([mixed.astype(BF16), grad_rows.astype(BF16)], axis=1)
    sums = jnp.concatenate(
        [
            grad_b_qkv[:, : 2 * width],
            jnp.concatenate([grad_b_qkv[:, 2 * width :], grad_b_out], axis=1),
            jnp.concatenate([grad_gain, jnp.zeros_like(grad_gain)], axis=1),
            jnp.zeros((5, 2 * width), F32),
        ],
        axis=0,
    )
    left = grad_w_qkv[:, : 2 * width]
    right = jnp.concatenate([grad_w_qkv[:, 2 * width :], grad_w_out], axis=1)
    back_ref[...] = back
    if near == 1:
        left_ref, right_ref, sums_ref = outs
        left_ref[...] = left.astype(BF16)
        right_ref[...] = right.astype(BF16)
        sums_ref[...] = sums.astype(BF16)
        return
    *part_refs, both_ref = outs
    both_ref[:width] = left
    both_ref[width:] = right
    span = 2 * width // near
    me = lax.axis_index("seq")
    for step, part_ref in enumerate(part_refs):
        first = ((me ^ step) & (near - 1)) * span
        part_ref[:span] = both_ref[pl.ds(pl.multiple_of(first, span), span)].astype(BF16)
        part_ref[span:] = sums.astype(BF16)


def tree(values):
    while len(values) > 1:
        values = [left + right for left, right in zip(values[::2], values[1::2])]
    return values[0]


def sum_kernel(*refs):
    *part_refs, out_ref = refs
    out_ref[...] = tree([part_ref[...].astype(F32) for part_ref in part_refs]).astype(BF16)


def return_kernel(block_rows, route_ref, back_ref, mixed_ref, grad_ref):
    rows, width = mixed_ref.shape
    target = send_rows(route_ref, (rows, 1), 0, block_rows)
    index = lax.broadcasted_iota(jnp.int32, (rows, back_ref.shape[0]), 1)
    pick = jnp.where(index == target, 1.0, 0.0).astype(BF16)
    moved = matmul(pick, back_ref[...]).astype(BF16)
    mixed_ref[...] = moved[:, :width]
    grad_ref[...] = moved[:, width:]


def weights_kernel(*refs):
    *part_refs, gain_ref, w_qkv_ref, b_qkv_ref, w_out_ref, b_out_ref, both_ref = refs
    width = w_out_ref.shape[1]
    near = len(part_refs)
    span = 2 * width // near
    me = lax.axis_index("seq")
    for step, part_ref in enumerate(part_refs):
        place = (me ^ step) & (near - 1)
        part = part_ref[...].astype(F32)
        both_ref[pl.ds(pl.multiple_of(place * span, span), span)] = part[:span]

        @pl.when(place == 0)
        def _():
            sums = part[span:]
            gain_ref[...] = sums[2:3, :width]
            b_qkv_ref[:, : 2 * width] = sums[0:1]
            b_qkv_ref[:, 2 * width :] = sums[1:2, :width]
            b_out_ref[...] = sums[1:2, width:]

    w_qkv_ref[:, : 2 * width] = both_ref[:width]
    w_qkv_ref[:, 2 * width :] = both_ref[width:, :width]
    w_out_ref[...] = both_ref[width:, width:]


def exchange(message):
    return lax.all_to_all(message, "seq", split_axis=0, concat_axis=0, tiled=True)


def swap(piece, step, devs):
    return lax.ppermute(piece, "seq", [(dev, dev ^ step) for dev in range(devs)])


def local(points, route, owned, cotangent, gain, w_qkv, b_qkv, w_out, b_out):
    devs = lax.axis_size("seq")
    rows, width = points.shape
    block_rows = rows // route.shape[1]
    held = devs * block_rows
    share = width // devs
    near = 4 if devs == 16 and width % 64 == 0 else 1

    def shape(*dims, dtype=BF16):
        return jax.ShapeDtypeStruct(dims, dtype)

    sent = pl.pallas_call(
        functools.partial(scatter_kernel, block_rows),
        out_shape=shape(held, 2 * width),
        in_specs=[ANY] * 3,
        out_specs=VMEM,
        scratch_shapes=[
            pltpu.SMEM(route.shape, route.dtype),
            pltpu.VMEM(points.shape, points.dtype),
            pltpu.VMEM(cotangent.shape, cotangent.dtype),
            pltpu.SemaphoreType.DMA((3,)),
        ],
    )(route, points, cotangent)
    got = exchange(sent.reshape(devs, block_rows, 2 * width)).reshape(held, 2 * width)

    weights = (gain[None, :], w_qkv, b_qkv[None, :], w_out, b_out[None, :])
    if near > 1:
        part = shape(2 * width // near + 8, 2 * width)
        back, *parts = pl.pallas_call(
            functools.partial(owner_kernel, near),
            out_shape=(shape(held, 2 * width),) + (part,) * near,
            in_specs=[VMEM] * 6,
            out_specs=(VMEM,) * (1 + near),
            scratch_shapes=[pltpu.VMEM((2 * width, 2 * width), F32)],
            compiler_params=PARAMS,
        )(got, *weights)
        back = exchange(back.reshape(devs, block_rows, 2 * width)).reshape(held, 2 * width)

        def add(pieces):
            return pl.pallas_call(
                sum_kernel, out_shape=part, in_specs=[VMEM] * len(pieces), out_specs=VMEM
            )(*pieces)

        total = add([parts[0]] + [swap(parts[step], step, devs) for step in range(1, near)])
        total = add([total] + [swap(total, step, devs) for step in range(near, devs, near)])
        parts = [total] + [swap(total, step, devs) for step in range(1, near)]
        grads = pl.pallas_call(
            weights_kernel,
            out_shape=tuple(
                shape(*dims, dtype=F32)
                for dims in ((1, width), (width, 3 * width), (1, 3 * width), (width, width), (1, width))
            ),
            in_specs=[VMEM] * near,
            out_specs=(VMEM,) * 5,
            scratch_shapes=[pltpu.VMEM((2 * width, 2 * width), F32)],
        )(*parts)
        grad_gain, grad_wq, grad_bq, grad_wo, grad_bo = (
            grad.reshape(-1) if grad.shape[0] == 1 else grad for grad in grads
        )
    else:
        back, left, right, sums = pl.pallas_call(
            functools.partial(owner_kernel, near),
            out_shape=(
                shape(held, 2 * width),
                shape(width, 2 * width),
                shape(width, 2 * width),
                shape(8, 2 * width),
            ),
            in_specs=[VMEM] * 6,
            out_specs=(VMEM,) * 4,
            compiler_params=PARAMS,
        )(got, *weights)
        message = jnp.concatenate(
            [
                back.reshape(devs, block_rows, 2 * width),
                left.reshape(devs, share, 2 * width),
                right.reshape(devs, share, 2 * width),
                jnp.broadcast_to(sums[None], (devs, 8, 2 * width)),
            ],
            axis=1,
        )
        message = exchange(message)
        total = jnp.sum(message[:, block_rows:].astype(F32), axis=0)
        mine = total[: 2 * share].astype(BF16)
        both = exchange(jnp.broadcast_to(mine[None], (devs, 2 * share, 2 * width))).astype(F32)
        back = message[:, :block_rows].reshape(held, 2 * width)
        left = both[:, :share].reshape(width, 2 * width)
        right = both[:, share:].reshape(width, 2 * width)
        grad_wq = jnp.concatenate([left, right[:, :width]], axis=1)
        grad_wo = right[:, width:]
        flat = total[2 * share :].reshape(-1)
        grad_bq = flat[: 3 * width]
        grad_bo = flat[3 * width : 4 * width]
        grad_gain = flat[4 * width : 5 * width]

    mixed, grad_points = pl.pallas_call(
        functools.partial(return_kernel, block_rows),
        out_shape=(shape(rows, width), shape(rows, width)),
        in_specs=[SMEM, VMEM],
        out_specs=(VMEM, VMEM),
    )(route, back)
    return (mixed, grad_points, grad_gain, grad_wq, grad_bq, grad_wo, grad_bo)


def solution(mesh):
    placed = (
        P(("parts", "seq"), None),
        P(None, ("parts", "seq")),
        P(("parts", "seq")),
        P(("parts", "seq"), None),
        P(),
        P(),
        P(),
        P(),
        P(),
    )
    return jax.shard_map(
        local,
        mesh=mesh,
        in_specs=placed,
        out_specs=(
            P(("parts", "seq"), None),
            P(("parts", "seq"), None),
            P("parts"),
            P("parts", None),
            P("parts"),
            P("parts", None),
            P("parts"),
        ),
        check_vma=False,
    )
```

```python
import functools

import jax
import jax.numpy as jnp
from jax import lax
from jax.experimental import pallas as pl
from jax.experimental.pallas import tpu as pltpu
from jax.sharding import PartitionSpec as P

HEADS = 8
EPS = 1e-05
EMPTY = 64.0
MASKED = -1e30

F32 = jnp.float32
BF16 = jnp.bfloat16

VMEM = pl.BlockSpec(memory_space=pltpu.VMEM)
ANY = pl.BlockSpec(memory_space=pl.ANY)
SMEM = pl.BlockSpec(memory_space=pltpu.SMEM)
MIB = 1024 * 1024
LARGE = pltpu.CompilerParams(vmem_limit_bytes=32 * MIB)
SMALL = pltpu.CompilerParams(vmem_limit_bytes=8 * MIB)


def matmul(left, right, dims=((1,), (0,))):
    return lax.dot_general(left, right, (dims, ((), ())), preferred_element_type=F32)


def send_rows(route_ref, shape, axis, block_rows):
    place = lax.broadcasted_iota(jnp.int32, shape, axis)
    target = jnp.zeros(shape, jnp.int32)
    for block in range(shape[axis] // block_rows):
        first = block * block_rows
        moved = route_ref[0, block] * block_rows + place - first
        target = jnp.where(place >= first, moved, target)
    return target


def scatter_kernel(block_rows, route_hbm, points_hbm, cot_hbm, out_ref, route_ref, points_ref, cot_ref, sems):
    copies = [
        pltpu.make_async_copy(source, target, sems.at[at])
        for at, (source, target) in enumerate(
            ((route_hbm, route_ref), (points_hbm, points_ref), (cot_hbm, cot_ref))
        )
    ]
    for copy in copies:
        copy.start()
    for copy in copies:
        copy.wait()
    rows, width = points_ref.shape
    target = send_rows(route_ref, (1, rows), 1, block_rows)
    index = lax.broadcasted_iota(jnp.int32, (out_ref.shape[0], rows), 0)
    pick = jnp.where(index == target, 1.0, 0.0).astype(BF16)
    ones = jnp.ones((rows, width), BF16)
    moved = matmul(pick, jnp.concatenate([points_ref[...], ones], axis=1))
    empty = (1.0 - moved[:, width:]) * EMPTY
    out_ref[:, :width] = (moved[:, :width] + empty).astype(BF16)
    out_ref[:, width:] = matmul(pick, cot_ref[...]).astype(BF16)


def normalize(points):
    centered = points - jnp.mean(points, axis=-1, keepdims=True)
    rstd = lax.rsqrt(jnp.mean(centered * centered, axis=-1, keepdims=True) + EPS)
    return centered * rstd, rstd


def owner_kernel(near, got_ref, gain_ref, w_qkv_hbm, b_qkv_ref, w_out_hbm, attn_ref, d_normed_ref, *refs):
    *outs, w_qkv_ref, w_out_ref, both_ref, sems = refs
    copies = [
        pltpu.make_async_copy(w_qkv_hbm, w_qkv_ref, sems.at[0]),
        pltpu.make_async_copy(w_out_hbm, w_out_ref, sems.at[1]),
    ]
    for copy in copies:
        copy.start()
    rows = got_ref.shape[0]
    width = got_ref.shape[1] // 2
    head = width // HEADS
    scale = head ** (-0.5)
    gain = gain_ref[...]

    points = got_ref[:, :width].astype(F32)
    cot = got_ref[:, width:]
    xhat, _ = normalize(points)
    normed = (xhat * gain).astype(BF16)
    for copy in copies:
        copy.wait()
    w_qkv = w_qkv_ref[...]
    w_out = w_out_ref[...]
    qkv = (matmul(normed, w_qkv) + b_qkv_ref[...]).astype(BF16)
    query, keys, values = qkv[:, :width], qkv[:, width : 2 * width], qkv[:, 2 * width :]
    d_attn = matmul(cot, w_out, ((1,), (1,))).astype(BF16)
    d_attn_t = matmul(w_out, cot, ((1,), (1,))).astype(BF16)
    d_attn_s = (d_attn.astype(F32) * scale).astype(BF16)

    keys_t = keys.T
    values_t = values.T
    keys_s = (keys.astype(F32) * scale).astype(BF16)
    lane = lax.broadcasted_iota(jnp.int32, (rows, width), 1)
    hidden = jnp.where(points > EMPTY / 2, MASKED, 0.0).astype(BF16)
    query_x = jnp.concatenate([query, jnp.where(lane == 0, 1.0, 0.0).astype(BF16)], axis=1)

    attn_t, dq_t = [], []
    d_keys = jnp.zeros((rows, width), F32)
    d_values = jnp.zeros((rows, width), F32)
    for h in range(HEADS):
        lo, hi = h * head, (h + 1) * head
        mine = (lane >= lo) & (lane < hi)
        keys_h = jnp.concatenate([jnp.where(mine, keys_s, 0), hidden], axis=1)
        scores = matmul(keys_h, query_x, ((1,), (1,)))
        expo = jnp.exp(scores - jnp.max(scores, axis=0, keepdims=True))
        probs = expo * (1.0 / jnp.sum(expo, axis=0, keepdims=True))
        probs_b = probs.astype(BF16)
        out_t = matmul(values_t[lo:hi, :], probs_b)
        attn_t.append(out_t)
        inner = jnp.sum(out_t * d_attn_t[lo:hi, :].astype(F32), axis=0, keepdims=True) * scale
        d_probs = matmul(jnp.where(mine, values, 0), d_attn_s, ((1,), (1,)))
        d_score = (probs * (d_probs - inner)).astype(BF16)
        dq_t.append(matmul(keys_t[lo:hi, :], d_score))
        d_values = jnp.where(mine, matmul(probs_b, d_attn), d_values)
        d_keys = jnp.where(mine, matmul(d_score, query), d_keys)

    attn_t = jnp.concatenate(attn_t, axis=0)
    attn_ref[...] = attn_t.T.astype(BF16)
    grad_w_out = matmul(attn_t.astype(BF16), cot)
    grad_b_out = jnp.sum(cot.astype(F32), axis=0, keepdims=True)

    d_query = jnp.concatenate(dq_t, axis=0).T
    d_qkv = jnp.concatenate([d_query, d_keys, d_values], axis=1).astype(BF16)
    d_normed = matmul(d_qkv, w_qkv, ((1,), (1,)))
    grad_w_qkv = matmul(normed, d_qkv, ((0,), (0,)))
    grad_b_qkv = jnp.sum(d_qkv.astype(F32), axis=0, keepdims=True)
    grad_gain = jnp.sum(d_normed * xhat, axis=0, keepdims=True)
    d_normed_ref[...] = d_normed
    sums = jnp.concatenate(
        [
            grad_b_qkv[:, : 2 * width],
            jnp.concatenate([grad_b_qkv[:, 2 * width :], grad_b_out], axis=1),
            jnp.concatenate([grad_gain, jnp.zeros_like(grad_gain)], axis=1),
            jnp.zeros((5, 2 * width), F32),
        ],
        axis=0,
    )
    left = grad_w_qkv[:, : 2 * width]
    right = jnp.concatenate([grad_w_qkv[:, 2 * width :], grad_w_out], axis=1)
    if near == 1:
        left_ref, right_ref, sums_ref = outs
        left_ref[...] = left.astype(BF16)
        right_ref[...] = right.astype(BF16)
        sums_ref[...] = sums.astype(BF16)
        return
    part_refs = outs
    both_ref[:width] = left
    both_ref[width:] = right
    span = 2 * width // near
    me = lax.axis_index("seq")
    for step, part_ref in enumerate(part_refs):
        first = ((me ^ step) & (near - 1)) * span
        part_ref[:span] = both_ref[pl.ds(pl.multiple_of(first, span), span)].astype(BF16)
        part_ref[span:] = sums.astype(BF16)


def rows_kernel(got_ref, attn_ref, d_normed_ref, gain_ref, w_out_ref, b_out_ref, back_ref):
    width = gain_ref.shape[1]
    points = got_ref[:, :width].astype(F32)
    cot = got_ref[:, width:].astype(F32)
    xhat, rstd = normalize(points)
    mixed = points + (matmul(attn_ref[...], w_out_ref[...]) + b_out_ref[...])
    d_xhat = d_normed_ref[...] * gain_ref[...]
    inner = (
        d_xhat
        - jnp.mean(d_xhat, axis=-1, keepdims=True)
        - xhat * jnp.mean(d_xhat * xhat, axis=-1, keepdims=True)
    )
    back_ref[:, :width] = mixed.astype(BF16)
    back_ref[:, width:] = (cot + rstd * inner).astype(BF16)


def tree(values):
    while len(values) > 1:
        values = [left + right for left, right in zip(values[::2], values[1::2])]
    return values[0]


def sum_kernel(*refs):
    *part_refs, out_ref = refs
    out_ref[...] = tree([part_ref[...].astype(F32) for part_ref in part_refs]).astype(BF16)


def return_kernel(block_rows, route_hbm, back_ref, mixed_ref, grad_ref, route_ref, sem):
    copy = pltpu.make_async_copy(route_hbm, route_ref, sem)
    copy.start()
    copy.wait()
    rows, width = mixed_ref.shape
    target = send_rows(route_ref, (rows, 1), 0, block_rows)
    index = lax.broadcasted_iota(jnp.int32, (rows, back_ref.shape[0]), 1)
    pick = jnp.where(index == target, 1.0, 0.0).astype(BF16)
    moved = matmul(pick, back_ref[...]).astype(BF16)
    mixed_ref[...] = moved[:, :width]
    grad_ref[...] = moved[:, width:]


def weights_kernel(*refs):
    *part_refs, _, gain_ref, w_qkv_ref, b_qkv_ref, w_out_ref, b_out_ref, both_ref = refs
    width = w_out_ref.shape[1]
    near = len(part_refs)
    span = 2 * width // near
    me = lax.axis_index("seq")
    for step, part_ref in enumerate(part_refs):
        place = (me ^ step) & (near - 1)
        part = part_ref[...].astype(F32)
        both_ref[pl.ds(pl.multiple_of(place * span, span), span)] = part[:span]

        @pl.when(place == 0)
        def _():
            sums = part[span:]
            gain_ref[...] = sums[2, :width]
            b_qkv_ref[: 2 * width] = sums[0]
            b_qkv_ref[2 * width :] = sums[1, :width]
            b_out_ref[...] = sums[1, width:]

    w_qkv_ref[:, : 2 * width] = both_ref[:width]
    w_qkv_ref[:, 2 * width :] = both_ref[width:, :width]
    w_out_ref[...] = both_ref[width:, width:]


def exchange(message):
    return lax.all_to_all(message, "seq", split_axis=0, concat_axis=0, tiled=True)


def swap(piece, step, devs):
    return lax.ppermute(piece, "seq", [(dev, dev ^ step) for dev in range(devs)])


def local(points, route, owned, cotangent, gain, w_qkv, b_qkv, w_out, b_out):
    devs = lax.axis_size("seq")
    rows, width = points.shape
    block_rows = rows // route.shape[1]
    held = devs * block_rows
    share = width // devs
    near = 4 if devs == 16 and width % 64 == 0 else 1

    def shape(*dims, dtype=BF16):
        return jax.ShapeDtypeStruct(dims, dtype)

    sent = pl.pallas_call(
        functools.partial(scatter_kernel, block_rows),
        out_shape=shape(held, 2 * width),
        in_specs=[ANY] * 3,
        out_specs=VMEM,
        scratch_shapes=[
            pltpu.SMEM(route.shape, route.dtype),
            pltpu.VMEM(points.shape, points.dtype),
            pltpu.VMEM(cotangent.shape, cotangent.dtype),
            pltpu.SemaphoreType.DMA((3,)),
        ],
    )(route, points, cotangent)
    got = exchange(sent.reshape(devs, block_rows, 2 * width)).reshape(held, 2 * width)

    part = shape(2 * width // near + 8, 2 * width)
    if near > 1:
        sums_shapes = (part,) * near
    else:
        sums_shapes = (shape(width, 2 * width),) * 2 + (shape(8, 2 * width),)
    attn, d_normed, *parts = pl.pallas_call(
        functools.partial(owner_kernel, near),
        out_shape=(shape(held, width), shape(held, width, dtype=F32)) + sums_shapes,
        in_specs=[VMEM, VMEM, ANY, VMEM, ANY],
        out_specs=(VMEM,) * (2 + len(sums_shapes)),
        scratch_shapes=[
            pltpu.VMEM(w_qkv.shape, w_qkv.dtype),
            pltpu.VMEM(w_out.shape, w_out.dtype),
            pltpu.VMEM((2 * width, 2 * width), F32),
            pltpu.SemaphoreType.DMA((2,)),
        ],
        compiler_params=LARGE,
    )(got, gain[None, :], w_qkv, b_qkv[None, :], w_out)
    back = pl.pallas_call(
        rows_kernel,
        out_shape=shape(held, 2 * width),
        in_specs=[VMEM] * 6,
        out_specs=VMEM,
        compiler_params=SMALL,
        cost_estimate=pl.CostEstimate(
            flops=64 * held * width * width, bytes_accessed=16 * held * width, transcendentals=0
        ),
    )(got, attn, d_normed, gain[None, :], w_out, b_out[None, :])

    def give_back(back):
        return pl.pallas_call(
            functools.partial(return_kernel, block_rows),
            out_shape=(shape(rows, width), shape(rows, width)),
            in_specs=[ANY, VMEM],
            out_specs=(VMEM, VMEM),
            scratch_shapes=[pltpu.SMEM(route.shape, route.dtype), pltpu.SemaphoreType.DMA],
            compiler_params=SMALL,
        )(route, back)

    if near > 1:
        back = exchange(back.reshape(devs, block_rows, 2 * width)).reshape(held, 2 * width)
        mixed, grad_points = give_back(back)

        def add(pieces):
            return pl.pallas_call(
                sum_kernel,
                out_shape=part,
                in_specs=[VMEM] * len(pieces),
                out_specs=VMEM,
                compiler_params=SMALL,
            )(*pieces)

        total = add([parts[0]] + [swap(parts[step], step, devs) for step in range(1, near)])
        total = add([total] + [swap(total, step, devs) for step in range(near, devs, near)])
        parts = [total] + [swap(total, step, devs) for step in range(1, near)]
        grad_gain, grad_wq, grad_bq, grad_wo, grad_bo = pl.pallas_call(
            weights_kernel,
            out_shape=tuple(
                shape(*dims, dtype=F32)
                for dims in ((width,), (width, 3 * width), (3 * width,), (width, width), (width,))
            ),
            in_specs=[VMEM] * near + [ANY],
            out_specs=(VMEM,) * 5,
            scratch_shapes=[pltpu.VMEM((2 * width, 2 * width), F32)],
            compiler_params=SMALL,
        )(*parts, mixed)
    else:
        left, right, sums = parts
        message = jnp.concatenate(
            [
                back.reshape(devs, block_rows, 2 * width),
                left.reshape(devs, share, 2 * width),
                right.reshape(devs, share, 2 * width),
                jnp.broadcast_to(sums[None], (devs, 8, 2 * width)),
            ],
            axis=1,
        )
        message = exchange(message)
        total = jnp.sum(message[:, block_rows:].astype(F32), axis=0)
        mine = total[: 2 * share].astype(BF16)
        both = exchange(jnp.broadcast_to(mine[None], (devs, 2 * share, 2 * width))).astype(F32)
        mixed, grad_points = give_back(message[:, :block_rows].reshape(held, 2 * width))
        left = both[:, :share].reshape(width, 2 * width)
        right = both[:, share:].reshape(width, 2 * width)
        grad_wq = jnp.concatenate([left, right[:, :width]], axis=1)
        grad_wo = right[:, width:]
        flat = total[2 * share :].reshape(-1)
        grad_bq = flat[: 3 * width]
        grad_bo = flat[3 * width : 4 * width]
        grad_gain = flat[4 * width : 5 * width]

    return (mixed, grad_points, grad_gain, grad_wq, grad_bq, grad_wo, grad_bo)


def solution(mesh):
    placed = (
        P(("parts", "seq"), None),
        P(None, ("parts", "seq")),
        P(("parts", "seq")),
        P(("parts", "seq"), None),
        P(),
        P(),
        P(),
        P(),
        P(),
    )
    return jax.shard_map(
        local,
        mesh=mesh,
        in_specs=placed,
        out_specs=(
            P(("parts", "seq"), None),
            P(("parts", "seq"), None),
            P("parts"),
            P("parts", None),
            P("parts"),
            P("parts", None),
            P("parts"),
        ),
        check_vma=False,
    )
```

```python
import functools

import jax
import jax.numpy as jnp
from jax import lax
from jax.experimental import pallas as pl
from jax.experimental.pallas import tpu as pltpu
from jax.sharding import PartitionSpec as P

HEADS = 8
EPS = 1e-05
EMPTY = 64.0
MASKED = -1e30

F32 = jnp.float32
BF16 = jnp.bfloat16

VMEM = pl.BlockSpec(memory_space=pltpu.VMEM)
ANY = pl.BlockSpec(memory_space=pl.ANY)
SMEM = pl.BlockSpec(memory_space=pltpu.SMEM)
MIB = 1024 * 1024
LARGE = pltpu.CompilerParams(vmem_limit_bytes=32 * MIB)
SMALL = pltpu.CompilerParams(vmem_limit_bytes=8 * MIB)


def matmul(left, right, dims=((1,), (0,))):
    return lax.dot_general(left, right, (dims, ((), ())), preferred_element_type=F32)


def send_rows(route_ref, shape, axis, block_rows):
    place = lax.broadcasted_iota(jnp.int32, shape, axis)
    target = jnp.zeros(shape, jnp.int32)
    for block in range(shape[axis] // block_rows):
        first = block * block_rows
        moved = route_ref[0, block] * block_rows + place - first
        target = jnp.where(place >= first, moved, target)
    return target


def scatter_kernel(block_rows, route_hbm, points_hbm, cot_hbm, out_ref, route_ref, points_ref, cot_ref, sems):
    copies = [
        pltpu.make_async_copy(source, target, sems.at[at])
        for at, (source, target) in enumerate(
            ((route_hbm, route_ref), (points_hbm, points_ref), (cot_hbm, cot_ref))
        )
    ]
    for copy in copies:
        copy.start()
    for copy in copies:
        copy.wait()
    rows, width = points_ref.shape
    target = send_rows(route_ref, (1, rows), 1, block_rows)
    index = lax.broadcasted_iota(jnp.int32, (out_ref.shape[0], rows), 0)
    pick = jnp.where(index == target, 1.0, 0.0).astype(BF16)
    ones = jnp.ones((rows, width), BF16)
    moved = matmul(pick, jnp.concatenate([points_ref[...], ones], axis=1))
    empty = (1.0 - moved[:, width:]) * EMPTY
    out_ref[:, :width] = (moved[:, :width] + empty).astype(BF16)
    out_ref[:, width:] = matmul(pick, cot_ref[...]).astype(BF16)


def normalize(points):
    centered = points - jnp.mean(points, axis=-1, keepdims=True)
    rstd = lax.rsqrt(jnp.mean(centered * centered, axis=-1, keepdims=True) + EPS)
    return centered * rstd, rstd


def owner_kernel(near, got_ref, vectors_ref, w_qkv_hbm, w_out_hbm, attn_ref, d_normed_ref, *refs):
    *outs, w_qkv_ref, w_out_ref, both_ref, sems = refs
    copies = [
        pltpu.make_async_copy(w_qkv_hbm, w_qkv_ref, sems.at[0]),
        pltpu.make_async_copy(w_out_hbm, w_out_ref, sems.at[1]),
    ]
    for copy in copies:
        copy.start()
    rows = got_ref.shape[0]
    width = got_ref.shape[1] // 2
    head = width // HEADS
    scale = head ** (-0.5)
    gain = vectors_ref[:, :width]
    b_qkv = vectors_ref[:, 2 * width :]

    points = got_ref[:, :width].astype(F32)
    cot = got_ref[:, width:]
    xhat, _ = normalize(points)
    normed = (xhat * gain).astype(BF16)
    for copy in copies:
        copy.wait()
    w_qkv = w_qkv_ref[...]
    w_out = w_out_ref[...]
    qkv = (matmul(normed, w_qkv) + b_qkv).astype(BF16)
    query, keys, values = qkv[:, :width], qkv[:, width : 2 * width], qkv[:, 2 * width :]
    d_attn = matmul(cot, w_out, ((1,), (1,))).astype(BF16)
    d_attn_t = matmul(w_out, cot, ((1,), (1,))).astype(BF16)
    d_attn_s = (d_attn.astype(F32) * scale).astype(BF16)

    keys_t = keys.T
    values_t = values.T
    keys_s = (keys.astype(F32) * scale).astype(BF16)
    lane = lax.broadcasted_iota(jnp.int32, (rows, width), 1)
    hidden = jnp.where(points > EMPTY / 2, MASKED, 0.0).astype(BF16)
    query_x = jnp.concatenate([query, jnp.where(lane == 0, 1.0, 0.0).astype(BF16)], axis=1)

    attn_t, dq_t = [], []
    d_keys = jnp.zeros((rows, width), F32)
    d_values = jnp.zeros((rows, width), F32)
    for h in range(HEADS):
        lo, hi = h * head, (h + 1) * head
        mine = (lane >= lo) & (lane < hi)
        keys_h = jnp.concatenate([jnp.where(mine, keys_s, 0), hidden], axis=1)
        scores = matmul(keys_h, query_x, ((1,), (1,)))
        expo = jnp.exp(scores - jnp.max(scores, axis=0, keepdims=True))
        probs = expo * (1.0 / jnp.sum(expo, axis=0, keepdims=True))
        probs_b = probs.astype(BF16)
        out_t = matmul(values_t[lo:hi, :], probs_b)
        attn_t.append(out_t)
        inner = jnp.sum(out_t * d_attn_t[lo:hi, :].astype(F32), axis=0, keepdims=True) * scale
        d_probs = matmul(jnp.where(mine, values, 0), d_attn_s, ((1,), (1,)))
        d_score = (probs * (d_probs - inner)).astype(BF16)
        dq_t.append(matmul(keys_t[lo:hi, :], d_score))
        d_values = jnp.where(mine, matmul(probs_b, d_attn), d_values)
        d_keys = jnp.where(mine, matmul(d_score, query), d_keys)

    attn_t = jnp.concatenate(attn_t, axis=0)
    attn_ref[...] = attn_t.T.astype(BF16)
    grad_w_out = matmul(attn_t.astype(BF16), cot)
    grad_b_out = jnp.sum(cot.astype(F32), axis=0, keepdims=True)

    d_query = jnp.concatenate(dq_t, axis=0).T
    d_qkv = jnp.concatenate([d_query, d_keys, d_values], axis=1).astype(BF16)
    d_normed = matmul(d_qkv, w_qkv, ((1,), (1,)))
    grad_w_qkv = matmul(normed, d_qkv, ((0,), (0,)))
    grad_b_qkv = jnp.sum(d_qkv.astype(F32), axis=0, keepdims=True)
    grad_gain = jnp.sum(d_normed * xhat, axis=0, keepdims=True)
    d_normed_ref[...] = d_normed
    sums = jnp.concatenate(
        [
            grad_b_qkv[:, : 2 * width],
            jnp.concatenate([grad_b_qkv[:, 2 * width :], grad_b_out], axis=1),
            jnp.concatenate([grad_gain, jnp.zeros_like(grad_gain)], axis=1),
            jnp.zeros((5, 2 * width), F32),
        ],
        axis=0,
    )
    left = grad_w_qkv[:, : 2 * width]
    right = jnp.concatenate([grad_w_qkv[:, 2 * width :], grad_w_out], axis=1)
    if near == 1:
        left_ref, right_ref, sums_ref = outs
        left_ref[...] = left.astype(BF16)
        right_ref[...] = right.astype(BF16)
        sums_ref[...] = sums.astype(BF16)
        return
    part_refs = outs
    both_ref[:width] = left
    both_ref[width:] = right
    span = 2 * width // near
    me = lax.axis_index("seq")
    for step, part_ref in enumerate(part_refs):
        first = ((me ^ step) & (near - 1)) * span
        part_ref[:span] = both_ref[pl.ds(pl.multiple_of(first, span), span)].astype(BF16)
        part_ref[span:] = sums.astype(BF16)


def rows_kernel(got_ref, attn_ref, d_normed_ref, vectors_ref, w_out_ref, *refs):
    back_ref = refs[-1]
    width = attn_ref.shape[1]
    gain = vectors_ref[:, :width]
    b_out = vectors_ref[:, width : 2 * width]
    points = got_ref[:, :width].astype(F32)
    cot = got_ref[:, width:].astype(F32)
    xhat, rstd = normalize(points)
    mixed = points + (matmul(attn_ref[...], w_out_ref[...]) + b_out)
    d_xhat = d_normed_ref[...] * gain
    inner = (
        d_xhat
        - jnp.mean(d_xhat, axis=-1, keepdims=True)
        - xhat * jnp.mean(d_xhat * xhat, axis=-1, keepdims=True)
    )
    back_ref[:, :width] = mixed.astype(BF16)
    back_ref[:, width:] = (cot + rstd * inner).astype(BF16)


def tree(values):
    while len(values) > 1:
        values = [left + right for left, right in zip(values[::2], values[1::2])]
    return values[0]


def sum_kernel(*refs):
    *part_refs, out_ref = refs
    out_ref[...] = tree([part_ref[...].astype(F32) for part_ref in part_refs]).astype(BF16)


def return_kernel(block_rows, route_hbm, back_ref, mixed_ref, grad_ref, token_ref, route_ref, sem):
    token_ref[...] = jnp.zeros_like(token_ref)
    copy = pltpu.make_async_copy(route_hbm, route_ref, sem)
    copy.start()
    copy.wait()
    rows, width = mixed_ref.shape
    target = send_rows(route_ref, (rows, 1), 0, block_rows)
    index = lax.broadcasted_iota(jnp.int32, (rows, back_ref.shape[0]), 1)
    pick = jnp.where(index == target, 1.0, 0.0).astype(BF16)
    moved = matmul(pick, back_ref[...]).astype(BF16)
    mixed_ref[...] = moved[:, :width]
    grad_ref[...] = moved[:, width:]


def weights_kernel(*refs):
    *part_refs, _, gain_ref, w_qkv_ref, b_qkv_ref, w_out_ref, b_out_ref, both_ref = refs
    width = w_out_ref.shape[1]
    near = len(part_refs)
    span = 2 * width // near
    me = lax.axis_index("seq")
    for step, part_ref in enumerate(part_refs):
        place = (me ^ step) & (near - 1)
        part = part_ref[...].astype(F32)
        both_ref[pl.ds(pl.multiple_of(place * span, span), span)] = part[:span]

        @pl.when(place == 0)
        def _():
            sums = part[span:]
            gain_ref[...] = sums[2, :width]
            b_qkv_ref[: 2 * width] = sums[0]
            b_qkv_ref[2 * width :] = sums[1, :width]
            b_out_ref[...] = sums[1, width:]

    w_qkv_ref[:, : 2 * width] = both_ref[:width]
    w_qkv_ref[:, 2 * width :] = both_ref[width:, :width]
    w_out_ref[...] = both_ref[width:, width:]


def exchange(message):
    return lax.all_to_all(message, "seq", split_axis=0, concat_axis=0, tiled=True)


def swap(piece, step, devs):
    return lax.ppermute(piece, "seq", [(dev, dev ^ step) for dev in range(devs)])


def local(points, route, owned, cotangent, gain, w_qkv, b_qkv, w_out, b_out):
    devs = lax.axis_size("seq")
    rows, width = points.shape
    block_rows = rows // route.shape[1]
    held = devs * block_rows
    share = width // devs
    near = 4 if devs == 16 and width % 64 == 0 else 1

    def shape(*dims, dtype=BF16):
        return jax.ShapeDtypeStruct(dims, dtype)

    sent = pl.pallas_call(
        functools.partial(scatter_kernel, block_rows),
        out_shape=shape(held, 2 * width),
        in_specs=[ANY] * 3,
        out_specs=VMEM,
        scratch_shapes=[
            pltpu.SMEM(route.shape, route.dtype),
            pltpu.VMEM(points.shape, points.dtype),
            pltpu.VMEM(cotangent.shape, cotangent.dtype),
            pltpu.SemaphoreType.DMA((3,)),
        ],
    )(route, points, cotangent)
    got = exchange(sent.reshape(devs, block_rows, 2 * width)).reshape(held, 2 * width)

    part = shape(2 * width // near + 8, 2 * width)
    if near > 1:
        sums_shapes = (part,) * near
    else:
        sums_shapes = (shape(width, 2 * width),) * 2 + (shape(8, 2 * width),)
    vectors = jnp.concatenate([gain, b_out, b_qkv])[None, :]
    attn, d_normed, *parts = pl.pallas_call(
        functools.partial(owner_kernel, near),
        out_shape=(shape(held, width), shape(held, width, dtype=F32)) + sums_shapes,
        in_specs=[VMEM, VMEM, ANY, ANY],
        out_specs=(VMEM,) * (2 + len(sums_shapes)),
        scratch_shapes=[
            pltpu.VMEM(w_qkv.shape, w_qkv.dtype),
            pltpu.VMEM(w_out.shape, w_out.dtype),
            pltpu.VMEM((2 * width, 2 * width), F32),
            pltpu.SemaphoreType.DMA((2,)),
        ],
        compiler_params=LARGE,
    )(got, vectors, w_qkv, w_out)
    first = []
    if near > 1:
        first = [swap(parts[step], step, devs) for step in range(1, near)]
    back = pl.pallas_call(
        rows_kernel,
        out_shape=shape(held, 2 * width),
        in_specs=[VMEM] * (5 + len(first[:1])),
        out_specs=VMEM,
        compiler_params=SMALL,
        cost_estimate=pl.CostEstimate(
            flops=64 * held * width * width, bytes_accessed=16 * held * width, transcendentals=0
        ),
    )(got, attn, d_normed, vectors, w_out, *first[:1])

    def give_back(back):
        return pl.pallas_call(
            functools.partial(return_kernel, block_rows),
            out_shape=(shape(rows, width), shape(rows, width), shape(8, 128, dtype=F32)),
            in_specs=[ANY, VMEM],
            out_specs=(VMEM,) * 3,
            scratch_shapes=[pltpu.SMEM(route.shape, route.dtype), pltpu.SemaphoreType.DMA],
            compiler_params=SMALL,
        )(route, back)

    if near > 1:
        back = exchange(back.reshape(devs, block_rows, 2 * width)).reshape(held, 2 * width)
        mixed, grad_points, token = give_back(back)

        def add(pieces):
            return pl.pallas_call(
                sum_kernel,
                out_shape=part,
                in_specs=[VMEM] * len(pieces),
                out_specs=VMEM,
                compiler_params=SMALL,
            )(*pieces)

        total = add([parts[0]] + first)
        step = near
        while step < devs:
            total = add([total, swap(total, step, devs)])
            step *= 2
        parts = [total] + [swap(total, step, devs) for step in range(1, near)]
        grad_gain, grad_wq, grad_bq, grad_wo, grad_bo = pl.pallas_call(
            weights_kernel,
            out_shape=tuple(
                shape(*dims, dtype=F32)
                for dims in ((width,), (width, 3 * width), (3 * width,), (width, width), (width,))
            ),
            in_specs=[VMEM] * (near + 1),
            out_specs=(VMEM,) * 5,
            scratch_shapes=[pltpu.VMEM((2 * width, 2 * width), F32)],
            compiler_params=SMALL,
        )(*parts, token)
    else:
        left, right, sums = parts
        message = jnp.concatenate(
            [
                back.reshape(devs, block_rows, 2 * width),
                left.reshape(devs, share, 2 * width),
                right.reshape(devs, share, 2 * width),
                jnp.broadcast_to(sums[None], (devs, 8, 2 * width)),
            ],
            axis=1,
        )
        message = exchange(message)
        total = jnp.sum(message[:, block_rows:].astype(F32), axis=0)
        mine = total[: 2 * share].astype(BF16)
        both = exchange(jnp.broadcast_to(mine[None], (devs, 2 * share, 2 * width))).astype(F32)
        mixed, grad_points, _ = give_back(message[:, :block_rows].reshape(held, 2 * width))
        left = both[:, :share].reshape(width, 2 * width)
        right = both[:, share:].reshape(width, 2 * width)
        grad_wq = jnp.concatenate([left, right[:, :width]], axis=1)
        grad_wo = right[:, width:]
        flat = total[2 * share :].reshape(-1)
        grad_bq = flat[: 3 * width]
        grad_bo = flat[3 * width : 4 * width]
        grad_gain = flat[4 * width : 5 * width]

    return (mixed, grad_points, grad_gain, grad_wq, grad_bq, grad_wo, grad_bo)


def solution(mesh):
    placed = (
        P(("parts", "seq"), None),
        P(None, ("parts", "seq")),
        P(("parts", "seq")),
        P(("parts", "seq"), None),
        P(),
        P(),
        P(),
        P(),
        P(),
    )
    return jax.shard_map(
        local,
        mesh=mesh,
        in_specs=placed,
        out_specs=(
            P(("parts", "seq"), None),
            P(("parts", "seq"), None),
            P("parts"),
            P("parts", None),
            P("parts"),
            P("parts", None),
            P("parts"),
        ),
        check_vma=False,
    )
```

```python
import functools

import jax
import jax.numpy as jnp
from jax import lax
from jax.experimental import pallas as pl
from jax.experimental.pallas import tpu as pltpu
from jax.sharding import PartitionSpec as P

HEADS = 8
EPS = 1e-05
EMPTY = 64.0
MASKED = -1e30

F32 = jnp.float32
BF16 = jnp.bfloat16

VMEM = pl.BlockSpec(memory_space=pltpu.VMEM)
ANY = pl.BlockSpec(memory_space=pl.ANY)
SMEM = pl.BlockSpec(memory_space=pltpu.SMEM)
MIB = 1024 * 1024
LARGE = pltpu.CompilerParams(vmem_limit_bytes=32 * MIB)
SMALL = pltpu.CompilerParams(vmem_limit_bytes=8 * MIB)


def matmul(left, right, dims=((1,), (0,))):
    return lax.dot_general(left, right, (dims, ((), ())), preferred_element_type=F32)


def send_rows(route_ref, shape, axis, block_rows):
    place = lax.broadcasted_iota(jnp.int32, shape, axis)
    target = jnp.zeros(shape, jnp.int32)
    for block in range(shape[axis] // block_rows):
        first = block * block_rows
        moved = route_ref[0, block] * block_rows + place - first
        target = jnp.where(place >= first, moved, target)
    return target


def scatter_kernel(block_rows, route_hbm, points_hbm, cot_hbm, out_ref, route_ref, points_ref, cot_ref, sems):
    copies = [
        pltpu.make_async_copy(source, target, sems.at[at])
        for at, (source, target) in enumerate(
            ((route_hbm, route_ref), (points_hbm, points_ref), (cot_hbm, cot_ref))
        )
    ]
    for copy in copies:
        copy.start()
    for copy in copies:
        copy.wait()
    rows, width = points_ref.shape
    target = send_rows(route_ref, (1, rows), 1, block_rows)
    index = lax.broadcasted_iota(jnp.int32, (out_ref.shape[0], rows), 0)
    pick = jnp.where(index == target, 1.0, 0.0).astype(BF16)
    ones = jnp.ones((rows, width), BF16)
    moved = matmul(pick, jnp.concatenate([points_ref[...], ones], axis=1))
    empty = (1.0 - moved[:, width:]) * EMPTY
    out_ref[:, :width] = (moved[:, :width] + empty).astype(BF16)
    out_ref[:, width:] = matmul(pick, cot_ref[...]).astype(BF16)


def normalize(points):
    centered = points - jnp.mean(points, axis=-1, keepdims=True)
    rstd = lax.rsqrt(jnp.mean(centered * centered, axis=-1, keepdims=True) + EPS)
    return centered * rstd, rstd


def owner_kernel(near, got_ref, vectors_ref, w_qkv_hbm, w_out_hbm, attn_ref, d_normed_ref, *refs):
    *outs, w_qkv_ref, w_out_ref, both_ref, sems = refs
    copies = [
        pltpu.make_async_copy(w_qkv_hbm, w_qkv_ref, sems.at[0]),
        pltpu.make_async_copy(w_out_hbm, w_out_ref, sems.at[1]),
    ]
    for copy in copies:
        copy.start()
    rows = got_ref.shape[0]
    width = got_ref.shape[1] // 2
    head = width // HEADS
    scale = head ** (-0.5)
    gain = vectors_ref[:, :width]
    b_qkv = vectors_ref[:, 2 * width :]

    points = got_ref[:, :width].astype(F32)
    cot = got_ref[:, width:]
    xhat, _ = normalize(points)
    normed = (xhat * gain).astype(BF16)
    for copy in copies:
        copy.wait()
    w_qkv = w_qkv_ref[...]
    w_out = w_out_ref[...]
    qkv = (matmul(normed, w_qkv) + b_qkv).astype(BF16)
    query, keys, values = qkv[:, :width], qkv[:, width : 2 * width], qkv[:, 2 * width :]
    d_attn = matmul(cot, w_out, ((1,), (1,))).astype(BF16)
    d_attn_t = matmul(w_out, cot, ((1,), (1,))).astype(BF16)
    d_attn_s = (d_attn.astype(F32) * scale).astype(BF16)

    keys_t = keys.T
    values_t = values.T
    keys_s = (keys.astype(F32) * scale).astype(BF16)
    lane = lax.broadcasted_iota(jnp.int32, (rows, width), 1)
    hidden = jnp.where(points > EMPTY / 2, MASKED, 0.0).astype(BF16)
    query_x = jnp.concatenate([query, jnp.where(lane == 0, 1.0, 0.0).astype(BF16)], axis=1)

    attn_t, dq_t = [], []
    d_keys = jnp.zeros((rows, width), F32)
    d_values = jnp.zeros((rows, width), F32)
    for h in range(HEADS):
        lo, hi = h * head, (h + 1) * head
        mine = (lane >= lo) & (lane < hi)
        keys_h = jnp.concatenate([jnp.where(mine, keys_s, 0), hidden], axis=1)
        scores = matmul(keys_h, query_x, ((1,), (1,)))
        expo = jnp.exp(scores - jnp.max(scores, axis=0, keepdims=True))
        probs = expo * (1.0 / jnp.sum(expo, axis=0, keepdims=True))
        probs_b = probs.astype(BF16)
        out_t = matmul(values_t[lo:hi, :], probs_b)
        attn_t.append(out_t)
        inner = jnp.sum(out_t * d_attn_t[lo:hi, :].astype(F32), axis=0, keepdims=True) * scale
        d_probs = matmul(jnp.where(mine, values, 0), d_attn_s, ((1,), (1,)))
        d_score = (probs * (d_probs - inner)).astype(BF16)
        dq_t.append(matmul(keys_t[lo:hi, :], d_score))
        d_values = jnp.where(mine, matmul(probs_b, d_attn), d_values)
        d_keys = jnp.where(mine, matmul(d_score, query), d_keys)

    attn_t = jnp.concatenate(attn_t, axis=0)
    attn_ref[...] = attn_t.T.astype(BF16)
    grad_w_out = matmul(attn_t.astype(BF16), cot)
    grad_b_out = jnp.sum(cot.astype(F32), axis=0, keepdims=True)

    d_query = jnp.concatenate(dq_t, axis=0).T
    d_qkv = jnp.concatenate([d_query, d_keys, d_values], axis=1).astype(BF16)
    d_normed = matmul(d_qkv, w_qkv, ((1,), (1,)))
    grad_w_qkv = matmul(normed, d_qkv, ((0,), (0,)))
    grad_b_qkv = jnp.sum(d_qkv.astype(F32), axis=0, keepdims=True)
    grad_gain = jnp.sum(d_normed * xhat, axis=0, keepdims=True)
    d_normed_ref[...] = d_normed
    sums = jnp.concatenate(
        [
            grad_b_qkv[:, : 2 * width],
            jnp.concatenate([grad_b_qkv[:, 2 * width :], grad_b_out], axis=1),
            jnp.concatenate([grad_gain, jnp.zeros_like(grad_gain)], axis=1),
            jnp.zeros((5, 2 * width), F32),
        ],
        axis=0,
    )
    left = grad_w_qkv[:, : 2 * width]
    right = jnp.concatenate([grad_w_qkv[:, 2 * width :], grad_w_out], axis=1)
    if near == 1:
        left_ref, right_ref, sums_ref = outs
        left_ref[...] = left.astype(BF16)
        right_ref[...] = right.astype(BF16)
        sums_ref[...] = sums.astype(BF16)
        return
    mine_ref, theirs_ref = outs
    both_ref[:width] = left
    both_ref[width:] = right
    core = lax.axis_index("seq") & 1
    for half, half_ref in ((core, mine_ref), (core ^ 1, theirs_ref)):
        span = pl.ds(pl.multiple_of(half * width, width), width)
        half_ref[:width] = both_ref[span].astype(half_ref.dtype)
        half_ref[width:] = sums.astype(half_ref.dtype)


def rows_kernel(got_ref, attn_ref, d_normed_ref, vectors_ref, w_out_ref, back_ref):
    width = attn_ref.shape[1]
    gain = vectors_ref[:, :width]
    b_out = vectors_ref[:, width : 2 * width]
    points = got_ref[:, :width].astype(F32)
    cot = got_ref[:, width:].astype(F32)
    xhat, rstd = normalize(points)
    mixed = points + (matmul(attn_ref[...], w_out_ref[...]) + b_out)
    d_xhat = d_normed_ref[...] * gain
    inner = (
        d_xhat
        - jnp.mean(d_xhat, axis=-1, keepdims=True)
        - xhat * jnp.mean(d_xhat * xhat, axis=-1, keepdims=True)
    )
    back_ref[:, :width] = mixed.astype(BF16)
    back_ref[:, width:] = (cot + rstd * inner).astype(BF16)


def halve_kernel(bit, mine_ref, got_ref, keep_ref, send_ref):
    rows = (mine_ref.shape[0] - 8) // 2
    place = (lax.axis_index("seq") >> bit) & 1
    sums = mine_ref[2 * rows :] + got_ref[2 * rows :].astype(F32)
    for half, half_ref in ((place, keep_ref), (place ^ 1, send_ref)):
        span = pl.ds(pl.multiple_of(half * rows, rows), rows)
        half_ref[:rows] = (mine_ref[span] + got_ref[span].astype(F32)).astype(half_ref.dtype)
        half_ref[rows:] = sums.astype(half_ref.dtype)


def sum_kernel(left_ref, right_ref, out_ref):
    out_ref[...] = (left_ref[...].astype(F32) + right_ref[...].astype(F32)).astype(BF16)


def tie_kernel(rows_ref, other_ref, out_ref):
    pass


def return_kernel(block_rows, route_hbm, back_ref, mixed_ref, grad_ref, token_ref, route_ref, sem):
    token_ref[...] = jnp.zeros_like(token_ref)
    copy = pltpu.make_async_copy(route_hbm, route_ref, sem)
    copy.start()
    copy.wait()
    rows, width = mixed_ref.shape
    target = send_rows(route_ref, (rows, 1), 0, block_rows)
    index = lax.broadcasted_iota(jnp.int32, (rows, back_ref.shape[0]), 1)
    pick = jnp.where(index == target, 1.0, 0.0).astype(BF16)
    moved = matmul(pick, back_ref[...]).astype(BF16)
    mixed_ref[...] = moved[:, :width]
    grad_ref[...] = moved[:, width:]


def weights_kernel(*refs):
    *part_refs, _, gain_ref, w_qkv_ref, b_qkv_ref, w_out_ref, b_out_ref, both_ref = refs
    width = w_out_ref.shape[1]
    near = len(part_refs)
    span = 2 * width // near
    me = lax.axis_index("seq")
    for step, part_ref in enumerate(part_refs):
        index = (me ^ step) & (near - 1)
        place = 2 * (index & 1) + (index >> 1)
        part = part_ref[...].astype(F32)
        both_ref[pl.ds(pl.multiple_of(place * span, span), span)] = part[:span]

        @pl.when(place == 0)
        def _():
            sums = part[span:]
            gain_ref[...] = sums[2, :width]
            b_qkv_ref[: 2 * width] = sums[0]
            b_qkv_ref[2 * width :] = sums[1, :width]
            b_out_ref[...] = sums[1, width:]

    w_qkv_ref[:, : 2 * width] = both_ref[:width]
    w_qkv_ref[:, 2 * width :] = both_ref[width:, :width]
    w_out_ref[...] = both_ref[width:, width:]


def exchange(message):
    return lax.all_to_all(message, "seq", split_axis=0, concat_axis=0, tiled=True)


def swap(piece, step, devs):
    return lax.ppermute(piece, "seq", [(dev, dev ^ step) for dev in range(devs)])


def local(points, route, owned, cotangent, gain, w_qkv, b_qkv, w_out, b_out):
    devs = lax.axis_size("seq")
    rows, width = points.shape
    block_rows = rows // route.shape[1]
    held = devs * block_rows
    share = width // devs
    near = 4 if devs == 16 and width % 64 == 0 else 1

    def shape(*dims, dtype=BF16):
        return jax.ShapeDtypeStruct(dims, dtype)

    sent = pl.pallas_call(
        functools.partial(scatter_kernel, block_rows),
        out_shape=shape(held, 2 * width),
        in_specs=[ANY] * 3,
        out_specs=VMEM,
        scratch_shapes=[
            pltpu.SMEM(route.shape, route.dtype),
            pltpu.VMEM(points.shape, points.dtype),
            pltpu.VMEM(cotangent.shape, cotangent.dtype),
            pltpu.SemaphoreType.DMA((3,)),
        ],
    )(route, points, cotangent)
    got = exchange(sent.reshape(devs, block_rows, 2 * width)).reshape(held, 2 * width)

    part = shape(2 * width // near + 8, 2 * width)
    if near > 1:
        half = (width + 8, 2 * width)
        sums_shapes = (shape(*half, dtype=F32), shape(*half))
    else:
        sums_shapes = (shape(width, 2 * width),) * 2 + (shape(8, 2 * width),)
    vectors = jnp.concatenate([gain, b_out, b_qkv])[None, :]
    attn, d_normed, *parts = pl.pallas_call(
        functools.partial(owner_kernel, near),
        out_shape=(shape(held, width), shape(held, width, dtype=F32)) + sums_shapes,
        in_specs=[VMEM, VMEM, ANY, ANY],
        out_specs=(VMEM,) * (2 + len(sums_shapes)),
        scratch_shapes=[
            pltpu.VMEM(w_qkv.shape, w_qkv.dtype),
            pltpu.VMEM(w_out.shape, w_out.dtype),
            pltpu.VMEM((2 * width, 2 * width), F32),
            pltpu.SemaphoreType.DMA((2,)),
        ],
        compiler_params=LARGE,
    )(got, vectors, w_qkv, w_out)
    back = pl.pallas_call(
        rows_kernel,
        out_shape=shape(held, 2 * width),
        in_specs=[VMEM] * 5,
        out_specs=VMEM,
        compiler_params=SMALL,
        cost_estimate=pl.CostEstimate(
            flops=64 * held * width * width, bytes_accessed=16 * held * width, transcendentals=0
        ),
    )(got, attn, d_normed, vectors, w_out)

    def give_back(back):
        return pl.pallas_call(
            functools.partial(return_kernel, block_rows),
            out_shape=(shape(rows, width), shape(rows, width), shape(8, 128, dtype=F32)),
            in_specs=[ANY, VMEM],
            out_specs=(VMEM,) * 3,
            scratch_shapes=[pltpu.SMEM(route.shape, route.dtype), pltpu.SemaphoreType.DMA],
            compiler_params=SMALL,
        )(route, back)

    if near > 1:
        mine, theirs = parts
        keep, send = pl.pallas_call(
            functools.partial(halve_kernel, 1),
            out_shape=(shape(*part.shape, dtype=F32), part),
            in_specs=[VMEM] * 2,
            out_specs=(VMEM,) * 2,
            compiler_params=SMALL,
        )(mine, swap(theirs, 1, devs))

        def add(left, right):
            return pl.pallas_call(
                sum_kernel,
                out_shape=part,
                in_specs=[VMEM] * 2,
                out_specs=VMEM,
                compiler_params=SMALL,
            )(left, right)

        total = add(keep, swap(send, 2, devs))
        back = pl.pallas_call(
            tie_kernel,
            out_shape=back,
            in_specs=[ANY, VMEM],
            out_specs=ANY,
            input_output_aliases={0: 0},
            compiler_params=SMALL,
        )(back, total)
        back = exchange(back.reshape(devs, block_rows, 2 * width)).reshape(held, 2 * width)
        mixed, grad_points, token = give_back(back)
        step = near
        while step < devs:
            total = add(total, swap(total, step, devs))
            step *= 2
        parts = [total] + [swap(total, step, devs) for step in range(1, near)]
        grad_gain, grad_wq, grad_bq, grad_wo, grad_bo = pl.pallas_call(
            weights_kernel,
            out_shape=tuple(
                shape(*dims, dtype=F32)
                for dims in ((width,), (width, 3 * width), (3 * width,), (width, width), (width,))
            ),
            in_specs=[VMEM] * (near + 1),
            out_specs=(VMEM,) * 5,
            scratch_shapes=[pltpu.VMEM((2 * width, 2 * width), F32)],
            compiler_params=SMALL,
        )(*parts, token)
    else:
        left, right, sums = parts
        message = jnp.concatenate(
            [
                back.reshape(devs, block_rows, 2 * width),
                left.reshape(devs, share, 2 * width),
                right.reshape(devs, share, 2 * width),
                jnp.broadcast_to(sums[None], (devs, 8, 2 * width)),
            ],
            axis=1,
        )
        message = exchange(message)
        total = jnp.sum(message[:, block_rows:].astype(F32), axis=0)
        mine = total[: 2 * share].astype(BF16)
        both = exchange(jnp.broadcast_to(mine[None], (devs, 2 * share, 2 * width))).astype(F32)
        mixed, grad_points, _ = give_back(message[:, :block_rows].reshape(held, 2 * width))
        left = both[:, :share].reshape(width, 2 * width)
        right = both[:, share:].reshape(width, 2 * width)
        grad_wq = jnp.concatenate([left, right[:, :width]], axis=1)
        grad_wo = right[:, width:]
        flat = total[2 * share :].reshape(-1)
        grad_bq = flat[: 3 * width]
        grad_bo = flat[3 * width : 4 * width]
        grad_gain = flat[4 * width : 5 * width]

    return (mixed, grad_points, grad_gain, grad_wq, grad_bq, grad_wo, grad_bo)


def solution(mesh):
    placed = (
        P(("parts", "seq"), None),
        P(None, ("parts", "seq")),
        P(("parts", "seq")),
        P(("parts", "seq"), None),
        P(),
        P(),
        P(),
        P(),
        P(),
    )
    return jax.shard_map(
        local,
        mesh=mesh,
        in_specs=placed,
        out_specs=(
            P(("parts", "seq"), None),
            P(("parts", "seq"), None),
            P("parts"),
            P("parts", None),
            P("parts"),
            P("parts", None),
            P("parts"),
        ),
        check_vma=False,
    )
```

```python
import functools

import jax
import jax.numpy as jnp
from jax import lax
from jax.experimental import pallas as pl
from jax.experimental.pallas import tpu as pltpu
from jax.sharding import PartitionSpec as P

HEADS = 8
EPS = 1e-05
EMPTY = 64.0
MASKED = -1e30

F32 = jnp.float32
BF16 = jnp.bfloat16

VMEM = pl.BlockSpec(memory_space=pltpu.VMEM)
ANY = pl.BlockSpec(memory_space=pl.ANY)
SMEM = pl.BlockSpec(memory_space=pltpu.SMEM)
MIB = 1024 * 1024
LARGE = pltpu.CompilerParams(vmem_limit_bytes=32 * MIB)
SMALL = pltpu.CompilerParams(vmem_limit_bytes=8 * MIB)


def matmul(left, right, dims=((1,), (0,))):
    return lax.dot_general(left, right, (dims, ((), ())), preferred_element_type=F32)


def send_rows(route_ref, shape, axis, block_rows):
    place = lax.broadcasted_iota(jnp.int32, shape, axis)
    target = jnp.zeros(shape, jnp.int32)
    for block in range(shape[axis] // block_rows):
        first = block * block_rows
        moved = route_ref[0, block] * block_rows + place - first
        target = jnp.where(place >= first, moved, target)
    return target


def scatter_kernel(block_rows, route_hbm, points_hbm, cot_hbm, out_ref, route_ref, points_ref, cot_ref, sems):
    copies = [
        pltpu.make_async_copy(source, target, sems.at[at])
        for at, (source, target) in enumerate(
            ((route_hbm, route_ref), (points_hbm, points_ref), (cot_hbm, cot_ref))
        )
    ]
    for copy in copies:
        copy.start()
    for copy in copies:
        copy.wait()
    rows, width = points_ref.shape
    target = send_rows(route_ref, (1, rows), 1, block_rows)
    index = lax.broadcasted_iota(jnp.int32, (out_ref.shape[0], rows), 0)
    pick = jnp.where(index == target, 1.0, 0.0).astype(BF16)
    ones = jnp.ones((rows, width), BF16)
    moved = matmul(pick, jnp.concatenate([points_ref[...], ones], axis=1))
    empty = (1.0 - moved[:, width:]) * EMPTY
    out_ref[:, :width] = (moved[:, :width] + empty).astype(BF16)
    out_ref[:, width:] = matmul(pick, cot_ref[...]).astype(BF16)


def normalize(points):
    centered = points - jnp.mean(points, axis=-1, keepdims=True)
    rstd = lax.rsqrt(jnp.mean(centered * centered, axis=-1, keepdims=True) + EPS)
    return centered * rstd, rstd


def owner_kernel(near, got_ref, vectors_ref, w_qkv_hbm, w_out_hbm, attn_ref, d_normed_ref, *refs):
    *outs, w_qkv_ref, w_out_ref, both_ref, sems = refs
    copies = [
        pltpu.make_async_copy(w_qkv_hbm, w_qkv_ref, sems.at[0]),
        pltpu.make_async_copy(w_out_hbm, w_out_ref, sems.at[1]),
    ]
    for copy in copies:
        copy.start()
    rows = got_ref.shape[0]
    width = got_ref.shape[1] // 2
    head = width // HEADS
    scale = head ** (-0.5)
    gain = vectors_ref[:, :width]
    b_qkv = vectors_ref[:, 2 * width :]

    points = got_ref[:, :width].astype(F32)
    cot = got_ref[:, width:]
    xhat, _ = normalize(points)
    normed = (xhat * gain).astype(BF16)
    for copy in copies:
        copy.wait()
    w_qkv = w_qkv_ref[...]
    w_out = w_out_ref[...]
    qkv = (matmul(normed, w_qkv) + b_qkv).astype(BF16)
    query, keys, values = qkv[:, :width], qkv[:, width : 2 * width], qkv[:, 2 * width :]
    d_attn = matmul(cot, w_out, ((1,), (1,))).astype(BF16)
    d_attn_t = matmul(w_out, cot, ((1,), (1,))).astype(BF16)
    d_attn_s = (d_attn.astype(F32) * scale).astype(BF16)

    keys_t = keys.T
    values_t = values.T
    keys_s = (keys.astype(F32) * scale).astype(BF16)
    lane = lax.broadcasted_iota(jnp.int32, (rows, width), 1)
    hidden = jnp.where(points > EMPTY / 2, MASKED, 0.0).astype(BF16)
    query_x = jnp.concatenate([query, jnp.where(lane == 0, 1.0, 0.0).astype(BF16)], axis=1)

    attn_t, dq_t = [], []
    d_keys = jnp.zeros((rows, width), F32)
    d_values = jnp.zeros((rows, width), F32)
    for h in range(HEADS):
        lo, hi = h * head, (h + 1) * head
        mine = (lane >= lo) & (lane < hi)
        keys_h = jnp.concatenate([jnp.where(mine, keys_s, 0), hidden], axis=1)
        scores = matmul(keys_h, query_x, ((1,), (1,)))
        expo = jnp.exp(scores - jnp.max(scores, axis=0, keepdims=True))
        probs = expo * (1.0 / jnp.sum(expo, axis=0, keepdims=True))
        probs_b = probs.astype(BF16)
        out_t = matmul(values_t[lo:hi, :], probs_b)
        attn_t.append(out_t)
        inner = jnp.sum(out_t * d_attn_t[lo:hi, :].astype(F32), axis=0, keepdims=True) * scale
        d_probs = matmul(jnp.where(mine, values, 0), d_attn_s, ((1,), (1,)))
        d_score = (probs * (d_probs - inner)).astype(BF16)
        dq_t.append(matmul(keys_t[lo:hi, :], d_score))
        d_values = jnp.where(mine, matmul(probs_b, d_attn), d_values)
        d_keys = jnp.where(mine, matmul(d_score, query), d_keys)

    attn_t = jnp.concatenate(attn_t, axis=0)
    attn_ref[...] = attn_t.T.astype(BF16)
    grad_w_out = matmul(attn_t.astype(BF16), cot)
    grad_b_out = jnp.sum(cot.astype(F32), axis=0, keepdims=True)

    d_query = jnp.concatenate(dq_t, axis=0).T
    d_qkv = jnp.concatenate([d_query, d_keys, d_values], axis=1).astype(BF16)
    d_normed = matmul(d_qkv, w_qkv, ((1,), (1,)))
    grad_w_qkv = matmul(normed, d_qkv, ((0,), (0,)))
    grad_b_qkv = jnp.sum(d_qkv.astype(F32), axis=0, keepdims=True)
    grad_gain = jnp.sum(d_normed * xhat, axis=0, keepdims=True)
    d_normed_ref[...] = d_normed
    sums = jnp.concatenate(
        [
            grad_b_qkv[:, : 2 * width],
            jnp.concatenate([grad_b_qkv[:, 2 * width :], grad_b_out], axis=1),
            jnp.concatenate([grad_gain, jnp.zeros_like(grad_gain)], axis=1),
            jnp.zeros((5, 2 * width), F32),
        ],
        axis=0,
    )
    left = grad_w_qkv[:, : 2 * width]
    right = jnp.concatenate([grad_w_qkv[:, 2 * width :], grad_w_out], axis=1)
    if near == 1:
        left_ref, right_ref, sums_ref = outs
        left_ref[...] = left.astype(BF16)
        right_ref[...] = right.astype(BF16)
        sums_ref[...] = sums.astype(BF16)
        return
    mine_ref, theirs_ref = outs
    both_ref[:width] = left
    both_ref[width:] = right
    core = lax.axis_index("seq") & 1
    for half, half_ref in ((core, mine_ref), (core ^ 1, theirs_ref)):
        span = pl.ds(pl.multiple_of(half * width, width), width)
        half_ref[:width] = both_ref[span].astype(half_ref.dtype)
        half_ref[width:] = sums.astype(half_ref.dtype)


def rows_kernel(got_ref, attn_ref, d_normed_ref, vectors_ref, w_out_ref, back_ref):
    width = attn_ref.shape[1]
    gain = vectors_ref[:, :width]
    b_out = vectors_ref[:, width : 2 * width]
    points = got_ref[:, :width].astype(F32)
    cot = got_ref[:, width:].astype(F32)
    xhat, rstd = normalize(points)
    mixed = points + (matmul(attn_ref[...], w_out_ref[...]) + b_out)
    d_xhat = d_normed_ref[...] * gain
    inner = (
        d_xhat
        - jnp.mean(d_xhat, axis=-1, keepdims=True)
        - xhat * jnp.mean(d_xhat * xhat, axis=-1, keepdims=True)
    )
    back_ref[:, :width] = mixed.astype(BF16)
    back_ref[:, width:] = (cot + rstd * inner).astype(BF16)


def halve_kernel(bit, mine_ref, got_ref, keep_ref, send_ref):
    rows = (mine_ref.shape[0] - 8) // 2
    place = (lax.axis_index("seq") >> bit) & 1
    sums = mine_ref[2 * rows :] + got_ref[2 * rows :].astype(F32)
    for half, half_ref in ((place, keep_ref), (place ^ 1, send_ref)):
        span = pl.ds(pl.multiple_of(half * rows, rows), rows)
        half_ref[:rows] = (mine_ref[span] + got_ref[span].astype(F32)).astype(half_ref.dtype)
        half_ref[rows:] = sums.astype(half_ref.dtype)


def sum_kernel(*refs):
    *piece_refs, out_ref = refs
    values = [piece_ref[...].astype(F32) for piece_ref in piece_refs]
    while len(values) > 1:
        values = [left + right for left, right in zip(values[::2], values[1::2])]
    out_ref[...] = values[0].astype(BF16)


def tie_kernel(rows_ref, other_ref, out_ref):
    pass


def pick_kernel(block_rows, route_hbm, pick_ref, route_ref, sem):
    copy = pltpu.make_async_copy(route_hbm, route_ref, sem)
    copy.start()
    copy.wait()
    target = send_rows(route_ref, (pick_ref.shape[0], 1), 0, block_rows)
    index = lax.broadcasted_iota(jnp.int32, pick_ref.shape, 1)
    pick_ref[...] = jnp.where(index == target, 1.0, 0.0).astype(BF16)


def return_kernel(pick_ref, back_ref, mixed_ref, grad_ref):
    width = mixed_ref.shape[1]
    moved = matmul(pick_ref[...], back_ref[...]).astype(BF16)
    mixed_ref[...] = moved[:, :width]
    grad_ref[...] = moved[:, width:]


def weights_kernel(*refs):
    *part_refs, gain_ref, w_qkv_ref, b_qkv_ref, w_out_ref, b_out_ref, both_ref = refs
    width = w_out_ref.shape[1]
    near = len(part_refs)
    span = 2 * width // near
    me = lax.axis_index("seq")
    for step, part_ref in enumerate(part_refs):
        index = (me ^ step) & (near - 1)
        place = 2 * (index & 1) + (index >> 1)
        part = part_ref[...].astype(F32)
        both_ref[pl.ds(pl.multiple_of(place * span, span), span)] = part[:span]

        @pl.when(place == 0)
        def _():
            sums = part[span:]
            gain_ref[...] = sums[2, :width]
            b_qkv_ref[: 2 * width] = sums[0]
            b_qkv_ref[2 * width :] = sums[1, :width]
            b_out_ref[...] = sums[1, width:]

    w_qkv_ref[:, : 2 * width] = both_ref[:width]
    w_qkv_ref[:, 2 * width :] = both_ref[width:, :width]
    w_out_ref[...] = both_ref[width:, width:]


def exchange(message):
    return lax.all_to_all(message, "seq", split_axis=0, concat_axis=0, tiled=True)


def swap(piece, step, devs):
    return lax.ppermute(piece, "seq", [(dev, dev ^ step) for dev in range(devs)])


def local(points, route, owned, cotangent, gain, w_qkv, b_qkv, w_out, b_out):
    devs = lax.axis_size("seq")
    rows, width = points.shape
    block_rows = rows // route.shape[1]
    held = devs * block_rows
    share = width // devs
    near = 4 if devs == 16 and width % 64 == 0 else 1

    def shape(*dims, dtype=BF16):
        return jax.ShapeDtypeStruct(dims, dtype)

    sent = pl.pallas_call(
        functools.partial(scatter_kernel, block_rows),
        out_shape=shape(held, 2 * width),
        in_specs=[ANY] * 3,
        out_specs=VMEM,
        scratch_shapes=[
            pltpu.SMEM(route.shape, route.dtype),
            pltpu.VMEM(points.shape, points.dtype),
            pltpu.VMEM(cotangent.shape, cotangent.dtype),
            pltpu.SemaphoreType.DMA((3,)),
        ],
    )(route, points, cotangent)
    got = exchange(sent.reshape(devs, block_rows, 2 * width)).reshape(held, 2 * width)

    part = shape(2 * width // near + 8, 2 * width)
    if near > 1:
        half = (width + 8, 2 * width)
        sums_shapes = (shape(*half, dtype=F32), shape(*half))
    else:
        sums_shapes = (shape(width, 2 * width),) * 2 + (shape(8, 2 * width),)
    vectors = jnp.concatenate([gain, b_out, b_qkv])[None, :]
    attn, d_normed, *parts = pl.pallas_call(
        functools.partial(owner_kernel, near),
        out_shape=(shape(held, width), shape(held, width, dtype=F32)) + sums_shapes,
        in_specs=[VMEM, VMEM, ANY, ANY],
        out_specs=(VMEM,) * (2 + len(sums_shapes)),
        scratch_shapes=[
            pltpu.VMEM(w_qkv.shape, w_qkv.dtype),
            pltpu.VMEM(w_out.shape, w_out.dtype),
            pltpu.VMEM((2 * width, 2 * width), F32),
            pltpu.SemaphoreType.DMA((2,)),
        ],
        compiler_params=LARGE,
    )(got, vectors, w_qkv, w_out)
    back = pl.pallas_call(
        rows_kernel,
        out_shape=shape(held, 2 * width),
        in_specs=[VMEM] * 5,
        out_specs=VMEM,
        compiler_params=SMALL,
        cost_estimate=pl.CostEstimate(
            flops=64 * held * width * width, bytes_accessed=16 * held * width, transcendentals=0
        ),
    )(got, attn, d_normed, vectors, w_out)

    pick = pl.pallas_call(
        functools.partial(pick_kernel, block_rows),
        out_shape=shape(rows, held),
        in_specs=[ANY],
        out_specs=VMEM,
        scratch_shapes=[pltpu.SMEM(route.shape, route.dtype), pltpu.SemaphoreType.DMA],
        compiler_params=SMALL,
    )(route)

    def give_back(back):
        return pl.pallas_call(
            return_kernel,
            out_shape=(shape(rows, width), shape(rows, width)),
            in_specs=[VMEM] * 2,
            out_specs=(VMEM,) * 2,
            compiler_params=SMALL,
        )(pick, back)

    if near > 1:
        mine, theirs = parts
        keep, send = pl.pallas_call(
            functools.partial(halve_kernel, 1),
            out_shape=(shape(*part.shape, dtype=F32), part),
            in_specs=[VMEM] * 2,
            out_specs=(VMEM,) * 2,
            compiler_params=SMALL,
        )(mine, swap(theirs, 1, devs))

        def add(*pieces):
            return pl.pallas_call(
                sum_kernel,
                out_shape=part,
                in_specs=[VMEM] * len(pieces),
                out_specs=VMEM,
                compiler_params=SMALL,
            )(*pieces)

        total = add(keep, swap(send, 2, devs))
        total = add(total, *(swap(total, step, devs) for step in range(near, devs, near)))
        back = pl.pallas_call(
            tie_kernel,
            out_shape=back,
            in_specs=[ANY, VMEM],
            out_specs=ANY,
            input_output_aliases={0: 0},
            compiler_params=SMALL,
        )(back, total)
        back = exchange(back.reshape(devs, block_rows, 2 * width)).reshape(held, 2 * width)
        mixed, grad_points = give_back(back)
        parts = [total] + [swap(total, step, devs) for step in range(1, near)]
        grad_gain, grad_wq, grad_bq, grad_wo, grad_bo = pl.pallas_call(
            weights_kernel,
            out_shape=tuple(
                shape(*dims, dtype=F32)
                for dims in ((width,), (width, 3 * width), (3 * width,), (width, width), (width,))
            ),
            in_specs=[VMEM] * near,
            out_specs=(VMEM,) * 5,
            scratch_shapes=[pltpu.VMEM((2 * width, 2 * width), F32)],
            compiler_params=SMALL,
        )(*parts)
    else:
        left, right, sums = parts
        message = jnp.concatenate(
            [
                back.reshape(devs, block_rows, 2 * width),
                left.reshape(devs, share, 2 * width),
                right.reshape(devs, share, 2 * width),
                jnp.broadcast_to(sums[None], (devs, 8, 2 * width)),
            ],
            axis=1,
        )
        message = exchange(message)
        total = jnp.sum(message[:, block_rows:].astype(F32), axis=0)
        mine = total[: 2 * share].astype(BF16)
        both = exchange(jnp.broadcast_to(mine[None], (devs, 2 * share, 2 * width))).astype(F32)
        mixed, grad_points = give_back(message[:, :block_rows].reshape(held, 2 * width))
        left = both[:, :share].reshape(width, 2 * width)
        right = both[:, share:].reshape(width, 2 * width)
        grad_wq = jnp.concatenate([left, right[:, :width]], axis=1)
        grad_wo = right[:, width:]
        flat = total[2 * share :].reshape(-1)
        grad_bq = flat[: 3 * width]
        grad_bo = flat[3 * width : 4 * width]
        grad_gain = flat[4 * width : 5 * width]

    return (mixed, grad_points, grad_gain, grad_wq, grad_bq, grad_wo, grad_bo)


def solution(mesh):
    placed = (
        P(("parts", "seq"), None),
        P(None, ("parts", "seq")),
        P(("parts", "seq")),
        P(("parts", "seq"), None),
        P(),
        P(),
        P(),
        P(),
        P(),
    )
    return jax.shard_map(
        local,
        mesh=mesh,
        in_specs=placed,
        out_specs=(
            P(("parts", "seq"), None),
            P(("parts", "seq"), None),
            P("parts"),
            P("parts", None),
            P("parts"),
            P("parts", None),
            P("parts"),
        ),
        check_vma=False,
    )
```

```python
import functools

import jax
import jax.numpy as jnp
from jax import lax
from jax.experimental import pallas as pl
from jax.experimental.pallas import tpu as pltpu
from jax.sharding import PartitionSpec as P

HEADS = 8
EPS = 1e-05
EMPTY = 64.0
MASKED = -1e30

F32 = jnp.float32
BF16 = jnp.bfloat16

VMEM = pl.BlockSpec(memory_space=pltpu.VMEM)
ANY = pl.BlockSpec(memory_space=pl.ANY)
SMEM = pl.BlockSpec(memory_space=pltpu.SMEM)
MIB = 1024 * 1024
LARGE = pltpu.CompilerParams(vmem_limit_bytes=32 * MIB)
SMALL = pltpu.CompilerParams(vmem_limit_bytes=8 * MIB)


def matmul(left, right, dims=((1,), (0,))):
    return lax.dot_general(left, right, (dims, ((), ())), preferred_element_type=F32)


def send_rows(route_ref, shape, axis, block_rows):
    place = lax.broadcasted_iota(jnp.int32, shape, axis)
    target = jnp.zeros(shape, jnp.int32)
    for block in range(shape[axis] // block_rows):
        first = block * block_rows
        moved = route_ref[0, block] * block_rows + place - first
        target = jnp.where(place >= first, moved, target)
    return target


def scatter_kernel(block_rows, route_hbm, points_hbm, cot_hbm, out_ref, route_ref, points_ref, cot_ref, sems):
    copies = [
        pltpu.make_async_copy(source, target, sems.at[at])
        for at, (source, target) in enumerate(
            ((route_hbm, route_ref), (points_hbm, points_ref), (cot_hbm, cot_ref))
        )
    ]
    for copy in copies:
        copy.start()
    for copy in copies:
        copy.wait()
    rows, width = points_ref.shape
    target = send_rows(route_ref, (1, rows), 1, block_rows)
    index = lax.broadcasted_iota(jnp.int32, (out_ref.shape[0], rows), 0)
    pick = jnp.where(index == target, 1.0, 0.0).astype(BF16)
    ones = jnp.ones((rows, width), BF16)
    moved = matmul(pick, jnp.concatenate([points_ref[...], ones], axis=1))
    empty = (1.0 - moved[:, width:]) * EMPTY
    out_ref[:, :width] = (moved[:, :width] + empty).astype(BF16)
    out_ref[:, width:] = matmul(pick, cot_ref[...]).astype(BF16)


def normalize(points):
    centered = points - jnp.mean(points, axis=-1, keepdims=True)
    rstd = lax.rsqrt(jnp.mean(centered * centered, axis=-1, keepdims=True) + EPS)
    return centered * rstd, rstd


def owner_kernel(near, got_ref, vectors_ref, w_qkv_hbm, w_out_hbm, attn_ref, d_normed_ref, *refs):
    *outs, w_qkv_ref, w_out_ref, both_ref, sems = refs
    copies = [
        pltpu.make_async_copy(w_qkv_hbm, w_qkv_ref, sems.at[0]),
        pltpu.make_async_copy(w_out_hbm, w_out_ref, sems.at[1]),
    ]
    for copy in copies:
        copy.start()
    rows = got_ref.shape[0]
    width = got_ref.shape[1] // 2
    head = width // HEADS
    scale = head ** (-0.5)
    gain = vectors_ref[:, :width]
    b_qkv = vectors_ref[:, 2 * width :]

    points = got_ref[:, :width].astype(F32)
    cot = got_ref[:, width:]
    xhat, _ = normalize(points)
    normed = (xhat * gain).astype(BF16)
    for copy in copies:
        copy.wait()
    w_qkv = w_qkv_ref[...]
    w_out = w_out_ref[...]
    qkv = (matmul(normed, w_qkv) + b_qkv).astype(BF16)
    query, keys, values = qkv[:, :width], qkv[:, width : 2 * width], qkv[:, 2 * width :]
    d_attn = matmul(cot, w_out, ((1,), (1,))).astype(BF16)
    d_attn_t = matmul(w_out, cot, ((1,), (1,))).astype(BF16)
    d_attn_s = (d_attn.astype(F32) * scale).astype(BF16)

    keys_t = keys.T
    values_t = values.T
    keys_s = (keys.astype(F32) * scale).astype(BF16)
    lane = lax.broadcasted_iota(jnp.int32, (rows, width), 1)
    hidden = jnp.where(points > EMPTY / 2, MASKED, 0.0).astype(BF16)
    query_x = jnp.concatenate([query, jnp.where(lane == 0, 1.0, 0.0).astype(BF16)], axis=1)

    attn_t, dq_t = [], []
    d_keys = jnp.zeros((rows, width), F32)
    d_values = jnp.zeros((rows, width), F32)
    for h in range(HEADS):
        lo, hi = h * head, (h + 1) * head
        mine = (lane >= lo) & (lane < hi)
        keys_h = jnp.concatenate([jnp.where(mine, keys_s, 0), hidden], axis=1)
        scores = matmul(keys_h, query_x, ((1,), (1,)))
        expo = jnp.exp(scores - jnp.max(scores, axis=0, keepdims=True))
        probs = expo * (1.0 / jnp.sum(expo, axis=0, keepdims=True))
        probs_b = probs.astype(BF16)
        out_t = matmul(values_t[lo:hi, :], probs_b)
        attn_t.append(out_t)
        inner = jnp.sum(out_t * d_attn_t[lo:hi, :].astype(F32), axis=0, keepdims=True) * scale
        d_probs = matmul(jnp.where(mine, values, 0), d_attn_s, ((1,), (1,)))
        d_score = (probs * (d_probs - inner)).astype(BF16)
        dq_t.append(matmul(keys_t[lo:hi, :], d_score))
        d_values = jnp.where(mine, matmul(probs_b, d_attn), d_values)
        d_keys = jnp.where(mine, matmul(d_score, query), d_keys)

    attn_t = jnp.concatenate(attn_t, axis=0)
    attn_ref[...] = attn_t.T.astype(BF16)
    grad_w_out = matmul(attn_t.astype(BF16), cot)
    grad_b_out = jnp.sum(cot.astype(F32), axis=0, keepdims=True)

    d_query = jnp.concatenate(dq_t, axis=0).T
    d_qkv = jnp.concatenate([d_query, d_keys, d_values], axis=1).astype(BF16)
    d_normed = matmul(d_qkv, w_qkv, ((1,), (1,)))
    grad_w_qkv = matmul(normed, d_qkv, ((0,), (0,)))
    grad_b_qkv = jnp.sum(d_qkv.astype(F32), axis=0, keepdims=True)
    grad_gain = jnp.sum(d_normed * xhat, axis=0, keepdims=True)
    d_normed_ref[...] = d_normed
    sums = jnp.concatenate(
        [
            grad_b_qkv[:, : 2 * width],
            jnp.concatenate([grad_b_qkv[:, 2 * width :], grad_b_out], axis=1),
            jnp.concatenate([grad_gain, jnp.zeros_like(grad_gain)], axis=1),
            jnp.zeros((5, 2 * width), F32),
        ],
        axis=0,
    )
    left = grad_w_qkv[:, : 2 * width]
    right = jnp.concatenate([grad_w_qkv[:, 2 * width :], grad_w_out], axis=1)
    if near == 1:
        left_ref, right_ref, sums_ref = outs
        left_ref[...] = left.astype(BF16)
        right_ref[...] = right.astype(BF16)
        sums_ref[...] = sums.astype(BF16)
        return
    mine_ref, theirs_ref = outs
    both_ref[:width] = left
    both_ref[width:] = right
    core = lax.axis_index("seq") & 1
    for half, half_ref in ((core, mine_ref), (core ^ 1, theirs_ref)):
        span = pl.ds(pl.multiple_of(half * width, width), width)
        half_ref[:width] = both_ref[span].astype(half_ref.dtype)
        half_ref[width:] = sums.astype(half_ref.dtype)


def rows_kernel(got_ref, attn_ref, d_normed_ref, vectors_ref, w_out_ref, back_ref):
    width = attn_ref.shape[1]
    gain = vectors_ref[:, :width]
    b_out = vectors_ref[:, width : 2 * width]
    points = got_ref[:, :width].astype(F32)
    cot = got_ref[:, width:].astype(F32)
    xhat, rstd = normalize(points)
    mixed = points + (matmul(attn_ref[...], w_out_ref[...]) + b_out)
    d_xhat = d_normed_ref[...] * gain
    inner = (
        d_xhat
        - jnp.mean(d_xhat, axis=-1, keepdims=True)
        - xhat * jnp.mean(d_xhat * xhat, axis=-1, keepdims=True)
    )
    back_ref[:, :width] = mixed.astype(BF16)
    back_ref[:, width:] = (cot + rstd * inner).astype(BF16)


def halve_kernel(bit, mine_ref, got_ref, keep_ref, send_ref):
    rows = (mine_ref.shape[0] - 8) // 2
    place = (lax.axis_index("seq") >> bit) & 1
    sums = mine_ref[2 * rows :] + got_ref[2 * rows :].astype(F32)
    for half, half_ref in ((place, keep_ref), (place ^ 1, send_ref)):
        span = pl.ds(pl.multiple_of(half * rows, rows), rows)
        half_ref[:rows] = (mine_ref[span] + got_ref[span].astype(F32)).astype(half_ref.dtype)
        half_ref[rows:] = sums.astype(half_ref.dtype)


def sum_kernel(*refs):
    *piece_refs, out_ref = refs
    values = [piece_ref[...].astype(F32) for piece_ref in piece_refs]
    while len(values) > 1:
        values = [left + right for left, right in zip(values[::2], values[1::2])]
    out_ref[...] = values[0].astype(BF16)


def tie_kernel(rows_ref, other_ref, out_ref):
    pass


def pick_kernel(block_rows, route_hbm, pick_ref, route_ref, sem):
    copy = pltpu.make_async_copy(route_hbm, route_ref, sem)
    copy.start()
    copy.wait()
    target = send_rows(route_ref, (pick_ref.shape[0], 1), 0, block_rows)
    index = lax.broadcasted_iota(jnp.int32, pick_ref.shape, 1)
    pick_ref[...] = jnp.where(index == target, 1.0, 0.0).astype(BF16)


def return_kernel(pick_ref, back_ref, mixed_ref, grad_ref, token_ref):
    token_ref[...] = jnp.zeros_like(token_ref)
    width = mixed_ref.shape[1]
    moved = matmul(pick_ref[...], back_ref[...]).astype(BF16)
    mixed_ref[...] = moved[:, :width]
    grad_ref[...] = moved[:, width:]


def weights_kernel(*refs):
    *part_refs, _, gain_ref, w_qkv_ref, b_qkv_ref, w_out_ref, b_out_ref, both_ref = refs
    width = w_out_ref.shape[1]
    near = len(part_refs)
    span = 2 * width // near
    me = lax.axis_index("seq")
    for step, part_ref in enumerate(part_refs):
        index = (me ^ step) & (near - 1)
        place = 2 * (index & 1) + (index >> 1)
        part = part_ref[...].astype(F32)
        both_ref[pl.ds(pl.multiple_of(place * span, span), span)] = part[:span]

        @pl.when(place == 0)
        def _():
            sums = part[span:]
            gain_ref[...] = sums[2, :width]
            b_qkv_ref[: 2 * width] = sums[0]
            b_qkv_ref[2 * width :] = sums[1, :width]
            b_out_ref[...] = sums[1, width:]

    w_qkv_ref[:, : 2 * width] = both_ref[:width]
    w_qkv_ref[:, 2 * width :] = both_ref[width:, :width]
    w_out_ref[...] = both_ref[width:, width:]


def exchange(message):
    return lax.all_to_all(message, "seq", split_axis=0, concat_axis=0, tiled=True)


def swap(piece, step, devs):
    return lax.ppermute(piece, "seq", [(dev, dev ^ step) for dev in range(devs)])


def local(points, route, owned, cotangent, gain, w_qkv, b_qkv, w_out, b_out):
    devs = lax.axis_size("seq")
    rows, width = points.shape
    block_rows = rows // route.shape[1]
    held = devs * block_rows
    share = width // devs
    near = 4 if devs == 16 and width % 64 == 0 else 1

    def shape(*dims, dtype=BF16):
        return jax.ShapeDtypeStruct(dims, dtype)

    sent = pl.pallas_call(
        functools.partial(scatter_kernel, block_rows),
        out_shape=shape(held, 2 * width),
        in_specs=[ANY] * 3,
        out_specs=VMEM,
        scratch_shapes=[
            pltpu.SMEM(route.shape, route.dtype),
            pltpu.VMEM(points.shape, points.dtype),
            pltpu.VMEM(cotangent.shape, cotangent.dtype),
            pltpu.SemaphoreType.DMA((3,)),
        ],
    )(route, points, cotangent)
    got = exchange(sent.reshape(devs, block_rows, 2 * width)).reshape(held, 2 * width)

    part = shape(2 * width // near + 8, 2 * width)
    if near > 1:
        half = (width + 8, 2 * width)
        sums_shapes = (shape(*half, dtype=F32), shape(*half))
    else:
        sums_shapes = (shape(width, 2 * width),) * 2 + (shape(8, 2 * width),)
    vectors = jnp.concatenate([gain, b_out, b_qkv])[None, :]
    attn, d_normed, *parts = pl.pallas_call(
        functools.partial(owner_kernel, near),
        out_shape=(shape(held, width), shape(held, width, dtype=F32)) + sums_shapes,
        in_specs=[VMEM, VMEM, ANY, ANY],
        out_specs=(VMEM,) * (2 + len(sums_shapes)),
        scratch_shapes=[
            pltpu.VMEM(w_qkv.shape, w_qkv.dtype),
            pltpu.VMEM(w_out.shape, w_out.dtype),
            pltpu.VMEM((2 * width, 2 * width), F32),
            pltpu.SemaphoreType.DMA((2,)),
        ],
        compiler_params=LARGE,
    )(got, vectors, w_qkv, w_out)
    back = pl.pallas_call(
        rows_kernel,
        out_shape=shape(held, 2 * width),
        in_specs=[VMEM] * 5,
        out_specs=VMEM,
        compiler_params=SMALL,
        cost_estimate=pl.CostEstimate(
            flops=64 * held * width * width, bytes_accessed=16 * held * width, transcendentals=0
        ),
    )(got, attn, d_normed, vectors, w_out)

    pick = pl.pallas_call(
        functools.partial(pick_kernel, block_rows),
        out_shape=shape(rows, held),
        in_specs=[ANY],
        out_specs=VMEM,
        scratch_shapes=[pltpu.SMEM(route.shape, route.dtype), pltpu.SemaphoreType.DMA],
        compiler_params=SMALL,
    )(route)

    def give_back(back):
        return pl.pallas_call(
            return_kernel,
            out_shape=(shape(rows, width), shape(rows, width), shape(8, 128, dtype=F32)),
            in_specs=[VMEM] * 2,
            out_specs=(VMEM,) * 3,
            compiler_params=SMALL,
        )(pick, back)

    if near > 1:
        mine, theirs = parts
        keep, send = pl.pallas_call(
            functools.partial(halve_kernel, 1),
            out_shape=(shape(*part.shape, dtype=F32), part),
            in_specs=[VMEM] * 2,
            out_specs=(VMEM,) * 2,
            compiler_params=SMALL,
        )(mine, swap(theirs, 1, devs))

        back = pl.pallas_call(
            tie_kernel,
            out_shape=back,
            in_specs=[ANY, VMEM],
            out_specs=ANY,
            input_output_aliases={0: 0},
            compiler_params=SMALL,
        )(back, send)
        back = exchange(back.reshape(devs, block_rows, 2 * width)).reshape(held, 2 * width)
        mixed, grad_points, token = give_back(back)

        def add(*pieces):
            return pl.pallas_call(
                sum_kernel,
                out_shape=part,
                in_specs=[VMEM] * len(pieces),
                out_specs=VMEM,
                compiler_params=SMALL,
            )(*pieces)

        total = add(keep, swap(send, 2, devs))
        total = add(total, *(swap(total, step, devs) for step in range(near, devs, near)))
        parts = [total] + [swap(total, step, devs) for step in range(1, near)]
        grad_gain, grad_wq, grad_bq, grad_wo, grad_bo = pl.pallas_call(
            weights_kernel,
            out_shape=tuple(
                shape(*dims, dtype=F32)
                for dims in ((width,), (width, 3 * width), (3 * width,), (width, width), (width,))
            ),
            in_specs=[VMEM] * (near + 1),
            out_specs=(VMEM,) * 5,
            scratch_shapes=[pltpu.VMEM((2 * width, 2 * width), F32)],
            compiler_params=SMALL,
        )(*parts, token)
    else:
        left, right, sums = parts
        message = jnp.concatenate(
            [
                back.reshape(devs, block_rows, 2 * width),
                left.reshape(devs, share, 2 * width),
                right.reshape(devs, share, 2 * width),
                jnp.broadcast_to(sums[None], (devs, 8, 2 * width)),
            ],
            axis=1,
        )
        message = exchange(message)
        total = jnp.sum(message[:, block_rows:].astype(F32), axis=0)
        mine = total[: 2 * share].astype(BF16)
        both = exchange(jnp.broadcast_to(mine[None], (devs, 2 * share, 2 * width))).astype(F32)
        mixed, grad_points, _ = give_back(message[:, :block_rows].reshape(held, 2 * width))
        left = both[:, :share].reshape(width, 2 * width)
        right = both[:, share:].reshape(width, 2 * width)
        grad_wq = jnp.concatenate([left, right[:, :width]], axis=1)
        grad_wo = right[:, width:]
        flat = total[2 * share :].reshape(-1)
        grad_bq = flat[: 3 * width]
        grad_bo = flat[3 * width : 4 * width]
        grad_gain = flat[4 * width : 5 * width]

    return (mixed, grad_points, grad_gain, grad_wq, grad_bq, grad_wo, grad_bo)


def solution(mesh):
    placed = (
        P(("parts", "seq"), None),
        P(None, ("parts", "seq")),
        P(("parts", "seq")),
        P(("parts", "seq"), None),
        P(),
        P(),
        P(),
        P(),
        P(),
    )
    return jax.shard_map(
        local,
        mesh=mesh,
        in_specs=placed,
        out_specs=(
            P(("parts", "seq"), None),
            P(("parts", "seq"), None),
            P("parts"),
            P("parts", None),
            P("parts"),
            P("parts", None),
            P("parts"),
        ),
        check_vma=False,
    )
```

```python
import functools

import jax
import jax.numpy as jnp
from jax import lax
from jax.experimental import pallas as pl
from jax.experimental.pallas import tpu as pltpu
from jax.sharding import PartitionSpec as P

HEADS = 8
EPS = 1e-05
EMPTY = 64.0
MASKED = -1e30

F32 = jnp.float32
BF16 = jnp.bfloat16

VMEM = pl.BlockSpec(memory_space=pltpu.VMEM)
ANY = pl.BlockSpec(memory_space=pl.ANY)
SMEM = pl.BlockSpec(memory_space=pltpu.SMEM)
MIB = 1024 * 1024
LARGE = pltpu.CompilerParams(vmem_limit_bytes=32 * MIB)
SMALL = pltpu.CompilerParams(vmem_limit_bytes=8 * MIB)


def matmul(left, right, dims=((1,), (0,))):
    return lax.dot_general(left, right, (dims, ((), ())), preferred_element_type=F32)


def send_rows(route_ref, shape, axis, block_rows):
    place = lax.broadcasted_iota(jnp.int32, shape, axis)
    target = jnp.zeros(shape, jnp.int32)
    for block in range(shape[axis] // block_rows):
        first = block * block_rows
        moved = route_ref[0, block] * block_rows + place - first
        target = jnp.where(place >= first, moved, target)
    return target


def scatter_kernel(block_rows, route_hbm, points_hbm, cot_hbm, out_ref, route_ref, points_ref, cot_ref, sems):
    copies = [
        pltpu.make_async_copy(source, target, sems.at[at])
        for at, (source, target) in enumerate(
            ((route_hbm, route_ref), (points_hbm, points_ref), (cot_hbm, cot_ref))
        )
    ]
    for copy in copies:
        copy.start()
    for copy in copies:
        copy.wait()
    rows, width = points_ref.shape
    target = send_rows(route_ref, (1, rows), 1, block_rows)
    index = lax.broadcasted_iota(jnp.int32, (out_ref.shape[0], rows), 0)
    pick = jnp.where(index == target, 1.0, 0.0).astype(BF16)
    ones = jnp.ones((rows, width), BF16)
    moved = matmul(pick, jnp.concatenate([points_ref[...], ones], axis=1))
    empty = (1.0 - moved[:, width:]) * EMPTY
    out_ref[:, :width] = (moved[:, :width] + empty).astype(BF16)
    out_ref[:, width:] = matmul(pick, cot_ref[...]).astype(BF16)


def normalize(points):
    centered = points - jnp.mean(points, axis=-1, keepdims=True)
    rstd = lax.rsqrt(jnp.mean(centered * centered, axis=-1, keepdims=True) + EPS)
    return centered * rstd, rstd


def owner_kernel(near, got_ref, vectors_ref, w_qkv_hbm, w_out_hbm, attn_ref, d_normed_ref, *refs):
    *outs, w_qkv_ref, w_out_ref, both_ref, sems = refs
    copies = [
        pltpu.make_async_copy(w_qkv_hbm, w_qkv_ref, sems.at[0]),
        pltpu.make_async_copy(w_out_hbm, w_out_ref, sems.at[1]),
    ]
    for copy in copies:
        copy.start()
    rows = got_ref.shape[0]
    width = got_ref.shape[1] // 2
    head = width // HEADS
    scale = head ** (-0.5)
    gain = vectors_ref[:, :width]
    b_qkv = vectors_ref[:, 2 * width :]

    points = got_ref[:, :width].astype(F32)
    cot = got_ref[:, width:]
    xhat, _ = normalize(points)
    normed = (xhat * gain).astype(BF16)
    for copy in copies:
        copy.wait()
    w_qkv = w_qkv_ref[...]
    w_out = w_out_ref[...]
    qkv = (matmul(normed, w_qkv) + b_qkv).astype(BF16)
    query, keys, values = qkv[:, :width], qkv[:, width : 2 * width], qkv[:, 2 * width :]
    d_attn = matmul(cot, w_out, ((1,), (1,))).astype(BF16)
    d_attn_t = matmul(w_out, cot, ((1,), (1,))).astype(BF16)
    d_attn_s = (d_attn.astype(F32) * scale).astype(BF16)

    keys_t = keys.T
    values_t = values.T
    keys_s = (keys.astype(F32) * scale).astype(BF16)
    lane = lax.broadcasted_iota(jnp.int32, (rows, width), 1)
    hidden = jnp.where(points > EMPTY / 2, MASKED, 0.0).astype(BF16)
    query_x = jnp.concatenate([query, jnp.where(lane == 0, 1.0, 0.0).astype(BF16)], axis=1)

    attn_t, dq_t = [], []
    d_keys = jnp.zeros((rows, width), F32)
    d_values = jnp.zeros((rows, width), F32)
    for h in range(HEADS):
        lo, hi = h * head, (h + 1) * head
        mine = (lane >= lo) & (lane < hi)
        keys_h = jnp.concatenate([jnp.where(mine, keys_s, 0), hidden], axis=1)
        scores = matmul(keys_h, query_x, ((1,), (1,)))
        expo = jnp.exp(scores - jnp.max(scores, axis=0, keepdims=True))
        probs = expo * (1.0 / jnp.sum(expo, axis=0, keepdims=True))
        probs_b = probs.astype(BF16)
        out_t = matmul(values_t[lo:hi, :], probs_b)
        attn_t.append(out_t)
        inner = jnp.sum(out_t * d_attn_t[lo:hi, :].astype(F32), axis=0, keepdims=True) * scale
        d_probs = matmul(jnp.where(mine, values, 0), d_attn_s, ((1,), (1,)))
        d_score = (probs * (d_probs - inner)).astype(BF16)
        dq_t.append(matmul(keys_t[lo:hi, :], d_score))
        d_values = jnp.where(mine, matmul(probs_b, d_attn), d_values)
        d_keys = jnp.where(mine, matmul(d_score, query), d_keys)

    attn_t = jnp.concatenate(attn_t, axis=0)
    attn_ref[...] = attn_t.T.astype(BF16)
    grad_w_out = matmul(attn_t.astype(BF16), cot)
    grad_b_out = jnp.sum(cot.astype(F32), axis=0, keepdims=True)

    d_query = jnp.concatenate(dq_t, axis=0).T
    d_qkv = jnp.concatenate([d_query, d_keys, d_values], axis=1).astype(BF16)
    d_normed = matmul(d_qkv, w_qkv, ((1,), (1,)))
    grad_w_qkv = matmul(normed, d_qkv, ((0,), (0,)))
    grad_b_qkv = jnp.sum(d_qkv.astype(F32), axis=0, keepdims=True)
    grad_gain = jnp.sum(d_normed * xhat, axis=0, keepdims=True)
    d_normed_ref[...] = d_normed
    sums = jnp.concatenate(
        [
            grad_b_qkv[:, : 2 * width],
            jnp.concatenate([grad_b_qkv[:, 2 * width :], grad_b_out], axis=1),
            jnp.concatenate([grad_gain, jnp.zeros_like(grad_gain)], axis=1),
            jnp.zeros((5, 2 * width), F32),
        ],
        axis=0,
    )
    left = grad_w_qkv[:, : 2 * width]
    right = jnp.concatenate([grad_w_qkv[:, 2 * width :], grad_w_out], axis=1)
    if near == 1:
        left_ref, right_ref, sums_ref = outs
        left_ref[...] = left.astype(BF16)
        right_ref[...] = right.astype(BF16)
        sums_ref[...] = sums.astype(BF16)
        return
    mine_ref, theirs_ref = outs
    both_ref[:width] = left
    both_ref[width:] = right
    core = lax.axis_index("seq") & 1
    for half, half_ref in ((core, mine_ref), (core ^ 1, theirs_ref)):
        span = pl.ds(pl.multiple_of(half * width, width), width)
        half_ref[:width] = both_ref[span].astype(half_ref.dtype)
        half_ref[width:] = sums.astype(half_ref.dtype)


def rows_kernel(got_ref, attn_ref, d_normed_ref, vectors_ref, w_out_ref, back_ref):
    width = attn_ref.shape[1]
    gain = vectors_ref[:, :width]
    b_out = vectors_ref[:, width : 2 * width]
    points = got_ref[:, :width].astype(F32)
    cot = got_ref[:, width:].astype(F32)
    xhat, rstd = normalize(points)
    mixed = points + (matmul(attn_ref[...], w_out_ref[...]) + b_out)
    d_xhat = d_normed_ref[...] * gain
    inner = (
        d_xhat
        - jnp.mean(d_xhat, axis=-1, keepdims=True)
        - xhat * jnp.mean(d_xhat * xhat, axis=-1, keepdims=True)
    )
    back_ref[:, :width] = mixed.astype(BF16)
    back_ref[:, width:] = (cot + rstd * inner).astype(BF16)


def halve_kernel(bit, mine_ref, got_ref, keep_ref, send_ref):
    rows = (mine_ref.shape[0] - 8) // 2
    place = (lax.axis_index("seq") >> bit) & 1
    sums = mine_ref[2 * rows :] + got_ref[2 * rows :].astype(F32)
    for half, half_ref in ((place, keep_ref), (place ^ 1, send_ref)):
        span = pl.ds(pl.multiple_of(half * rows, rows), rows)
        half_ref[:rows] = (mine_ref[span] + got_ref[span].astype(F32)).astype(half_ref.dtype)
        half_ref[rows:] = sums.astype(half_ref.dtype)


def sum_kernel(*refs):
    *piece_refs, out_ref = refs
    values = [piece_ref[...].astype(F32) for piece_ref in piece_refs]
    while len(values) > 1:
        values = [left + right for left, right in zip(values[::2], values[1::2])]
    out_ref[...] = values[0].astype(BF16)


def tie_kernel(rows_ref, other_ref, out_ref):
    pass


def pick_kernel(block_rows, route_hbm, pick_ref, route_ref, sem):
    copy = pltpu.make_async_copy(route_hbm, route_ref, sem)
    copy.start()
    copy.wait()
    target = send_rows(route_ref, (pick_ref.shape[0], 1), 0, block_rows)
    index = lax.broadcasted_iota(jnp.int32, pick_ref.shape, 1)
    pick_ref[...] = jnp.where(index == target, 1.0, 0.0).astype(BF16)


def return_kernel(pick_ref, back_ref, mixed_ref, grad_ref):
    width = mixed_ref.shape[1]
    moved = matmul(pick_ref[...], back_ref[...]).astype(BF16)
    mixed_ref[...] = moved[:, :width]
    grad_ref[...] = moved[:, width:]


def weights_kernel(*refs):
    *part_refs, gain_ref, w_qkv_ref, b_qkv_ref, w_out_ref, b_out_ref, both_ref = refs
    width = w_out_ref.shape[1]
    near = len(part_refs)
    span = 2 * width // near
    me = lax.axis_index("seq")
    for step, part_ref in enumerate(part_refs):
        index = (me ^ step) & (near - 1)
        place = 2 * (index & 1) + (index >> 1)
        part = part_ref[...].astype(F32)
        both_ref[pl.ds(pl.multiple_of(place * span, span), span)] = part[:span]

        @pl.when(place == 0)
        def _():
            sums = part[span:]
            gain_ref[...] = sums[2, :width]
            b_qkv_ref[: 2 * width] = sums[0]
            b_qkv_ref[2 * width :] = sums[1, :width]
            b_out_ref[...] = sums[1, width:]

    w_qkv_ref[:, : 2 * width] = both_ref[:width]
    w_qkv_ref[:, 2 * width :] = both_ref[width:, :width]
    w_out_ref[...] = both_ref[width:, width:]


def exchange(message):
    return lax.all_to_all(message, "seq", split_axis=0, concat_axis=0, tiled=True)


def swap(piece, step, devs):
    return lax.ppermute(piece, "seq", [(dev, dev ^ step) for dev in range(devs)])


def local(points, route, owned, cotangent, gain, w_qkv, b_qkv, w_out, b_out):
    devs = lax.axis_size("seq")
    rows, width = points.shape
    block_rows = rows // route.shape[1]
    held = devs * block_rows
    share = width // devs
    near = 4 if devs == 16 and width % 64 == 0 else 1

    def shape(*dims, dtype=BF16):
        return jax.ShapeDtypeStruct(dims, dtype)

    sent = pl.pallas_call(
        functools.partial(scatter_kernel, block_rows),
        out_shape=shape(held, 2 * width),
        in_specs=[ANY] * 3,
        out_specs=VMEM,
        scratch_shapes=[
            pltpu.SMEM(route.shape, route.dtype),
            pltpu.VMEM(points.shape, points.dtype),
            pltpu.VMEM(cotangent.shape, cotangent.dtype),
            pltpu.SemaphoreType.DMA((3,)),
        ],
    )(route, points, cotangent)
    got = exchange(sent.reshape(devs, block_rows, 2 * width)).reshape(held, 2 * width)

    part = shape(2 * width // near + 8, 2 * width)
    if near > 1:
        half = (width + 8, 2 * width)
        sums_shapes = (shape(*half, dtype=F32), shape(*half))
    else:
        sums_shapes = (shape(width, 2 * width),) * 2 + (shape(8, 2 * width),)
    vectors = jnp.concatenate([gain, b_out, b_qkv])[None, :]
    attn, d_normed, *parts = pl.pallas_call(
        functools.partial(owner_kernel, near),
        out_shape=(shape(held, width), shape(held, width, dtype=F32)) + sums_shapes,
        in_specs=[VMEM, VMEM, ANY, ANY],
        out_specs=(VMEM,) * (2 + len(sums_shapes)),
        scratch_shapes=[
            pltpu.VMEM(w_qkv.shape, w_qkv.dtype),
            pltpu.VMEM(w_out.shape, w_out.dtype),
            pltpu.VMEM((2 * width, 2 * width), F32),
            pltpu.SemaphoreType.DMA((2,)),
        ],
        compiler_params=LARGE,
    )(got, vectors, w_qkv, w_out)
    back = pl.pallas_call(
        rows_kernel,
        out_shape=shape(held, 2 * width),
        in_specs=[VMEM] * 5,
        out_specs=VMEM,
        compiler_params=SMALL,
        cost_estimate=pl.CostEstimate(
            flops=64 * held * width * width, bytes_accessed=16 * held * width, transcendentals=0
        ),
    )(got, attn, d_normed, vectors, w_out)

    pick = pl.pallas_call(
        functools.partial(pick_kernel, block_rows),
        out_shape=shape(rows, held),
        in_specs=[ANY],
        out_specs=VMEM,
        scratch_shapes=[pltpu.SMEM(route.shape, route.dtype), pltpu.SemaphoreType.DMA],
        compiler_params=SMALL,
    )(route)

    def give_back(back):
        return pl.pallas_call(
            return_kernel,
            out_shape=(shape(rows, width), shape(rows, width)),
            in_specs=[VMEM] * 2,
            out_specs=(VMEM,) * 2,
            compiler_params=SMALL,
        )(pick, back)

    if near > 1:
        mine, theirs = parts
        keep, send = pl.pallas_call(
            functools.partial(halve_kernel, 1),
            out_shape=(shape(*part.shape, dtype=F32), part),
            in_specs=[VMEM] * 2,
            out_specs=(VMEM,) * 2,
            compiler_params=SMALL,
        )(mine, swap(theirs, 1, devs))

        def add(*pieces, flops=0):
            return pl.pallas_call(
                sum_kernel,
                out_shape=part,
                in_specs=[VMEM] * len(pieces),
                out_specs=VMEM,
                compiler_params=SMALL,
                cost_estimate=pl.CostEstimate(flops=flops, bytes_accessed=0, transcendentals=0),
            )(*pieces)

        total = add(keep, swap(send, 2, devs))
        back = pl.pallas_call(
            tie_kernel,
            out_shape=back,
            in_specs=[ANY, VMEM],
            out_specs=ANY,
            input_output_aliases={0: 0},
            compiler_params=SMALL,
        )(back, total)
        back = exchange(back.reshape(devs, block_rows, 2 * width)).reshape(held, 2 * width)
        mixed, grad_points = give_back(back)
        far = [swap(total, step, devs) for step in range(near, devs, near)]
        total = add(total, *far, flops=40_000_000_000)
        parts = [total] + [swap(total, step, devs) for step in range(1, near)]
        grad_gain, grad_wq, grad_bq, grad_wo, grad_bo = pl.pallas_call(
            weights_kernel,
            out_shape=tuple(
                shape(*dims, dtype=F32)
                for dims in ((width,), (width, 3 * width), (3 * width,), (width, width), (width,))
            ),
            in_specs=[VMEM] * near,
            out_specs=(VMEM,) * 5,
            scratch_shapes=[pltpu.VMEM((2 * width, 2 * width), F32)],
            compiler_params=SMALL,
        )(*parts)
    else:
        left, right, sums = parts
        message = jnp.concatenate(
            [
                back.reshape(devs, block_rows, 2 * width),
                left.reshape(devs, share, 2 * width),
                right.reshape(devs, share, 2 * width),
                jnp.broadcast_to(sums[None], (devs, 8, 2 * width)),
            ],
            axis=1,
        )
        message = exchange(message)
        total = jnp.sum(message[:, block_rows:].astype(F32), axis=0)
        mine = total[: 2 * share].astype(BF16)
        both = exchange(jnp.broadcast_to(mine[None], (devs, 2 * share, 2 * width))).astype(F32)
        mixed, grad_points = give_back(message[:, :block_rows].reshape(held, 2 * width))
        left = both[:, :share].reshape(width, 2 * width)
        right = both[:, share:].reshape(width, 2 * width)
        grad_wq = jnp.concatenate([left, right[:, :width]], axis=1)
        grad_wo = right[:, width:]
        flat = total[2 * share :].reshape(-1)
        grad_bq = flat[: 3 * width]
        grad_bo = flat[3 * width : 4 * width]
        grad_gain = flat[4 * width : 5 * width]

    return (mixed, grad_points, grad_gain, grad_wq, grad_bq, grad_wo, grad_bo)


def solution(mesh):
    placed = (
        P(("parts", "seq"), None),
        P(None, ("parts", "seq")),
        P(("parts", "seq")),
        P(("parts", "seq"), None),
        P(),
        P(),
        P(),
        P(),
        P(),
    )
    return jax.shard_map(
        local,
        mesh=mesh,
        in_specs=placed,
        out_specs=(
            P(("parts", "seq"), None),
            P(("parts", "seq"), None),
            P("parts"),
            P("parts", None),
            P("parts"),
            P("parts", None),
            P("parts"),
        ),
        check_vma=False,
    )
```

```python
import functools

import jax
import jax.numpy as jnp
from jax import lax
from jax.experimental import pallas as pl
from jax.experimental.pallas import tpu as pltpu
from jax.sharding import PartitionSpec as P

HEADS = 8
EPS = 1e-05
EMPTY = 64.0
MASKED = -1e30

F32 = jnp.float32
BF16 = jnp.bfloat16

VMEM = pl.BlockSpec(memory_space=pltpu.VMEM)
ANY = pl.BlockSpec(memory_space=pl.ANY)
SMEM = pl.BlockSpec(memory_space=pltpu.SMEM)
MIB = 1024 * 1024
LARGE = pltpu.CompilerParams(vmem_limit_bytes=32 * MIB)
SMALL = pltpu.CompilerParams(vmem_limit_bytes=8 * MIB)


def matmul(left, right, dims=((1,), (0,))):
    return lax.dot_general(left, right, (dims, ((), ())), preferred_element_type=F32)


def send_rows(route_ref, shape, axis, block_rows):
    place = lax.broadcasted_iota(jnp.int32, shape, axis)
    target = jnp.zeros(shape, jnp.int32)
    for block in range(shape[axis] // block_rows):
        first = block * block_rows
        moved = route_ref[0, block] * block_rows + place - first
        target = jnp.where(place >= first, moved, target)
    return target


def scatter_kernel(block_rows, route_hbm, points_hbm, cot_hbm, out_ref, route_ref, points_ref, cot_ref, sems):
    copies = [
        pltpu.make_async_copy(source, target, sems.at[at])
        for at, (source, target) in enumerate(
            ((route_hbm, route_ref), (points_hbm, points_ref), (cot_hbm, cot_ref))
        )
    ]
    for copy in copies:
        copy.start()
    for copy in copies:
        copy.wait()
    rows, width = points_ref.shape
    target = send_rows(route_ref, (1, rows), 1, block_rows)
    index = lax.broadcasted_iota(jnp.int32, (out_ref.shape[0], rows), 0)
    pick = jnp.where(index == target, 1.0, 0.0).astype(BF16)
    ones = jnp.ones((rows, width), BF16)
    moved = matmul(pick, jnp.concatenate([points_ref[...], ones], axis=1))
    empty = (1.0 - moved[:, width:]) * EMPTY
    out_ref[:, :width] = (moved[:, :width] + empty).astype(BF16)
    out_ref[:, width:] = matmul(pick, cot_ref[...]).astype(BF16)


def normalize(points):
    centered = points - jnp.mean(points, axis=-1, keepdims=True)
    rstd = lax.rsqrt(jnp.mean(centered * centered, axis=-1, keepdims=True) + EPS)
    return centered * rstd, rstd


def owner_kernel(near, got_ref, vectors_ref, w_qkv_hbm, w_out_hbm, attn_ref, d_normed_ref, *refs):
    *outs, w_qkv_ref, w_out_ref, both_ref, sems = refs
    copies = [
        pltpu.make_async_copy(w_qkv_hbm, w_qkv_ref, sems.at[0]),
        pltpu.make_async_copy(w_out_hbm, w_out_ref, sems.at[1]),
    ]
    for copy in copies:
        copy.start()
    rows = got_ref.shape[0]
    width = got_ref.shape[1] // 2
    head = width // HEADS
    scale = head ** (-0.5)
    gain = vectors_ref[:, :width]
    b_qkv = vectors_ref[:, 2 * width :]

    points = got_ref[:, :width].astype(F32)
    cot = got_ref[:, width:]
    xhat, _ = normalize(points)
    normed = (xhat * gain).astype(BF16)
    for copy in copies:
        copy.wait()
    w_qkv = w_qkv_ref[...]
    w_out = w_out_ref[...]
    qkv = (matmul(normed, w_qkv) + b_qkv).astype(BF16)
    query, keys, values = qkv[:, :width], qkv[:, width : 2 * width], qkv[:, 2 * width :]
    d_attn = matmul(cot, w_out, ((1,), (1,))).astype(BF16)
    d_attn_t = matmul(w_out, cot, ((1,), (1,))).astype(BF16)
    d_attn_s = (d_attn.astype(F32) * scale).astype(BF16)

    keys_t = keys.T
    values_t = values.T
    keys_s = (keys.astype(F32) * scale).astype(BF16)
    lane = lax.broadcasted_iota(jnp.int32, (rows, width), 1)
    hidden = jnp.where(points > EMPTY / 2, MASKED, 0.0).astype(BF16)
    query_x = jnp.concatenate([query, jnp.where(lane == 0, 1.0, 0.0).astype(BF16)], axis=1)

    attn_t, dq_t = [], []
    d_keys = jnp.zeros((rows, width), F32)
    d_values = jnp.zeros((rows, width), F32)
    for h in range(HEADS):
        lo, hi = h * head, (h + 1) * head
        mine = (lane >= lo) & (lane < hi)
        keys_h = jnp.concatenate([jnp.where(mine, keys_s, 0), hidden], axis=1)
        scores = matmul(keys_h, query_x, ((1,), (1,)))
        expo = jnp.exp(scores - jnp.max(scores, axis=0, keepdims=True))
        probs = expo * (1.0 / jnp.sum(expo, axis=0, keepdims=True))
        probs_b = probs.astype(BF16)
        out_t = matmul(values_t[lo:hi, :], probs_b)
        attn_t.append(out_t)
        inner = jnp.sum(out_t * d_attn_t[lo:hi, :].astype(F32), axis=0, keepdims=True) * scale
        d_probs = matmul(jnp.where(mine, values, 0), d_attn_s, ((1,), (1,)))
        d_score = (probs * (d_probs - inner)).astype(BF16)
        dq_t.append(matmul(keys_t[lo:hi, :], d_score))
        d_values = jnp.where(mine, matmul(probs_b, d_attn), d_values)
        d_keys = jnp.where(mine, matmul(d_score, query), d_keys)

    attn_t = jnp.concatenate(attn_t, axis=0)
    attn_ref[...] = attn_t.T.astype(BF16)
    grad_w_out = matmul(attn_t.astype(BF16), cot)
    grad_b_out = jnp.sum(cot.astype(F32), axis=0, keepdims=True)

    d_query = jnp.concatenate(dq_t, axis=0).T
    d_qkv = jnp.concatenate([d_query, d_keys, d_values], axis=1).astype(BF16)
    d_normed = matmul(d_qkv, w_qkv, ((1,), (1,)))
    grad_w_qkv = matmul(normed, d_qkv, ((0,), (0,)))
    grad_b_qkv = jnp.sum(d_qkv.astype(F32), axis=0, keepdims=True)
    grad_gain = jnp.sum(d_normed * xhat, axis=0, keepdims=True)
    d_normed_ref[...] = d_normed
    sums = jnp.concatenate(
        [
            grad_b_qkv[:, : 2 * width],
            jnp.concatenate([grad_b_qkv[:, 2 * width :], grad_b_out], axis=1),
            jnp.concatenate([grad_gain, jnp.zeros_like(grad_gain)], axis=1),
            jnp.zeros((5, 2 * width), F32),
        ],
        axis=0,
    )
    left = grad_w_qkv[:, : 2 * width]
    right = jnp.concatenate([grad_w_qkv[:, 2 * width :], grad_w_out], axis=1)
    if near == 1:
        left_ref, right_ref, sums_ref = outs
        left_ref[...] = left.astype(BF16)
        right_ref[...] = right.astype(BF16)
        sums_ref[...] = sums.astype(BF16)
        return
    mine_ref, theirs_ref = outs
    both_ref[:width] = left
    both_ref[width:] = right
    core = lax.axis_index("seq") & 1
    for half, half_ref in ((core, mine_ref), (core ^ 1, theirs_ref)):
        span = pl.ds(pl.multiple_of(half * width, width), width)
        half_ref[:width] = both_ref[span].astype(half_ref.dtype)
        half_ref[width:] = sums.astype(half_ref.dtype)


def rows_kernel(got_ref, attn_ref, d_normed_ref, vectors_ref, w_out_ref, back_ref, token_ref):
    token_ref[...] = jnp.zeros_like(token_ref)
    width = attn_ref.shape[1]
    gain = vectors_ref[:, :width]
    b_out = vectors_ref[:, width : 2 * width]
    points = got_ref[:, :width].astype(F32)
    cot = got_ref[:, width:].astype(F32)
    xhat, rstd = normalize(points)
    mixed = points + (matmul(attn_ref[...], w_out_ref[...]) + b_out)
    d_xhat = d_normed_ref[...] * gain
    inner = (
        d_xhat
        - jnp.mean(d_xhat, axis=-1, keepdims=True)
        - xhat * jnp.mean(d_xhat * xhat, axis=-1, keepdims=True)
    )
    back_ref[:, :width] = mixed.astype(BF16)
    back_ref[:, width:] = (cot + rstd * inner).astype(BF16)


def sum_kernel(count, *refs):
    piece_refs, out_ref = refs[:count], refs[-1]
    values = [piece_ref[...].astype(F32) for piece_ref in piece_refs]
    while len(values) > 1:
        values = [left + right for left, right in zip(values[::2], values[1::2])]
    out_ref[...] = values[0].astype(BF16)


def tie_kernel(rows_ref, other_ref, out_ref):
    pass


def pick_kernel(block_rows, route_hbm, pick_ref, route_ref, sem):
    copy = pltpu.make_async_copy(route_hbm, route_ref, sem)
    copy.start()
    copy.wait()
    target = send_rows(route_ref, (pick_ref.shape[0], 1), 0, block_rows)
    index = lax.broadcasted_iota(jnp.int32, pick_ref.shape, 1)
    pick_ref[...] = jnp.where(index == target, 1.0, 0.0).astype(BF16)


def return_kernel(pick_ref, back_ref, mixed_ref, grad_ref):
    width = mixed_ref.shape[1]
    moved = matmul(pick_ref[...], back_ref[...]).astype(BF16)
    mixed_ref[...] = moved[:, :width]
    grad_ref[...] = moved[:, width:]


def weights_kernel(*refs):
    *half_refs, gain_ref, w_qkv_ref, b_qkv_ref, w_out_ref, b_out_ref, both_ref = refs
    width = w_out_ref.shape[1]
    core = lax.axis_index("seq") & 1
    for step, half_ref in enumerate(half_refs):
        place = core ^ step
        half = half_ref[...].astype(F32)
        both_ref[pl.ds(pl.multiple_of(place * width, width), width)] = half[:width]

        @pl.when(place == 0)
        def _():
            sums = half[width:]
            gain_ref[...] = sums[2, :width]
            b_qkv_ref[: 2 * width] = sums[0]
            b_qkv_ref[2 * width :] = sums[1, :width]
            b_out_ref[...] = sums[1, width:]

    w_qkv_ref[:, : 2 * width] = both_ref[:width]
    w_qkv_ref[:, 2 * width :] = both_ref[width:, :width]
    w_out_ref[...] = both_ref[width:, width:]


def exchange(message):
    return lax.all_to_all(message, "seq", split_axis=0, concat_axis=0, tiled=True)


def swap(piece, step, devs):
    return lax.ppermute(piece, "seq", [(dev, dev ^ step) for dev in range(devs)])


def local(points, route, owned, cotangent, gain, w_qkv, b_qkv, w_out, b_out):
    devs = lax.axis_size("seq")
    rows, width = points.shape
    block_rows = rows // route.shape[1]
    held = devs * block_rows
    share = width // devs
    near = 4 if devs == 16 and width % 64 == 0 else 1

    def shape(*dims, dtype=BF16):
        return jax.ShapeDtypeStruct(dims, dtype)

    sent = pl.pallas_call(
        functools.partial(scatter_kernel, block_rows),
        out_shape=shape(held, 2 * width),
        in_specs=[ANY] * 3,
        out_specs=VMEM,
        scratch_shapes=[
            pltpu.SMEM(route.shape, route.dtype),
            pltpu.VMEM(points.shape, points.dtype),
            pltpu.VMEM(cotangent.shape, cotangent.dtype),
            pltpu.SemaphoreType.DMA((3,)),
        ],
    )(route, points, cotangent)
    got = exchange(sent.reshape(devs, block_rows, 2 * width)).reshape(held, 2 * width)

    half = shape(width + 8, 2 * width)
    if near > 1:
        sums_shapes = (half, half)
    else:
        sums_shapes = (shape(width, 2 * width),) * 2 + (shape(8, 2 * width),)
    vectors = jnp.concatenate([gain, b_out, b_qkv])[None, :]
    attn, d_normed, *parts = pl.pallas_call(
        functools.partial(owner_kernel, near),
        out_shape=(shape(held, width), shape(held, width, dtype=F32)) + sums_shapes,
        in_specs=[VMEM, VMEM, ANY, ANY],
        out_specs=(VMEM,) * (2 + len(sums_shapes)),
        scratch_shapes=[
            pltpu.VMEM(w_qkv.shape, w_qkv.dtype),
            pltpu.VMEM(w_out.shape, w_out.dtype),
            pltpu.VMEM((2 * width, 2 * width), F32),
            pltpu.SemaphoreType.DMA((2,)),
        ],
        compiler_params=LARGE,
    )(got, vectors, w_qkv, w_out)
    back, token = pl.pallas_call(
        rows_kernel,
        out_shape=(shape(held, 2 * width), shape(8, 128, dtype=F32)),
        in_specs=[VMEM] * 5,
        out_specs=(VMEM,) * 2,
        compiler_params=SMALL,
        cost_estimate=pl.CostEstimate(
            flops=64 * held * width * width, bytes_accessed=16 * held * width, transcendentals=0
        ),
    )(got, attn, d_normed, vectors, w_out)

    pick = pl.pallas_call(
        functools.partial(pick_kernel, block_rows),
        out_shape=shape(rows, held),
        in_specs=[ANY],
        out_specs=VMEM,
        scratch_shapes=[pltpu.SMEM(route.shape, route.dtype), pltpu.SemaphoreType.DMA],
        compiler_params=SMALL,
    )(route)

    def give_back(back):
        return pl.pallas_call(
            return_kernel,
            out_shape=(shape(rows, width), shape(rows, width)),
            in_specs=[VMEM] * 2,
            out_specs=(VMEM,) * 2,
            compiler_params=SMALL,
        )(pick, back)

    if near > 1:
        mine, theirs = parts

        def add(*pieces, after=(), flops=0):
            return pl.pallas_call(
                functools.partial(sum_kernel, len(pieces)),
                out_shape=half,
                in_specs=[VMEM] * (len(pieces) + len(after)),
                out_specs=VMEM,
                compiler_params=SMALL,
                cost_estimate=pl.CostEstimate(flops=flops, bytes_accessed=0, transcendentals=0),
            )(*pieces, *after)

        total = add(mine, swap(theirs, 1, devs), after=(token,))
        back = pl.pallas_call(
            tie_kernel,
            out_shape=back,
            in_specs=[ANY, VMEM],
            out_specs=ANY,
            input_output_aliases={0: 0},
            compiler_params=SMALL,
        )(back, total)
        back = exchange(back.reshape(devs, block_rows, 2 * width)).reshape(held, 2 * width)
        mixed, grad_points = give_back(back)
        far = [swap(total, step, devs) for step in range(near, devs, near)]
        total = add(total, *far, flops=40_000_000_000)
        total = add(total, swap(total, 2, devs))
        parts = [total, swap(total, 1, devs)]
        grad_gain, grad_wq, grad_bq, grad_wo, grad_bo = pl.pallas_call(
            weights_kernel,
            out_shape=tuple(
                shape(*dims, dtype=F32)
                for dims in ((width,), (width, 3 * width), (3 * width,), (width, width), (width,))
            ),
            in_specs=[VMEM] * 2,
            out_specs=(VMEM,) * 5,
            scratch_shapes=[pltpu.VMEM((2 * width, 2 * width), F32)],
            compiler_params=SMALL,
        )(*parts)
    else:
        left, right, sums = parts
        message = jnp.concatenate(
            [
                back.reshape(devs, block_rows, 2 * width),
                left.reshape(devs, share, 2 * width),
                right.reshape(devs, share, 2 * width),
                jnp.broadcast_to(sums[None], (devs, 8, 2 * width)),
            ],
            axis=1,
        )
        message = exchange(message)
        total = jnp.sum(message[:, block_rows:].astype(F32), axis=0)
        mine = total[: 2 * share].astype(BF16)
        both = exchange(jnp.broadcast_to(mine[None], (devs, 2 * share, 2 * width))).astype(F32)
        mixed, grad_points = give_back(message[:, :block_rows].reshape(held, 2 * width))
        left = both[:, :share].reshape(width, 2 * width)
        right = both[:, share:].reshape(width, 2 * width)
        grad_wq = jnp.concatenate([left, right[:, :width]], axis=1)
        grad_wo = right[:, width:]
        flat = total[2 * share :].reshape(-1)
        grad_bq = flat[: 3 * width]
        grad_bo = flat[3 * width : 4 * width]
        grad_gain = flat[4 * width : 5 * width]

    return (mixed, grad_points, grad_gain, grad_wq, grad_bq, grad_wo, grad_bo)


def solution(mesh):
    placed = (
        P(("parts", "seq"), None),
        P(None, ("parts", "seq")),
        P(("parts", "seq")),
        P(("parts", "seq"), None),
        P(),
        P(),
        P(),
        P(),
        P(),
    )
    return jax.shard_map(
        local,
        mesh=mesh,
        in_specs=placed,
        out_specs=(
            P(("parts", "seq"), None),
            P(("parts", "seq"), None),
            P("parts"),
            P("parts", None),
            P("parts"),
            P("parts", None),
            P("parts"),
        ),
        check_vma=False,
    )
```

```python
import functools

import jax
import jax.numpy as jnp
from jax import lax
from jax.experimental import pallas as pl
from jax.experimental.pallas import tpu as pltpu
from jax.sharding import PartitionSpec as P

HEADS = 8
EPS = 1e-05
EMPTY = 64.0
MASKED = -1e30

F32 = jnp.float32
BF16 = jnp.bfloat16

VMEM = pl.BlockSpec(memory_space=pltpu.VMEM)
ANY = pl.BlockSpec(memory_space=pl.ANY)
SMEM = pl.BlockSpec(memory_space=pltpu.SMEM)
MIB = 1024 * 1024
LARGE = pltpu.CompilerParams(vmem_limit_bytes=32 * MIB)
SMALL = pltpu.CompilerParams(vmem_limit_bytes=8 * MIB)


def matmul(left, right, dims=((1,), (0,))):
    return lax.dot_general(left, right, (dims, ((), ())), preferred_element_type=F32)


def send_rows(route_ref, shape, axis, block_rows):
    place = lax.broadcasted_iota(jnp.int32, shape, axis)
    target = jnp.zeros(shape, jnp.int32)
    for block in range(shape[axis] // block_rows):
        first = block * block_rows
        moved = route_ref[0, block] * block_rows + place - first
        target = jnp.where(place >= first, moved, target)
    return target


def scatter_kernel(block_rows, route_hbm, points_hbm, cot_hbm, out_ref, route_ref, points_ref, cot_ref, sems):
    copies = [
        pltpu.make_async_copy(source, target, sems.at[at])
        for at, (source, target) in enumerate(
            ((route_hbm, route_ref), (points_hbm, points_ref), (cot_hbm, cot_ref))
        )
    ]
    for copy in copies:
        copy.start()
    for copy in copies:
        copy.wait()
    rows, width = points_ref.shape
    target = send_rows(route_ref, (1, rows), 1, block_rows)
    index = lax.broadcasted_iota(jnp.int32, (out_ref.shape[0], rows), 0)
    pick = jnp.where(index == target, 1.0, 0.0).astype(BF16)
    ones = jnp.ones((rows, width), BF16)
    moved = matmul(pick, jnp.concatenate([points_ref[...], ones], axis=1))
    empty = (1.0 - moved[:, width:]) * EMPTY
    out_ref[:, :width] = (moved[:, :width] + empty).astype(BF16)
    out_ref[:, width:] = matmul(pick, cot_ref[...]).astype(BF16)


def normalize(points):
    centered = points - jnp.mean(points, axis=-1, keepdims=True)
    rstd = lax.rsqrt(jnp.mean(centered * centered, axis=-1, keepdims=True) + EPS)
    return centered * rstd, rstd


def owner_kernel(near, got_ref, vectors_ref, w_qkv_hbm, w_out_hbm, attn_ref, d_normed_ref, *refs):
    *outs, w_qkv_ref, w_out_ref, both_ref, sems = refs
    copies = [
        pltpu.make_async_copy(w_qkv_hbm, w_qkv_ref, sems.at[0]),
        pltpu.make_async_copy(w_out_hbm, w_out_ref, sems.at[1]),
    ]
    for copy in copies:
        copy.start()
    rows = got_ref.shape[0]
    width = got_ref.shape[1] // 2
    head = width // HEADS
    scale = head ** (-0.5)
    gain = vectors_ref[:, :width]
    b_qkv = vectors_ref[:, 2 * width :]

    points = got_ref[:, :width].astype(F32)
    cot = got_ref[:, width:]
    xhat, _ = normalize(points)
    normed = (xhat * gain).astype(BF16)
    for copy in copies:
        copy.wait()
    w_qkv = w_qkv_ref[...]
    w_out = w_out_ref[...]
    qkv = (matmul(normed, w_qkv) + b_qkv).astype(BF16)
    query, keys, values = qkv[:, :width], qkv[:, width : 2 * width], qkv[:, 2 * width :]
    d_attn = matmul(cot, w_out, ((1,), (1,))).astype(BF16)
    d_attn_t = matmul(w_out, cot, ((1,), (1,))).astype(BF16)
    d_attn_s = (d_attn.astype(F32) * scale).astype(BF16)

    keys_t = keys.T
    values_t = values.T
    keys_s = (keys.astype(F32) * scale).astype(BF16)
    lane = lax.broadcasted_iota(jnp.int32, (rows, width), 1)
    hidden = jnp.where(points > EMPTY / 2, MASKED, 0.0).astype(BF16)
    query_x = jnp.concatenate([query, jnp.where(lane == 0, 1.0, 0.0).astype(BF16)], axis=1)

    attn_t, dq_t = [], []
    d_keys = jnp.zeros((rows, width), F32)
    d_values = jnp.zeros((rows, width), F32)
    for h in range(HEADS):
        lo, hi = h * head, (h + 1) * head
        mine = (lane >= lo) & (lane < hi)
        keys_h = jnp.concatenate([jnp.where(mine, keys_s, 0), hidden], axis=1)
        scores = matmul(keys_h, query_x, ((1,), (1,)))
        expo = jnp.exp(scores - jnp.max(scores, axis=0, keepdims=True))
        probs = expo * (1.0 / jnp.sum(expo, axis=0, keepdims=True))
        probs_b = probs.astype(BF16)
        out_t = matmul(values_t[lo:hi, :], probs_b)
        attn_t.append(out_t)
        inner = jnp.sum(out_t * d_attn_t[lo:hi, :].astype(F32), axis=0, keepdims=True) * scale
        d_probs = matmul(jnp.where(mine, values, 0), d_attn_s, ((1,), (1,)))
        d_score = (probs * (d_probs - inner)).astype(BF16)
        dq_t.append(matmul(keys_t[lo:hi, :], d_score))
        d_values = jnp.where(mine, matmul(probs_b, d_attn), d_values)
        d_keys = jnp.where(mine, matmul(d_score, query), d_keys)

    attn_t = jnp.concatenate(attn_t, axis=0)
    attn_ref[...] = attn_t.T.astype(BF16)
    grad_w_out = matmul(attn_t.astype(BF16), cot)
    grad_b_out = jnp.sum(cot.astype(F32), axis=0, keepdims=True)

    d_query = jnp.concatenate(dq_t, axis=0).T
    d_qkv = jnp.concatenate([d_query, d_keys, d_values], axis=1).astype(BF16)
    d_normed = matmul(d_qkv, w_qkv, ((1,), (1,)))
    grad_w_qkv = matmul(normed, d_qkv, ((0,), (0,)))
    grad_b_qkv = jnp.sum(d_qkv.astype(F32), axis=0, keepdims=True)
    grad_gain = jnp.sum(d_normed * xhat, axis=0, keepdims=True)
    d_normed_ref[...] = d_normed
    sums = jnp.concatenate(
        [
            grad_b_qkv[:, : 2 * width],
            jnp.concatenate([grad_b_qkv[:, 2 * width :], grad_b_out], axis=1),
            jnp.concatenate([grad_gain, jnp.zeros_like(grad_gain)], axis=1),
            jnp.zeros((5, 2 * width), F32),
        ],
        axis=0,
    )
    left = grad_w_qkv[:, : 2 * width]
    right = jnp.concatenate([grad_w_qkv[:, 2 * width :], grad_w_out], axis=1)
    if near == 1:
        left_ref, right_ref, sums_ref = outs
        left_ref[...] = left.astype(BF16)
        right_ref[...] = right.astype(BF16)
        sums_ref[...] = sums.astype(BF16)
        return
    mine_ref, theirs_ref = outs
    both_ref[:width] = left
    both_ref[width:] = right
    core = lax.axis_index("seq") & 1
    for half, half_ref in ((core, mine_ref), (core ^ 1, theirs_ref)):
        span = pl.ds(pl.multiple_of(half * width, width), width)
        half_ref[:width] = both_ref[span].astype(half_ref.dtype)
        half_ref[width:] = sums.astype(half_ref.dtype)


def rows_kernel(got_ref, attn_ref, d_normed_ref, vectors_ref, w_out_ref, back_ref, token_ref):
    token_ref[...] = jnp.zeros_like(token_ref)
    width = attn_ref.shape[1]
    gain = vectors_ref[:, :width]
    b_out = vectors_ref[:, width : 2 * width]
    points = got_ref[:, :width].astype(F32)
    cot = got_ref[:, width:].astype(F32)
    xhat, rstd = normalize(points)
    mixed = points + (matmul(attn_ref[...], w_out_ref[...]) + b_out)
    d_xhat = d_normed_ref[...] * gain
    inner = (
        d_xhat
        - jnp.mean(d_xhat, axis=-1, keepdims=True)
        - xhat * jnp.mean(d_xhat * xhat, axis=-1, keepdims=True)
    )
    back_ref[:, :width] = mixed.astype(BF16)
    back_ref[:, width:] = (cot + rstd * inner).astype(BF16)


def sum_kernel(count, *refs):
    piece_refs, out_ref = refs[:count], refs[-1]
    values = [piece_ref[...].astype(F32) for piece_ref in piece_refs]
    while len(values) > 1:
        values = [left + right for left, right in zip(values[::2], values[1::2])]
    out_ref[...] = values[0].astype(BF16)


def tie_kernel(rows_ref, other_ref, out_ref):
    pass


def pick_kernel(block_rows, route_hbm, pick_ref, route_ref, sem):
    copy = pltpu.make_async_copy(route_hbm, route_ref, sem)
    copy.start()
    copy.wait()
    target = send_rows(route_ref, (pick_ref.shape[0], 1), 0, block_rows)
    index = lax.broadcasted_iota(jnp.int32, pick_ref.shape, 1)
    pick_ref[...] = jnp.where(index == target, 1.0, 0.0).astype(BF16)


def return_kernel(pick_ref, back_ref, mixed_ref, grad_ref):
    width = mixed_ref.shape[1]
    moved = matmul(pick_ref[...], back_ref[...]).astype(BF16)
    mixed_ref[...] = moved[:, :width]
    grad_ref[...] = moved[:, width:]


def weights_kernel(*refs):
    *half_refs, gain_ref, w_qkv_ref, b_qkv_ref, w_out_ref, b_out_ref, both_ref = refs
    width = w_out_ref.shape[1]
    core = lax.axis_index("seq") & 1
    for step, half_ref in enumerate(half_refs):
        place = core ^ step
        half = half_ref[...].astype(F32)
        both_ref[pl.ds(pl.multiple_of(place * width, width), width)] = half[:width]

        @pl.when(place == 0)
        def _():
            sums = half[width:]
            gain_ref[...] = sums[2, :width]
            b_qkv_ref[: 2 * width] = sums[0]
            b_qkv_ref[2 * width :] = sums[1, :width]
            b_out_ref[...] = sums[1, width:]

    w_qkv_ref[:, : 2 * width] = both_ref[:width]
    w_qkv_ref[:, 2 * width :] = both_ref[width:, :width]
    w_out_ref[...] = both_ref[width:, width:]


def exchange(message):
    return lax.all_to_all(message, "seq", split_axis=0, concat_axis=0, tiled=True)


def swap(piece, step, devs):
    return lax.ppermute(piece, "seq", [(dev, dev ^ step) for dev in range(devs)])


def local(points, route, owned, cotangent, gain, w_qkv, b_qkv, w_out, b_out):
    devs = lax.axis_size("seq")
    rows, width = points.shape
    block_rows = rows // route.shape[1]
    held = devs * block_rows
    share = width // devs
    near = 4 if devs == 16 and width % 64 == 0 else 1

    def shape(*dims, dtype=BF16):
        return jax.ShapeDtypeStruct(dims, dtype)

    sent = pl.pallas_call(
        functools.partial(scatter_kernel, block_rows),
        out_shape=shape(held, 2 * width),
        in_specs=[ANY] * 3,
        out_specs=VMEM,
        scratch_shapes=[
            pltpu.SMEM(route.shape, route.dtype),
            pltpu.VMEM(points.shape, points.dtype),
            pltpu.VMEM(cotangent.shape, cotangent.dtype),
            pltpu.SemaphoreType.DMA((3,)),
        ],
    )(route, points, cotangent)
    got = exchange(sent.reshape(devs, block_rows, 2 * width)).reshape(held, 2 * width)

    half = shape(width + 8, 2 * width)
    if near > 1:
        sums_shapes = (half, half)
    else:
        sums_shapes = (shape(width, 2 * width),) * 2 + (shape(8, 2 * width),)
    vectors = jnp.concatenate([gain, b_out, b_qkv])[None, :]
    attn, d_normed, *parts = pl.pallas_call(
        functools.partial(owner_kernel, near),
        out_shape=(shape(held, width), shape(held, width, dtype=F32)) + sums_shapes,
        in_specs=[VMEM, VMEM, ANY, ANY],
        out_specs=(VMEM,) * (2 + len(sums_shapes)),
        scratch_shapes=[
            pltpu.VMEM(w_qkv.shape, w_qkv.dtype),
            pltpu.VMEM(w_out.shape, w_out.dtype),
            pltpu.VMEM((2 * width, 2 * width), F32),
            pltpu.SemaphoreType.DMA((2,)),
        ],
        compiler_params=LARGE,
    )(got, vectors, w_qkv, w_out)
    back, token = pl.pallas_call(
        rows_kernel,
        out_shape=(shape(held, 2 * width), shape(8, 128, dtype=F32)),
        in_specs=[VMEM] * 5,
        out_specs=(VMEM,) * 2,
        compiler_params=SMALL,
        cost_estimate=pl.CostEstimate(
            flops=64 * held * width * width, bytes_accessed=16 * held * width, transcendentals=0
        ),
    )(got, attn, d_normed, vectors, w_out)

    pick = pl.pallas_call(
        functools.partial(pick_kernel, block_rows),
        out_shape=shape(rows, held),
        in_specs=[ANY],
        out_specs=VMEM,
        scratch_shapes=[pltpu.SMEM(route.shape, route.dtype), pltpu.SemaphoreType.DMA],
        compiler_params=SMALL,
    )(route)

    def give_back(back):
        return pl.pallas_call(
            return_kernel,
            out_shape=(shape(rows, width), shape(rows, width)),
            in_specs=[VMEM] * 2,
            out_specs=(VMEM,) * 2,
            compiler_params=SMALL,
        )(pick, back)

    if near > 1:
        mine, theirs = parts

        def add(*pieces, after=(), flops=0):
            return pl.pallas_call(
                functools.partial(sum_kernel, len(pieces)),
                out_shape=half,
                in_specs=[VMEM] * (len(pieces) + len(after)),
                out_specs=VMEM,
                compiler_params=SMALL,
                cost_estimate=pl.CostEstimate(flops=flops, bytes_accessed=0, transcendentals=0),
            )(*pieces, *after)

        total = add(mine, swap(theirs, 1, devs), after=(token,))
        back = pl.pallas_call(
            tie_kernel,
            out_shape=back,
            in_specs=[ANY, VMEM],
            out_specs=ANY,
            input_output_aliases={0: 0},
            compiler_params=SMALL,
        )(back, total)
        back = exchange(back.reshape(devs, block_rows, 2 * width)).reshape(held, 2 * width)
        mixed, grad_points = give_back(back)
        total = add(total, swap(total, devs // 2, devs), flops=40_000_000_000)
        steps = [step for step in range(2, devs // 2, 2)]
        total = add(total, *(swap(total, step, devs) for step in steps))
        parts = [total, swap(total, 1, devs)]
        grad_gain, grad_wq, grad_bq, grad_wo, grad_bo = pl.pallas_call(
            weights_kernel,
            out_shape=tuple(
                shape(*dims, dtype=F32)
                for dims in ((width,), (width, 3 * width), (3 * width,), (width, width), (width,))
            ),
            in_specs=[VMEM] * 2,
            out_specs=(VMEM,) * 5,
            scratch_shapes=[pltpu.VMEM((2 * width, 2 * width), F32)],
            compiler_params=SMALL,
        )(*parts)
    else:
        left, right, sums = parts
        message = jnp.concatenate(
            [
                back.reshape(devs, block_rows, 2 * width),
                left.reshape(devs, share, 2 * width),
                right.reshape(devs, share, 2 * width),
                jnp.broadcast_to(sums[None], (devs, 8, 2 * width)),
            ],
            axis=1,
        )
        message = exchange(message)
        total = jnp.sum(message[:, block_rows:].astype(F32), axis=0)
        mine = total[: 2 * share].astype(BF16)
        both = exchange(jnp.broadcast_to(mine[None], (devs, 2 * share, 2 * width))).astype(F32)
        mixed, grad_points = give_back(message[:, :block_rows].reshape(held, 2 * width))
        left = both[:, :share].reshape(width, 2 * width)
        right = both[:, share:].reshape(width, 2 * width)
        grad_wq = jnp.concatenate([left, right[:, :width]], axis=1)
        grad_wo = right[:, width:]
        flat = total[2 * share :].reshape(-1)
        grad_bq = flat[: 3 * width]
        grad_bo = flat[3 * width : 4 * width]
        grad_gain = flat[4 * width : 5 * width]

    return (mixed, grad_points, grad_gain, grad_wq, grad_bq, grad_wo, grad_bo)


def solution(mesh):
    placed = (
        P(("parts", "seq"), None),
        P(None, ("parts", "seq")),
        P(("parts", "seq")),
        P(("parts", "seq"), None),
        P(),
        P(),
        P(),
        P(),
        P(),
    )
    return jax.shard_map(
        local,
        mesh=mesh,
        in_specs=placed,
        out_specs=(
            P(("parts", "seq"), None),
            P(("parts", "seq"), None),
            P("parts"),
            P("parts", None),
            P("parts"),
            P("parts", None),
            P("parts"),
        ),
        check_vma=False,
    )
```

```python
import functools

import jax
import jax.numpy as jnp
from jax import lax
from jax.experimental import pallas as pl
from jax.experimental.pallas import tpu as pltpu
from jax.sharding import PartitionSpec as P

HEADS = 8
EPS = 1e-05
EMPTY = 64.0
MASKED = -1e30

F32 = jnp.float32
BF16 = jnp.bfloat16

VMEM = pl.BlockSpec(memory_space=pltpu.VMEM)
ANY = pl.BlockSpec(memory_space=pl.ANY)
SMEM = pl.BlockSpec(memory_space=pltpu.SMEM)
MIB = 1024 * 1024
LARGE = pltpu.CompilerParams(vmem_limit_bytes=32 * MIB)
SMALL = pltpu.CompilerParams(vmem_limit_bytes=8 * MIB)


def matmul(left, right, dims=((1,), (0,))):
    return lax.dot_general(left, right, (dims, ((), ())), preferred_element_type=F32)


def send_rows(route_ref, shape, axis, block_rows):
    place = lax.broadcasted_iota(jnp.int32, shape, axis)
    target = jnp.zeros(shape, jnp.int32)
    for block in range(shape[axis] // block_rows):
        first = block * block_rows
        moved = route_ref[0, block] * block_rows + place - first
        target = jnp.where(place >= first, moved, target)
    return target


def scatter_kernel(block_rows, route_hbm, points_hbm, cot_hbm, out_ref, route_ref, points_ref, cot_ref, sems):
    copies = [
        pltpu.make_async_copy(source, target, sems.at[at])
        for at, (source, target) in enumerate(
            ((route_hbm, route_ref), (points_hbm, points_ref), (cot_hbm, cot_ref))
        )
    ]
    for copy in copies:
        copy.start()
    for copy in copies:
        copy.wait()
    rows, width = points_ref.shape
    target = send_rows(route_ref, (1, rows), 1, block_rows)
    index = lax.broadcasted_iota(jnp.int32, (out_ref.shape[0], rows), 0)
    pick = jnp.where(index == target, 1.0, 0.0).astype(BF16)
    ones = jnp.ones((rows, width), BF16)
    moved = matmul(pick, jnp.concatenate([points_ref[...], ones], axis=1))
    empty = (1.0 - moved[:, width:]) * EMPTY
    out_ref[:, :width] = (moved[:, :width] + empty).astype(BF16)
    out_ref[:, width:] = matmul(pick, cot_ref[...]).astype(BF16)


def normalize(points):
    centered = points - jnp.mean(points, axis=-1, keepdims=True)
    rstd = lax.rsqrt(jnp.mean(centered * centered, axis=-1, keepdims=True) + EPS)
    return centered * rstd, rstd


def owner_kernel(near, got_ref, vectors_ref, w_qkv_hbm, w_out_hbm, attn_ref, d_normed_ref, *refs):
    *outs, w_qkv_ref, w_out_ref, both_ref, probs_ref, d_score_ref, sems = refs
    copies = [
        pltpu.make_async_copy(w_qkv_hbm, w_qkv_ref, sems.at[0]),
        pltpu.make_async_copy(w_out_hbm, w_out_ref, sems.at[1]),
    ]
    for copy in copies:
        copy.start()
    rows = got_ref.shape[0]
    width = got_ref.shape[1] // 2
    head = width // HEADS
    scale = head ** (-0.5)
    gain = vectors_ref[:, :width]
    b_qkv = vectors_ref[:, 2 * width :]

    points = got_ref[:, :width].astype(F32)
    cot = got_ref[:, width:]
    xhat, _ = normalize(points)
    normed = (xhat * gain).astype(BF16)
    for copy in copies:
        copy.wait()
    w_qkv = w_qkv_ref[...]
    w_out = w_out_ref[...]
    qkv = (matmul(normed, w_qkv) + b_qkv).astype(BF16)
    query, keys, values = qkv[:, :width], qkv[:, width : 2 * width], qkv[:, 2 * width :]
    d_attn = matmul(cot, w_out, ((1,), (1,))).astype(BF16)
    d_attn_t = matmul(w_out, cot, ((1,), (1,))).astype(BF16)
    d_attn_s = (d_attn.astype(F32) * scale).astype(BF16)

    keys_t = keys.T
    values_t = values.T
    keys_s = (keys.astype(F32) * scale).astype(BF16)
    lane = lax.broadcasted_iota(jnp.int32, (rows, width), 1)
    hidden = jnp.where(points > EMPTY / 2, MASKED, 0.0).astype(BF16)
    query_x = jnp.concatenate([query, jnp.where(lane == 0, 1.0, 0.0).astype(BF16)], axis=1)

    spans = [slice(at, at + rows // 2) for at in (0, rows // 2)]
    mines = [(lane >= h * head) & (lane < (h + 1) * head) for h in range(HEADS)]

    def scores_of(h, span):
        keys_h = jnp.concatenate([jnp.where(mines[h], keys_s, 0), hidden], axis=1)
        return matmul(keys_h, query_x[span], ((1,), (1,)))

    tiles = [(h, span) for h in range(HEADS) for span in spans]
    scores = scores_of(*tiles[0])
    attn_t = {span.start: [] for span in spans}
    dq_t = {span.start: [] for span in spans}
    for at, (h, span) in enumerate(tiles):
        now = scores
        if at + 1 < len(tiles):
            scores = scores_of(*tiles[at + 1])
        lo, hi = h * head, (h + 1) * head
        d_probs = matmul(jnp.where(mines[h], values, 0), d_attn_s[span], ((1,), (1,)))
        expo = jnp.exp(now - jnp.max(now, axis=0, keepdims=True))
        probs = expo * (1.0 / jnp.sum(expo, axis=0, keepdims=True))
        probs_b = probs.astype(BF16)
        wide = slice(h * rows + span.start, h * rows + span.stop)
        probs_ref[:, wide] = probs_b
        out_t = matmul(values_t[lo:hi, :], probs_b)
        attn_t[span.start].append(out_t)
        inner = out_t * d_attn_t[lo:hi, span].astype(F32)
        inner = jnp.sum(inner, axis=0, keepdims=True) * scale
        d_score = (probs * (d_probs - inner)).astype(BF16)
        d_score_ref[:, wide] = d_score
        dq_t[span.start].append(matmul(keys_t[lo:hi, :], d_score))
    attn_t, dq_t = (
        jnp.concatenate([jnp.concatenate(part[span.start], axis=0) for span in spans], axis=1)
        for part in (attn_t, dq_t)
    )
    uppers = jnp.concatenate([jnp.where(mine, d_attn, 0) for mine in mines], axis=0)
    d_values = matmul(probs_ref[...], uppers)
    queries = jnp.concatenate([jnp.where(mine, query, 0) for mine in mines], axis=0)
    d_keys = matmul(d_score_ref[...], queries)

    attn_ref[...] = attn_t.T.astype(BF16)
    grad_w_out = matmul(attn_t.astype(BF16), cot)
    grad_b_out = jnp.sum(cot.astype(F32), axis=0, keepdims=True)

    d_query = dq_t.T
    d_qkv = jnp.concatenate([d_query, d_keys, d_values], axis=1).astype(BF16)
    d_normed = matmul(d_qkv, w_qkv, ((1,), (1,)))
    grad_w_qkv = matmul(normed, d_qkv, ((0,), (0,)))
    grad_b_qkv = jnp.sum(d_qkv.astype(F32), axis=0, keepdims=True)
    grad_gain = jnp.sum(d_normed * xhat, axis=0, keepdims=True)
    d_normed_ref[...] = d_normed
    sums = jnp.concatenate(
        [
            grad_b_qkv[:, : 2 * width],
            jnp.concatenate([grad_b_qkv[:, 2 * width :], grad_b_out], axis=1),
            jnp.concatenate([grad_gain, jnp.zeros_like(grad_gain)], axis=1),
            jnp.zeros((5, 2 * width), F32),
        ],
        axis=0,
    )
    left = grad_w_qkv[:, : 2 * width]
    right = jnp.concatenate([grad_w_qkv[:, 2 * width :], grad_w_out], axis=1)
    if near == 1:
        left_ref, right_ref, sums_ref = outs
        left_ref[...] = left.astype(BF16)
        right_ref[...] = right.astype(BF16)
        sums_ref[...] = sums.astype(BF16)
        return
    mine_ref, theirs_ref = outs
    both_ref[:width] = left
    both_ref[width:] = right
    core = lax.axis_index("seq") & 1
    for half, half_ref in ((core, mine_ref), (core ^ 1, theirs_ref)):
        span = pl.ds(pl.multiple_of(half * width, width), width)
        half_ref[:width] = both_ref[span].astype(half_ref.dtype)
        half_ref[width:] = sums.astype(half_ref.dtype)


def rows_kernel(got_ref, attn_ref, d_normed_ref, vectors_ref, w_out_ref, back_ref, token_ref):
    token_ref[...] = jnp.zeros_like(token_ref)
    width = attn_ref.shape[1]
    gain = vectors_ref[:, :width]
    b_out = vectors_ref[:, width : 2 * width]
    points = got_ref[:, :width].astype(F32)
    cot = got_ref[:, width:].astype(F32)
    xhat, rstd = normalize(points)
    mixed = points + (matmul(attn_ref[...], w_out_ref[...]) + b_out)
    d_xhat = d_normed_ref[...] * gain
    inner = (
        d_xhat
        - jnp.mean(d_xhat, axis=-1, keepdims=True)
        - xhat * jnp.mean(d_xhat * xhat, axis=-1, keepdims=True)
    )
    back_ref[:, :width] = mixed.astype(BF16)
    back_ref[:, width:] = (cot + rstd * inner).astype(BF16)


def sum_kernel(count, *refs):
    piece_refs, out_ref = refs[:count], refs[-1]
    values = [piece_ref[...].astype(F32) for piece_ref in piece_refs]
    while len(values) > 1:
        values = [left + right for left, right in zip(values[::2], values[1::2])]
    out_ref[...] = values[0].astype(BF16)


def tie_kernel(rows_ref, other_ref, out_ref):
    pass


def pick_kernel(block_rows, route_hbm, pick_ref, route_ref, sem):
    copy = pltpu.make_async_copy(route_hbm, route_ref, sem)
    copy.start()
    copy.wait()
    target = send_rows(route_ref, (pick_ref.shape[0], 1), 0, block_rows)
    index = lax.broadcasted_iota(jnp.int32, pick_ref.shape, 1)
    pick_ref[...] = jnp.where(index == target, 1.0, 0.0).astype(BF16)


def return_kernel(pick_ref, back_ref, mixed_ref, grad_ref, token_ref):
    token_ref[...] = jnp.zeros_like(token_ref)
    width = mixed_ref.shape[1]
    moved = matmul(pick_ref[...], back_ref[...]).astype(BF16)
    mixed_ref[...] = moved[:, :width]
    grad_ref[...] = moved[:, width:]


def weights_kernel(*refs):
    *half_refs, gain_ref, w_qkv_ref, b_qkv_ref, w_out_ref, b_out_ref, both_ref = refs
    width = w_out_ref.shape[1]
    core = lax.axis_index("seq") & 1
    for step, half_ref in enumerate(half_refs):
        place = core ^ step
        half = half_ref[...].astype(F32)
        both_ref[pl.ds(pl.multiple_of(place * width, width), width)] = half[:width]

        @pl.when(place == 0)
        def _():
            sums = half[width:]
            gain_ref[...] = sums[2, :width]
            b_qkv_ref[: 2 * width] = sums[0]
            b_qkv_ref[2 * width :] = sums[1, :width]
            b_out_ref[...] = sums[1, width:]

    w_qkv_ref[:, : 2 * width] = both_ref[:width]
    w_qkv_ref[:, 2 * width :] = both_ref[width:, :width]
    w_out_ref[...] = both_ref[width:, width:]


def exchange(message):
    return lax.all_to_all(message, "seq", split_axis=0, concat_axis=0, tiled=True)


def swap(piece, step, devs):
    return lax.ppermute(piece, "seq", [(dev, dev ^ step) for dev in range(devs)])


def local(points, route, owned, cotangent, gain, w_qkv, b_qkv, w_out, b_out):
    devs = lax.axis_size("seq")
    rows, width = points.shape
    block_rows = rows // route.shape[1]
    held = devs * block_rows
    share = width // devs
    near = 4 if devs == 16 and width % 64 == 0 else 1

    def shape(*dims, dtype=BF16):
        return jax.ShapeDtypeStruct(dims, dtype)

    sent = pl.pallas_call(
        functools.partial(scatter_kernel, block_rows),
        out_shape=shape(held, 2 * width),
        in_specs=[ANY] * 3,
        out_specs=VMEM,
        scratch_shapes=[
            pltpu.SMEM(route.shape, route.dtype),
            pltpu.VMEM(points.shape, points.dtype),
            pltpu.VMEM(cotangent.shape, cotangent.dtype),
            pltpu.SemaphoreType.DMA((3,)),
        ],
    )(route, points, cotangent)
    got = exchange(sent.reshape(devs, block_rows, 2 * width)).reshape(held, 2 * width)

    half = shape(width + 8, 2 * width)
    if near > 1:
        sums_shapes = (half, half)
    else:
        sums_shapes = (shape(width, 2 * width),) * 2 + (shape(8, 2 * width),)
    vectors = jnp.concatenate([gain, b_out, b_qkv])[None, :]
    attn, d_normed, *parts = pl.pallas_call(
        functools.partial(owner_kernel, near),
        out_shape=(shape(held, width), shape(held, width, dtype=F32)) + sums_shapes,
        in_specs=[VMEM, VMEM, ANY, ANY],
        out_specs=(VMEM,) * (2 + len(sums_shapes)),
        scratch_shapes=[
            pltpu.VMEM(w_qkv.shape, w_qkv.dtype),
            pltpu.VMEM(w_out.shape, w_out.dtype),
            pltpu.VMEM((2 * width, 2 * width), F32),
            pltpu.VMEM((held, HEADS * held), BF16),
            pltpu.VMEM((held, HEADS * held), BF16),
            pltpu.SemaphoreType.DMA((2,)),
        ],
        compiler_params=LARGE,
    )(got, vectors, w_qkv, w_out)
    back, token = pl.pallas_call(
        rows_kernel,
        out_shape=(shape(held, 2 * width), shape(8, 128, dtype=F32)),
        in_specs=[VMEM] * 5,
        out_specs=(VMEM,) * 2,
        compiler_params=SMALL,
        cost_estimate=pl.CostEstimate(
            flops=64 * held * width * width, bytes_accessed=16 * held * width, transcendentals=0
        ),
    )(got, attn, d_normed, vectors, w_out)

    pick = pl.pallas_call(
        functools.partial(pick_kernel, block_rows),
        out_shape=shape(rows, held),
        in_specs=[ANY],
        out_specs=VMEM,
        scratch_shapes=[pltpu.SMEM(route.shape, route.dtype), pltpu.SemaphoreType.DMA],
        compiler_params=SMALL,
    )(route)

    def give_back(back):
        return pl.pallas_call(
            return_kernel,
            out_shape=(shape(rows, width), shape(rows, width), shape(8, 128, dtype=F32)),
            in_specs=[VMEM] * 2,
            out_specs=(VMEM,) * 3,
            compiler_params=SMALL,
        )(pick, back)

    if near > 1:
        mine, theirs = parts

        def add(*pieces, after=(), flops=0):
            return pl.pallas_call(
                functools.partial(sum_kernel, len(pieces)),
                out_shape=half,
                in_specs=[VMEM] * (len(pieces) + len(after)),
                out_specs=VMEM,
                compiler_params=SMALL,
                cost_estimate=pl.CostEstimate(flops=flops, bytes_accessed=0, transcendentals=0),
            )(*pieces, *after)

        total = add(mine, swap(theirs, 1, devs), after=(token,))
        back = pl.pallas_call(
            tie_kernel,
            out_shape=back,
            in_specs=[ANY, VMEM],
            out_specs=ANY,
            input_output_aliases={0: 0},
            compiler_params=SMALL,
        )(back, total)
        back = exchange(back.reshape(devs, block_rows, 2 * width)).reshape(held, 2 * width)
        mixed, grad_points, token = give_back(back)
        total = add(total, swap(total, devs // 2, devs), flops=40_000_000_000)
        steps = [step for step in range(2, devs // 2, 2)]
        total = add(total, *(swap(total, step, devs) for step in steps), after=(token,))
        parts = [total, swap(total, 1, devs)]
        grad_gain, grad_wq, grad_bq, grad_wo, grad_bo = pl.pallas_call(
            weights_kernel,
            out_shape=tuple(
                shape(*dims, dtype=F32)
                for dims in ((width,), (width, 3 * width), (3 * width,), (width, width), (width,))
            ),
            in_specs=[VMEM] * 2,
            out_specs=(VMEM,) * 5,
            scratch_shapes=[pltpu.VMEM((2 * width, 2 * width), F32)],
            compiler_params=SMALL,
        )(*parts)
    else:
        left, right, sums = parts
        message = jnp.concatenate(
            [
                back.reshape(devs, block_rows, 2 * width),
                left.reshape(devs, share, 2 * width),
                right.reshape(devs, share, 2 * width),
                jnp.broadcast_to(sums[None], (devs, 8, 2 * width)),
            ],
            axis=1,
        )
        message = exchange(message)
        total = jnp.sum(message[:, block_rows:].astype(F32), axis=0)
        mine = total[: 2 * share].astype(BF16)
        both = exchange(jnp.broadcast_to(mine[None], (devs, 2 * share, 2 * width))).astype(F32)
        mixed, grad_points, _ = give_back(message[:, :block_rows].reshape(held, 2 * width))
        left = both[:, :share].reshape(width, 2 * width)
        right = both[:, share:].reshape(width, 2 * width)
        grad_wq = jnp.concatenate([left, right[:, :width]], axis=1)
        grad_wo = right[:, width:]
        flat = total[2 * share :].reshape(-1)
        grad_bq = flat[: 3 * width]
        grad_bo = flat[3 * width : 4 * width]
        grad_gain = flat[4 * width : 5 * width]

    return (mixed, grad_points, grad_gain, grad_wq, grad_bq, grad_wo, grad_bo)


def solution(mesh):
    placed = (
        P(("parts", "seq"), None),
        P(None, ("parts", "seq")),
        P(("parts", "seq")),
        P(("parts", "seq"), None),
        P(),
        P(),
        P(),
        P(),
        P(),
    )
    return jax.shard_map(
        local,
        mesh=mesh,
        in_specs=placed,
        out_specs=(
            P(("parts", "seq"), None),
            P(("parts", "seq"), None),
            P("parts"),
            P("parts", None),
            P("parts"),
            P("parts", None),
            P("parts"),
        ),
        check_vma=False,
    )
```

```python
import functools

import jax
import jax.numpy as jnp
from jax import lax
from jax.experimental import pallas as pl
from jax.experimental.pallas import tpu as pltpu
from jax.sharding import PartitionSpec as P

HEADS = 8
EPS = 1e-05
EMPTY = 64.0
MASKED = -1e30

F32 = jnp.float32
BF16 = jnp.bfloat16

VMEM = pl.BlockSpec(memory_space=pltpu.VMEM)
ANY = pl.BlockSpec(memory_space=pl.ANY)
SMEM = pl.BlockSpec(memory_space=pltpu.SMEM)
MIB = 1024 * 1024
LARGE = pltpu.CompilerParams(vmem_limit_bytes=32 * MIB)
SMALL = pltpu.CompilerParams(vmem_limit_bytes=8 * MIB)


def matmul(left, right, dims=((1,), (0,))):
    return lax.dot_general(left, right, (dims, ((), ())), preferred_element_type=F32)


def send_rows(route_ref, shape, axis, block_rows):
    place = lax.broadcasted_iota(jnp.int32, shape, axis)
    target = jnp.zeros(shape, jnp.int32)
    for block in range(shape[axis] // block_rows):
        first = block * block_rows
        moved = route_ref[0, block] * block_rows + place - first
        target = jnp.where(place >= first, moved, target)
    return target


def scatter_kernel(block_rows, route_hbm, points_hbm, cot_hbm, out_ref, route_ref, points_ref, cot_ref, sems):
    copies = [
        pltpu.make_async_copy(source, target, sems.at[at])
        for at, (source, target) in enumerate(
            ((route_hbm, route_ref), (points_hbm, points_ref), (cot_hbm, cot_ref))
        )
    ]
    for copy in copies:
        copy.start()
    for copy in copies:
        copy.wait()
    rows, width = points_ref.shape
    target = send_rows(route_ref, (1, rows), 1, block_rows)
    index = lax.broadcasted_iota(jnp.int32, (out_ref.shape[0], rows), 0)
    pick = jnp.where(index == target, 1.0, 0.0).astype(BF16)
    ones = jnp.ones((rows, width), BF16)
    moved = matmul(pick, jnp.concatenate([points_ref[...], ones], axis=1))
    empty = (1.0 - moved[:, width:]) * EMPTY
    out_ref[:, :width] = (moved[:, :width] + empty).astype(BF16)
    out_ref[:, width:] = matmul(pick, cot_ref[...]).astype(BF16)


def normalize(points):
    centered = points - jnp.mean(points, axis=-1, keepdims=True)
    rstd = lax.rsqrt(jnp.mean(centered * centered, axis=-1, keepdims=True) + EPS)
    return centered * rstd, rstd


def owner_kernel(near, got_ref, vectors_ref, w_qkv_hbm, w_out_hbm, attn_ref, d_normed_ref, *refs):
    *outs, w_qkv_ref, w_out_ref, both_ref, sems = refs
    copies = [
        pltpu.make_async_copy(w_qkv_hbm, w_qkv_ref, sems.at[0]),
        pltpu.make_async_copy(w_out_hbm, w_out_ref, sems.at[1]),
    ]
    for copy in copies:
        copy.start()
    rows = got_ref.shape[0]
    width = got_ref.shape[1] // 2
    head = width // HEADS
    scale = head ** (-0.5)
    gain = vectors_ref[:, :width]
    b_qkv = vectors_ref[:, 2 * width :]

    points = got_ref[:, :width].astype(F32)
    cot = got_ref[:, width:]
    xhat, _ = normalize(points)
    normed = (xhat * gain).astype(BF16)
    for copy in copies:
        copy.wait()
    w_qkv = w_qkv_ref[...]
    w_out = w_out_ref[...]
    qkv = (matmul(normed, w_qkv) + b_qkv).astype(BF16)
    query, keys, values = qkv[:, :width], qkv[:, width : 2 * width], qkv[:, 2 * width :]
    d_attn = matmul(cot, w_out, ((1,), (1,))).astype(BF16)
    d_attn_t = matmul(w_out, cot, ((1,), (1,))).astype(BF16)
    d_attn_s = (d_attn.astype(F32) * scale).astype(BF16)

    keys_t = keys.T
    values_t = values.T
    keys_s = (keys.astype(F32) * scale).astype(BF16)
    lane = lax.broadcasted_iota(jnp.int32, (rows, width), 1)
    hidden = jnp.where(points > EMPTY / 2, MASKED, 0.0).astype(BF16)
    query_x = jnp.concatenate([query, jnp.where(lane == 0, 1.0, 0.0).astype(BF16)], axis=1)

    attn_t, dq_t = [], []
    d_keys = jnp.zeros((rows, width), F32)
    d_values = jnp.zeros((rows, width), F32)
    for h in range(HEADS):
        lo, hi = h * head, (h + 1) * head
        mine = (lane >= lo) & (lane < hi)
        keys_h = jnp.concatenate([jnp.where(mine, keys_s, 0), hidden], axis=1)
        scores = matmul(keys_h, query_x, ((1,), (1,)))
        expo = jnp.exp(scores - jnp.max(scores, axis=0, keepdims=True))
        probs = expo * (1.0 / jnp.sum(expo, axis=0, keepdims=True))
        probs_b = probs.astype(BF16)
        out_t = matmul(values_t[lo:hi, :], probs_b)
        attn_t.append(out_t)
        inner = jnp.sum(out_t * d_attn_t[lo:hi, :].astype(F32), axis=0, keepdims=True) * scale
        d_probs = matmul(jnp.where(mine, values, 0), d_attn_s, ((1,), (1,)))
        d_score = (probs * (d_probs - inner)).astype(BF16)
        dq_t.append(matmul(keys_t[lo:hi, :], d_score))
        d_values = jnp.where(mine, matmul(probs_b, d_attn), d_values)
        d_keys = jnp.where(mine, matmul(d_score, query), d_keys)

    attn_t = jnp.concatenate(attn_t, axis=0)
    attn_ref[...] = attn_t.T.astype(BF16)
    grad_w_out = matmul(attn_t.astype(BF16), cot)
    grad_b_out = jnp.sum(cot.astype(F32), axis=0, keepdims=True)

    d_query = jnp.concatenate(dq_t, axis=0).T
    d_qkv = jnp.concatenate([d_query, d_keys, d_values], axis=1).astype(BF16)
    d_normed = matmul(d_qkv, w_qkv, ((1,), (1,)))
    grad_w_qkv = matmul(normed, d_qkv, ((0,), (0,)))
    grad_b_qkv = jnp.sum(d_qkv.astype(F32), axis=0, keepdims=True)
    grad_gain = jnp.sum(d_normed * xhat, axis=0, keepdims=True)
    d_normed_ref[...] = d_normed
    sums = jnp.concatenate(
        [
            grad_b_qkv[:, : 2 * width],
            jnp.concatenate([grad_b_qkv[:, 2 * width :], grad_b_out], axis=1),
            jnp.concatenate([grad_gain, jnp.zeros_like(grad_gain)], axis=1),
            jnp.zeros((5, 2 * width), F32),
        ],
        axis=0,
    )
    left = grad_w_qkv[:, : 2 * width]
    right = jnp.concatenate([grad_w_qkv[:, 2 * width :], grad_w_out], axis=1)
    if near == 1:
        left_ref, right_ref, sums_ref = outs
        left_ref[...] = left.astype(BF16)
        right_ref[...] = right.astype(BF16)
        sums_ref[...] = sums.astype(BF16)
        return
    mine_ref, theirs_ref = outs
    both_ref[:width] = left
    both_ref[width:] = right
    core = lax.axis_index("seq") & 1
    for half, half_ref in ((core, mine_ref), (core ^ 1, theirs_ref)):
        span = pl.ds(pl.multiple_of(half * width, width), width)
        half_ref[:width] = both_ref[span].astype(half_ref.dtype)
        half_ref[width:] = sums.astype(half_ref.dtype)


def rows_kernel(got_ref, attn_ref, d_normed_ref, vectors_ref, w_out_ref, back_ref, token_ref):
    token_ref[...] = jnp.zeros_like(token_ref)
    width = attn_ref.shape[1]
    gain = vectors_ref[:, :width]
    b_out = vectors_ref[:, width : 2 * width]
    points = got_ref[:, :width].astype(F32)
    cot = got_ref[:, width:].astype(F32)
    xhat, rstd = normalize(points)
    mixed = points + (matmul(attn_ref[...], w_out_ref[...]) + b_out)
    d_xhat = d_normed_ref[...] * gain
    inner = (
        d_xhat
        - jnp.mean(d_xhat, axis=-1, keepdims=True)
        - xhat * jnp.mean(d_xhat * xhat, axis=-1, keepdims=True)
    )
    back_ref[:, :width] = mixed.astype(BF16)
    back_ref[:, width:] = (cot + rstd * inner).astype(BF16)


def sum_kernel(count, *refs):
    piece_refs, out_ref = refs[:count], refs[-1]
    values = [piece_ref[...].astype(F32) for piece_ref in piece_refs]
    while len(values) > 1:
        values = [left + right for left, right in zip(values[::2], values[1::2])]
    out_ref[...] = values[0].astype(BF16)


def tie_kernel(rows_ref, other_ref, out_ref):
    pass


def pick_kernel(block_rows, route_hbm, pick_ref, route_ref, sem):
    copy = pltpu.make_async_copy(route_hbm, route_ref, sem)
    copy.start()
    copy.wait()
    target = send_rows(route_ref, (pick_ref.shape[0], 1), 0, block_rows)
    index = lax.broadcasted_iota(jnp.int32, pick_ref.shape, 1)
    pick_ref[...] = jnp.where(index == target, 1.0, 0.0).astype(BF16)


def return_kernel(pick_ref, back_ref, mixed_ref, grad_ref, token_ref):
    token_ref[...] = jnp.zeros_like(token_ref)
    width = mixed_ref.shape[1]
    moved = matmul(pick_ref[...], back_ref[...]).astype(BF16)
    mixed_ref[...] = moved[:, :width]
    grad_ref[...] = moved[:, width:]


def weights_kernel(*refs):
    *half_refs, _, gain_ref, w_qkv_ref, b_qkv_ref, w_out_ref, b_out_ref, both_ref = refs
    width = w_out_ref.shape[1]
    core = lax.axis_index("seq") & 1
    for step, half_ref in enumerate(half_refs):
        place = core ^ step
        half = half_ref[...].astype(F32)
        both_ref[pl.ds(pl.multiple_of(place * width, width), width)] = half[:width]

        @pl.when(place == 0)
        def _():
            sums = half[width:]
            gain_ref[...] = sums[2, :width]
            b_qkv_ref[: 2 * width] = sums[0]
            b_qkv_ref[2 * width :] = sums[1, :width]
            b_out_ref[...] = sums[1, width:]

    w_qkv_ref[:, : 2 * width] = both_ref[:width]
    w_qkv_ref[:, 2 * width :] = both_ref[width:, :width]
    w_out_ref[...] = both_ref[width:, width:]


def exchange(message):
    return lax.all_to_all(message, "seq", split_axis=0, concat_axis=0, tiled=True)


def swap(piece, step, devs):
    return lax.ppermute(piece, "seq", [(dev, dev ^ step) for dev in range(devs)])


def local(points, route, owned, cotangent, gain, w_qkv, b_qkv, w_out, b_out):
    devs = lax.axis_size("seq")
    rows, width = points.shape
    block_rows = rows // route.shape[1]
    held = devs * block_rows
    share = width // devs
    near = 4 if devs == 16 and width % 64 == 0 else 1

    def shape(*dims, dtype=BF16):
        return jax.ShapeDtypeStruct(dims, dtype)

    sent = pl.pallas_call(
        functools.partial(scatter_kernel, block_rows),
        out_shape=shape(held, 2 * width),
        in_specs=[ANY] * 3,
        out_specs=VMEM,
        scratch_shapes=[
            pltpu.SMEM(route.shape, route.dtype),
            pltpu.VMEM(points.shape, points.dtype),
            pltpu.VMEM(cotangent.shape, cotangent.dtype),
            pltpu.SemaphoreType.DMA((3,)),
        ],
    )(route, points, cotangent)
    got = exchange(sent.reshape(devs, block_rows, 2 * width)).reshape(held, 2 * width)

    half = shape(width + 8, 2 * width)
    if near > 1:
        sums_shapes = (half, half)
    else:
        sums_shapes = (shape(width, 2 * width),) * 2 + (shape(8, 2 * width),)
    vectors = jnp.concatenate([gain, b_out, b_qkv])[None, :]
    attn, d_normed, *parts = pl.pallas_call(
        functools.partial(owner_kernel, near),
        out_shape=(shape(held, width), shape(held, width, dtype=F32)) + sums_shapes,
        in_specs=[VMEM, VMEM, ANY, ANY],
        out_specs=(VMEM,) * (2 + len(sums_shapes)),
        scratch_shapes=[
            pltpu.VMEM(w_qkv.shape, w_qkv.dtype),
            pltpu.VMEM(w_out.shape, w_out.dtype),
            pltpu.VMEM((2 * width, 2 * width), F32),
            pltpu.SemaphoreType.DMA((2,)),
        ],
        compiler_params=LARGE,
    )(got, vectors, w_qkv, w_out)
    back, token = pl.pallas_call(
        rows_kernel,
        out_shape=(shape(held, 2 * width), shape(8, 128, dtype=F32)),
        in_specs=[VMEM] * 5,
        out_specs=(VMEM,) * 2,
        compiler_params=SMALL,
        cost_estimate=pl.CostEstimate(
            flops=64 * held * width * width, bytes_accessed=16 * held * width, transcendentals=0
        ),
    )(got, attn, d_normed, vectors, w_out)

    pick = pl.pallas_call(
        functools.partial(pick_kernel, block_rows),
        out_shape=shape(rows, held),
        in_specs=[ANY],
        out_specs=VMEM,
        scratch_shapes=[pltpu.SMEM(route.shape, route.dtype), pltpu.SemaphoreType.DMA],
        compiler_params=SMALL,
    )(route)

    def give_back(back):
        return pl.pallas_call(
            return_kernel,
            out_shape=(shape(rows, width), shape(rows, width), shape(8, 128, dtype=F32)),
            in_specs=[VMEM] * 2,
            out_specs=(VMEM,) * 3,
            compiler_params=SMALL,
        )(pick, back)

    if near > 1:
        mine, theirs = parts

        def add(*pieces, after=(), flops=0):
            return pl.pallas_call(
                functools.partial(sum_kernel, len(pieces)),
                out_shape=half,
                in_specs=[VMEM] * (len(pieces) + len(after)),
                out_specs=VMEM,
                compiler_params=SMALL,
                cost_estimate=pl.CostEstimate(flops=flops, bytes_accessed=0, transcendentals=0),
            )(*pieces, *after)

        total = add(mine, swap(theirs, 1, devs), after=(token,))
        back = pl.pallas_call(
            tie_kernel,
            out_shape=back,
            in_specs=[ANY, VMEM],
            out_specs=ANY,
            input_output_aliases={0: 0},
            compiler_params=SMALL,
        )(back, total)
        back = exchange(back.reshape(devs, block_rows, 2 * width)).reshape(held, 2 * width)
        mixed, grad_points, token = give_back(back)
        total = add(total, swap(total, devs // 2, devs), flops=40_000_000_000)
        steps = [step for step in range(2, devs // 2, 2)]
        total = add(total, *(swap(total, step, devs) for step in steps))
        parts = [total, swap(total, 1, devs)]
        grad_gain, grad_wq, grad_bq, grad_wo, grad_bo = pl.pallas_call(
            weights_kernel,
            out_shape=tuple(
                shape(*dims, dtype=F32)
                for dims in ((width,), (width, 3 * width), (3 * width,), (width, width), (width,))
            ),
            in_specs=[VMEM] * 3,
            out_specs=(VMEM,) * 5,
            scratch_shapes=[pltpu.VMEM((2 * width, 2 * width), F32)],
            compiler_params=SMALL,
        )(*parts, token)
    else:
        left, right, sums = parts
        message = jnp.concatenate(
            [
                back.reshape(devs, block_rows, 2 * width),
                left.reshape(devs, share, 2 * width),
                right.reshape(devs, share, 2 * width),
                jnp.broadcast_to(sums[None], (devs, 8, 2 * width)),
            ],
            axis=1,
        )
        message = exchange(message)
        total = jnp.sum(message[:, block_rows:].astype(F32), axis=0)
        mine = total[: 2 * share].astype(BF16)
        both = exchange(jnp.broadcast_to(mine[None], (devs, 2 * share, 2 * width))).astype(F32)
        mixed, grad_points, _ = give_back(message[:, :block_rows].reshape(held, 2 * width))
        left = both[:, :share].reshape(width, 2 * width)
        right = both[:, share:].reshape(width, 2 * width)
        grad_wq = jnp.concatenate([left, right[:, :width]], axis=1)
        grad_wo = right[:, width:]
        flat = total[2 * share :].reshape(-1)
        grad_bq = flat[: 3 * width]
        grad_bo = flat[3 * width : 4 * width]
        grad_gain = flat[4 * width : 5 * width]

    return (mixed, grad_points, grad_gain, grad_wq, grad_bq, grad_wo, grad_bo)


def solution(mesh):
    placed = (
        P(("parts", "seq"), None),
        P(None, ("parts", "seq")),
        P(("parts", "seq")),
        P(("parts", "seq"), None),
        P(),
        P(),
        P(),
        P(),
        P(),
    )
    return jax.shard_map(
        local,
        mesh=mesh,
        in_specs=placed,
        out_specs=(
            P(("parts", "seq"), None),
            P(("parts", "seq"), None),
            P("parts"),
            P("parts", None),
            P("parts"),
            P("parts", None),
            P("parts"),
        ),
        check_vma=False,
    )
```

```python
import functools

import jax
import jax.numpy as jnp
from jax import lax
from jax.experimental import pallas as pl
from jax.experimental.pallas import tpu as pltpu
from jax.sharding import PartitionSpec as P

HEADS = 8
EPS = 1e-05
EMPTY = 64.0
MASKED = -1e30

F32 = jnp.float32
BF16 = jnp.bfloat16

VMEM = pl.BlockSpec(memory_space=pltpu.VMEM)
ANY = pl.BlockSpec(memory_space=pl.ANY)
SMEM = pl.BlockSpec(memory_space=pltpu.SMEM)
MIB = 1024 * 1024
LARGE = pltpu.CompilerParams(vmem_limit_bytes=32 * MIB)
SMALL = pltpu.CompilerParams(vmem_limit_bytes=8 * MIB)


def matmul(left, right, dims=((1,), (0,))):
    return lax.dot_general(left, right, (dims, ((), ())), preferred_element_type=F32)


def turned(index, devs):
    top = devs.bit_length() - 2
    place = 0
    for bit in range(top + 1):
        place = place + (((index >> bit) & 1) << (top - bit))
    return place


def send_rows(route_ref, shape, axis, block_rows, devs):
    place = lax.broadcasted_iota(jnp.int32, shape, axis)
    target = jnp.zeros(shape, jnp.int32)
    for block in range(shape[axis] // block_rows):
        first = block * block_rows
        moved = turned(route_ref[0, block], devs) * block_rows + place - first
        target = jnp.where(place >= first, moved, target)
    return target


def scatter_kernel(block_rows, route_hbm, points_hbm, cot_hbm, out_ref, route_ref, points_ref, cot_ref, sems):
    copies = [
        pltpu.make_async_copy(source, target, sems.at[at])
        for at, (source, target) in enumerate(
            ((route_hbm, route_ref), (points_hbm, points_ref), (cot_hbm, cot_ref))
        )
    ]
    for copy in copies:
        copy.start()
    for copy in copies:
        copy.wait()
    rows, width = points_ref.shape
    target = send_rows(route_ref, (1, rows), 1, block_rows, out_ref.shape[0] // block_rows)
    index = lax.broadcasted_iota(jnp.int32, (out_ref.shape[0], rows), 0)
    pick = jnp.where(index == target, 1.0, 0.0).astype(BF16)
    ones = jnp.ones((rows, width), BF16)
    moved = matmul(pick, jnp.concatenate([points_ref[...], ones], axis=1))
    empty = (1.0 - moved[:, width:]) * EMPTY
    out_ref[:, :width] = (moved[:, :width] + empty).astype(BF16)
    out_ref[:, width:] = matmul(pick, cot_ref[...]).astype(BF16)


def normalize(points):
    centered = points - jnp.mean(points, axis=-1, keepdims=True)
    rstd = lax.rsqrt(jnp.mean(centered * centered, axis=-1, keepdims=True) + EPS)
    return centered * rstd, rstd


def owner_kernel(near, got_ref, vectors_ref, w_qkv_hbm, w_out_hbm, _, attn_ref, d_normed_ref, *refs):
    *outs, w_qkv_ref, w_out_ref, both_ref, sems = refs
    copies = [
        pltpu.make_async_copy(w_qkv_hbm, w_qkv_ref, sems.at[0]),
        pltpu.make_async_copy(w_out_hbm, w_out_ref, sems.at[1]),
    ]
    for copy in copies:
        copy.start()
    rows = got_ref.shape[0]
    width = got_ref.shape[1] // 2
    head = width // HEADS
    scale = head ** (-0.5)
    gain = vectors_ref[:, :width]
    b_qkv = vectors_ref[:, 2 * width :]

    points = got_ref[:, :width].astype(F32)
    cot = got_ref[:, width:]
    xhat, _ = normalize(points)
    normed = (xhat * gain).astype(BF16)
    for copy in copies:
        copy.wait()
    w_qkv = w_qkv_ref[...]
    w_out = w_out_ref[...]
    qkv = (matmul(normed, w_qkv) + b_qkv).astype(BF16)
    query, keys, values = qkv[:, :width], qkv[:, width : 2 * width], qkv[:, 2 * width :]
    d_attn = matmul(cot, w_out, ((1,), (1,))).astype(BF16)
    d_attn_t = matmul(w_out, cot, ((1,), (1,))).astype(BF16)
    d_attn_s = (d_attn.astype(F32) * scale).astype(BF16)

    keys_t = keys.T
    values_t = values.T
    keys_s = (keys.astype(F32) * scale).astype(BF16)
    lane = lax.broadcasted_iota(jnp.int32, (rows, width), 1)
    hidden = jnp.where(points > EMPTY / 2, MASKED, 0.0).astype(BF16)
    query_x = jnp.concatenate([query, jnp.where(lane == 0, 1.0, 0.0).astype(BF16)], axis=1)

    attn_t, dq_t = [], []
    d_keys = jnp.zeros((rows, width), F32)
    d_values = jnp.zeros((rows, width), F32)
    for h in range(HEADS):
        lo, hi = h * head, (h + 1) * head
        mine = (lane >= lo) & (lane < hi)
        keys_h = jnp.concatenate([jnp.where(mine, keys_s, 0), hidden], axis=1)
        scores = matmul(keys_h, query_x, ((1,), (1,)))
        expo = jnp.exp(scores - jnp.max(scores, axis=0, keepdims=True))
        probs = expo * (1.0 / jnp.sum(expo, axis=0, keepdims=True))
        probs_b = probs.astype(BF16)
        out_t = matmul(values_t[lo:hi, :], probs_b)
        attn_t.append(out_t)
        inner = jnp.sum(out_t * d_attn_t[lo:hi, :].astype(F32), axis=0, keepdims=True) * scale
        d_probs = matmul(jnp.where(mine, values, 0), d_attn_s, ((1,), (1,)))
        d_score = (probs * (d_probs - inner)).astype(BF16)
        dq_t.append(matmul(keys_t[lo:hi, :], d_score))
        d_values = jnp.where(mine, matmul(probs_b, d_attn), d_values)
        d_keys = jnp.where(mine, matmul(d_score, query), d_keys)

    attn_t = jnp.concatenate(attn_t, axis=0)
    attn_ref[...] = attn_t.T.astype(BF16)
    grad_w_out = matmul(attn_t.astype(BF16), cot)
    grad_b_out = jnp.sum(cot.astype(F32), axis=0, keepdims=True)

    d_query = jnp.concatenate(dq_t, axis=0).T
    d_qkv = jnp.concatenate([d_query, d_keys, d_values], axis=1).astype(BF16)
    d_normed = matmul(d_qkv, w_qkv, ((1,), (1,)))
    grad_w_qkv = matmul(normed, d_qkv, ((0,), (0,)))
    grad_b_qkv = jnp.sum(d_qkv.astype(F32), axis=0, keepdims=True)
    grad_gain = jnp.sum(d_normed * xhat, axis=0, keepdims=True)
    d_normed_ref[...] = d_normed
    sums = jnp.concatenate(
        [
            grad_b_qkv[:, : 2 * width],
            jnp.concatenate([grad_b_qkv[:, 2 * width :], grad_b_out], axis=1),
            jnp.concatenate([grad_gain, jnp.zeros_like(grad_gain)], axis=1),
            jnp.zeros((5, 2 * width), F32),
        ],
        axis=0,
    )
    left = grad_w_qkv[:, : 2 * width]
    right = jnp.concatenate([grad_w_qkv[:, 2 * width :], grad_w_out], axis=1)
    if near == 1:
        left_ref, right_ref, sums_ref = outs
        left_ref[...] = left.astype(BF16)
        right_ref[...] = right.astype(BF16)
        sums_ref[...] = sums.astype(BF16)
        return
    mine_ref, theirs_ref = outs
    both_ref[:width] = left
    both_ref[width:] = right
    core = lax.axis_index("seq") & 1
    for half, half_ref in ((core, mine_ref), (core ^ 1, theirs_ref)):
        span = pl.ds(pl.multiple_of(half * width, width), width)
        half_ref[:width] = both_ref[span].astype(half_ref.dtype)
        half_ref[width:] = sums.astype(half_ref.dtype)


def rows_kernel(got_ref, attn_ref, d_normed_ref, vectors_ref, w_out_ref, back_ref, token_ref):
    token_ref[...] = jnp.zeros_like(token_ref)
    width = attn_ref.shape[1]
    gain = vectors_ref[:, :width]
    b_out = vectors_ref[:, width : 2 * width]
    points = got_ref[:, :width].astype(F32)
    cot = got_ref[:, width:].astype(F32)
    xhat, rstd = normalize(points)
    mixed = points + (matmul(attn_ref[...], w_out_ref[...]) + b_out)
    d_xhat = d_normed_ref[...] * gain
    inner = (
        d_xhat
        - jnp.mean(d_xhat, axis=-1, keepdims=True)
        - xhat * jnp.mean(d_xhat * xhat, axis=-1, keepdims=True)
    )
    back_ref[:, :width] = mixed.astype(BF16)
    back_ref[:, width:] = (cot + rstd * inner).astype(BF16)


def sum_kernel(count, *refs):
    piece_refs, out_ref = refs[:count], refs[-1]
    values = [piece_ref[...].astype(F32) for piece_ref in piece_refs]
    while len(values) > 1:
        values = [left + right for left, right in zip(values[::2], values[1::2])]
    out_ref[...] = values[0].astype(BF16)


def tie_kernel(rows_ref, other_ref, out_ref):
    pass


def pick_kernel(block_rows, route_hbm, pick_ref, token_ref, route_ref, sem):
    token_ref[...] = jnp.zeros_like(token_ref)
    copy = pltpu.make_async_copy(route_hbm, route_ref, sem)
    copy.start()
    copy.wait()
    rows, held = pick_ref.shape
    target = send_rows(route_ref, (rows, 1), 0, block_rows, held // block_rows)
    index = lax.broadcasted_iota(jnp.int32, pick_ref.shape, 1)
    pick_ref[...] = jnp.where(index == target, 1.0, 0.0).astype(BF16)


def return_kernel(pick_ref, back_ref, mixed_ref, grad_ref, token_ref):
    token_ref[...] = jnp.zeros_like(token_ref)
    width = mixed_ref.shape[1]
    moved = matmul(pick_ref[...], back_ref[...]).astype(BF16)
    mixed_ref[...] = moved[:, :width]
    grad_ref[...] = moved[:, width:]


def weights_kernel(*refs):
    *half_refs, _, gain_ref, w_qkv_ref, b_qkv_ref, w_out_ref, b_out_ref, both_ref = refs
    width = w_out_ref.shape[1]
    core = lax.axis_index("seq") & 1
    for step, half_ref in enumerate(half_refs):
        place = core ^ step
        half = half_ref[...].astype(F32)
        both_ref[pl.ds(pl.multiple_of(place * width, width), width)] = half[:width]

        @pl.when(place == 0)
        def _():
            sums = half[width:]
            gain_ref[...] = sums[2, :width]
            b_qkv_ref[: 2 * width] = sums[0]
            b_qkv_ref[2 * width :] = sums[1, :width]
            b_out_ref[...] = sums[1, width:]

    w_qkv_ref[:, : 2 * width] = both_ref[:width]
    w_qkv_ref[:, 2 * width :] = both_ref[width:, :width]
    w_out_ref[...] = both_ref[width:, width:]


def exchange(message):
    devs = message.shape[0]
    order = [turned(place, devs) for place in range(devs)]
    return lax.all_to_all(
        message, "seq", split_axis=0, concat_axis=0, axis_index_groups=[order], tiled=True
    )


def swap(piece, step, devs):
    return lax.ppermute(piece, "seq", [(dev, dev ^ step) for dev in range(devs)])


def local(points, route, owned, cotangent, gain, w_qkv, b_qkv, w_out, b_out):
    devs = lax.axis_size("seq")
    rows, width = points.shape
    block_rows = rows // route.shape[1]
    held = devs * block_rows
    share = width // devs
    near = 4 if devs == 16 and width % 64 == 0 else 1

    def shape(*dims, dtype=BF16):
        return jax.ShapeDtypeStruct(dims, dtype)

    sent = pl.pallas_call(
        functools.partial(scatter_kernel, block_rows),
        out_shape=shape(held, 2 * width),
        in_specs=[ANY] * 3,
        out_specs=VMEM,
        scratch_shapes=[
            pltpu.SMEM(route.shape, route.dtype),
            pltpu.VMEM(points.shape, points.dtype),
            pltpu.VMEM(cotangent.shape, cotangent.dtype),
            pltpu.SemaphoreType.DMA((3,)),
        ],
    )(route, points, cotangent)
    got = exchange(sent.reshape(devs, block_rows, 2 * width)).reshape(held, 2 * width)

    pick, early = pl.pallas_call(
        functools.partial(pick_kernel, block_rows),
        out_shape=(shape(rows, held), shape(8, 128, dtype=F32)),
        in_specs=[ANY],
        out_specs=(VMEM,) * 2,
        scratch_shapes=[pltpu.SMEM(route.shape, route.dtype), pltpu.SemaphoreType.DMA],
        compiler_params=SMALL,
    )(route)

    half = shape(width + 8, 2 * width)
    if near > 1:
        sums_shapes = (half, half)
    else:
        sums_shapes = (shape(width, 2 * width),) * 2 + (shape(8, 2 * width),)
    vectors = jnp.concatenate([gain, b_out, b_qkv])[None, :]
    attn, d_normed, *parts = pl.pallas_call(
        functools.partial(owner_kernel, near),
        out_shape=(shape(held, width), shape(held, width, dtype=F32)) + sums_shapes,
        in_specs=[VMEM, VMEM, ANY, ANY, VMEM],
        out_specs=(VMEM,) * (2 + len(sums_shapes)),
        scratch_shapes=[
            pltpu.VMEM(w_qkv.shape, w_qkv.dtype),
            pltpu.VMEM(w_out.shape, w_out.dtype),
            pltpu.VMEM((2 * width, 2 * width), F32),
            pltpu.SemaphoreType.DMA((2,)),
        ],
        compiler_params=LARGE,
    )(got, vectors, w_qkv, w_out, early)
    back, token = pl.pallas_call(
        rows_kernel,
        out_shape=(shape(held, 2 * width), shape(8, 128, dtype=F32)),
        in_specs=[VMEM] * 5,
        out_specs=(VMEM,) * 2,
        compiler_params=SMALL,
        cost_estimate=pl.CostEstimate(
            flops=64 * held * width * width, bytes_accessed=16 * held * width, transcendentals=0
        ),
    )(got, attn, d_normed, vectors, w_out)

    def give_back(back):
        return pl.pallas_call(
            return_kernel,
            out_shape=(shape(rows, width), shape(rows, width), shape(8, 128, dtype=F32)),
            in_specs=[VMEM] * 2,
            out_specs=(VMEM,) * 3,
            compiler_params=SMALL,
        )(pick, back)

    if near > 1:
        mine, theirs = parts

        def add(*pieces, after=(), flops=0):
            return pl.pallas_call(
                functools.partial(sum_kernel, len(pieces)),
                out_shape=half,
                in_specs=[VMEM] * (len(pieces) + len(after)),
                out_specs=VMEM,
                compiler_params=SMALL,
                cost_estimate=pl.CostEstimate(flops=flops, bytes_accessed=0, transcendentals=0),
            )(*pieces, *after)

        total = add(mine, swap(theirs, 1, devs), after=(token,))
        back = pl.pallas_call(
            tie_kernel,
            out_shape=back,
            in_specs=[ANY, VMEM],
            out_specs=ANY,
            input_output_aliases={0: 0},
            compiler_params=SMALL,
        )(back, total)
        back = exchange(back.reshape(devs, block_rows, 2 * width)).reshape(held, 2 * width)
        mixed, grad_points, token = give_back(back)
        total = add(total, swap(total, devs // 2, devs), flops=40_000_000_000)
        steps = [step for step in range(2, devs // 2, 2)]
        total = add(total, *(swap(total, step, devs) for step in steps))
        parts = [total, swap(total, 1, devs)]
        grad_gain, grad_wq, grad_bq, grad_wo, grad_bo = pl.pallas_call(
            weights_kernel,
            out_shape=tuple(
                shape(*dims, dtype=F32)
                for dims in ((width,), (width, 3 * width), (3 * width,), (width, width), (width,))
            ),
            in_specs=[VMEM] * 3,
            out_specs=(VMEM,) * 5,
            scratch_shapes=[pltpu.VMEM((2 * width, 2 * width), F32)],
            compiler_params=SMALL,
        )(*parts, token)
    else:
        left, right, sums = parts
        message = jnp.concatenate(
            [
                back.reshape(devs, block_rows, 2 * width),
                left.reshape(devs, share, 2 * width),
                right.reshape(devs, share, 2 * width),
                jnp.broadcast_to(sums[None], (devs, 8, 2 * width)),
            ],
            axis=1,
        )
        message = exchange(message)
        total = jnp.sum(message[:, block_rows:].astype(F32), axis=0)
        mine = total[: 2 * share].astype(BF16)
        both = exchange(jnp.broadcast_to(mine[None], (devs, 2 * share, 2 * width))).astype(F32)
        mixed, grad_points, _ = give_back(message[:, :block_rows].reshape(held, 2 * width))
        left = both[:, :share].reshape(width, 2 * width)
        right = both[:, share:].reshape(width, 2 * width)
        grad_wq = jnp.concatenate([left, right[:, :width]], axis=1)
        grad_wo = right[:, width:]
        flat = total[2 * share :].reshape(-1)
        grad_bq = flat[: 3 * width]
        grad_bo = flat[3 * width : 4 * width]
        grad_gain = flat[4 * width : 5 * width]

    return (mixed, grad_points, grad_gain, grad_wq, grad_bq, grad_wo, grad_bo)


def solution(mesh):
    placed = (
        P(("parts", "seq"), None),
        P(None, ("parts", "seq")),
        P(("parts", "seq")),
        P(("parts", "seq"), None),
        P(),
        P(),
        P(),
        P(),
        P(),
    )
    return jax.shard_map(
        local,
        mesh=mesh,
        in_specs=placed,
        out_specs=(
            P(("parts", "seq"), None),
            P(("parts", "seq"), None),
            P("parts"),
            P("parts", None),
            P("parts"),
            P("parts", None),
            P("parts"),
        ),
        check_vma=False,
    )
```

```python
import functools

import jax
import jax.numpy as jnp
from jax import lax
from jax.experimental import pallas as pl
from jax.experimental.pallas import tpu as pltpu
from jax.sharding import PartitionSpec as P

HEADS = 8
EPS = 1e-05
EMPTY = 64.0
MASKED = -1e30

F32 = jnp.float32
BF16 = jnp.bfloat16

VMEM = pl.BlockSpec(memory_space=pltpu.VMEM)
ANY = pl.BlockSpec(memory_space=pl.ANY)
SMEM = pl.BlockSpec(memory_space=pltpu.SMEM)
MIB = 1024 * 1024
LARGE = pltpu.CompilerParams(vmem_limit_bytes=32 * MIB)
SMALL = pltpu.CompilerParams(vmem_limit_bytes=8 * MIB)


def matmul(left, right, dims=((1,), (0,))):
    return lax.dot_general(left, right, (dims, ((), ())), preferred_element_type=F32)


def turned(index, devs):
    top = devs.bit_length() - 2
    place = 0
    for bit in range(top + 1):
        place = place + (((index >> bit) & 1) << (top - bit))
    return place


def send_rows(route_ref, shape, axis, block_rows, devs):
    place = lax.broadcasted_iota(jnp.int32, shape, axis)
    target = jnp.zeros(shape, jnp.int32)
    for block in range(shape[axis] // block_rows):
        first = block * block_rows
        moved = turned(route_ref[0, block], devs) * block_rows + place - first
        target = jnp.where(place >= first, moved, target)
    return target


def scatter_kernel(block_rows, route_hbm, points_hbm, cot_hbm, out_ref, route_ref, points_ref, cot_ref, sems):
    copies = [
        pltpu.make_async_copy(source, target, sems.at[at])
        for at, (source, target) in enumerate(
            ((route_hbm, route_ref), (points_hbm, points_ref), (cot_hbm, cot_ref))
        )
    ]
    for copy in copies:
        copy.start()
    for copy in copies:
        copy.wait()
    rows, width = points_ref.shape
    target = send_rows(route_ref, (1, rows), 1, block_rows, out_ref.shape[0] // block_rows)
    index = lax.broadcasted_iota(jnp.int32, (out_ref.shape[0], rows), 0)
    pick = jnp.where(index == target, 1.0, 0.0).astype(BF16)
    ones = jnp.ones((rows, width), BF16)
    moved = matmul(pick, jnp.concatenate([points_ref[...], ones], axis=1))
    empty = (1.0 - moved[:, width:]) * EMPTY
    out_ref[:, :width] = (moved[:, :width] + empty).astype(BF16)
    out_ref[:, width:] = matmul(pick, cot_ref[...]).astype(BF16)


def normalize(points):
    centered = points - jnp.mean(points, axis=-1, keepdims=True)
    rstd = lax.rsqrt(jnp.mean(centered * centered, axis=-1, keepdims=True) + EPS)
    return centered * rstd, rstd


def owner_kernel(near, got_ref, vectors_ref, w_qkv_hbm, w_out_hbm, _, attn_ref, d_normed_ref, *refs):
    *outs, w_qkv_ref, w_out_ref, both_ref, d_keys_ref, d_values_ref, sems = refs
    copies = [
        pltpu.make_async_copy(w_qkv_hbm, w_qkv_ref, sems.at[0]),
        pltpu.make_async_copy(w_out_hbm, w_out_ref, sems.at[1]),
    ]
    for copy in copies:
        copy.start()
    rows = got_ref.shape[0]
    width = got_ref.shape[1] // 2
    head = width // HEADS
    scale = head ** (-0.5)
    gain = vectors_ref[:, :width]
    b_qkv = vectors_ref[:, 2 * width :]

    points = got_ref[:, :width].astype(F32)
    cot = got_ref[:, width:]
    xhat, _ = normalize(points)
    normed = (xhat * gain).astype(BF16)
    for copy in copies:
        copy.wait()
    w_qkv = w_qkv_ref[...]
    w_out = w_out_ref[...]
    qkv = (matmul(normed, w_qkv) + b_qkv).astype(BF16)
    query, keys, values = qkv[:, :width], qkv[:, width : 2 * width], qkv[:, 2 * width :]
    d_attn = matmul(cot, w_out, ((1,), (1,))).astype(BF16)
    d_attn_t = matmul(w_out, cot, ((1,), (1,))).astype(BF16)
    d_attn_s = (d_attn.astype(F32) * scale).astype(BF16)

    keys_t = keys.T
    values_t = values.T
    keys_s = (keys.astype(F32) * scale).astype(BF16)
    lane = lax.broadcasted_iota(jnp.int32, (rows, width), 1)
    hidden = jnp.where(points[:, :1] > EMPTY / 2, MASKED, 0.0)

    attn_t, dq_t = [], []
    for h in range(HEADS):
        lo, hi = h * head, (h + 1) * head
        mine = (lane >= lo) & (lane < hi)
        scores = matmul(jnp.where(mine, keys_s, 0), query, ((1,), (1,))) + hidden
        expo = jnp.exp(scores - jnp.max(scores, axis=0, keepdims=True))
        probs = expo * (1.0 / jnp.sum(expo, axis=0, keepdims=True))
        probs_b = probs.astype(BF16)
        out_t = matmul(values_t[lo:hi, :], probs_b)
        attn_t.append(out_t)
        inner = jnp.sum(out_t * d_attn_t[lo:hi, :].astype(F32), axis=0, keepdims=True) * scale
        d_probs = matmul(jnp.where(mine, values, 0), d_attn_s, ((1,), (1,)))
        d_score = (probs * (d_probs - inner)).astype(BF16)
        dq_t.append(matmul(keys_t[lo:hi, :], d_score))
        d_values_ref[:, lo:hi] = matmul(probs_b, d_attn)[:, lo:hi]
        d_keys_ref[:, lo:hi] = matmul(d_score, query)[:, lo:hi]

    attn_t = jnp.concatenate(attn_t, axis=0)
    attn_ref[...] = attn_t.T.astype(BF16)
    grad_w_out = matmul(attn_t.astype(BF16), cot)
    grad_b_out = jnp.sum(cot.astype(F32), axis=0, keepdims=True)

    d_query = jnp.concatenate(dq_t, axis=0).T
    d_qkv = jnp.concatenate([d_query, d_keys_ref[...], d_values_ref[...]], axis=1).astype(BF16)
    d_normed = matmul(d_qkv, w_qkv, ((1,), (1,)))
    grad_w_qkv = matmul(normed, d_qkv, ((0,), (0,)))
    grad_b_qkv = jnp.sum(d_qkv.astype(F32), axis=0, keepdims=True)
    grad_gain = jnp.sum(d_normed * xhat, axis=0, keepdims=True)
    d_normed_ref[...] = d_normed
    sums = jnp.concatenate(
        [
            grad_b_qkv[:, : 2 * width],
            jnp.concatenate([grad_b_qkv[:, 2 * width :], grad_b_out], axis=1),
            jnp.concatenate([grad_gain, jnp.zeros_like(grad_gain)], axis=1),
            jnp.zeros((5, 2 * width), F32),
        ],
        axis=0,
    )
    left = grad_w_qkv[:, : 2 * width]
    right = jnp.concatenate([grad_w_qkv[:, 2 * width :], grad_w_out], axis=1)
    if near == 1:
        left_ref, right_ref, sums_ref = outs
        left_ref[...] = left.astype(BF16)
        right_ref[...] = right.astype(BF16)
        sums_ref[...] = sums.astype(BF16)
        return
    mine_ref, theirs_ref = outs
    both_ref[:width] = left
    both_ref[width:] = right
    core = lax.axis_index("seq") & 1
    for half, half_ref in ((core, mine_ref), (core ^ 1, theirs_ref)):
        span = pl.ds(pl.multiple_of(half * width, width), width)
        half_ref[:width] = both_ref[span].astype(half_ref.dtype)
        half_ref[width:] = sums.astype(half_ref.dtype)


def rows_kernel(got_ref, attn_ref, d_normed_ref, vectors_ref, w_out_ref, back_ref, token_ref):
    token_ref[...] = jnp.zeros_like(token_ref)
    width = attn_ref.shape[1]
    gain = vectors_ref[:, :width]
    b_out = vectors_ref[:, width : 2 * width]
    points = got_ref[:, :width].astype(F32)
    cot = got_ref[:, width:].astype(F32)
    xhat, rstd = normalize(points)
    mixed = points + (matmul(attn_ref[...], w_out_ref[...]) + b_out)
    d_xhat = d_normed_ref[...] * gain
    inner = (
        d_xhat
        - jnp.mean(d_xhat, axis=-1, keepdims=True)
        - xhat * jnp.mean(d_xhat * xhat, axis=-1, keepdims=True)
    )
    back_ref[:, :width] = mixed.astype(BF16)
    back_ref[:, width:] = (cot + rstd * inner).astype(BF16)


def sum_kernel(count, *refs):
    piece_refs, out_ref = refs[:count], refs[-1]
    values = [piece_ref[...].astype(F32) for piece_ref in piece_refs]
    while len(values) > 1:
        values = [left + right for left, right in zip(values[::2], values[1::2])]
    out_ref[...] = values[0].astype(BF16)


def tie_kernel(rows_ref, other_ref, out_ref):
    pass


def pick_kernel(block_rows, route_hbm, pick_ref, token_ref, route_ref, sem):
    token_ref[...] = jnp.zeros_like(token_ref)
    copy = pltpu.make_async_copy(route_hbm, route_ref, sem)
    copy.start()
    copy.wait()
    rows, held = pick_ref.shape
    target = send_rows(route_ref, (rows, 1), 0, block_rows, held // block_rows)
    index = lax.broadcasted_iota(jnp.int32, pick_ref.shape, 1)
    pick_ref[...] = jnp.where(index == target, 1.0, 0.0).astype(BF16)


def return_kernel(pick_ref, back_ref, mixed_ref, grad_ref, token_ref):
    token_ref[...] = jnp.zeros_like(token_ref)
    width = mixed_ref.shape[1]
    moved = matmul(pick_ref[...], back_ref[...]).astype(BF16)
    mixed_ref[...] = moved[:, :width]
    grad_ref[...] = moved[:, width:]


def weights_kernel(*refs):
    *half_refs, _, gain_ref, w_qkv_ref, b_qkv_ref, w_out_ref, b_out_ref, both_ref = refs
    width = w_out_ref.shape[1]
    core = lax.axis_index("seq") & 1
    for step, half_ref in enumerate(half_refs):
        place = core ^ step
        half = half_ref[...].astype(F32)
        both_ref[pl.ds(pl.multiple_of(place * width, width), width)] = half[:width]

        @pl.when(place == 0)
        def _():
            sums = half[width:]
            gain_ref[...] = sums[2, :width]
            b_qkv_ref[: 2 * width] = sums[0]
            b_qkv_ref[2 * width :] = sums[1, :width]
            b_out_ref[...] = sums[1, width:]

    w_qkv_ref[:, : 2 * width] = both_ref[:width]
    w_qkv_ref[:, 2 * width :] = both_ref[width:, :width]
    w_out_ref[...] = both_ref[width:, width:]


def exchange(message):
    devs = message.shape[0]
    order = [turned(place, devs) for place in range(devs)]
    return lax.all_to_all(
        message, "seq", split_axis=0, concat_axis=0, axis_index_groups=[order], tiled=True
    )


def swap(piece, step, devs):
    return lax.ppermute(piece, "seq", [(dev, dev ^ step) for dev in range(devs)])


def local(points, route, owned, cotangent, gain, w_qkv, b_qkv, w_out, b_out):
    devs = lax.axis_size("seq")
    rows, width = points.shape
    block_rows = rows // route.shape[1]
    held = devs * block_rows
    share = width // devs
    near = 4 if devs == 16 and width % 64 == 0 else 1

    def shape(*dims, dtype=BF16):
        return jax.ShapeDtypeStruct(dims, dtype)

    sent = pl.pallas_call(
        functools.partial(scatter_kernel, block_rows),
        out_shape=shape(held, 2 * width),
        in_specs=[ANY] * 3,
        out_specs=VMEM,
        scratch_shapes=[
            pltpu.SMEM(route.shape, route.dtype),
            pltpu.VMEM(points.shape, points.dtype),
            pltpu.VMEM(cotangent.shape, cotangent.dtype),
            pltpu.SemaphoreType.DMA((3,)),
        ],
    )(route, points, cotangent)
    got = exchange(sent.reshape(devs, block_rows, 2 * width)).reshape(held, 2 * width)

    pick, early = pl.pallas_call(
        functools.partial(pick_kernel, block_rows),
        out_shape=(shape(rows, held), shape(8, 128, dtype=F32)),
        in_specs=[ANY],
        out_specs=(VMEM,) * 2,
        scratch_shapes=[pltpu.SMEM(route.shape, route.dtype), pltpu.SemaphoreType.DMA],
        compiler_params=SMALL,
    )(route)

    half = shape(width + 8, 2 * width)
    if near > 1:
        sums_shapes = (half, half)
    else:
        sums_shapes = (shape(width, 2 * width),) * 2 + (shape(8, 2 * width),)
    vectors = jnp.concatenate([gain, b_out, b_qkv])[None, :]
    attn, d_normed, *parts = pl.pallas_call(
        functools.partial(owner_kernel, near),
        out_shape=(shape(held, width), shape(held, width, dtype=F32)) + sums_shapes,
        in_specs=[VMEM, VMEM, ANY, ANY, VMEM],
        out_specs=(VMEM,) * (2 + len(sums_shapes)),
        scratch_shapes=[
            pltpu.VMEM(w_qkv.shape, w_qkv.dtype),
            pltpu.VMEM(w_out.shape, w_out.dtype),
            pltpu.VMEM((2 * width, 2 * width), F32),
            pltpu.VMEM((held, width), F32),
            pltpu.VMEM((held, width), F32),
            pltpu.SemaphoreType.DMA((2,)),
        ],
        compiler_params=LARGE,
    )(got, vectors, w_qkv, w_out, early)
    back, token = pl.pallas_call(
        rows_kernel,
        out_shape=(shape(held, 2 * width), shape(8, 128, dtype=F32)),
        in_specs=[VMEM] * 5,
        out_specs=(VMEM,) * 2,
        compiler_params=SMALL,
        cost_estimate=pl.CostEstimate(
            flops=64 * held * width * width, bytes_accessed=16 * held * width, transcendentals=0
        ),
    )(got, attn, d_normed, vectors, w_out)

    def give_back(back):
        return pl.pallas_call(
            return_kernel,
            out_shape=(shape(rows, width), shape(rows, width), shape(8, 128, dtype=F32)),
            in_specs=[VMEM] * 2,
            out_specs=(VMEM,) * 3,
            compiler_params=SMALL,
        )(pick, back)

    if near > 1:
        mine, theirs = parts

        def add(*pieces, after=(), flops=0):
            return pl.pallas_call(
                functools.partial(sum_kernel, len(pieces)),
                out_shape=half,
                in_specs=[VMEM] * (len(pieces) + len(after)),
                out_specs=VMEM,
                compiler_params=SMALL,
                cost_estimate=pl.CostEstimate(flops=flops, bytes_accessed=0, transcendentals=0),
            )(*pieces, *after)

        total = add(mine, swap(theirs, 1, devs), after=(token,))
        back = pl.pallas_call(
            tie_kernel,
            out_shape=back,
            in_specs=[ANY, VMEM],
            out_specs=ANY,
            input_output_aliases={0: 0},
            compiler_params=SMALL,
        )(back, total)
        back = exchange(back.reshape(devs, block_rows, 2 * width)).reshape(held, 2 * width)
        mixed, grad_points, token = give_back(back)
        total = add(total, swap(total, devs // 2, devs), flops=40_000_000_000)
        steps = [step for step in range(2, devs // 2, 2)]
        total = add(total, *(swap(total, step, devs) for step in steps))
        parts = [total, swap(total, 1, devs)]
        grad_gain, grad_wq, grad_bq, grad_wo, grad_bo = pl.pallas_call(
            weights_kernel,
            out_shape=tuple(
                shape(*dims, dtype=F32)
                for dims in ((width,), (width, 3 * width), (3 * width,), (width, width), (width,))
            ),
            in_specs=[VMEM] * 3,
            out_specs=(VMEM,) * 5,
            scratch_shapes=[pltpu.VMEM((2 * width, 2 * width), F32)],
            compiler_params=SMALL,
        )(*parts, token)
    else:
        left, right, sums = parts
        message = jnp.concatenate(
            [
                back.reshape(devs, block_rows, 2 * width),
                left.reshape(devs, share, 2 * width),
                right.reshape(devs, share, 2 * width),
                jnp.broadcast_to(sums[None], (devs, 8, 2 * width)),
            ],
            axis=1,
        )
        message = exchange(message)
        total = jnp.sum(message[:, block_rows:].astype(F32), axis=0)
        mine = total[: 2 * share].astype(BF16)
        both = exchange(jnp.broadcast_to(mine[None], (devs, 2 * share, 2 * width))).astype(F32)
        mixed, grad_points, _ = give_back(message[:, :block_rows].reshape(held, 2 * width))
        left = both[:, :share].reshape(width, 2 * width)
        right = both[:, share:].reshape(width, 2 * width)
        grad_wq = jnp.concatenate([left, right[:, :width]], axis=1)
        grad_wo = right[:, width:]
        flat = total[2 * share :].reshape(-1)
        grad_bq = flat[: 3 * width]
        grad_bo = flat[3 * width : 4 * width]
        grad_gain = flat[4 * width : 5 * width]

    return (mixed, grad_points, grad_gain, grad_wq, grad_bq, grad_wo, grad_bo)


def solution(mesh):
    placed = (
        P(("parts", "seq"), None),
        P(None, ("parts", "seq")),
        P(("parts", "seq")),
        P(("parts", "seq"), None),
        P(),
        P(),
        P(),
        P(),
        P(),
    )
    return jax.shard_map(
        local,
        mesh=mesh,
        in_specs=placed,
        out_specs=(
            P(("parts", "seq"), None),
            P(("parts", "seq"), None),
            P("parts"),
            P("parts", None),
            P("parts"),
            P("parts", None),
            P("parts"),
        ),
        check_vma=False,
    )
```

```python
import functools

import jax
import jax.numpy as jnp
from jax import lax
from jax.experimental import pallas as pl
from jax.experimental.pallas import tpu as pltpu
from jax.sharding import PartitionSpec as P

HEADS = 8
EPS = 1e-05
EMPTY = 64.0
MASKED = -1e30

F32 = jnp.float32
BF16 = jnp.bfloat16

VMEM = pl.BlockSpec(memory_space=pltpu.VMEM)
ANY = pl.BlockSpec(memory_space=pl.ANY)
SMEM = pl.BlockSpec(memory_space=pltpu.SMEM)
MIB = 1024 * 1024
LARGE = pltpu.CompilerParams(vmem_limit_bytes=32 * MIB)
SMALL = pltpu.CompilerParams(vmem_limit_bytes=8 * MIB)


def matmul(left, right, dims=((1,), (0,))):
    return lax.dot_general(left, right, (dims, ((), ())), preferred_element_type=F32)


def turned(index, devs):
    top = devs.bit_length() - 2
    place = 0
    for bit in range(top + 1):
        place = place + (((index >> bit) & 1) << (top - bit))
    return place


def send_rows(route_ref, shape, axis, block_rows, place_of):
    place = lax.broadcasted_iota(jnp.int32, shape, axis)
    target = jnp.zeros(shape, jnp.int32)
    for block in range(shape[axis] // block_rows):
        first = block * block_rows
        moved = place_of(route_ref[0, block]) * block_rows + place - first
        target = jnp.where(place >= first, moved, target)
    return target


def scatter_kernel(block_rows, route_hbm, points_hbm, cot_hbm, *refs):
    *outs, route_ref, points_ref, cot_ref, sems = refs
    copies = [
        pltpu.make_async_copy(source, target, sems.at[at])
        for at, (source, target) in enumerate(
            ((route_hbm, route_ref), (points_hbm, points_ref), (cot_hbm, cot_ref))
        )
    ]
    for copy in copies:
        copy.start()
    for copy in copies:
        copy.wait()
    rows, width = points_ref.shape
    part = outs[0].shape[0]
    held = part * len(outs)
    if len(outs) > 1:
        me = lax.axis_index("seq")
        target = send_rows(route_ref, (1, rows), 1, block_rows, lambda owner: owner ^ me)
    else:
        devs = held // block_rows
        target = send_rows(route_ref, (1, rows), 1, block_rows, lambda owner: turned(owner, devs))
    index = lax.broadcasted_iota(jnp.int32, (held, rows), 0)
    pick = jnp.where(index == target, 1.0, 0.0).astype(BF16)
    ones = jnp.ones((rows, width), BF16)
    moved = matmul(pick, jnp.concatenate([points_ref[...], ones], axis=1))
    empty = (1.0 - moved[:, width:]) * EMPTY
    points = (moved[:, :width] + empty).astype(BF16)
    cot = matmul(pick, cot_ref[...]).astype(BF16)
    for at, out_ref in enumerate(outs):
        span = slice(at * part, (at + 1) * part)
        out_ref[:, :width] = points[span]
        out_ref[:, width:] = cot[span]


def regroup_kernel(block_rows, *refs):
    count = len(refs) // 2
    for high, got_ref in enumerate(refs[:count]):
        for low, out_ref in enumerate(refs[count:]):
            block = got_ref[low * block_rows : (low + 1) * block_rows]
            out_ref[high * block_rows : (high + 1) * block_rows] = block


def normalize(points):
    centered = points - jnp.mean(points, axis=-1, keepdims=True)
    rstd = lax.rsqrt(jnp.mean(centered * centered, axis=-1, keepdims=True) + EPS)
    return centered * rstd, rstd


def owner_kernel(near, *refs):
    got_refs, refs = refs[:near], refs[near:]
    vectors_ref, w_qkv_hbm, w_out_hbm, _, attn_ref, d_normed_ref, *refs = refs
    *outs, w_qkv_ref, w_out_ref, both_ref, d_keys_ref, d_values_ref, sems = refs
    copies = [
        pltpu.make_async_copy(w_qkv_hbm, w_qkv_ref, sems.at[0]),
        pltpu.make_async_copy(w_out_hbm, w_out_ref, sems.at[1]),
    ]
    for copy in copies:
        copy.start()
    got = jnp.concatenate([got_ref[...] for got_ref in got_refs], axis=0)
    rows, width = got.shape[0], got.shape[1] // 2
    head = width // HEADS
    scale = head ** (-0.5)
    gain = vectors_ref[:, :width]
    b_qkv = vectors_ref[:, 2 * width :]

    points = got[:, :width].astype(F32)
    cot = got[:, width:]
    xhat, _ = normalize(points)
    normed = (xhat * gain).astype(BF16)
    for copy in copies:
        copy.wait()
    w_qkv = w_qkv_ref[...]
    w_out = w_out_ref[...]
    qkv = (matmul(normed, w_qkv) + b_qkv).astype(BF16)
    query, keys, values = qkv[:, :width], qkv[:, width : 2 * width], qkv[:, 2 * width :]
    d_attn = matmul(cot, w_out, ((1,), (1,))).astype(BF16)
    d_attn_t = matmul(w_out, cot, ((1,), (1,))).astype(BF16)
    d_attn_s = (d_attn.astype(F32) * scale).astype(BF16)

    keys_t = keys.T
    values_t = values.T
    keys_s = (keys.astype(F32) * scale).astype(BF16)
    lane = lax.broadcasted_iota(jnp.int32, (rows, width), 1)
    hidden = jnp.where(points[:, :1] > EMPTY / 2, MASKED, 0.0)

    attn_t, dq_t = [], []
    for h in range(HEADS):
        lo, hi = h * head, (h + 1) * head
        mine = (lane >= lo) & (lane < hi)
        scores = matmul(jnp.where(mine, keys_s, 0), query, ((1,), (1,))) + hidden
        expo = jnp.exp(scores - jnp.max(scores, axis=0, keepdims=True))
        probs = expo * (1.0 / jnp.sum(expo, axis=0, keepdims=True))
        probs_b = probs.astype(BF16)
        out_t = matmul(values_t[lo:hi, :], probs_b)
        attn_t.append(out_t)
        inner = jnp.sum(out_t * d_attn_t[lo:hi, :].astype(F32), axis=0, keepdims=True) * scale
        d_probs = matmul(jnp.where(mine, values, 0), d_attn_s, ((1,), (1,)))
        d_score = (probs * (d_probs - inner)).astype(BF16)
        dq_t.append(matmul(keys_t[lo:hi, :], d_score))
        d_values_ref[:, lo:hi] = matmul(probs_b, d_attn)[:, lo:hi]
        d_keys_ref[:, lo:hi] = matmul(d_score, query)[:, lo:hi]

    attn_t = jnp.concatenate(attn_t, axis=0)
    attn_ref[...] = attn_t.T.astype(BF16)
    grad_w_out = matmul(attn_t.astype(BF16), cot)
    grad_b_out = jnp.sum(cot.astype(F32), axis=0, keepdims=True)

    d_query = jnp.concatenate(dq_t, axis=0).T
    d_qkv = jnp.concatenate([d_query, d_keys_ref[...], d_values_ref[...]], axis=1).astype(BF16)
    d_normed = matmul(d_qkv, w_qkv, ((1,), (1,)))
    grad_w_qkv = matmul(normed, d_qkv, ((0,), (0,)))
    grad_b_qkv = jnp.sum(d_qkv.astype(F32), axis=0, keepdims=True)
    grad_gain = jnp.sum(d_normed * xhat, axis=0, keepdims=True)
    d_normed_ref[...] = d_normed
    sums = jnp.concatenate(
        [
            grad_b_qkv[:, : 2 * width],
            jnp.concatenate([grad_b_qkv[:, 2 * width :], grad_b_out], axis=1),
            jnp.concatenate([grad_gain, jnp.zeros_like(grad_gain)], axis=1),
            jnp.zeros((5, 2 * width), F32),
        ],
        axis=0,
    )
    left = grad_w_qkv[:, : 2 * width]
    right = jnp.concatenate([grad_w_qkv[:, 2 * width :], grad_w_out], axis=1)
    if near == 1:
        left_ref, right_ref, sums_ref = outs
        left_ref[...] = left.astype(BF16)
        right_ref[...] = right.astype(BF16)
        sums_ref[...] = sums.astype(BF16)
        return
    mine_ref, theirs_ref = outs
    both_ref[:width] = left
    both_ref[width:] = right
    core = lax.axis_index("seq") & 1
    for half, half_ref in ((core, mine_ref), (core ^ 1, theirs_ref)):
        span = pl.ds(pl.multiple_of(half * width, width), width)
        half_ref[:width] = both_ref[span].astype(half_ref.dtype)
        half_ref[width:] = sums.astype(half_ref.dtype)


def rows_kernel(near, block_rows, *refs):
    got_refs, refs = refs[:near], refs[near:]
    attn_ref, d_normed_ref, vectors_ref, w_out_ref, back_ref, token_ref = refs
    token_ref[...] = jnp.zeros_like(token_ref)
    width = attn_ref.shape[1]
    gain = vectors_ref[:, :width]
    b_out = vectors_ref[:, width : 2 * width]
    got = jnp.concatenate([got_ref[...] for got_ref in got_refs], axis=0)
    points = got[:, :width].astype(F32)
    cot = got[:, width:].astype(F32)
    xhat, rstd = normalize(points)
    mixed = points + (matmul(attn_ref[...], w_out_ref[...]) + b_out)
    d_xhat = d_normed_ref[...] * gain
    inner = (
        d_xhat
        - jnp.mean(d_xhat, axis=-1, keepdims=True)
        - xhat * jnp.mean(d_xhat * xhat, axis=-1, keepdims=True)
    )
    mixed = mixed.astype(BF16)
    grad = (cot + rstd * inner).astype(BF16)
    if near == 1:
        back_ref[:, :width] = mixed
        back_ref[:, width:] = grad
        return
    me = lax.axis_index("seq")
    devs = got.shape[0] // block_rows
    for at in range(devs):
        source = me ^ (at % (devs // near) * near + at // (devs // near))
        held = slice(at * block_rows, (at + 1) * block_rows)
        span = pl.ds(pl.multiple_of(turned(source, devs) * block_rows, block_rows), block_rows)
        back_ref[span, :width] = mixed[held]
        back_ref[span, width:] = grad[held]


def sum_kernel(count, *refs):
    piece_refs, out_ref = refs[:count], refs[-1]
    values = [piece_ref[...].astype(F32) for piece_ref in piece_refs]
    while len(values) > 1:
        values = [left + right for left, right in zip(values[::2], values[1::2])]
    out_ref[...] = values[0].astype(BF16)


def tie_kernel(rows_ref, other_ref, out_ref):
    pass


def pick_kernel(block_rows, route_hbm, pick_ref, token_ref, route_ref, sem):
    token_ref[...] = jnp.zeros_like(token_ref)
    copy = pltpu.make_async_copy(route_hbm, route_ref, sem)
    copy.start()
    copy.wait()
    rows, held = pick_ref.shape
    devs = held // block_rows
    target = send_rows(route_ref, (rows, 1), 0, block_rows, lambda owner: turned(owner, devs))
    index = lax.broadcasted_iota(jnp.int32, pick_ref.shape, 1)
    pick_ref[...] = jnp.where(index == target, 1.0, 0.0).astype(BF16)


def return_kernel(pick_ref, back_ref, mixed_ref, grad_ref, token_ref):
    token_ref[...] = jnp.zeros_like(token_ref)
    width = mixed_ref.shape[1]
    moved = matmul(pick_ref[...], back_ref[...]).astype(BF16)
    mixed_ref[...] = moved[:, :width]
    grad_ref[...] = moved[:, width:]


def weights_kernel(*refs):
    *half_refs, _, gain_ref, w_qkv_ref, b_qkv_ref, w_out_ref, b_out_ref, both_ref = refs
    width = w_out_ref.shape[1]
    core = lax.axis_index("seq") & 1
    for step, half_ref in enumerate(half_refs):
        place = core ^ step
        half = half_ref[...].astype(F32)
        both_ref[pl.ds(pl.multiple_of(place * width, width), width)] = half[:width]

        @pl.when(place == 0)
        def _():
            sums = half[width:]
            gain_ref[...] = sums[2, :width]
            b_qkv_ref[: 2 * width] = sums[0]
            b_qkv_ref[2 * width :] = sums[1, :width]
            b_out_ref[...] = sums[1, width:]

    w_qkv_ref[:, : 2 * width] = both_ref[:width]
    w_qkv_ref[:, 2 * width :] = both_ref[width:, :width]
    w_out_ref[...] = both_ref[width:, width:]


def exchange(message):
    devs = message.shape[0]
    order = [turned(place, devs) for place in range(devs)]
    return lax.all_to_all(
        message, "seq", split_axis=0, concat_axis=0, axis_index_groups=[order], tiled=True
    )


def swap(piece, step, devs):
    return lax.ppermute(piece, "seq", [(dev, dev ^ step) for dev in range(devs)])


def local(points, route, owned, cotangent, gain, w_qkv, b_qkv, w_out, b_out):
    devs = lax.axis_size("seq")
    rows, width = points.shape
    block_rows = rows // route.shape[1]
    held = devs * block_rows
    share = width // devs
    near = 4 if devs == 16 and width % 64 == 0 else 1

    def shape(*dims, dtype=BF16):
        return jax.ShapeDtypeStruct(dims, dtype)

    sent = pl.pallas_call(
        functools.partial(scatter_kernel, block_rows),
        out_shape=(shape(held // near, 2 * width),) * near,
        in_specs=[ANY] * 3,
        out_specs=(VMEM,) * near,
        scratch_shapes=[
            pltpu.SMEM(route.shape, route.dtype),
            pltpu.VMEM(points.shape, points.dtype),
            pltpu.VMEM(cotangent.shape, cotangent.dtype),
            pltpu.SemaphoreType.DMA((3,)),
        ],
    )(route, points, cotangent)
    if near > 1:
        got = [sent[0]] + [swap(sent[step], near * step, devs) for step in range(1, near)]
        got = pl.pallas_call(
            functools.partial(regroup_kernel, block_rows),
            out_shape=(shape(held // near, 2 * width),) * near,
            in_specs=[VMEM] * near,
            out_specs=(VMEM,) * near,
            compiler_params=SMALL,
        )(*got)
        got = [got[0]] + [swap(got[step], step, devs) for step in range(1, near)]
    else:
        got = [exchange(sent[0].reshape(devs, block_rows, 2 * width)).reshape(held, 2 * width)]

    pick, early = pl.pallas_call(
        functools.partial(pick_kernel, block_rows),
        out_shape=(shape(rows, held), shape(8, 128, dtype=F32)),
        in_specs=[ANY],
        out_specs=(VMEM,) * 2,
        scratch_shapes=[pltpu.SMEM(route.shape, route.dtype), pltpu.SemaphoreType.DMA],
        compiler_params=SMALL,
    )(route)

    half = shape(width + 8, 2 * width)
    if near > 1:
        sums_shapes = (half, half)
    else:
        sums_shapes = (shape(width, 2 * width),) * 2 + (shape(8, 2 * width),)
    vectors = jnp.concatenate([gain, b_out, b_qkv])[None, :]
    attn, d_normed, *parts = pl.pallas_call(
        functools.partial(owner_kernel, near),
        out_shape=(shape(held, width), shape(held, width, dtype=F32)) + sums_shapes,
        in_specs=[VMEM] * (near + 1) + [ANY, ANY, VMEM],
        out_specs=(VMEM,) * (2 + len(sums_shapes)),
        scratch_shapes=[
            pltpu.VMEM(w_qkv.shape, w_qkv.dtype),
            pltpu.VMEM(w_out.shape, w_out.dtype),
            pltpu.VMEM((2 * width, 2 * width), F32),
            pltpu.VMEM((held, width), F32),
            pltpu.VMEM((held, width), F32),
            pltpu.SemaphoreType.DMA((2,)),
        ],
        compiler_params=LARGE,
    )(*got, vectors, w_qkv, w_out, early)
    back, token = pl.pallas_call(
        functools.partial(rows_kernel, near, block_rows),
        out_shape=(shape(held, 2 * width), shape(8, 128, dtype=F32)),
        in_specs=[VMEM] * (near + 4),
        out_specs=(VMEM,) * 2,
        compiler_params=SMALL,
        cost_estimate=pl.CostEstimate(
            flops=64 * held * width * width, bytes_accessed=16 * held * width, transcendentals=0
        ),
    )(*got, attn, d_normed, vectors, w_out)

    def give_back(back):
        return pl.pallas_call(
            return_kernel,
            out_shape=(shape(rows, width), shape(rows, width), shape(8, 128, dtype=F32)),
            in_specs=[VMEM] * 2,
            out_specs=(VMEM,) * 3,
            compiler_params=SMALL,
        )(pick, back)

    if near > 1:
        mine, theirs = parts

        def add(*pieces, after=(), flops=0):
            return pl.pallas_call(
                functools.partial(sum_kernel, len(pieces)),
                out_shape=half,
                in_specs=[VMEM] * (len(pieces) + len(after)),
                out_specs=VMEM,
                compiler_params=SMALL,
                cost_estimate=pl.CostEstimate(flops=flops, bytes_accessed=0, transcendentals=0),
            )(*pieces, *after)

        total = add(mine, swap(theirs, 1, devs), after=(token,))
        back = pl.pallas_call(
            tie_kernel,
            out_shape=back,
            in_specs=[ANY, VMEM],
            out_specs=ANY,
            input_output_aliases={0: 0},
            compiler_params=SMALL,
        )(back, total)
        back = exchange(back.reshape(devs, block_rows, 2 * width)).reshape(held, 2 * width)
        mixed, grad_points, token = give_back(back)
        total = add(total, swap(total, devs // 2, devs), flops=40_000_000_000)
        steps = [step for step in range(2, devs // 2, 2)]
        total = add(total, *(swap(total, step, devs) for step in steps))
        parts = [total, swap(total, 1, devs)]
        grad_gain, grad_wq, grad_bq, grad_wo, grad_bo = pl.pallas_call(
            weights_kernel,
            out_shape=tuple(
                shape(*dims, dtype=F32)
                for dims in ((width,), (width, 3 * width), (3 * width,), (width, width), (width,))
            ),
            in_specs=[VMEM] * 3,
            out_specs=(VMEM,) * 5,
            scratch_shapes=[pltpu.VMEM((2 * width, 2 * width), F32)],
            compiler_params=SMALL,
        )(*parts, token)
    else:
        left, right, sums = parts
        message = jnp.concatenate(
            [
                back.reshape(devs, block_rows, 2 * width),
                left.reshape(devs, share, 2 * width),
                right.reshape(devs, share, 2 * width),
                jnp.broadcast_to(sums[None], (devs, 8, 2 * width)),
            ],
            axis=1,
        )
        message = exchange(message)
        total = jnp.sum(message[:, block_rows:].astype(F32), axis=0)
        mine = total[: 2 * share].astype(BF16)
        both = exchange(jnp.broadcast_to(mine[None], (devs, 2 * share, 2 * width))).astype(F32)
        mixed, grad_points, _ = give_back(message[:, :block_rows].reshape(held, 2 * width))
        left = both[:, :share].reshape(width, 2 * width)
        right = both[:, share:].reshape(width, 2 * width)
        grad_wq = jnp.concatenate([left, right[:, :width]], axis=1)
        grad_wo = right[:, width:]
        flat = total[2 * share :].reshape(-1)
        grad_bq = flat[: 3 * width]
        grad_bo = flat[3 * width : 4 * width]
        grad_gain = flat[4 * width : 5 * width]

    return (mixed, grad_points, grad_gain, grad_wq, grad_bq, grad_wo, grad_bo)


def solution(mesh):
    placed = (
        P(("parts", "seq"), None),
        P(None, ("parts", "seq")),
        P(("parts", "seq")),
        P(("parts", "seq"), None),
        P(),
        P(),
        P(),
        P(),
        P(),
    )
    return jax.shard_map(
        local,
        mesh=mesh,
        in_specs=placed,
        out_specs=(
            P(("parts", "seq"), None),
            P(("parts", "seq"), None),
            P("parts"),
            P("parts", None),
            P("parts"),
            P("parts", None),
            P("parts"),
        ),
        check_vma=False,
    )
```

```python
import functools

import jax
import jax.numpy as jnp
from jax import lax
from jax.experimental import pallas as pl
from jax.experimental.pallas import tpu as pltpu
from jax.sharding import PartitionSpec as P

HEADS = 8
EPS = 1e-05
EMPTY = 64.0
MASKED = -1e30

F32 = jnp.float32
BF16 = jnp.bfloat16

VMEM = pl.BlockSpec(memory_space=pltpu.VMEM)
ANY = pl.BlockSpec(memory_space=pl.ANY)
SMEM = pl.BlockSpec(memory_space=pltpu.SMEM)
MIB = 1024 * 1024
LARGE = pltpu.CompilerParams(vmem_limit_bytes=32 * MIB)
SMALL = pltpu.CompilerParams(vmem_limit_bytes=8 * MIB)


def matmul(left, right, dims=((1,), (0,))):
    return lax.dot_general(left, right, (dims, ((), ())), preferred_element_type=F32)


def turned(index, devs):
    top = devs.bit_length() - 2
    place = 0
    for bit in range(top + 1):
        place = place + (((index >> bit) & 1) << (top - bit))
    return place


def send_rows(route_ref, shape, axis, block_rows, devs):
    place = lax.broadcasted_iota(jnp.int32, shape, axis)
    target = jnp.zeros(shape, jnp.int32)
    for block in range(shape[axis] // block_rows):
        first = block * block_rows
        moved = turned(route_ref[0, block], devs) * block_rows + place - first
        target = jnp.where(place >= first, moved, target)
    return target


def scatter_kernel(block_rows, route_hbm, points_hbm, cot_hbm, out_ref, route_ref, points_ref, cot_ref, sems):
    copies = [
        pltpu.make_async_copy(source, target, sems.at[at])
        for at, (source, target) in enumerate(
            ((route_hbm, route_ref), (points_hbm, points_ref), (cot_hbm, cot_ref))
        )
    ]
    for copy in copies:
        copy.start()
    copies[0].wait()
    rows, width = points_ref.shape
    target = send_rows(route_ref, (1, rows), 1, block_rows, out_ref.shape[0] // block_rows)
    index = lax.broadcasted_iota(jnp.int32, (out_ref.shape[0], rows), 0)
    pick = jnp.where(index == target, 1.0, 0.0).astype(BF16)
    for copy in copies[1:]:
        copy.wait()
    ones = jnp.ones((rows, width), BF16)
    moved = matmul(pick, jnp.concatenate([points_ref[...], ones], axis=1))
    empty = (1.0 - moved[:, width:]) * EMPTY
    out_ref[:, :width] = (moved[:, :width] + empty).astype(BF16)
    out_ref[:, width:] = matmul(pick, cot_ref[...]).astype(BF16)


def normalize(points):
    centered = points - jnp.mean(points, axis=-1, keepdims=True)
    rstd = lax.rsqrt(jnp.mean(centered * centered, axis=-1, keepdims=True) + EPS)
    return centered * rstd, rstd


def owner_kernel(near, got_ref, vectors_ref, w_qkv_hbm, w_out_hbm, _, attn_ref, d_normed_ref, *refs):
    *outs, w_qkv_ref, w_out_ref, both_ref, d_keys_ref, d_values_ref, sems = refs
    copies = [
        pltpu.make_async_copy(w_qkv_hbm, w_qkv_ref, sems.at[0]),
        pltpu.make_async_copy(w_out_hbm, w_out_ref, sems.at[1]),
    ]
    for copy in copies:
        copy.start()
    rows = got_ref.shape[0]
    width = got_ref.shape[1] // 2
    head = width // HEADS
    scale = head ** (-0.5)
    gain = vectors_ref[:, :width]
    b_qkv = vectors_ref[:, 2 * width :]

    points = got_ref[:, :width].astype(F32)
    cot = got_ref[:, width:]
    xhat, _ = normalize(points)
    normed = (xhat * gain).astype(BF16)
    for copy in copies:
        copy.wait()
    w_qkv = w_qkv_ref[...]
    w_out = w_out_ref[...]
    qkv = (matmul(normed, w_qkv) + b_qkv).astype(BF16)
    query, keys, values = qkv[:, :width], qkv[:, width : 2 * width], qkv[:, 2 * width :]
    d_attn = matmul(cot, w_out, ((1,), (1,))).astype(BF16)
    d_attn_t = matmul(w_out, cot, ((1,), (1,))).astype(BF16)
    d_attn_s = (d_attn.astype(F32) * scale).astype(BF16)

    keys_t = keys.T
    values_t = values.T
    keys_s = (keys.astype(F32) * scale).astype(BF16)
    lane = lax.broadcasted_iota(jnp.int32, (rows, width), 1)
    hidden = jnp.where(points[:, :1] > EMPTY / 2, MASKED, 0.0)

    def products(h):
        mine = (lane >= h * head) & (lane < (h + 1) * head)
        scores = matmul(jnp.where(mine, keys_s, 0), query, ((1,), (1,))) + hidden
        return scores, matmul(jnp.where(mine, values, 0), d_attn_s, ((1,), (1,)))

    def finish(h, probs_b, d_score):
        lanes = slice(h * head, (h + 1) * head)
        d_values_ref[:, lanes] = matmul(probs_b, d_attn)[:, lanes]
        d_keys_ref[:, lanes] = matmul(d_score, query)[:, lanes]

    attn_t, dq_t = [], []
    following = products(0)
    done = None
    for h in range(HEADS):
        lo, hi = h * head, (h + 1) * head
        scores, d_probs = following
        if h + 1 < HEADS:
            following = products(h + 1)
        if done is not None:
            finish(h - 1, *done)
        expo = jnp.exp(scores - jnp.max(scores, axis=0, keepdims=True))
        probs = expo * (1.0 / jnp.sum(expo, axis=0, keepdims=True))
        probs_b = probs.astype(BF16)
        out_t = matmul(values_t[lo:hi, :], probs_b)
        attn_t.append(out_t)
        inner = jnp.sum(out_t * d_attn_t[lo:hi, :].astype(F32), axis=0, keepdims=True) * scale
        d_score = (probs * (d_probs - inner)).astype(BF16)
        dq_t.append(matmul(keys_t[lo:hi, :], d_score))
        done = probs_b, d_score
    finish(HEADS - 1, *done)

    attn_t = jnp.concatenate(attn_t, axis=0)
    attn_ref[...] = attn_t.T.astype(BF16)
    grad_w_out = matmul(attn_t.astype(BF16), cot)
    grad_b_out = jnp.sum(cot.astype(F32), axis=0, keepdims=True)

    d_query = jnp.concatenate(dq_t, axis=0).T
    d_qkv = jnp.concatenate([d_query, d_keys_ref[...], d_values_ref[...]], axis=1).astype(BF16)
    d_normed = matmul(d_qkv, w_qkv, ((1,), (1,)))
    grad_w_qkv = matmul(normed, d_qkv, ((0,), (0,)))
    grad_b_qkv = jnp.sum(d_qkv.astype(F32), axis=0, keepdims=True)
    grad_gain = jnp.sum(d_normed * xhat, axis=0, keepdims=True)
    d_normed_ref[...] = d_normed
    sums = jnp.concatenate(
        [
            grad_b_qkv[:, : 2 * width],
            jnp.concatenate([grad_b_qkv[:, 2 * width :], grad_b_out], axis=1),
            jnp.concatenate([grad_gain, jnp.zeros_like(grad_gain)], axis=1),
            jnp.zeros((5, 2 * width), F32),
        ],
        axis=0,
    )
    left = grad_w_qkv[:, : 2 * width]
    right = jnp.concatenate([grad_w_qkv[:, 2 * width :], grad_w_out], axis=1)
    if near == 1:
        left_ref, right_ref, sums_ref = outs
        left_ref[...] = left.astype(BF16)
        right_ref[...] = right.astype(BF16)
        sums_ref[...] = sums.astype(BF16)
        return
    mine_ref, theirs_ref = outs
    both_ref[:width] = left
    both_ref[width:] = right
    core = lax.axis_index("seq") & 1
    for half, half_ref in ((core, mine_ref), (core ^ 1, theirs_ref)):
        span = pl.ds(pl.multiple_of(half * width, width), width)
        half_ref[:width] = both_ref[span].astype(half_ref.dtype)
        half_ref[width:] = sums.astype(half_ref.dtype)


def rows_kernel(got_ref, attn_ref, d_normed_ref, vectors_ref, w_out_ref, back_ref, token_ref):
    token_ref[...] = jnp.zeros_like(token_ref)
    width = attn_ref.shape[1]
    gain = vectors_ref[:, :width]
    b_out = vectors_ref[:, width : 2 * width]
    points = got_ref[:, :width].astype(F32)
    cot = got_ref[:, width:].astype(F32)
    xhat, rstd = normalize(points)
    mixed = points + (matmul(attn_ref[...], w_out_ref[...]) + b_out)
    d_xhat = d_normed_ref[...] * gain
    inner = (
        d_xhat
        - jnp.mean(d_xhat, axis=-1, keepdims=True)
        - xhat * jnp.mean(d_xhat * xhat, axis=-1, keepdims=True)
    )
    back_ref[:, :width] = mixed.astype(BF16)
    back_ref[:, width:] = (cot + rstd * inner).astype(BF16)


def sum_kernel(count, *refs):
    piece_refs, out_ref = refs[:count], refs[-1]
    values = [piece_ref[...].astype(F32) for piece_ref in piece_refs]
    while len(values) > 1:
        values = [left + right for left, right in zip(values[::2], values[1::2])]
    out_ref[...] = values[0].astype(BF16)


def tie_kernel(rows_ref, other_ref, out_ref):
    pass


def pick_kernel(block_rows, route_hbm, pick_ref, token_ref, route_ref, sem):
    token_ref[...] = jnp.zeros_like(token_ref)
    copy = pltpu.make_async_copy(route_hbm, route_ref, sem)
    copy.start()
    copy.wait()
    rows, held = pick_ref.shape
    target = send_rows(route_ref, (rows, 1), 0, block_rows, held // block_rows)
    index = lax.broadcasted_iota(jnp.int32, pick_ref.shape, 1)
    pick_ref[...] = jnp.where(index == target, 1.0, 0.0).astype(BF16)


def return_kernel(pick_ref, back_ref, mixed_ref, grad_ref, token_ref):
    token_ref[...] = jnp.zeros_like(token_ref)
    width = mixed_ref.shape[1]
    moved = matmul(pick_ref[...], back_ref[...]).astype(BF16)
    mixed_ref[...] = moved[:, :width]
    grad_ref[...] = moved[:, width:]


def weights_kernel(*refs):
    *half_refs, _, gain_ref, w_qkv_ref, b_qkv_ref, w_out_ref, b_out_ref, both_ref = refs
    width = w_out_ref.shape[1]
    core = lax.axis_index("seq") & 1
    for step, half_ref in enumerate(half_refs):
        place = core ^ step
        half = half_ref[...].astype(F32)
        both_ref[pl.ds(pl.multiple_of(place * width, width), width)] = half[:width]

        @pl.when(place == 0)
        def _():
            sums = half[width:]
            gain_ref[...] = sums[2, :width]
            b_qkv_ref[: 2 * width] = sums[0]
            b_qkv_ref[2 * width :] = sums[1, :width]
            b_out_ref[...] = sums[1, width:]

    w_qkv_ref[:, : 2 * width] = both_ref[:width]
    w_qkv_ref[:, 2 * width :] = both_ref[width:, :width]
    w_out_ref[...] = both_ref[width:, width:]


def exchange(message):
    devs = message.shape[0]
    order = [turned(place, devs) for place in range(devs)]
    return lax.all_to_all(
        message, "seq", split_axis=0, concat_axis=0, axis_index_groups=[order], tiled=True
    )


def swap(piece, step, devs):
    return lax.ppermute(piece, "seq", [(dev, dev ^ step) for dev in range(devs)])


def local(points, route, owned, cotangent, gain, w_qkv, b_qkv, w_out, b_out):
    devs = lax.axis_size("seq")
    rows, width = points.shape
    block_rows = rows // route.shape[1]
    held = devs * block_rows
    share = width // devs
    near = 4 if devs == 16 and width % 64 == 0 else 1

    def shape(*dims, dtype=BF16):
        return jax.ShapeDtypeStruct(dims, dtype)

    sent = pl.pallas_call(
        functools.partial(scatter_kernel, block_rows),
        out_shape=shape(held, 2 * width),
        in_specs=[ANY] * 3,
        out_specs=VMEM,
        scratch_shapes=[
            pltpu.SMEM(route.shape, route.dtype),
            pltpu.VMEM(points.shape, points.dtype),
            pltpu.VMEM(cotangent.shape, cotangent.dtype),
            pltpu.SemaphoreType.DMA((3,)),
        ],
    )(route, points, cotangent)
    got = exchange(sent.reshape(devs, block_rows, 2 * width)).reshape(held, 2 * width)

    pick, early = pl.pallas_call(
        functools.partial(pick_kernel, block_rows),
        out_shape=(shape(rows, held), shape(8, 128, dtype=F32)),
        in_specs=[ANY],
        out_specs=(VMEM,) * 2,
        scratch_shapes=[pltpu.SMEM(route.shape, route.dtype), pltpu.SemaphoreType.DMA],
        compiler_params=SMALL,
    )(route)

    half = shape(width + 8, 2 * width)
    if near > 1:
        sums_shapes = (half, half)
    else:
        sums_shapes = (shape(width, 2 * width),) * 2 + (shape(8, 2 * width),)
    vectors = jnp.concatenate([gain, b_out, b_qkv])[None, :]
    attn, d_normed, *parts = pl.pallas_call(
        functools.partial(owner_kernel, near),
        out_shape=(shape(held, width), shape(held, width, dtype=F32)) + sums_shapes,
        in_specs=[VMEM, VMEM, ANY, ANY, VMEM],
        out_specs=(VMEM,) * (2 + len(sums_shapes)),
        scratch_shapes=[
            pltpu.VMEM(w_qkv.shape, w_qkv.dtype),
            pltpu.VMEM(w_out.shape, w_out.dtype),
            pltpu.VMEM((2 * width, 2 * width), F32),
            pltpu.VMEM((held, width), F32),
            pltpu.VMEM((held, width), F32),
            pltpu.SemaphoreType.DMA((2,)),
        ],
        compiler_params=LARGE,
    )(got, vectors, w_qkv, w_out, early)
    back, token = pl.pallas_call(
        rows_kernel,
        out_shape=(shape(held, 2 * width), shape(8, 128, dtype=F32)),
        in_specs=[VMEM] * 5,
        out_specs=(VMEM,) * 2,
        compiler_params=SMALL,
        cost_estimate=pl.CostEstimate(
            flops=64 * held * width * width, bytes_accessed=16 * held * width, transcendentals=0
        ),
    )(got, attn, d_normed, vectors, w_out)

    def give_back(back):
        return pl.pallas_call(
            return_kernel,
            out_shape=(shape(rows, width), shape(rows, width), shape(8, 128, dtype=F32)),
            in_specs=[VMEM] * 2,
            out_specs=(VMEM,) * 3,
            compiler_params=SMALL,
        )(pick, back)

    if near > 1:
        mine, theirs = parts

        def add(*pieces, after=(), flops=0):
            return pl.pallas_call(
                functools.partial(sum_kernel, len(pieces)),
                out_shape=half,
                in_specs=[VMEM] * (len(pieces) + len(after)),
                out_specs=VMEM,
                compiler_params=SMALL,
                cost_estimate=pl.CostEstimate(flops=flops, bytes_accessed=0, transcendentals=0),
            )(*pieces, *after)

        total = add(mine, swap(theirs, 1, devs), after=(token,))
        back = pl.pallas_call(
            tie_kernel,
            out_shape=back,
            in_specs=[ANY, VMEM],
            out_specs=ANY,
            input_output_aliases={0: 0},
            compiler_params=SMALL,
        )(back, total)
        back = exchange(back.reshape(devs, block_rows, 2 * width)).reshape(held, 2 * width)
        mixed, grad_points, token = give_back(back)
        total = add(total, swap(total, devs // 2, devs), flops=40_000_000_000)
        steps = [step for step in range(2, devs // 2, 2)]
        total = add(total, *(swap(total, step, devs) for step in steps))
        parts = [total, swap(total, 1, devs)]
        grad_gain, grad_wq, grad_bq, grad_wo, grad_bo = pl.pallas_call(
            weights_kernel,
            out_shape=tuple(
                shape(*dims, dtype=F32)
                for dims in ((width,), (width, 3 * width), (3 * width,), (width, width), (width,))
            ),
            in_specs=[VMEM] * 3,
            out_specs=(VMEM,) * 5,
            scratch_shapes=[pltpu.VMEM((2 * width, 2 * width), F32)],
            compiler_params=SMALL,
        )(*parts, token)
    else:
        left, right, sums = parts
        message = jnp.concatenate(
            [
                back.reshape(devs, block_rows, 2 * width),
                left.reshape(devs, share, 2 * width),
                right.reshape(devs, share, 2 * width),
                jnp.broadcast_to(sums[None], (devs, 8, 2 * width)),
            ],
            axis=1,
        )
        message = exchange(message)
        total = jnp.sum(message[:, block_rows:].astype(F32), axis=0)
        mine = total[: 2 * share].astype(BF16)
        both = exchange(jnp.broadcast_to(mine[None], (devs, 2 * share, 2 * width))).astype(F32)
        mixed, grad_points, _ = give_back(message[:, :block_rows].reshape(held, 2 * width))
        left = both[:, :share].reshape(width, 2 * width)
        right = both[:, share:].reshape(width, 2 * width)
        grad_wq = jnp.concatenate([left, right[:, :width]], axis=1)
        grad_wo = right[:, width:]
        flat = total[2 * share :].reshape(-1)
        grad_bq = flat[: 3 * width]
        grad_bo = flat[3 * width : 4 * width]
        grad_gain = flat[4 * width : 5 * width]

    return (mixed, grad_points, grad_gain, grad_wq, grad_bq, grad_wo, grad_bo)


def solution(mesh):
    placed = (
        P(("parts", "seq"), None),
        P(None, ("parts", "seq")),
        P(("parts", "seq")),
        P(("parts", "seq"), None),
        P(),
        P(),
        P(),
        P(),
        P(),
    )
    return jax.shard_map(
        local,
        mesh=mesh,
        in_specs=placed,
        out_specs=(
            P(("parts", "seq"), None),
            P(("parts", "seq"), None),
            P("parts"),
            P("parts", None),
            P("parts"),
            P("parts", None),
            P("parts"),
        ),
        check_vma=False,
    )
```

```python
import functools

import jax
import jax.numpy as jnp
from jax import lax
from jax.experimental import pallas as pl
from jax.experimental.pallas import tpu as pltpu
from jax.sharding import PartitionSpec as P

HEADS = 8
EPS = 1e-05
EMPTY = 64.0
MASKED = -1e30

F32 = jnp.float32
BF16 = jnp.bfloat16

VMEM = pl.BlockSpec(memory_space=pltpu.VMEM)
ANY = pl.BlockSpec(memory_space=pl.ANY)
SMEM = pl.BlockSpec(memory_space=pltpu.SMEM)
MIB = 1024 * 1024
LARGE = pltpu.CompilerParams(vmem_limit_bytes=32 * MIB)
SMALL = pltpu.CompilerParams(vmem_limit_bytes=8 * MIB)


def matmul(left, right, dims=((1,), (0,))):
    return lax.dot_general(left, right, (dims, ((), ())), preferred_element_type=F32)


def turned(index, devs):
    top = devs.bit_length() - 2
    place = 0
    for bit in range(top + 1):
        place = place + (((index >> bit) & 1) << (top - bit))
    return place


def send_rows(route_ref, shape, axis, block_rows, devs):
    place = lax.broadcasted_iota(jnp.int32, shape, axis)
    target = jnp.zeros(shape, jnp.int32)
    for block in range(shape[axis] // block_rows):
        first = block * block_rows
        moved = turned(route_ref[0, block], devs) * block_rows + place - first
        target = jnp.where(place >= first, moved, target)
    return target


def scatter_kernel(block_rows, route_hbm, points_hbm, cot_hbm, out_ref, route_ref, points_ref, cot_ref, sems):
    copies = [
        pltpu.make_async_copy(source, target, sems.at[at])
        for at, (source, target) in enumerate(
            ((route_hbm, route_ref), (points_hbm, points_ref), (cot_hbm, cot_ref))
        )
    ]
    for copy in copies:
        copy.start()
    copies[0].wait()
    rows, width = points_ref.shape
    target = send_rows(route_ref, (1, rows), 1, block_rows, out_ref.shape[0] // block_rows)
    index = lax.broadcasted_iota(jnp.int32, (out_ref.shape[0], rows), 0)
    pick = jnp.where(index == target, 1.0, 0.0).astype(BF16)
    for copy in copies[1:]:
        copy.wait()
    ones = jnp.ones((rows, width), BF16)
    moved = matmul(pick, jnp.concatenate([points_ref[...], ones], axis=1))
    empty = (1.0 - moved[:, width:]) * EMPTY
    out_ref[:, :width] = (moved[:, :width] + empty).astype(BF16)
    out_ref[:, width:] = matmul(pick, cot_ref[...]).astype(BF16)


def normalize(points):
    centered = points - jnp.mean(points, axis=-1, keepdims=True)
    rstd = lax.rsqrt(jnp.mean(centered * centered, axis=-1, keepdims=True) + EPS)
    return centered * rstd, rstd


def owner_kernel(near, got_ref, vectors_ref, w_qkv_hbm, w_out_hbm, _, attn_ref, d_normed_ref, *refs):
    *outs, w_qkv_ref, w_out_ref, both_ref, d_keys_ref, d_values_ref, sems = refs
    copies = [
        pltpu.make_async_copy(w_qkv_hbm, w_qkv_ref, sems.at[0]),
        pltpu.make_async_copy(w_out_hbm, w_out_ref, sems.at[1]),
    ]
    for copy in copies:
        copy.start()
    rows = got_ref.shape[0]
    width = got_ref.shape[1] // 2
    head = width // HEADS
    scale = head ** (-0.5)
    gain = vectors_ref[:, :width]
    b_qkv = vectors_ref[:, 2 * width :]

    points = got_ref[:, :width].astype(F32)
    cot = got_ref[:, width:]
    xhat, _ = normalize(points)
    normed = (xhat * gain).astype(BF16)
    for copy in copies:
        copy.wait()
    w_qkv = w_qkv_ref[...]
    w_out = w_out_ref[...]
    qkv = (matmul(normed, w_qkv) + b_qkv).astype(BF16)
    query, keys, values = qkv[:, :width], qkv[:, width : 2 * width], qkv[:, 2 * width :]
    d_attn = matmul(cot, w_out, ((1,), (1,))).astype(BF16)
    d_attn_t = matmul(w_out, cot, ((1,), (1,))).astype(BF16)
    d_attn_s = (d_attn.astype(F32) * scale).astype(BF16)

    keys_t = keys.T
    values_t = values.T
    keys_s = (keys.astype(F32) * scale).astype(BF16)
    lane = lax.broadcasted_iota(jnp.int32, (rows, width), 1)
    hidden = jnp.where(points[:, :1] > EMPTY / 2, MASKED, 0.0)

    def own(h, array):
        return jnp.where((lane >= h * head) & (lane < (h + 1) * head), array, 0)

    def scores_of(h):
        return matmul(own(h, keys_s), query, ((1,), (1,))) + hidden

    scores, probs, probs_b, d_probs, d_score = {}, {}, {}, {}, {}
    attn_t, dq_t = [], []
    scores[0] = scores_of(0)
    for step in range(HEADS + 2):
        if step + 1 < HEADS:
            scores[step + 1] = scores_of(step + 1)
        if step < HEADS:
            d_probs[step] = matmul(own(step, values), d_attn_s, ((1,), (1,)))
        if 1 <= step <= HEADS:
            lanes = slice((step - 1) * head, step * head)
            attn_t.append(matmul(values_t[lanes, :], probs_b[step - 1]))
        if step >= 2:
            h = step - 2
            lanes = slice(h * head, (h + 1) * head)
            d_values_ref[:, lanes] = matmul(probs_b[h], d_attn)[:, lanes]
            d_keys_ref[:, lanes] = matmul(d_score[h], query)[:, lanes]
            dq_t.append(matmul(keys_t[lanes, :], d_score[h]))
        if step < HEADS:
            now = scores.pop(step)
            expo = jnp.exp(now - jnp.max(now, axis=0, keepdims=True))
            probs[step] = expo * (1.0 / jnp.sum(expo, axis=0, keepdims=True))
            probs_b[step] = probs[step].astype(BF16)
        if 1 <= step <= HEADS:
            h = step - 1
            inner = attn_t[h] * d_attn_t[h * head : (h + 1) * head, :].astype(F32)
            inner = jnp.sum(inner, axis=0, keepdims=True) * scale
            d_score[h] = (probs.pop(h) * (d_probs.pop(h) - inner)).astype(BF16)

    attn_t = jnp.concatenate(attn_t, axis=0)
    attn_ref[...] = attn_t.T.astype(BF16)
    grad_w_out = matmul(attn_t.astype(BF16), cot)
    grad_b_out = jnp.sum(cot.astype(F32), axis=0, keepdims=True)

    d_query = jnp.concatenate(dq_t, axis=0).T
    d_qkv = jnp.concatenate([d_query, d_keys_ref[...], d_values_ref[...]], axis=1).astype(BF16)
    d_normed = matmul(d_qkv, w_qkv, ((1,), (1,)))
    grad_w_qkv = matmul(normed, d_qkv, ((0,), (0,)))
    grad_b_qkv = jnp.sum(d_qkv.astype(F32), axis=0, keepdims=True)
    grad_gain = jnp.sum(d_normed * xhat, axis=0, keepdims=True)
    d_normed_ref[...] = d_normed
    sums = jnp.concatenate(
        [
            grad_b_qkv[:, : 2 * width],
            jnp.concatenate([grad_b_qkv[:, 2 * width :], grad_b_out], axis=1),
            jnp.concatenate([grad_gain, jnp.zeros_like(grad_gain)], axis=1),
            jnp.zeros((5, 2 * width), F32),
        ],
        axis=0,
    )
    left = grad_w_qkv[:, : 2 * width]
    right = jnp.concatenate([grad_w_qkv[:, 2 * width :], grad_w_out], axis=1)
    if near == 1:
        left_ref, right_ref, sums_ref = outs
        left_ref[...] = left.astype(BF16)
        right_ref[...] = right.astype(BF16)
        sums_ref[...] = sums.astype(BF16)
        return
    mine_ref, theirs_ref = outs
    both_ref[:width] = left
    both_ref[width:] = right
    core = lax.axis_index("seq") & 1
    for half, half_ref in ((core, mine_ref), (core ^ 1, theirs_ref)):
        span = pl.ds(pl.multiple_of(half * width, width), width)
        half_ref[:width] = both_ref[span].astype(half_ref.dtype)
        half_ref[width:] = sums.astype(half_ref.dtype)


def rows_kernel(got_ref, attn_ref, d_normed_ref, vectors_ref, w_out_ref, back_ref, token_ref):
    token_ref[...] = jnp.zeros_like(token_ref)
    width = attn_ref.shape[1]
    gain = vectors_ref[:, :width]
    b_out = vectors_ref[:, width : 2 * width]
    points = got_ref[:, :width].astype(F32)
    cot = got_ref[:, width:].astype(F32)
    xhat, rstd = normalize(points)
    mixed = points + (matmul(attn_ref[...], w_out_ref[...]) + b_out)
    d_xhat = d_normed_ref[...] * gain
    inner = (
        d_xhat
        - jnp.mean(d_xhat, axis=-1, keepdims=True)
        - xhat * jnp.mean(d_xhat * xhat, axis=-1, keepdims=True)
    )
    back_ref[:, :width] = mixed.astype(BF16)
    back_ref[:, width:] = (cot + rstd * inner).astype(BF16)


def sum_kernel(count, *refs):
    piece_refs, out_ref = refs[:count], refs[-1]
    values = [piece_ref[...].astype(F32) for piece_ref in piece_refs]
    while len(values) > 1:
        values = [left + right for left, right in zip(values[::2], values[1::2])]
    out_ref[...] = values[0].astype(BF16)


def tie_kernel(rows_ref, other_ref, out_ref):
    pass


def pick_kernel(block_rows, route_hbm, pick_ref, token_ref, route_ref, sem):
    token_ref[...] = jnp.zeros_like(token_ref)
    copy = pltpu.make_async_copy(route_hbm, route_ref, sem)
    copy.start()
    copy.wait()
    rows, held = pick_ref.shape
    target = send_rows(route_ref, (rows, 1), 0, block_rows, held // block_rows)
    index = lax.broadcasted_iota(jnp.int32, pick_ref.shape, 1)
    pick_ref[...] = jnp.where(index == target, 1.0, 0.0).astype(BF16)


def return_kernel(pick_ref, back_ref, mixed_ref, grad_ref, token_ref):
    token_ref[...] = jnp.zeros_like(token_ref)
    width = mixed_ref.shape[1]
    moved = matmul(pick_ref[...], back_ref[...]).astype(BF16)
    mixed_ref[...] = moved[:, :width]
    grad_ref[...] = moved[:, width:]


def weights_kernel(*refs):
    *half_refs, _, gain_ref, w_qkv_ref, b_qkv_ref, w_out_ref, b_out_ref, both_ref = refs
    width = w_out_ref.shape[1]
    core = lax.axis_index("seq") & 1
    for step, half_ref in enumerate(half_refs):
        place = core ^ step
        half = half_ref[...].astype(F32)
        both_ref[pl.ds(pl.multiple_of(place * width, width), width)] = half[:width]

        @pl.when(place == 0)
        def _():
            sums = half[width:]
            gain_ref[...] = sums[2, :width]
            b_qkv_ref[: 2 * width] = sums[0]
            b_qkv_ref[2 * width :] = sums[1, :width]
            b_out_ref[...] = sums[1, width:]

    w_qkv_ref[:, : 2 * width] = both_ref[:width]
    w_qkv_ref[:, 2 * width :] = both_ref[width:, :width]
    w_out_ref[...] = both_ref[width:, width:]


def exchange(message):
    devs = message.shape[0]
    order = [turned(place, devs) for place in range(devs)]
    return lax.all_to_all(
        message, "seq", split_axis=0, concat_axis=0, axis_index_groups=[order], tiled=True
    )


def swap(piece, step, devs):
    return lax.ppermute(piece, "seq", [(dev, dev ^ step) for dev in range(devs)])


def local(points, route, owned, cotangent, gain, w_qkv, b_qkv, w_out, b_out):
    devs = lax.axis_size("seq")
    rows, width = points.shape
    block_rows = rows // route.shape[1]
    held = devs * block_rows
    share = width // devs
    near = 4 if devs == 16 and width % 64 == 0 else 1

    def shape(*dims, dtype=BF16):
        return jax.ShapeDtypeStruct(dims, dtype)

    sent = pl.pallas_call(
        functools.partial(scatter_kernel, block_rows),
        out_shape=shape(held, 2 * width),
        in_specs=[ANY] * 3,
        out_specs=VMEM,
        scratch_shapes=[
            pltpu.SMEM(route.shape, route.dtype),
            pltpu.VMEM(points.shape, points.dtype),
            pltpu.VMEM(cotangent.shape, cotangent.dtype),
            pltpu.SemaphoreType.DMA((3,)),
        ],
    )(route, points, cotangent)
    got = exchange(sent.reshape(devs, block_rows, 2 * width)).reshape(held, 2 * width)

    pick, early = pl.pallas_call(
        functools.partial(pick_kernel, block_rows),
        out_shape=(shape(rows, held), shape(8, 128, dtype=F32)),
        in_specs=[ANY],
        out_specs=(VMEM,) * 2,
        scratch_shapes=[pltpu.SMEM(route.shape, route.dtype), pltpu.SemaphoreType.DMA],
        compiler_params=SMALL,
    )(route)

    half = shape(width + 8, 2 * width)
    if near > 1:
        sums_shapes = (half, half)
    else:
        sums_shapes = (shape(width, 2 * width),) * 2 + (shape(8, 2 * width),)
    vectors = jnp.concatenate([gain, b_out, b_qkv])[None, :]
    attn, d_normed, *parts = pl.pallas_call(
        functools.partial(owner_kernel, near),
        out_shape=(shape(held, width), shape(held, width, dtype=F32)) + sums_shapes,
        in_specs=[VMEM, VMEM, ANY, ANY, VMEM],
        out_specs=(VMEM,) * (2 + len(sums_shapes)),
        scratch_shapes=[
            pltpu.VMEM(w_qkv.shape, w_qkv.dtype),
            pltpu.VMEM(w_out.shape, w_out.dtype),
            pltpu.VMEM((2 * width, 2 * width), F32),
            pltpu.VMEM((held, width), F32),
            pltpu.VMEM((held, width), F32),
            pltpu.SemaphoreType.DMA((2,)),
        ],
        compiler_params=LARGE,
    )(got, vectors, w_qkv, w_out, early)
    back, token = pl.pallas_call(
        rows_kernel,
        out_shape=(shape(held, 2 * width), shape(8, 128, dtype=F32)),
        in_specs=[VMEM] * 5,
        out_specs=(VMEM,) * 2,
        compiler_params=SMALL,
        cost_estimate=pl.CostEstimate(
            flops=64 * held * width * width, bytes_accessed=16 * held * width, transcendentals=0
        ),
    )(got, attn, d_normed, vectors, w_out)

    def give_back(back):
        return pl.pallas_call(
            return_kernel,
            out_shape=(shape(rows, width), shape(rows, width), shape(8, 128, dtype=F32)),
            in_specs=[VMEM] * 2,
            out_specs=(VMEM,) * 3,
            compiler_params=SMALL,
        )(pick, back)

    if near > 1:
        mine, theirs = parts

        def add(*pieces, after=(), flops=0):
            return pl.pallas_call(
                functools.partial(sum_kernel, len(pieces)),
                out_shape=half,
                in_specs=[VMEM] * (len(pieces) + len(after)),
                out_specs=VMEM,
                compiler_params=SMALL,
                cost_estimate=pl.CostEstimate(flops=flops, bytes_accessed=0, transcendentals=0),
            )(*pieces, *after)

        total = add(mine, swap(theirs, 1, devs), after=(token,))
        back = pl.pallas_call(
            tie_kernel,
            out_shape=back,
            in_specs=[ANY, VMEM],
            out_specs=ANY,
            input_output_aliases={0: 0},
            compiler_params=SMALL,
        )(back, total)
        back = exchange(back.reshape(devs, block_rows, 2 * width)).reshape(held, 2 * width)
        mixed, grad_points, token = give_back(back)
        total = add(total, swap(total, devs // 2, devs), flops=40_000_000_000)
        steps = [step for step in range(2, devs // 2, 2)]
        total = add(total, *(swap(total, step, devs) for step in steps))
        parts = [total, swap(total, 1, devs)]
        grad_gain, grad_wq, grad_bq, grad_wo, grad_bo = pl.pallas_call(
            weights_kernel,
            out_shape=tuple(
                shape(*dims, dtype=F32)
                for dims in ((width,), (width, 3 * width), (3 * width,), (width, width), (width,))
            ),
            in_specs=[VMEM] * 3,
            out_specs=(VMEM,) * 5,
            scratch_shapes=[pltpu.VMEM((2 * width, 2 * width), F32)],
            compiler_params=SMALL,
        )(*parts, token)
    else:
        left, right, sums = parts
        message = jnp.concatenate(
            [
                back.reshape(devs, block_rows, 2 * width),
                left.reshape(devs, share, 2 * width),
                right.reshape(devs, share, 2 * width),
                jnp.broadcast_to(sums[None], (devs, 8, 2 * width)),
            ],
            axis=1,
        )
        message = exchange(message)
        total = jnp.sum(message[:, block_rows:].astype(F32), axis=0)
        mine = total[: 2 * share].astype(BF16)
        both = exchange(jnp.broadcast_to(mine[None], (devs, 2 * share, 2 * width))).astype(F32)
        mixed, grad_points, _ = give_back(message[:, :block_rows].reshape(held, 2 * width))
        left = both[:, :share].reshape(width, 2 * width)
        right = both[:, share:].reshape(width, 2 * width)
        grad_wq = jnp.concatenate([left, right[:, :width]], axis=1)
        grad_wo = right[:, width:]
        flat = total[2 * share :].reshape(-1)
        grad_bq = flat[: 3 * width]
        grad_bo = flat[3 * width : 4 * width]
        grad_gain = flat[4 * width : 5 * width]

    return (mixed, grad_points, grad_gain, grad_wq, grad_bq, grad_wo, grad_bo)


def solution(mesh):
    placed = (
        P(("parts", "seq"), None),
        P(None, ("parts", "seq")),
        P(("parts", "seq")),
        P(("parts", "seq"), None),
        P(),
        P(),
        P(),
        P(),
        P(),
    )
    return jax.shard_map(
        local,
        mesh=mesh,
        in_specs=placed,
        out_specs=(
            P(("parts", "seq"), None),
            P(("parts", "seq"), None),
            P("parts"),
            P("parts", None),
            P("parts"),
            P("parts", None),
            P("parts"),
        ),
        check_vma=False,
    )
```

```python
import functools

import jax
import jax.numpy as jnp
from jax import lax
from jax.experimental import pallas as pl
from jax.experimental.pallas import tpu as pltpu
from jax.sharding import PartitionSpec as P

HEADS = 8
EPS = 1e-05
EMPTY = 64.0
MASKED = -1e30

F32 = jnp.float32
BF16 = jnp.bfloat16

VMEM = pl.BlockSpec(memory_space=pltpu.VMEM)
ANY = pl.BlockSpec(memory_space=pl.ANY)
SMEM = pl.BlockSpec(memory_space=pltpu.SMEM)
MIB = 1024 * 1024
LARGE = pltpu.CompilerParams(vmem_limit_bytes=32 * MIB)
SMALL = pltpu.CompilerParams(vmem_limit_bytes=8 * MIB)


def matmul(left, right, dims=((1,), (0,))):
    return lax.dot_general(left, right, (dims, ((), ())), preferred_element_type=F32)


def turned(index, devs):
    top = devs.bit_length() - 2
    place = 0
    for bit in range(top + 1):
        place = place + ((((index >> bit) & 1) ^ 1) << (top - bit))
    return place


def send_rows(route_ref, shape, axis, block_rows, devs):
    place = lax.broadcasted_iota(jnp.int32, shape, axis)
    target = jnp.zeros(shape, jnp.int32)
    for block in range(shape[axis] // block_rows):
        first = block * block_rows
        moved = turned(route_ref[0, block], devs) * block_rows + place - first
        target = jnp.where(place >= first, moved, target)
    return target


def scatter_kernel(block_rows, route_hbm, points_hbm, cot_hbm, out_ref, route_ref, points_ref, cot_ref, sems):
    copies = [
        pltpu.make_async_copy(source, target, sems.at[at])
        for at, (source, target) in enumerate(
            ((route_hbm, route_ref), (points_hbm, points_ref), (cot_hbm, cot_ref))
        )
    ]
    for copy in copies:
        copy.start()
    copies[0].wait()
    rows, width = points_ref.shape
    target = send_rows(route_ref, (1, rows), 1, block_rows, out_ref.shape[0] // block_rows)
    index = lax.broadcasted_iota(jnp.int32, (out_ref.shape[0], rows), 0)
    pick = jnp.where(index == target, 1.0, 0.0).astype(BF16)
    for copy in copies[1:]:
        copy.wait()
    ones = jnp.ones((rows, width), BF16)
    moved = matmul(pick, jnp.concatenate([points_ref[...], ones], axis=1))
    empty = (1.0 - moved[:, width:]) * EMPTY
    out_ref[:, :width] = (moved[:, :width] + empty).astype(BF16)
    out_ref[:, width:] = matmul(pick, cot_ref[...]).astype(BF16)


def normalize(points):
    centered = points - jnp.mean(points, axis=-1, keepdims=True)
    rstd = lax.rsqrt(jnp.mean(centered * centered, axis=-1, keepdims=True) + EPS)
    return centered * rstd, rstd


def owner_kernel(near, got_ref, vectors_ref, w_qkv_hbm, w_out_hbm, _, attn_ref, d_normed_ref, *refs):
    *outs, w_qkv_ref, w_out_ref, both_ref, d_keys_ref, d_values_ref, sems = refs
    copies = [
        pltpu.make_async_copy(w_qkv_hbm, w_qkv_ref, sems.at[0]),
        pltpu.make_async_copy(w_out_hbm, w_out_ref, sems.at[1]),
    ]
    for copy in copies:
        copy.start()
    rows = got_ref.shape[0]
    width = got_ref.shape[1] // 2
    head = width // HEADS
    scale = head ** (-0.5)
    gain = vectors_ref[:, :width]
    b_qkv = vectors_ref[:, 2 * width :]

    points = got_ref[:, :width].astype(F32)
    cot = got_ref[:, width:]
    xhat, _ = normalize(points)
    normed = (xhat * gain).astype(BF16)
    for copy in copies:
        copy.wait()
    w_qkv = w_qkv_ref[...]
    w_out = w_out_ref[...]
    qkv = (matmul(normed, w_qkv) + b_qkv).astype(BF16)
    query, keys, values = qkv[:, :width], qkv[:, width : 2 * width], qkv[:, 2 * width :]
    d_attn = matmul(cot, w_out, ((1,), (1,))).astype(BF16)
    d_attn_t = matmul(w_out, cot, ((1,), (1,))).astype(BF16)
    d_attn_s = (d_attn.astype(F32) * scale).astype(BF16)

    keys_t = keys.T
    values_t = values.T
    keys_s = (keys.astype(F32) * scale).astype(BF16)
    lane = lax.broadcasted_iota(jnp.int32, (rows, width), 1)
    hidden = jnp.where(points > EMPTY / 2, MASKED, 0.0).astype(BF16)
    query_x = jnp.concatenate([query, jnp.where(lane == 0, 1.0, 0.0).astype(BF16)], axis=1)

    def own(h, array):
        return jnp.where((lane >= h * head) & (lane < (h + 1) * head), array, 0)

    def scores_of(h):
        keys_x = jnp.concatenate([own(h, keys_s), hidden], axis=1)
        return matmul(keys_x, query_x, ((1,), (1,)))

    scores, probs, probs_b, d_probs, d_score = {}, {}, {}, {}, {}
    attn_t, dq_t = [], []
    scores[0] = scores_of(0)
    for step in range(HEADS + 2):
        if step + 1 < HEADS:
            scores[step + 1] = scores_of(step + 1)
        if step < HEADS:
            d_probs[step] = matmul(own(step, values), d_attn_s, ((1,), (1,)))
        if 1 <= step <= HEADS:
            lanes = slice((step - 1) * head, step * head)
            attn_t.append(matmul(values_t[lanes, :], probs_b[step - 1]))
        if step >= 2:
            h = step - 2
            lanes = slice(h * head, (h + 1) * head)
            d_values_ref[:, lanes] = matmul(probs_b[h], d_attn)[:, lanes]
            d_keys_ref[:, lanes] = matmul(d_score[h], query)[:, lanes]
            dq_t.append(matmul(keys_t[lanes, :], d_score[h]))
        if step < HEADS:
            now = scores.pop(step)
            expo = jnp.exp(now - jnp.max(now, axis=0, keepdims=True))
            probs[step] = expo * (1.0 / jnp.sum(expo, axis=0, keepdims=True))
            probs_b[step] = probs[step].astype(BF16)
        if 1 <= step <= HEADS:
            h = step - 1
            inner = attn_t[h] * d_attn_t[h * head : (h + 1) * head, :].astype(F32)
            inner = jnp.sum(inner, axis=0, keepdims=True) * scale
            d_score[h] = (probs.pop(h) * (d_probs.pop(h) - inner)).astype(BF16)

    attn_t = jnp.concatenate(attn_t, axis=0)
    attn_ref[...] = attn_t.T.astype(BF16)
    grad_w_out = matmul(attn_t.astype(BF16), cot)
    grad_b_out = jnp.sum(cot.astype(F32), axis=0, keepdims=True)

    d_query = jnp.concatenate(dq_t, axis=0).T
    d_qkv = jnp.concatenate([d_query, d_keys_ref[...], d_values_ref[...]], axis=1).astype(BF16)
    d_normed = matmul(d_qkv, w_qkv, ((1,), (1,)))
    grad_w_qkv = matmul(normed, d_qkv, ((0,), (0,)))
    grad_b_qkv = jnp.sum(d_qkv.astype(F32), axis=0, keepdims=True)
    grad_gain = jnp.sum(d_normed * xhat, axis=0, keepdims=True)
    d_normed_ref[...] = d_normed
    sums = jnp.concatenate(
        [
            grad_b_qkv[:, : 2 * width],
            jnp.concatenate([grad_b_qkv[:, 2 * width :], grad_b_out], axis=1),
            jnp.concatenate([grad_gain, jnp.zeros_like(grad_gain)], axis=1),
            jnp.zeros((5, 2 * width), F32),
        ],
        axis=0,
    )
    left = grad_w_qkv[:, : 2 * width]
    right = jnp.concatenate([grad_w_qkv[:, 2 * width :], grad_w_out], axis=1)
    if near == 1:
        left_ref, right_ref, sums_ref = outs
        left_ref[...] = left.astype(BF16)
        right_ref[...] = right.astype(BF16)
        sums_ref[...] = sums.astype(BF16)
        return
    mine_ref, theirs_ref = outs
    both_ref[:width] = left
    both_ref[width:] = right
    core = lax.axis_index("seq") & 1
    for half, half_ref in ((core, mine_ref), (core ^ 1, theirs_ref)):
        span = pl.ds(pl.multiple_of(half * width, width), width)
        half_ref[:width] = both_ref[span].astype(half_ref.dtype)
        half_ref[width:] = sums.astype(half_ref.dtype)


def rows_kernel(got_ref, attn_ref, d_normed_ref, vectors_ref, w_out_ref, back_ref, token_ref):
    token_ref[...] = jnp.zeros_like(token_ref)
    width = attn_ref.shape[1]
    gain = vectors_ref[:, :width]
    b_out = vectors_ref[:, width : 2 * width]
    points = got_ref[:, :width].astype(F32)
    cot = got_ref[:, width:].astype(F32)
    xhat, rstd = normalize(points)
    mixed = points + (matmul(attn_ref[...], w_out_ref[...]) + b_out)
    d_xhat = d_normed_ref[...] * gain
    inner = (
        d_xhat
        - jnp.mean(d_xhat, axis=-1, keepdims=True)
        - xhat * jnp.mean(d_xhat * xhat, axis=-1, keepdims=True)
    )
    back_ref[:, :width] = mixed.astype(BF16)
    back_ref[:, width:] = (cot + rstd * inner).astype(BF16)


def sum_kernel(count, *refs):
    piece_refs, out_ref = refs[:count], refs[-1]
    values = [piece_ref[...].astype(F32) for piece_ref in piece_refs]
    while len(values) > 1:
        values = [left + right for left, right in zip(values[::2], values[1::2])]
    out_ref[...] = values[0].astype(BF16)


def tie_kernel(rows_ref, other_ref, out_ref):
    pass


def pick_kernel(block_rows, route_hbm, pick_ref, token_ref, route_ref, sem):
    token_ref[...] = jnp.zeros_like(token_ref)
    copy = pltpu.make_async_copy(route_hbm, route_ref, sem)
    copy.start()
    copy.wait()
    rows, held = pick_ref.shape
    target = send_rows(route_ref, (rows, 1), 0, block_rows, held // block_rows)
    index = lax.broadcasted_iota(jnp.int32, pick_ref.shape, 1)
    pick_ref[...] = jnp.where(index == target, 1.0, 0.0).astype(BF16)


def return_kernel(pick_ref, back_ref, mixed_ref, grad_ref, token_ref):
    token_ref[...] = jnp.zeros_like(token_ref)
    width = mixed_ref.shape[1]
    moved = matmul(pick_ref[...], back_ref[...]).astype(BF16)
    mixed_ref[...] = moved[:, :width]
    grad_ref[...] = moved[:, width:]


def weights_kernel(*refs):
    *half_refs, _, gain_ref, w_qkv_ref, b_qkv_ref, w_out_ref, b_out_ref, both_ref = refs
    width = w_out_ref.shape[1]
    core = lax.axis_index("seq") & 1
    for step, half_ref in enumerate(half_refs):
        place = core ^ step
        half = half_ref[...].astype(F32)
        both_ref[pl.ds(pl.multiple_of(place * width, width), width)] = half[:width]

        @pl.when(place == 0)
        def _():
            sums = half[width:]
            gain_ref[...] = sums[2, :width]
            b_qkv_ref[: 2 * width] = sums[0]
            b_qkv_ref[2 * width :] = sums[1, :width]
            b_out_ref[...] = sums[1, width:]

    w_qkv_ref[:, : 2 * width] = both_ref[:width]
    w_qkv_ref[:, 2 * width :] = both_ref[width:, :width]
    w_out_ref[...] = both_ref[width:, width:]


def exchange(message):
    devs = message.shape[0]
    order = [turned(place, devs) for place in range(devs)]
    return lax.all_to_all(
        message, "seq", split_axis=0, concat_axis=0, axis_index_groups=[order], tiled=True
    )


def swap(piece, step, devs):
    return lax.ppermute(piece, "seq", [(dev, dev ^ step) for dev in range(devs)])


def local(points, route, owned, cotangent, gain, w_qkv, b_qkv, w_out, b_out):
    devs = lax.axis_size("seq")
    rows, width = points.shape
    block_rows = rows // route.shape[1]
    held = devs * block_rows
    share = width // devs
    near = 4 if devs == 16 and width % 64 == 0 else 1

    def shape(*dims, dtype=BF16):
        return jax.ShapeDtypeStruct(dims, dtype)

    sent = pl.pallas_call(
        functools.partial(scatter_kernel, block_rows),
        out_shape=shape(held, 2 * width),
        in_specs=[ANY] * 3,
        out_specs=VMEM,
        scratch_shapes=[
            pltpu.SMEM(route.shape, route.dtype),
            pltpu.VMEM(points.shape, points.dtype),
            pltpu.VMEM(cotangent.shape, cotangent.dtype),
            pltpu.SemaphoreType.DMA((3,)),
        ],
    )(route, points, cotangent)
    got = exchange(sent.reshape(devs, block_rows, 2 * width)).reshape(held, 2 * width)

    pick, early = pl.pallas_call(
        functools.partial(pick_kernel, block_rows),
        out_shape=(shape(rows, held), shape(8, 128, dtype=F32)),
        in_specs=[ANY],
        out_specs=(VMEM,) * 2,
        scratch_shapes=[pltpu.SMEM(route.shape, route.dtype), pltpu.SemaphoreType.DMA],
        compiler_params=SMALL,
    )(route)

    half = shape(width + 8, 2 * width)
    if near > 1:
        sums_shapes = (half, half)
    else:
        sums_shapes = (shape(width, 2 * width),) * 2 + (shape(8, 2 * width),)
    vectors = jnp.concatenate([gain, b_out, b_qkv])[None, :]
    attn, d_normed, *parts = pl.pallas_call(
        functools.partial(owner_kernel, near),
        out_shape=(shape(held, width), shape(held, width, dtype=F32)) + sums_shapes,
        in_specs=[VMEM, VMEM, ANY, ANY, VMEM],
        out_specs=(VMEM,) * (2 + len(sums_shapes)),
        scratch_shapes=[
            pltpu.VMEM(w_qkv.shape, w_qkv.dtype),
            pltpu.VMEM(w_out.shape, w_out.dtype),
            pltpu.VMEM((2 * width, 2 * width), F32),
            pltpu.VMEM((held, width), F32),
            pltpu.VMEM((held, width), F32),
            pltpu.SemaphoreType.DMA((2,)),
        ],
        compiler_params=LARGE,
    )(got, vectors, w_qkv, w_out, early)
    back, token = pl.pallas_call(
        rows_kernel,
        out_shape=(shape(held, 2 * width), shape(8, 128, dtype=F32)),
        in_specs=[VMEM] * 5,
        out_specs=(VMEM,) * 2,
        compiler_params=SMALL,
        cost_estimate=pl.CostEstimate(
            flops=64 * held * width * width, bytes_accessed=16 * held * width, transcendentals=0
        ),
    )(got, attn, d_normed, vectors, w_out)

    def give_back(back):
        return pl.pallas_call(
            return_kernel,
            out_shape=(shape(rows, width), shape(rows, width), shape(8, 128, dtype=F32)),
            in_specs=[VMEM] * 2,
            out_specs=(VMEM,) * 3,
            compiler_params=SMALL,
        )(pick, back)

    if near > 1:
        mine, theirs = parts

        def add(*pieces, after=(), flops=0):
            return pl.pallas_call(
                functools.partial(sum_kernel, len(pieces)),
                out_shape=half,
                in_specs=[VMEM] * (len(pieces) + len(after)),
                out_specs=VMEM,
                compiler_params=SMALL,
                cost_estimate=pl.CostEstimate(flops=flops, bytes_accessed=0, transcendentals=0),
            )(*pieces, *after)

        total = add(mine, swap(theirs, 1, devs), after=(token,))
        back = pl.pallas_call(
            tie_kernel,
            out_shape=back,
            in_specs=[ANY, VMEM],
            out_specs=ANY,
            input_output_aliases={0: 0},
            compiler_params=SMALL,
        )(back, total)
        back = exchange(back.reshape(devs, block_rows, 2 * width)).reshape(held, 2 * width)
        mixed, grad_points, token = give_back(back)
        total = add(total, swap(total, devs // 2, devs), flops=40_000_000_000)
        steps = [step for step in range(2, devs // 2, 2)]
        total = add(total, *(swap(total, step, devs) for step in steps))
        parts = [total, swap(total, 1, devs)]
        grad_gain, grad_wq, grad_bq, grad_wo, grad_bo = pl.pallas_call(
            weights_kernel,
            out_shape=tuple(
                shape(*dims, dtype=F32)
                for dims in ((width,), (width, 3 * width), (3 * width,), (width, width), (width,))
            ),
            in_specs=[VMEM] * 3,
            out_specs=(VMEM,) * 5,
            scratch_shapes=[pltpu.VMEM((2 * width, 2 * width), F32)],
            compiler_params=SMALL,
        )(*parts, token)
    else:
        left, right, sums = parts
        message = jnp.concatenate(
            [
                back.reshape(devs, block_rows, 2 * width),
                left.reshape(devs, share, 2 * width),
                right.reshape(devs, share, 2 * width),
                jnp.broadcast_to(sums[None], (devs, 8, 2 * width)),
            ],
            axis=1,
        )
        message = exchange(message)
        total = jnp.sum(message[:, block_rows:].astype(F32), axis=0)
        mine = total[: 2 * share].astype(BF16)
        both = exchange(jnp.broadcast_to(mine[None], (devs, 2 * share, 2 * width))).astype(F32)
        mixed, grad_points, _ = give_back(message[:, :block_rows].reshape(held, 2 * width))
        left = both[:, :share].reshape(width, 2 * width)
        right = both[:, share:].reshape(width, 2 * width)
        grad_wq = jnp.concatenate([left, right[:, :width]], axis=1)
        grad_wo = right[:, width:]
        flat = total[2 * share :].reshape(-1)
        grad_bq = flat[: 3 * width]
        grad_bo = flat[3 * width : 4 * width]
        grad_gain = flat[4 * width : 5 * width]

    return (mixed, grad_points, grad_gain, grad_wq, grad_bq, grad_wo, grad_bo)


def solution(mesh):
    placed = (
        P(("parts", "seq"), None),
        P(None, ("parts", "seq")),
        P(("parts", "seq")),
        P(("parts", "seq"), None),
        P(),
        P(),
        P(),
        P(),
        P(),
    )
    return jax.shard_map(
        local,
        mesh=mesh,
        in_specs=placed,
        out_specs=(
            P(("parts", "seq"), None),
            P(("parts", "seq"), None),
            P("parts"),
            P("parts", None),
            P("parts"),
            P("parts", None),
            P("parts"),
        ),
        check_vma=False,
    )
```

```python
import functools

import jax
import jax.numpy as jnp
from jax import lax
from jax.experimental import pallas as pl
from jax.experimental.pallas import tpu as pltpu
from jax.sharding import PartitionSpec as P

HEADS = 8
EPS = 1e-05
EMPTY = 64.0
MASKED = -1e30

F32 = jnp.float32
BF16 = jnp.bfloat16

VMEM = pl.BlockSpec(memory_space=pltpu.VMEM)
ANY = pl.BlockSpec(memory_space=pl.ANY)
SMEM = pl.BlockSpec(memory_space=pltpu.SMEM)
MIB = 1024 * 1024
LARGE = pltpu.CompilerParams(vmem_limit_bytes=32 * MIB)
SMALL = pltpu.CompilerParams(vmem_limit_bytes=8 * MIB)


def matmul(left, right, dims=((1,), (0,))):
    return lax.dot_general(left, right, (dims, ((), ())), preferred_element_type=F32)


def turned(index, devs):
    top = devs.bit_length() - 2
    place = 0
    for bit in range(top + 1):
        place = place + ((((index >> bit) & 1) ^ 1) << (top - bit))
    return place


def send_rows(route_ref, shape, axis, block_rows, devs):
    place = lax.broadcasted_iota(jnp.int32, shape, axis)
    target = jnp.zeros(shape, jnp.int32)
    for block in range(shape[axis] // block_rows):
        first = block * block_rows
        moved = turned(route_ref[0, block], devs) * block_rows + place - first
        target = jnp.where(place >= first, moved, target)
    return target


def scatter_kernel(block_rows, route_hbm, points_hbm, cot_hbm, out_hbm, *refs):
    route_ref, points_ref, cot_ref, points_out, cot_out, sems = refs
    copies = [
        pltpu.make_async_copy(source, target, sems.at[at])
        for at, (source, target) in enumerate(
            ((route_hbm, route_ref), (points_hbm, points_ref), (cot_hbm, cot_ref))
        )
    ]
    for copy in copies:
        copy.start()
    copies[0].wait()
    rows, width = points_ref.shape
    target = send_rows(route_ref, (1, rows), 1, block_rows, out_hbm.shape[0] // block_rows)
    index = lax.broadcasted_iota(jnp.int32, (out_hbm.shape[0], rows), 0)
    pick = jnp.where(index == target, 1.0, 0.0).astype(BF16)
    backs = [
        pltpu.make_async_copy(cot_out, out_hbm.at[:, width:], sems.at[3]),
        pltpu.make_async_copy(points_out, out_hbm.at[:, :width], sems.at[4]),
    ]
    copies[2].wait()
    cot_out[...] = matmul(pick, cot_ref[...]).astype(BF16)
    backs[0].start()
    copies[1].wait()
    ones = jnp.ones((rows, width), BF16)
    moved = matmul(pick, jnp.concatenate([points_ref[...], ones], axis=1))
    empty = (1.0 - moved[:, width:]) * EMPTY
    points_out[...] = (moved[:, :width] + empty).astype(BF16)
    backs[1].start()
    for back in backs:
        back.wait()


def normalize(points):
    centered = points - jnp.mean(points, axis=-1, keepdims=True)
    rstd = lax.rsqrt(jnp.mean(centered * centered, axis=-1, keepdims=True) + EPS)
    return centered * rstd, rstd


def owner_kernel(near, got_ref, vectors_ref, w_qkv_hbm, w_out_hbm, _, attn_ref, d_normed_ref, *refs):
    *outs, w_qkv_ref, w_out_ref, both_ref, d_keys_ref, d_values_ref, sems = refs
    copies = [
        pltpu.make_async_copy(w_qkv_hbm, w_qkv_ref, sems.at[0]),
        pltpu.make_async_copy(w_out_hbm, w_out_ref, sems.at[1]),
    ]
    for copy in copies:
        copy.start()
    rows = got_ref.shape[0]
    width = got_ref.shape[1] // 2
    head = width // HEADS
    scale = head ** (-0.5)
    gain = vectors_ref[:, :width]
    b_qkv = vectors_ref[:, 2 * width :]

    points = got_ref[:, :width].astype(F32)
    cot = got_ref[:, width:]
    xhat, _ = normalize(points)
    normed = (xhat * gain).astype(BF16)
    for copy in copies:
        copy.wait()
    w_qkv = w_qkv_ref[...]
    w_out = w_out_ref[...]
    qkv = (matmul(normed, w_qkv) + b_qkv).astype(BF16)
    query, keys, values = qkv[:, :width], qkv[:, width : 2 * width], qkv[:, 2 * width :]
    d_attn = matmul(cot, w_out, ((1,), (1,))).astype(BF16)
    d_attn_t = matmul(w_out, cot, ((1,), (1,))).astype(BF16)
    d_attn_s = (d_attn.astype(F32) * scale).astype(BF16)

    keys_t = keys.T
    values_t = values.T
    keys_s = (keys.astype(F32) * scale).astype(BF16)
    lane = lax.broadcasted_iota(jnp.int32, (rows, width), 1)
    hidden = jnp.where(points[:, :1] > EMPTY / 2, MASKED, 0.0)

    def own(h, array):
        return jnp.where((lane >= h * head) & (lane < (h + 1) * head), array, 0)

    def scores_of(h):
        return matmul(own(h, keys_s), query, ((1,), (1,))) + hidden

    scores, probs, probs_b, d_probs, d_score = {}, {}, {}, {}, {}
    attn_t, dq_t = [], []
    scores[0] = scores_of(0)
    for step in range(HEADS + 2):
        if step + 1 < HEADS:
            scores[step + 1] = scores_of(step + 1)
        if step < HEADS:
            d_probs[step] = matmul(own(step, values), d_attn_s, ((1,), (1,)))
        if 1 <= step <= HEADS:
            lanes = slice((step - 1) * head, step * head)
            attn_t.append(matmul(values_t[lanes, :], probs_b[step - 1]))
        if step >= 2:
            h = step - 2
            lanes = slice(h * head, (h + 1) * head)
            d_values_ref[:, lanes] = matmul(probs_b[h], d_attn)[:, lanes]
            d_keys_ref[:, lanes] = matmul(d_score[h], query)[:, lanes]
            dq_t.append(matmul(keys_t[lanes, :], d_score[h]))
        if step < HEADS:
            now = scores.pop(step)
            expo = jnp.exp(now - jnp.max(now, axis=0, keepdims=True))
            probs[step] = expo * (1.0 / jnp.sum(expo, axis=0, keepdims=True))
            probs_b[step] = probs[step].astype(BF16)
        if 1 <= step <= HEADS:
            h = step - 1
            inner = attn_t[h] * d_attn_t[h * head : (h + 1) * head, :].astype(F32)
            inner = jnp.sum(inner, axis=0, keepdims=True) * scale
            d_score[h] = (probs.pop(h) * (d_probs.pop(h) - inner)).astype(BF16)

    attn_t = jnp.concatenate(attn_t, axis=0)
    attn_ref[...] = attn_t.T.astype(BF16)
    grad_w_out = matmul(attn_t.astype(BF16), cot)
    grad_b_out = jnp.sum(cot.astype(F32), axis=0, keepdims=True)

    d_query = jnp.concatenate(dq_t, axis=0).T
    d_qkv = jnp.concatenate([d_query, d_keys_ref[...], d_values_ref[...]], axis=1).astype(BF16)
    d_normed = matmul(d_qkv, w_qkv, ((1,), (1,)))
    grad_w_qkv = matmul(normed, d_qkv, ((0,), (0,)))
    grad_b_qkv = jnp.sum(d_qkv.astype(F32), axis=0, keepdims=True)
    grad_gain = jnp.sum(d_normed * xhat, axis=0, keepdims=True)
    d_normed_ref[...] = d_normed
    sums = jnp.concatenate(
        [
            grad_b_qkv[:, : 2 * width],
            jnp.concatenate([grad_b_qkv[:, 2 * width :], grad_b_out], axis=1),
            jnp.concatenate([grad_gain, jnp.zeros_like(grad_gain)], axis=1),
            jnp.zeros((5, 2 * width), F32),
        ],
        axis=0,
    )
    left = grad_w_qkv[:, : 2 * width]
    right = jnp.concatenate([grad_w_qkv[:, 2 * width :], grad_w_out], axis=1)
    if near == 1:
        left_ref, right_ref, sums_ref = outs
        left_ref[...] = left.astype(BF16)
        right_ref[...] = right.astype(BF16)
        sums_ref[...] = sums.astype(BF16)
        return
    mine_ref, theirs_ref = outs
    both_ref[:width] = left
    both_ref[width:] = right
    core = lax.axis_index("seq") & 1
    for half, half_ref in ((core, mine_ref), (core ^ 1, theirs_ref)):
        span = pl.ds(pl.multiple_of(half * width, width), width)
        half_ref[:width] = both_ref[span].astype(half_ref.dtype)
        half_ref[width:] = sums.astype(half_ref.dtype)


def rows_kernel(got_ref, attn_ref, d_normed_ref, vectors_ref, w_out_ref, back_ref, token_ref):
    token_ref[...] = jnp.zeros_like(token_ref)
    width = attn_ref.shape[1]
    gain = vectors_ref[:, :width]
    b_out = vectors_ref[:, width : 2 * width]
    points = got_ref[:, :width].astype(F32)
    cot = got_ref[:, width:].astype(F32)
    xhat, rstd = normalize(points)
    mixed = points + (matmul(attn_ref[...], w_out_ref[...]) + b_out)
    d_xhat = d_normed_ref[...] * gain
    inner = (
        d_xhat
        - jnp.mean(d_xhat, axis=-1, keepdims=True)
        - xhat * jnp.mean(d_xhat * xhat, axis=-1, keepdims=True)
    )
    back_ref[:, :width] = mixed.astype(BF16)
    back_ref[:, width:] = (cot + rstd * inner).astype(BF16)


def sum_kernel(count, *refs):
    piece_refs, out_ref = refs[:count], refs[-1]
    values = [piece_ref[...].astype(F32) for piece_ref in piece_refs]
    while len(values) > 1:
        values = [left + right for left, right in zip(values[::2], values[1::2])]
    out_ref[...] = values[0].astype(BF16)


def tie_kernel(rows_ref, other_ref, out_ref):
    pass


def pick_kernel(block_rows, route_hbm, pick_ref, token_ref, route_ref, sem):
    token_ref[...] = jnp.zeros_like(token_ref)
    copy = pltpu.make_async_copy(route_hbm, route_ref, sem)
    copy.start()
    copy.wait()
    rows, held = pick_ref.shape
    target = send_rows(route_ref, (rows, 1), 0, block_rows, held // block_rows)
    index = lax.broadcasted_iota(jnp.int32, pick_ref.shape, 1)
    pick_ref[...] = jnp.where(index == target, 1.0, 0.0).astype(BF16)


def return_kernel(pick_ref, back_ref, mixed_ref, grad_ref, token_ref):
    token_ref[...] = jnp.zeros_like(token_ref)
    width = mixed_ref.shape[1]
    moved = matmul(pick_ref[...], back_ref[...]).astype(BF16)
    mixed_ref[...] = moved[:, :width]
    grad_ref[...] = moved[:, width:]


def weights_kernel(*refs):
    *half_refs, _, gain_ref, w_qkv_ref, b_qkv_ref, w_out_ref, b_out_ref, both_ref = refs
    width = w_out_ref.shape[1]
    core = lax.axis_index("seq") & 1
    for step, half_ref in enumerate(half_refs):
        place = core ^ step
        half = half_ref[...].astype(F32)
        both_ref[pl.ds(pl.multiple_of(place * width, width), width)] = half[:width]

        @pl.when(place == 0)
        def _():
            sums = half[width:]
            gain_ref[...] = sums[2, :width]
            b_qkv_ref[: 2 * width] = sums[0]
            b_qkv_ref[2 * width :] = sums[1, :width]
            b_out_ref[...] = sums[1, width:]

    w_qkv_ref[:, : 2 * width] = both_ref[:width]
    w_qkv_ref[:, 2 * width :] = both_ref[width:, :width]
    w_out_ref[...] = both_ref[width:, width:]


def exchange(message):
    devs = message.shape[0]
    order = [turned(place, devs) for place in range(devs)]
    return lax.all_to_all(
        message, "seq", split_axis=0, concat_axis=0, axis_index_groups=[order], tiled=True
    )


def swap(piece, step, devs):
    return lax.ppermute(piece, "seq", [(dev, dev ^ step) for dev in range(devs)])


def local(points, route, owned, cotangent, gain, w_qkv, b_qkv, w_out, b_out):
    devs = lax.axis_size("seq")
    rows, width = points.shape
    block_rows = rows // route.shape[1]
    held = devs * block_rows
    share = width // devs
    near = 4 if devs == 16 and width % 64 == 0 else 1

    def shape(*dims, dtype=BF16):
        return jax.ShapeDtypeStruct(dims, dtype)

    sent = pl.pallas_call(
        functools.partial(scatter_kernel, block_rows),
        out_shape=shape(held, 2 * width),
        in_specs=[ANY] * 3,
        out_specs=ANY,
        scratch_shapes=[
            pltpu.SMEM(route.shape, route.dtype),
            pltpu.VMEM(points.shape, points.dtype),
            pltpu.VMEM(cotangent.shape, cotangent.dtype),
            pltpu.VMEM((held, width), BF16),
            pltpu.VMEM((held, width), BF16),
            pltpu.SemaphoreType.DMA((5,)),
        ],
    )(route, points, cotangent)
    got = exchange(sent.reshape(devs, block_rows, 2 * width)).reshape(held, 2 * width)

    pick, early = pl.pallas_call(
        functools.partial(pick_kernel, block_rows),
        out_shape=(shape(rows, held), shape(8, 128, dtype=F32)),
        in_specs=[ANY],
        out_specs=(VMEM,) * 2,
        scratch_shapes=[pltpu.SMEM(route.shape, route.dtype), pltpu.SemaphoreType.DMA],
        compiler_params=SMALL,
    )(route)

    half = shape(width + 8, 2 * width)
    if near > 1:
        sums_shapes = (half, half)
    else:
        sums_shapes = (shape(width, 2 * width),) * 2 + (shape(8, 2 * width),)
    vectors = jnp.concatenate([gain, b_out, b_qkv])[None, :]
    attn, d_normed, *parts = pl.pallas_call(
        functools.partial(owner_kernel, near),
        out_shape=(shape(held, width), shape(held, width, dtype=F32)) + sums_shapes,
        in_specs=[VMEM, VMEM, ANY, ANY, VMEM],
        out_specs=(VMEM,) * (2 + len(sums_shapes)),
        scratch_shapes=[
            pltpu.VMEM(w_qkv.shape, w_qkv.dtype),
            pltpu.VMEM(w_out.shape, w_out.dtype),
            pltpu.VMEM((2 * width, 2 * width), F32),
            pltpu.VMEM((held, width), F32),
            pltpu.VMEM((held, width), F32),
            pltpu.SemaphoreType.DMA((2,)),
        ],
        compiler_params=LARGE,
    )(got, vectors, w_qkv, w_out, early)
    back, token = pl.pallas_call(
        rows_kernel,
        out_shape=(shape(held, 2 * width), shape(8, 128, dtype=F32)),
        in_specs=[VMEM] * 5,
        out_specs=(VMEM,) * 2,
        compiler_params=SMALL,
        cost_estimate=pl.CostEstimate(
            flops=64 * held * width * width, bytes_accessed=16 * held * width, transcendentals=0
        ),
    )(got, attn, d_normed, vectors, w_out)

    def give_back(back):
        return pl.pallas_call(
            return_kernel,
            out_shape=(shape(rows, width), shape(rows, width), shape(8, 128, dtype=F32)),
            in_specs=[VMEM] * 2,
            out_specs=(VMEM,) * 3,
            compiler_params=SMALL,
        )(pick, back)

    if near > 1:
        mine, theirs = parts

        def add(*pieces, after=(), flops=0):
            return pl.pallas_call(
                functools.partial(sum_kernel, len(pieces)),
                out_shape=half,
                in_specs=[VMEM] * (len(pieces) + len(after)),
                out_specs=VMEM,
                compiler_params=SMALL,
                cost_estimate=pl.CostEstimate(flops=flops, bytes_accessed=0, transcendentals=0),
            )(*pieces, *after)

        total = add(mine, swap(theirs, 1, devs), after=(token,))
        back = pl.pallas_call(
            tie_kernel,
            out_shape=back,
            in_specs=[ANY, VMEM],
            out_specs=ANY,
            input_output_aliases={0: 0},
            compiler_params=SMALL,
        )(back, total)
        back = exchange(back.reshape(devs, block_rows, 2 * width)).reshape(held, 2 * width)
        mixed, grad_points, token = give_back(back)
        total = add(total, swap(total, devs // 2, devs), flops=40_000_000_000)
        steps = [step for step in range(2, devs // 2, 2)]
        total = add(total, *(swap(total, step, devs) for step in steps))
        parts = [total, swap(total, 1, devs)]
        grad_gain, grad_wq, grad_bq, grad_wo, grad_bo = pl.pallas_call(
            weights_kernel,
            out_shape=tuple(
                shape(*dims, dtype=F32)
                for dims in ((width,), (width, 3 * width), (3 * width,), (width, width), (width,))
            ),
            in_specs=[VMEM] * 3,
            out_specs=(VMEM,) * 5,
            scratch_shapes=[pltpu.VMEM((2 * width, 2 * width), F32)],
            compiler_params=SMALL,
        )(*parts, token)
    else:
        left, right, sums = parts
        message = jnp.concatenate(
            [
                back.reshape(devs, block_rows, 2 * width),
                left.reshape(devs, share, 2 * width),
                right.reshape(devs, share, 2 * width),
                jnp.broadcast_to(sums[None], (devs, 8, 2 * width)),
            ],
            axis=1,
        )
        message = exchange(message)
        total = jnp.sum(message[:, block_rows:].astype(F32), axis=0)
        mine = total[: 2 * share].astype(BF16)
        both = exchange(jnp.broadcast_to(mine[None], (devs, 2 * share, 2 * width))).astype(F32)
        mixed, grad_points, _ = give_back(message[:, :block_rows].reshape(held, 2 * width))
        left = both[:, :share].reshape(width, 2 * width)
        right = both[:, share:].reshape(width, 2 * width)
        grad_wq = jnp.concatenate([left, right[:, :width]], axis=1)
        grad_wo = right[:, width:]
        flat = total[2 * share :].reshape(-1)
        grad_bq = flat[: 3 * width]
        grad_bo = flat[3 * width : 4 * width]
        grad_gain = flat[4 * width : 5 * width]

    return (mixed, grad_points, grad_gain, grad_wq, grad_bq, grad_wo, grad_bo)


def solution(mesh):
    placed = (
        P(("parts", "seq"), None),
        P(None, ("parts", "seq")),
        P(("parts", "seq")),
        P(("parts", "seq"), None),
        P(),
        P(),
        P(),
        P(),
        P(),
    )
    return jax.shard_map(
        local,
        mesh=mesh,
        in_specs=placed,
        out_specs=(
            P(("parts", "seq"), None),
            P(("parts", "seq"), None),
            P("parts"),
            P("parts", None),
            P("parts"),
            P("parts", None),
            P("parts"),
        ),
        check_vma=False,
    )
```

```python
import functools

import jax
import jax.numpy as jnp
from jax import lax
from jax.experimental import pallas as pl
from jax.experimental.pallas import tpu as pltpu
from jax.sharding import PartitionSpec as P

HEADS = 8
EPS = 1e-05
EMPTY = 64.0
MASKED = -1e30

F32 = jnp.float32
BF16 = jnp.bfloat16

VMEM = pl.BlockSpec(memory_space=pltpu.VMEM)
ANY = pl.BlockSpec(memory_space=pl.ANY)
SMEM = pl.BlockSpec(memory_space=pltpu.SMEM)
MIB = 1024 * 1024
LARGE = pltpu.CompilerParams(vmem_limit_bytes=32 * MIB)
SMALL = pltpu.CompilerParams(vmem_limit_bytes=8 * MIB)


def matmul(left, right, dims=((1,), (0,))):
    return lax.dot_general(left, right, (dims, ((), ())), preferred_element_type=F32)


def turned(index, devs):
    top = devs.bit_length() - 2
    place = 0
    for bit in range(top + 1):
        place = place + (((index >> bit) & 1) << (top - bit))
    return place


def send_rows(route_ref, shape, axis, block_rows, devs, flip=0):
    place = lax.broadcasted_iota(jnp.int32, shape, axis)
    target = jnp.zeros(shape, jnp.int32)
    for block in range(shape[axis] // block_rows):
        first = block * block_rows
        moved = (turned(route_ref[0, block], devs) ^ flip) * block_rows + place - first
        target = jnp.where(place >= first, moved, target)
    return target


def scatter_kernel(block_rows, flip, route_hbm, points_hbm, cot_hbm, out_ref, route_ref, points_ref, cot_ref, sems):
    copies = [
        pltpu.make_async_copy(source, target, sems.at[at])
        for at, (source, target) in enumerate(
            ((route_hbm, route_ref), (points_hbm, points_ref), (cot_hbm, cot_ref))
        )
    ]
    for copy in copies:
        copy.start()
    copies[0].wait()
    rows, width = points_ref.shape
    devs = out_ref.shape[0] // block_rows
    target = send_rows(route_ref, (1, rows), 1, block_rows, devs, flip)
    index = lax.broadcasted_iota(jnp.int32, (out_ref.shape[0], rows), 0)
    pick = jnp.where(index == target, 1.0, 0.0).astype(BF16)
    for copy in copies[1:]:
        copy.wait()
    ones = jnp.ones((rows, width), BF16)
    moved = matmul(pick, jnp.concatenate([points_ref[...], ones], axis=1))
    empty = (1.0 - moved[:, width:]) * EMPTY
    out_ref[:, :width] = (moved[:, :width] + empty).astype(BF16)
    out_ref[:, width:] = matmul(pick, cot_ref[...]).astype(BF16)


def normalize(points):
    centered = points - jnp.mean(points, axis=-1, keepdims=True)
    rstd = lax.rsqrt(jnp.mean(centered * centered, axis=-1, keepdims=True) + EPS)
    return centered * rstd, rstd


def owner_kernel(near, got_ref, vectors_ref, w_qkv_hbm, w_out_hbm, _, attn_ref, d_normed_ref, *refs):
    *outs, w_qkv_ref, w_out_ref, both_ref, d_keys_ref, d_values_ref, sems = refs
    copies = [
        pltpu.make_async_copy(w_qkv_hbm, w_qkv_ref, sems.at[0]),
        pltpu.make_async_copy(w_out_hbm, w_out_ref, sems.at[1]),
    ]
    for copy in copies:
        copy.start()
    rows = got_ref.shape[0]
    width = got_ref.shape[1] // 2
    head = width // HEADS
    scale = head ** (-0.5)
    gain = vectors_ref[:, :width]
    b_qkv = vectors_ref[:, 2 * width :]

    points = got_ref[:, :width].astype(F32)
    cot = got_ref[:, width:]
    xhat, _ = normalize(points)
    normed = (xhat * gain).astype(BF16)
    for copy in copies:
        copy.wait()
    w_qkv = w_qkv_ref[...]
    w_out = w_out_ref[...]
    qkv = (matmul(normed, w_qkv) + b_qkv).astype(BF16)
    query, keys, values = qkv[:, :width], qkv[:, width : 2 * width], qkv[:, 2 * width :]
    d_attn = matmul(cot, w_out, ((1,), (1,))).astype(BF16)
    d_attn_t = matmul(w_out, cot, ((1,), (1,))).astype(BF16)
    d_attn_s = (d_attn.astype(F32) * scale).astype(BF16)

    keys_t = keys.T
    values_t = values.T
    keys_s = (keys.astype(F32) * scale).astype(BF16)
    lane = lax.broadcasted_iota(jnp.int32, (rows, width), 1)
    hidden = jnp.where(points[:, :1] > EMPTY / 2, MASKED, 0.0)

    def own(h, array):
        return jnp.where((lane >= h * head) & (lane < (h + 1) * head), array, 0)

    def scores_of(h):
        return matmul(own(h, keys_s), query, ((1,), (1,))) + hidden

    scores, probs, probs_b, d_probs, d_score = {}, {}, {}, {}, {}
    attn_t, dq_t = [], []
    scores[0] = scores_of(0)
    for step in range(HEADS + 2):
        if step + 1 < HEADS:
            scores[step + 1] = scores_of(step + 1)
        if step < HEADS:
            d_probs[step] = matmul(own(step, values), d_attn_s, ((1,), (1,)))
        if 1 <= step <= HEADS:
            lanes = slice((step - 1) * head, step * head)
            attn_t.append(matmul(values_t[lanes, :], probs_b[step - 1]))
        if step >= 2:
            h = step - 2
            lanes = slice(h * head, (h + 1) * head)
            d_values_ref[:, lanes] = matmul(probs_b[h], d_attn)[:, lanes]
            d_keys_ref[:, lanes] = matmul(d_score[h], query)[:, lanes]
            dq_t.append(matmul(keys_t[lanes, :], d_score[h]))
        if step < HEADS:
            now = scores.pop(step)
            expo = jnp.exp(now - jnp.max(now, axis=0, keepdims=True))
            probs[step] = expo * (1.0 / jnp.sum(expo, axis=0, keepdims=True))
            probs_b[step] = probs[step].astype(BF16)
        if 1 <= step <= HEADS:
            h = step - 1
            inner = attn_t[h] * d_attn_t[h * head : (h + 1) * head, :].astype(F32)
            inner = jnp.sum(inner, axis=0, keepdims=True) * scale
            d_score[h] = (probs.pop(h) * (d_probs.pop(h) - inner)).astype(BF16)

    attn_t = jnp.concatenate(attn_t, axis=0)
    attn_ref[...] = attn_t.T.astype(BF16)
    grad_w_out = matmul(attn_t.astype(BF16), cot)
    grad_b_out = jnp.sum(cot.astype(F32), axis=0, keepdims=True)

    d_query = jnp.concatenate(dq_t, axis=0).T
    d_qkv = jnp.concatenate([d_query, d_keys_ref[...], d_values_ref[...]], axis=1).astype(BF16)
    d_normed = matmul(d_qkv, w_qkv, ((1,), (1,)))
    grad_w_qkv = matmul(normed, d_qkv, ((0,), (0,)))
    grad_b_qkv = jnp.sum(d_qkv.astype(F32), axis=0, keepdims=True)
    grad_gain = jnp.sum(d_normed * xhat, axis=0, keepdims=True)
    d_normed_ref[...] = d_normed
    sums = jnp.concatenate(
        [
            grad_b_qkv[:, : 2 * width],
            jnp.concatenate([grad_b_qkv[:, 2 * width :], grad_b_out], axis=1),
            jnp.concatenate([grad_gain, jnp.zeros_like(grad_gain)], axis=1),
            jnp.zeros((5, 2 * width), F32),
        ],
        axis=0,
    )
    left = grad_w_qkv[:, : 2 * width]
    right = jnp.concatenate([grad_w_qkv[:, 2 * width :], grad_w_out], axis=1)
    if near == 1:
        left_ref, right_ref, sums_ref = outs
        left_ref[...] = left.astype(BF16)
        right_ref[...] = right.astype(BF16)
        sums_ref[...] = sums.astype(BF16)
        return
    mine_ref, theirs_ref = outs
    both_ref[:width] = left
    both_ref[width:] = right
    core = lax.axis_index("seq") & 1
    for half, half_ref in ((core, mine_ref), (core ^ 1, theirs_ref)):
        span = pl.ds(pl.multiple_of(half * width, width), width)
        half_ref[:width] = both_ref[span].astype(half_ref.dtype)
        half_ref[width:] = sums.astype(half_ref.dtype)


def rows_kernel(blocks, got_ref, attn_ref, d_normed_ref, vectors_ref, w_out_ref, back_ref, token_ref):
    token_ref[...] = jnp.zeros_like(token_ref)
    width = attn_ref.shape[1]
    gain = vectors_ref[:, :width]
    b_out = vectors_ref[:, width : 2 * width]
    points = got_ref[:, :width].astype(F32)
    cot = got_ref[:, width:].astype(F32)
    xhat, rstd = normalize(points)
    mixed = points + (matmul(attn_ref[...], w_out_ref[...]) + b_out)
    d_xhat = d_normed_ref[...] * gain
    inner = (
        d_xhat
        - jnp.mean(d_xhat, axis=-1, keepdims=True)
        - xhat * jnp.mean(d_xhat * xhat, axis=-1, keepdims=True)
    )
    both = jnp.concatenate([mixed.astype(BF16), (cot + rstd * inner).astype(BF16)], axis=1)
    rows = both.shape[0] // blocks
    for block in range(blocks):
        end = (blocks - block) * rows
        back_ref[end - rows : end] = both[block * rows : (block + 1) * rows]


def sum_kernel(count, *refs):
    piece_refs, out_ref = refs[:count], refs[-1]
    values = [piece_ref[...].astype(F32) for piece_ref in piece_refs]
    while len(values) > 1:
        values = [left + right for left, right in zip(values[::2], values[1::2])]
    out_ref[...] = values[0].astype(BF16)


def tie_kernel(rows_ref, other_ref, out_ref):
    pass


def pick_kernel(block_rows, route_hbm, pick_ref, token_ref, route_ref, sem):
    token_ref[...] = jnp.zeros_like(token_ref)
    copy = pltpu.make_async_copy(route_hbm, route_ref, sem)
    copy.start()
    copy.wait()
    rows, held = pick_ref.shape
    target = send_rows(route_ref, (rows, 1), 0, block_rows, held // block_rows)
    index = lax.broadcasted_iota(jnp.int32, pick_ref.shape, 1)
    pick_ref[...] = jnp.where(index == target, 1.0, 0.0).astype(BF16)


def return_kernel(pick_ref, back_ref, mixed_ref, grad_ref, token_ref):
    token_ref[...] = jnp.zeros_like(token_ref)
    width = mixed_ref.shape[1]
    moved = matmul(pick_ref[...], back_ref[...]).astype(BF16)
    mixed_ref[...] = moved[:, :width]
    grad_ref[...] = moved[:, width:]


def weights_kernel(*refs):
    *half_refs, _, gain_ref, w_qkv_ref, b_qkv_ref, w_out_ref, b_out_ref, both_ref = refs
    width = w_out_ref.shape[1]
    core = lax.axis_index("seq") & 1
    for step, half_ref in enumerate(half_refs):
        place = core ^ step
        half = half_ref[...].astype(F32)
        both_ref[pl.ds(pl.multiple_of(place * width, width), width)] = half[:width]

        @pl.when(place == 0)
        def _():
            sums = half[width:]
            gain_ref[...] = sums[2, :width]
            b_qkv_ref[: 2 * width] = sums[0]
            b_qkv_ref[2 * width :] = sums[1, :width]
            b_out_ref[...] = sums[1, width:]

    w_qkv_ref[:, : 2 * width] = both_ref[:width]
    w_qkv_ref[:, 2 * width :] = both_ref[width:, :width]
    w_out_ref[...] = both_ref[width:, width:]


def exchange(message, flip=0):
    devs = message.shape[0]
    order = [turned(place ^ flip, devs) for place in range(devs)]
    return lax.all_to_all(
        message, "seq", split_axis=0, concat_axis=0, axis_index_groups=[order], tiled=True
    )


def swap(piece, step, devs):
    return lax.ppermute(piece, "seq", [(dev, dev ^ step) for dev in range(devs)])


def local(points, route, owned, cotangent, gain, w_qkv, b_qkv, w_out, b_out):
    devs = lax.axis_size("seq")
    rows, width = points.shape
    block_rows = rows // route.shape[1]
    held = devs * block_rows
    share = width // devs
    near = 4 if devs == 16 and width % 64 == 0 else 1
    flip = devs - 1 if near > 1 else 0

    def shape(*dims, dtype=BF16):
        return jax.ShapeDtypeStruct(dims, dtype)

    sent = pl.pallas_call(
        functools.partial(scatter_kernel, block_rows, flip),
        out_shape=shape(held, 2 * width),
        in_specs=[ANY] * 3,
        out_specs=VMEM,
        scratch_shapes=[
            pltpu.SMEM(route.shape, route.dtype),
            pltpu.VMEM(points.shape, points.dtype),
            pltpu.VMEM(cotangent.shape, cotangent.dtype),
            pltpu.SemaphoreType.DMA((3,)),
        ],
    )(route, points, cotangent)
    got = exchange(sent.reshape(devs, block_rows, 2 * width), flip).reshape(held, 2 * width)

    pick, early = pl.pallas_call(
        functools.partial(pick_kernel, block_rows),
        out_shape=(shape(rows, held), shape(8, 128, dtype=F32)),
        in_specs=[ANY],
        out_specs=(VMEM,) * 2,
        scratch_shapes=[pltpu.SMEM(route.shape, route.dtype), pltpu.SemaphoreType.DMA],
        compiler_params=SMALL,
    )(route)

    half = shape(width + 8, 2 * width)
    if near > 1:
        sums_shapes = (half, half)
    else:
        sums_shapes = (shape(width, 2 * width),) * 2 + (shape(8, 2 * width),)
    vectors = jnp.concatenate([gain, b_out, b_qkv])[None, :]
    attn, d_normed, *parts = pl.pallas_call(
        functools.partial(owner_kernel, near),
        out_shape=(shape(held, width), shape(held, width, dtype=F32)) + sums_shapes,
        in_specs=[VMEM, VMEM, ANY, ANY, VMEM],
        out_specs=(VMEM,) * (2 + len(sums_shapes)),
        scratch_shapes=[
            pltpu.VMEM(w_qkv.shape, w_qkv.dtype),
            pltpu.VMEM(w_out.shape, w_out.dtype),
            pltpu.VMEM((2 * width, 2 * width), F32),
            pltpu.VMEM((held, width), F32),
            pltpu.VMEM((held, width), F32),
            pltpu.SemaphoreType.DMA((2,)),
        ],
        compiler_params=LARGE,
    )(got, vectors, w_qkv, w_out, early)
    back, token = pl.pallas_call(
        functools.partial(rows_kernel, devs if flip else 1),
        out_shape=(shape(held, 2 * width), shape(8, 128, dtype=F32)),
        in_specs=[VMEM] * 5,
        out_specs=(VMEM,) * 2,
        compiler_params=SMALL,
        cost_estimate=pl.CostEstimate(
            flops=64 * held * width * width, bytes_accessed=16 * held * width, transcendentals=0
        ),
    )(got, attn, d_normed, vectors, w_out)

    def give_back(back):
        return pl.pallas_call(
            return_kernel,
            out_shape=(shape(rows, width), shape(rows, width), shape(8, 128, dtype=F32)),
            in_specs=[VMEM] * 2,
            out_specs=(VMEM,) * 3,
            compiler_params=SMALL,
        )(pick, back)

    if near > 1:
        mine, theirs = parts

        def add(*pieces, after=(), flops=0):
            return pl.pallas_call(
                functools.partial(sum_kernel, len(pieces)),
                out_shape=half,
                in_specs=[VMEM] * (len(pieces) + len(after)),
                out_specs=VMEM,
                compiler_params=SMALL,
                cost_estimate=pl.CostEstimate(flops=flops, bytes_accessed=0, transcendentals=0),
            )(*pieces, *after)

        total = add(mine, swap(theirs, 1, devs), after=(token,))
        back = pl.pallas_call(
            tie_kernel,
            out_shape=back,
            in_specs=[ANY, VMEM],
            out_specs=ANY,
            input_output_aliases={0: 0},
            compiler_params=SMALL,
        )(back, total)
        back = exchange(back.reshape(devs, block_rows, 2 * width)).reshape(held, 2 * width)
        mixed, grad_points, token = give_back(back)
        total = add(total, swap(total, devs // 2, devs), flops=40_000_000_000)
        steps = [step for step in range(2, devs // 2, 2)]
        total = add(total, *(swap(total, step, devs) for step in steps))
        parts = [total, swap(total, 1, devs)]
        grad_gain, grad_wq, grad_bq, grad_wo, grad_bo = pl.pallas_call(
            weights_kernel,
            out_shape=tuple(
                shape(*dims, dtype=F32)
                for dims in ((width,), (width, 3 * width), (3 * width,), (width, width), (width,))
            ),
            in_specs=[VMEM] * 3,
            out_specs=(VMEM,) * 5,
            scratch_shapes=[pltpu.VMEM((2 * width, 2 * width), F32)],
            compiler_params=SMALL,
        )(*parts, token)
    else:
        left, right, sums = parts
        message = jnp.concatenate(
            [
                back.reshape(devs, block_rows, 2 * width),
                left.reshape(devs, share, 2 * width),
                right.reshape(devs, share, 2 * width),
                jnp.broadcast_to(sums[None], (devs, 8, 2 * width)),
            ],
            axis=1,
        )
        message = exchange(message)
        total = jnp.sum(message[:, block_rows:].astype(F32), axis=0)
        mine = total[: 2 * share].astype(BF16)
        both = exchange(jnp.broadcast_to(mine[None], (devs, 2 * share, 2 * width))).astype(F32)
        mixed, grad_points, _ = give_back(message[:, :block_rows].reshape(held, 2 * width))
        left = both[:, :share].reshape(width, 2 * width)
        right = both[:, share:].reshape(width, 2 * width)
        grad_wq = jnp.concatenate([left, right[:, :width]], axis=1)
        grad_wo = right[:, width:]
        flat = total[2 * share :].reshape(-1)
        grad_bq = flat[: 3 * width]
        grad_bo = flat[3 * width : 4 * width]
        grad_gain = flat[4 * width : 5 * width]

    return (mixed, grad_points, grad_gain, grad_wq, grad_bq, grad_wo, grad_bo)


def solution(mesh):
    placed = (
        P(("parts", "seq"), None),
        P(None, ("parts", "seq")),
        P(("parts", "seq")),
        P(("parts", "seq"), None),
        P(),
        P(),
        P(),
        P(),
        P(),
    )
    return jax.shard_map(
        local,
        mesh=mesh,
        in_specs=placed,
        out_specs=(
            P(("parts", "seq"), None),
            P(("parts", "seq"), None),
            P("parts"),
            P("parts", None),
            P("parts"),
            P("parts", None),
            P("parts"),
        ),
        check_vma=False,
    )
```

```python
import functools

import jax
import jax.numpy as jnp
from jax import lax
from jax.experimental import pallas as pl
from jax.experimental.pallas import tpu as pltpu
from jax.sharding import PartitionSpec as P

HEADS = 8
EPS = 1e-05
EMPTY = 64.0
MASKED = -1e30

F32 = jnp.float32
BF16 = jnp.bfloat16

VMEM = pl.BlockSpec(memory_space=pltpu.VMEM)
ANY = pl.BlockSpec(memory_space=pl.ANY)
SMEM = pl.BlockSpec(memory_space=pltpu.SMEM)
MIB = 1024 * 1024
LARGE = pltpu.CompilerParams(vmem_limit_bytes=32 * MIB)
SMALL = pltpu.CompilerParams(vmem_limit_bytes=8 * MIB)


def matmul(left, right, dims=((1,), (0,))):
    return lax.dot_general(left, right, (dims, ((), ())), preferred_element_type=F32)


def turned(index, devs):
    top = devs.bit_length() - 2
    place = 0
    for bit in range(top + 1):
        place = place + (((index >> bit) & 1) << (top - bit))
    return place


def send_rows(route_ref, shape, axis, block_rows, devs, flip=0):
    place = lax.broadcasted_iota(jnp.int32, shape, axis)
    target = jnp.zeros(shape, jnp.int32)
    for block in range(shape[axis] // block_rows):
        first = block * block_rows
        moved = (turned(route_ref[0, block], devs) ^ flip) * block_rows + place - first
        target = jnp.where(place >= first, moved, target)
    return target


def scatter_kernel(block_rows, flip, route_hbm, points_hbm, cot_hbm, out_ref, route_ref, points_ref, cot_ref, sems):
    copies = [
        pltpu.make_async_copy(source, target, sems.at[at])
        for at, (source, target) in enumerate(
            ((route_hbm, route_ref), (points_hbm, points_ref), (cot_hbm, cot_ref))
        )
    ]
    for copy in copies:
        copy.start()
    copies[0].wait()
    rows, width = points_ref.shape
    devs = out_ref.shape[0] // block_rows
    target = send_rows(route_ref, (1, rows), 1, block_rows, devs, flip)
    index = lax.broadcasted_iota(jnp.int32, (out_ref.shape[0], rows), 0)
    pick = jnp.where(index == target, 1.0, 0.0).astype(BF16)
    for copy in copies[1:]:
        copy.wait()
    ones = jnp.ones((rows, width), BF16)
    moved = matmul(pick, jnp.concatenate([points_ref[...], ones], axis=1))
    empty = (1.0 - moved[:, width:]) * EMPTY
    out_ref[:, :width] = (moved[:, :width] + empty).astype(BF16)
    out_ref[:, width:] = matmul(pick, cot_ref[...]).astype(BF16)


def normalize(points):
    width = points.shape[1]
    mean_of = jnp.full((width, width), 1.0 / width, BF16)
    centered = points - matmul(points.astype(BF16), mean_of)
    squares = centered * centered
    high = squares.astype(BF16)
    low = (squares - high.astype(F32)).astype(BF16)
    rstd = lax.rsqrt(matmul(high, mean_of) + matmul(low, mean_of) + EPS)
    return centered * rstd, rstd


def owner_kernel(near, got_ref, vectors_ref, w_qkv_hbm, w_out_hbm, _, attn_ref, d_normed_ref, *refs):
    *outs, w_qkv_ref, w_out_ref, both_ref, d_keys_ref, d_values_ref, sems = refs
    copies = [
        pltpu.make_async_copy(w_qkv_hbm, w_qkv_ref, sems.at[0]),
        pltpu.make_async_copy(w_out_hbm, w_out_ref, sems.at[1]),
    ]
    for copy in copies:
        copy.start()
    rows = got_ref.shape[0]
    width = got_ref.shape[1] // 2
    head = width // HEADS
    scale = head ** (-0.5)
    gain = vectors_ref[:, :width]
    b_qkv = vectors_ref[:, 2 * width :]

    points = got_ref[:, :width].astype(F32)
    cot = got_ref[:, width:]
    xhat, _ = normalize(points)
    normed = (xhat * gain).astype(BF16)
    for copy in copies:
        copy.wait()
    w_qkv = w_qkv_ref[...]
    w_out = w_out_ref[...]
    qkv = (matmul(normed, w_qkv) + b_qkv).astype(BF16)
    query, keys, values = qkv[:, :width], qkv[:, width : 2 * width], qkv[:, 2 * width :]
    d_attn = matmul(cot, w_out, ((1,), (1,))).astype(BF16)
    d_attn_t = matmul(w_out, cot, ((1,), (1,))).astype(BF16)
    d_attn_s = (d_attn.astype(F32) * scale).astype(BF16)

    keys_t = keys.T
    values_t = values.T
    keys_s = (keys.astype(F32) * scale).astype(BF16)
    lane = lax.broadcasted_iota(jnp.int32, (rows, width), 1)
    hidden = jnp.where(points[:, :1] > EMPTY / 2, MASKED, 0.0)

    def own(h, array):
        return jnp.where((lane >= h * head) & (lane < (h + 1) * head), array, 0)

    def scores_of(h):
        return matmul(own(h, keys_s), query, ((1,), (1,))) + hidden

    scores, probs, probs_b, d_probs, d_score = {}, {}, {}, {}, {}
    attn_t, dq_t = [], []
    scores[0] = scores_of(0)
    for step in range(HEADS + 2):
        if step + 1 < HEADS:
            scores[step + 1] = scores_of(step + 1)
        if step < HEADS:
            d_probs[step] = matmul(own(step, values), d_attn_s, ((1,), (1,)))
        if 1 <= step <= HEADS:
            lanes = slice((step - 1) * head, step * head)
            attn_t.append(matmul(values_t[lanes, :], probs_b[step - 1]))
        if step >= 2:
            h = step - 2
            lanes = slice(h * head, (h + 1) * head)
            d_values_ref[:, lanes] = matmul(probs_b[h], d_attn)[:, lanes]
            d_keys_ref[:, lanes] = matmul(d_score[h], query)[:, lanes]
            dq_t.append(matmul(keys_t[lanes, :], d_score[h]))
        if step < HEADS:
            now = scores.pop(step)
            expo = jnp.exp(now - jnp.max(now, axis=0, keepdims=True))
            probs[step] = expo * (1.0 / jnp.sum(expo, axis=0, keepdims=True))
            probs_b[step] = probs[step].astype(BF16)
        if 1 <= step <= HEADS:
            h = step - 1
            inner = attn_t[h] * d_attn_t[h * head : (h + 1) * head, :].astype(F32)
            inner = jnp.sum(inner, axis=0, keepdims=True) * scale
            d_score[h] = (probs.pop(h) * (d_probs.pop(h) - inner)).astype(BF16)

    attn_t = jnp.concatenate(attn_t, axis=0)
    attn_ref[...] = attn_t.T.astype(BF16)
    grad_w_out = matmul(attn_t.astype(BF16), cot)
    grad_b_out = jnp.sum(cot.astype(F32), axis=0, keepdims=True)

    d_query = jnp.concatenate(dq_t, axis=0).T
    d_qkv = jnp.concatenate([d_query, d_keys_ref[...], d_values_ref[...]], axis=1).astype(BF16)
    d_normed = matmul(d_qkv, w_qkv, ((1,), (1,)))
    grad_w_qkv = matmul(normed, d_qkv, ((0,), (0,)))
    grad_b_qkv = jnp.sum(d_qkv.astype(F32), axis=0, keepdims=True)
    grad_gain = jnp.sum(d_normed * xhat, axis=0, keepdims=True)
    d_normed_ref[...] = d_normed
    sums = jnp.concatenate(
        [
            grad_b_qkv[:, : 2 * width],
            jnp.concatenate([grad_b_qkv[:, 2 * width :], grad_b_out], axis=1),
            jnp.concatenate([grad_gain, jnp.zeros_like(grad_gain)], axis=1),
            jnp.zeros((5, 2 * width), F32),
        ],
        axis=0,
    )
    left = grad_w_qkv[:, : 2 * width]
    right = jnp.concatenate([grad_w_qkv[:, 2 * width :], grad_w_out], axis=1)
    if near == 1:
        left_ref, right_ref, sums_ref = outs
        left_ref[...] = left.astype(BF16)
        right_ref[...] = right.astype(BF16)
        sums_ref[...] = sums.astype(BF16)
        return
    mine_ref, theirs_ref = outs
    both_ref[:width] = left
    both_ref[width:] = right
    core = lax.axis_index("seq") & 1
    for half, half_ref in ((core, mine_ref), (core ^ 1, theirs_ref)):
        span = pl.ds(pl.multiple_of(half * width, width), width)
        half_ref[:width] = both_ref[span].astype(half_ref.dtype)
        half_ref[width:] = sums.astype(half_ref.dtype)


def rows_kernel(blocks, got_ref, attn_ref, d_normed_ref, vectors_ref, w_out_ref, back_ref, token_ref):
    token_ref[...] = jnp.zeros_like(token_ref)
    width = attn_ref.shape[1]
    gain = vectors_ref[:, :width]
    b_out = vectors_ref[:, width : 2 * width]
    points = got_ref[:, :width].astype(F32)
    cot = got_ref[:, width:].astype(F32)
    xhat, rstd = normalize(points)
    mixed = points + (matmul(attn_ref[...], w_out_ref[...]) + b_out)
    d_xhat = d_normed_ref[...] * gain
    inner = (
        d_xhat
        - jnp.mean(d_xhat, axis=-1, keepdims=True)
        - xhat * jnp.mean(d_xhat * xhat, axis=-1, keepdims=True)
    )
    both = jnp.concatenate([mixed.astype(BF16), (cot + rstd * inner).astype(BF16)], axis=1)
    rows = both.shape[0] // blocks
    for block in range(blocks):
        end = (blocks - block) * rows
        back_ref[end - rows : end] = both[block * rows : (block + 1) * rows]


def sum_kernel(count, *refs):
    piece_refs, out_ref = refs[:count], refs[-1]
    values = [piece_ref[...].astype(F32) for piece_ref in piece_refs]
    while len(values) > 1:
        values = [left + right for left, right in zip(values[::2], values[1::2])]
    out_ref[...] = values[0].astype(BF16)


def tie_kernel(rows_ref, other_ref, out_ref):
    pass


def pick_kernel(block_rows, route_hbm, pick_ref, token_ref, route_ref, sem):
    token_ref[...] = jnp.zeros_like(token_ref)
    copy = pltpu.make_async_copy(route_hbm, route_ref, sem)
    copy.start()
    copy.wait()
    rows, held = pick_ref.shape
    target = send_rows(route_ref, (rows, 1), 0, block_rows, held // block_rows)
    index = lax.broadcasted_iota(jnp.int32, pick_ref.shape, 1)
    pick_ref[...] = jnp.where(index == target, 1.0, 0.0).astype(BF16)


def return_kernel(pick_ref, back_ref, mixed_ref, grad_ref, token_ref):
    token_ref[...] = jnp.zeros_like(token_ref)
    width = mixed_ref.shape[1]
    moved = matmul(pick_ref[...], back_ref[...]).astype(BF16)
    mixed_ref[...] = moved[:, :width]
    grad_ref[...] = moved[:, width:]


def weights_kernel(*refs):
    *half_refs, _, gain_ref, w_qkv_ref, b_qkv_ref, w_out_ref, b_out_ref, both_ref = refs
    width = w_out_ref.shape[1]
    core = lax.axis_index("seq") & 1
    for step, half_ref in enumerate(half_refs):
        place = core ^ step
        half = half_ref[...].astype(F32)
        both_ref[pl.ds(pl.multiple_of(place * width, width), width)] = half[:width]

        @pl.when(place == 0)
        def _():
            sums = half[width:]
            gain_ref[...] = sums[2, :width]
            b_qkv_ref[: 2 * width] = sums[0]
            b_qkv_ref[2 * width :] = sums[1, :width]
            b_out_ref[...] = sums[1, width:]

    w_qkv_ref[:, : 2 * width] = both_ref[:width]
    w_qkv_ref[:, 2 * width :] = both_ref[width:, :width]
    w_out_ref[...] = both_ref[width:, width:]


def exchange(message, flip=0):
    devs = message.shape[0]
    order = [turned(place ^ flip, devs) for place in range(devs)]
    return lax.all_to_all(
        message, "seq", split_axis=0, concat_axis=0, axis_index_groups=[order], tiled=True
    )


def swap(piece, step, devs):
    return lax.ppermute(piece, "seq", [(dev, dev ^ step) for dev in range(devs)])


def local(points, route, owned, cotangent, gain, w_qkv, b_qkv, w_out, b_out):
    devs = lax.axis_size("seq")
    rows, width = points.shape
    block_rows = rows // route.shape[1]
    held = devs * block_rows
    share = width // devs
    near = 4 if devs == 16 and width % 64 == 0 else 1
    flip = devs - 1 if near > 1 else 0

    def shape(*dims, dtype=BF16):
        return jax.ShapeDtypeStruct(dims, dtype)

    sent = pl.pallas_call(
        functools.partial(scatter_kernel, block_rows, flip),
        out_shape=shape(held, 2 * width),
        in_specs=[ANY] * 3,
        out_specs=VMEM,
        scratch_shapes=[
            pltpu.SMEM(route.shape, route.dtype),
            pltpu.VMEM(points.shape, points.dtype),
            pltpu.VMEM(cotangent.shape, cotangent.dtype),
            pltpu.SemaphoreType.DMA((3,)),
        ],
    )(route, points, cotangent)
    got = exchange(sent.reshape(devs, block_rows, 2 * width), flip).reshape(held, 2 * width)

    pick, early = pl.pallas_call(
        functools.partial(pick_kernel, block_rows),
        out_shape=(shape(rows, held), shape(8, 128, dtype=F32)),
        in_specs=[ANY],
        out_specs=(VMEM,) * 2,
        scratch_shapes=[pltpu.SMEM(route.shape, route.dtype), pltpu.SemaphoreType.DMA],
        compiler_params=SMALL,
    )(route)

    half = shape(width + 8, 2 * width)
    if near > 1:
        sums_shapes = (half, half)
    else:
        sums_shapes = (shape(width, 2 * width),) * 2 + (shape(8, 2 * width),)
    vectors = jnp.concatenate([gain, b_out, b_qkv])[None, :]
    attn, d_normed, *parts = pl.pallas_call(
        functools.partial(owner_kernel, near),
        out_shape=(shape(held, width), shape(held, width, dtype=F32)) + sums_shapes,
        in_specs=[VMEM, VMEM, ANY, ANY, VMEM],
        out_specs=(VMEM,) * (2 + len(sums_shapes)),
        scratch_shapes=[
            pltpu.VMEM(w_qkv.shape, w_qkv.dtype),
            pltpu.VMEM(w_out.shape, w_out.dtype),
            pltpu.VMEM((2 * width, 2 * width), F32),
            pltpu.VMEM((held, width), F32),
            pltpu.VMEM((held, width), F32),
            pltpu.SemaphoreType.DMA((2,)),
        ],
        compiler_params=LARGE,
    )(got, vectors, w_qkv, w_out, early)
    back, token = pl.pallas_call(
        functools.partial(rows_kernel, devs if flip else 1),
        out_shape=(shape(held, 2 * width), shape(8, 128, dtype=F32)),
        in_specs=[VMEM] * 5,
        out_specs=(VMEM,) * 2,
        compiler_params=SMALL,
        cost_estimate=pl.CostEstimate(
            flops=64 * held * width * width, bytes_accessed=16 * held * width, transcendentals=0
        ),
    )(got, attn, d_normed, vectors, w_out)

    def give_back(back):
        return pl.pallas_call(
            return_kernel,
            out_shape=(shape(rows, width), shape(rows, width), shape(8, 128, dtype=F32)),
            in_specs=[VMEM] * 2,
            out_specs=(VMEM,) * 3,
            compiler_params=SMALL,
        )(pick, back)

    if near > 1:
        mine, theirs = parts

        def add(*pieces, after=(), flops=0):
            return pl.pallas_call(
                functools.partial(sum_kernel, len(pieces)),
                out_shape=half,
                in_specs=[VMEM] * (len(pieces) + len(after)),
                out_specs=VMEM,
                compiler_params=SMALL,
                cost_estimate=pl.CostEstimate(flops=flops, bytes_accessed=0, transcendentals=0),
            )(*pieces, *after)

        total = add(mine, swap(theirs, 1, devs), after=(token,))
        back = pl.pallas_call(
            tie_kernel,
            out_shape=back,
            in_specs=[ANY, VMEM],
            out_specs=ANY,
            input_output_aliases={0: 0},
            compiler_params=SMALL,
        )(back, total)
        back = exchange(back.reshape(devs, block_rows, 2 * width)).reshape(held, 2 * width)
        mixed, grad_points, token = give_back(back)
        total = add(total, swap(total, devs // 2, devs), flops=40_000_000_000)
        steps = [step for step in range(2, devs // 2, 2)]
        total = add(total, *(swap(total, step, devs) for step in steps))
        parts = [total, swap(total, 1, devs)]
        grad_gain, grad_wq, grad_bq, grad_wo, grad_bo = pl.pallas_call(
            weights_kernel,
            out_shape=tuple(
                shape(*dims, dtype=F32)
                for dims in ((width,), (width, 3 * width), (3 * width,), (width, width), (width,))
            ),
            in_specs=[VMEM] * 3,
            out_specs=(VMEM,) * 5,
            scratch_shapes=[pltpu.VMEM((2 * width, 2 * width), F32)],
            compiler_params=SMALL,
        )(*parts, token)
    else:
        left, right, sums = parts
        message = jnp.concatenate(
            [
                back.reshape(devs, block_rows, 2 * width),
                left.reshape(devs, share, 2 * width),
                right.reshape(devs, share, 2 * width),
                jnp.broadcast_to(sums[None], (devs, 8, 2 * width)),
            ],
            axis=1,
        )
        message = exchange(message)
        total = jnp.sum(message[:, block_rows:].astype(F32), axis=0)
        mine = total[: 2 * share].astype(BF16)
        both = exchange(jnp.broadcast_to(mine[None], (devs, 2 * share, 2 * width))).astype(F32)
        mixed, grad_points, _ = give_back(message[:, :block_rows].reshape(held, 2 * width))
        left = both[:, :share].reshape(width, 2 * width)
        right = both[:, share:].reshape(width, 2 * width)
        grad_wq = jnp.concatenate([left, right[:, :width]], axis=1)
        grad_wo = right[:, width:]
        flat = total[2 * share :].reshape(-1)
        grad_bq = flat[: 3 * width]
        grad_bo = flat[3 * width : 4 * width]
        grad_gain = flat[4 * width : 5 * width]

    return (mixed, grad_points, grad_gain, grad_wq, grad_bq, grad_wo, grad_bo)


def solution(mesh):
    placed = (
        P(("parts", "seq"), None),
        P(None, ("parts", "seq")),
        P(("parts", "seq")),
        P(("parts", "seq"), None),
        P(),
        P(),
        P(),
        P(),
        P(),
    )
    return jax.shard_map(
        local,
        mesh=mesh,
        in_specs=placed,
        out_specs=(
            P(("parts", "seq"), None),
            P(("parts", "seq"), None),
            P("parts"),
            P("parts", None),
            P("parts"),
            P("parts", None),
            P("parts"),
        ),
        check_vma=False,
    )
```

```python
import functools

import jax
import jax.numpy as jnp
from jax import lax
from jax.experimental import pallas as pl
from jax.experimental.pallas import tpu as pltpu
from jax.sharding import PartitionSpec as P

HEADS = 8
EPS = 1e-05
EMPTY = 64.0
MASKED = -1e30

F32 = jnp.float32
BF16 = jnp.bfloat16

VMEM = pl.BlockSpec(memory_space=pltpu.VMEM)
ANY = pl.BlockSpec(memory_space=pl.ANY)
SMEM = pl.BlockSpec(memory_space=pltpu.SMEM)
MIB = 1024 * 1024
LARGE = pltpu.CompilerParams(vmem_limit_bytes=32 * MIB)
SMALL = pltpu.CompilerParams(vmem_limit_bytes=8 * MIB)


def matmul(left, right, dims=((1,), (0,))):
    return lax.dot_general(left, right, (dims, ((), ())), preferred_element_type=F32)


def turned(index, devs):
    top = devs.bit_length() - 2
    place = 0
    for bit in range(top + 1):
        place = place + (((index >> bit) & 1) << (top - bit))
    return place


def send_rows(route_ref, shape, axis, block_rows, devs, flip=0):
    place = lax.broadcasted_iota(jnp.int32, shape, axis)
    target = jnp.zeros(shape, jnp.int32)
    for block in range(shape[axis] // block_rows):
        first = block * block_rows
        moved = (turned(route_ref[0, block], devs) ^ flip) * block_rows + place - first
        target = jnp.where(place >= first, moved, target)
    return target


def scatter_kernel(block_rows, flip, route_hbm, points_hbm, cot_hbm, out_ref, route_ref, points_ref, cot_ref, sems):
    copies = [
        pltpu.make_async_copy(source, target, sems.at[at])
        for at, (source, target) in enumerate(
            ((route_hbm, route_ref), (points_hbm, points_ref), (cot_hbm, cot_ref))
        )
    ]
    for copy in copies:
        copy.start()
    copies[0].wait()
    rows, width = points_ref.shape
    devs = out_ref.shape[0] // block_rows
    target = send_rows(route_ref, (1, rows), 1, block_rows, devs, flip)
    index = lax.broadcasted_iota(jnp.int32, (out_ref.shape[0], rows), 0)
    pick = jnp.where(index == target, 1.0, 0.0).astype(BF16)
    for copy in copies[1:]:
        copy.wait()
    ones = jnp.ones((rows, width), BF16)
    moved = matmul(pick, jnp.concatenate([points_ref[...], ones], axis=1))
    empty = (1.0 - moved[:, width:]) * EMPTY
    out_ref[:, :width] = (moved[:, :width] + empty).astype(BF16)
    out_ref[:, width:] = matmul(pick, cot_ref[...]).astype(BF16)


def normalize(points):
    centered = points - jnp.mean(points, axis=-1, keepdims=True)
    rstd = lax.rsqrt(jnp.mean(centered * centered, axis=-1, keepdims=True) + EPS)
    return centered * rstd, rstd


def owner_kernel(near, got_ref, vectors_ref, w_qkv_hbm, w_out_hbm, _, attn_ref, d_normed_ref, *refs):
    *outs, w_qkv_ref, w_out_ref, both_ref, d_keys_ref, d_values_ref, sems = refs
    copies = [
        pltpu.make_async_copy(w_qkv_hbm, w_qkv_ref, sems.at[0]),
        pltpu.make_async_copy(w_out_hbm, w_out_ref, sems.at[1]),
    ]
    for copy in copies:
        copy.start()
    rows = got_ref.shape[0]
    width = got_ref.shape[1] // 2
    head = width // HEADS
    scale = head ** (-0.5)
    gain = vectors_ref[:, :width]
    b_qkv = vectors_ref[:, 2 * width :]

    points = got_ref[:, :width].astype(F32)
    cot = got_ref[:, width:]
    xhat, _ = normalize(points)
    normed = (xhat * gain).astype(BF16)
    for copy in copies:
        copy.wait()
    w_qkv = w_qkv_ref[...]
    w_out = w_out_ref[...]
    qkv = (matmul(normed, w_qkv) + b_qkv).astype(BF16)
    query, keys, values = qkv[:, :width], qkv[:, width : 2 * width], qkv[:, 2 * width :]
    d_attn = matmul(cot, w_out, ((1,), (1,))).astype(BF16)
    d_attn_t = matmul(w_out, cot, ((1,), (1,))).astype(BF16)
    d_attn_s = (d_attn.astype(F32) * scale).astype(BF16)

    keys_t = keys.T
    values_t = values.T
    keys_s = (keys.astype(F32) * scale).astype(BF16)
    lane = lax.broadcasted_iota(jnp.int32, (rows, width), 1)
    hidden = jnp.where(points[:, :1] > EMPTY / 2, MASKED, 0.0)

    def own(h, array):
        return jnp.where((lane >= h * head) & (lane < (h + 1) * head), array, 0)

    def scores_of(h):
        return matmul(own(h, keys_s), query, ((1,), (1,))) + hidden

    scores, probs, probs_b, d_score = {}, {}, {}, {}
    attn_t, dq_t = [], []
    scores[0] = scores_of(0)
    for step in range(HEADS + 2):
        if step + 1 < HEADS:
            scores[step + 1] = scores_of(step + 1)
        if 1 <= step <= HEADS:
            lanes = slice((step - 1) * head, step * head)
            attn_t.append(matmul(values_t[lanes, :], probs_b[step - 1]))
        if step >= 2:
            h = step - 2
            lanes = slice(h * head, (h + 1) * head)
            d_values_ref[:, lanes] = matmul(probs_b[h], d_attn)[:, lanes]
            d_keys_ref[:, lanes] = matmul(d_score[h], query)[:, lanes]
            dq_t.append(matmul(keys_t[lanes, :], d_score[h]))
        if step < HEADS:
            now = scores.pop(step)
            expo = jnp.exp(now - jnp.max(now, axis=0, keepdims=True))
            probs[step] = expo * (1.0 / jnp.sum(expo, axis=0, keepdims=True))
            probs_b[step] = probs[step].astype(BF16)
        if 1 <= step <= HEADS:
            h = step - 1
            inner = attn_t[h] * d_attn_t[h * head : (h + 1) * head, :].astype(F32)
            inner = jnp.sum(inner, axis=0, keepdims=True) * scale
            d_probs = matmul(own(h, values), d_attn_s, ((1,), (1,)))
            d_score[h] = (probs.pop(h) * (d_probs - inner)).astype(BF16)

    attn_t = jnp.concatenate(attn_t, axis=0)
    attn_ref[...] = attn_t.T.astype(BF16)
    grad_w_out = matmul(attn_t.astype(BF16), cot)
    grad_b_out = jnp.sum(cot.astype(F32), axis=0, keepdims=True)

    d_query = jnp.concatenate(dq_t, axis=0).T
    d_qkv = jnp.concatenate([d_query, d_keys_ref[...], d_values_ref[...]], axis=1).astype(BF16)
    d_normed = matmul(d_qkv, w_qkv, ((1,), (1,)))
    grad_w_qkv = matmul(normed, d_qkv, ((0,), (0,)))
    grad_b_qkv = jnp.sum(d_qkv.astype(F32), axis=0, keepdims=True)
    grad_gain = jnp.sum(d_normed * xhat, axis=0, keepdims=True)
    d_normed_ref[...] = d_normed
    sums = jnp.concatenate(
        [
            grad_b_qkv[:, : 2 * width],
            jnp.concatenate([grad_b_qkv[:, 2 * width :], grad_b_out], axis=1),
            jnp.concatenate([grad_gain, jnp.zeros_like(grad_gain)], axis=1),
            jnp.zeros((5, 2 * width), F32),
        ],
        axis=0,
    )
    left = grad_w_qkv[:, : 2 * width]
    right = jnp.concatenate([grad_w_qkv[:, 2 * width :], grad_w_out], axis=1)
    if near == 1:
        left_ref, right_ref, sums_ref = outs
        left_ref[...] = left.astype(BF16)
        right_ref[...] = right.astype(BF16)
        sums_ref[...] = sums.astype(BF16)
        return
    mine_ref, theirs_ref = outs
    both_ref[:width] = left
    both_ref[width:] = right
    core = lax.axis_index("seq") & 1
    for half, half_ref in ((core, mine_ref), (core ^ 1, theirs_ref)):
        span = pl.ds(pl.multiple_of(half * width, width), width)
        half_ref[:width] = both_ref[span].astype(half_ref.dtype)
        half_ref[width:] = sums.astype(half_ref.dtype)


def rows_kernel(blocks, got_ref, attn_ref, d_normed_ref, vectors_ref, w_out_ref, back_ref, token_ref):
    token_ref[...] = jnp.zeros_like(token_ref)
    width = attn_ref.shape[1]
    gain = vectors_ref[:, :width]
    b_out = vectors_ref[:, width : 2 * width]
    points = got_ref[:, :width].astype(F32)
    cot = got_ref[:, width:].astype(F32)
    xhat, rstd = normalize(points)
    mixed = points + (matmul(attn_ref[...], w_out_ref[...]) + b_out)
    d_xhat = d_normed_ref[...] * gain
    inner = (
        d_xhat
        - jnp.mean(d_xhat, axis=-1, keepdims=True)
        - xhat * jnp.mean(d_xhat * xhat, axis=-1, keepdims=True)
    )
    both = jnp.concatenate([mixed.astype(BF16), (cot + rstd * inner).astype(BF16)], axis=1)
    rows = both.shape[0] // blocks
    for block in range(blocks):
        end = (blocks - block) * rows
        back_ref[end - rows : end] = both[block * rows : (block + 1) * rows]


def sum_kernel(count, *refs):
    piece_refs, out_ref = refs[:count], refs[-1]
    values = [piece_ref[...].astype(F32) for piece_ref in piece_refs]
    while len(values) > 1:
        values = [left + right for left, right in zip(values[::2], values[1::2])]
    out_ref[...] = values[0].astype(BF16)


def tie_kernel(rows_ref, other_ref, out_ref):
    pass


def pick_kernel(block_rows, route_hbm, pick_ref, token_ref, route_ref, sem):
    token_ref[...] = jnp.zeros_like(token_ref)
    copy = pltpu.make_async_copy(route_hbm, route_ref, sem)
    copy.start()
    copy.wait()
    rows, held = pick_ref.shape
    target = send_rows(route_ref, (rows, 1), 0, block_rows, held // block_rows)
    index = lax.broadcasted_iota(jnp.int32, pick_ref.shape, 1)
    pick_ref[...] = jnp.where(index == target, 1.0, 0.0).astype(BF16)


def return_kernel(pick_ref, back_ref, mixed_ref, grad_ref, token_ref):
    token_ref[...] = jnp.zeros_like(token_ref)
    width = mixed_ref.shape[1]
    moved = matmul(pick_ref[...], back_ref[...]).astype(BF16)
    mixed_ref[...] = moved[:, :width]
    grad_ref[...] = moved[:, width:]


def weights_kernel(*refs):
    *half_refs, _, gain_ref, w_qkv_ref, b_qkv_ref, w_out_ref, b_out_ref, both_ref = refs
    width = w_out_ref.shape[1]
    core = lax.axis_index("seq") & 1
    for step, half_ref in enumerate(half_refs):
        place = core ^ step
        half = half_ref[...].astype(F32)
        both_ref[pl.ds(pl.multiple_of(place * width, width), width)] = half[:width]

        @pl.when(place == 0)
        def _():
            sums = half[width:]
            gain_ref[...] = sums[2, :width]
            b_qkv_ref[: 2 * width] = sums[0]
            b_qkv_ref[2 * width :] = sums[1, :width]
            b_out_ref[...] = sums[1, width:]

    w_qkv_ref[:, : 2 * width] = both_ref[:width]
    w_qkv_ref[:, 2 * width :] = both_ref[width:, :width]
    w_out_ref[...] = both_ref[width:, width:]


def exchange(message, flip=0):
    devs = message.shape[0]
    order = [turned(place ^ flip, devs) for place in range(devs)]
    return lax.all_to_all(
        message, "seq", split_axis=0, concat_axis=0, axis_index_groups=[order], tiled=True
    )


def swap(piece, step, devs):
    return lax.ppermute(piece, "seq", [(dev, dev ^ step) for dev in range(devs)])


def local(points, route, owned, cotangent, gain, w_qkv, b_qkv, w_out, b_out):
    devs = lax.axis_size("seq")
    rows, width = points.shape
    block_rows = rows // route.shape[1]
    held = devs * block_rows
    share = width // devs
    near = 4 if devs == 16 and width % 64 == 0 else 1
    flip = devs - 1 if near > 1 else 0

    def shape(*dims, dtype=BF16):
        return jax.ShapeDtypeStruct(dims, dtype)

    sent = pl.pallas_call(
        functools.partial(scatter_kernel, block_rows, flip),
        out_shape=shape(held, 2 * width),
        in_specs=[ANY] * 3,
        out_specs=VMEM,
        scratch_shapes=[
            pltpu.SMEM(route.shape, route.dtype),
            pltpu.VMEM(points.shape, points.dtype),
            pltpu.VMEM(cotangent.shape, cotangent.dtype),
            pltpu.SemaphoreType.DMA((3,)),
        ],
    )(route, points, cotangent)
    got = exchange(sent.reshape(devs, block_rows, 2 * width), flip).reshape(held, 2 * width)

    pick, early = pl.pallas_call(
        functools.partial(pick_kernel, block_rows),
        out_shape=(shape(rows, held), shape(8, 128, dtype=F32)),
        in_specs=[ANY],
        out_specs=(VMEM,) * 2,
        scratch_shapes=[pltpu.SMEM(route.shape, route.dtype), pltpu.SemaphoreType.DMA],
        compiler_params=SMALL,
    )(route)

    half = shape(width + 8, 2 * width)
    if near > 1:
        sums_shapes = (half, half)
    else:
        sums_shapes = (shape(width, 2 * width),) * 2 + (shape(8, 2 * width),)
    vectors = jnp.concatenate([gain, b_out, b_qkv])[None, :]
    attn, d_normed, *parts = pl.pallas_call(
        functools.partial(owner_kernel, near),
        out_shape=(shape(held, width), shape(held, width, dtype=F32)) + sums_shapes,
        in_specs=[VMEM, VMEM, ANY, ANY, VMEM],
        out_specs=(VMEM,) * (2 + len(sums_shapes)),
        scratch_shapes=[
            pltpu.VMEM(w_qkv.shape, w_qkv.dtype),
            pltpu.VMEM(w_out.shape, w_out.dtype),
            pltpu.VMEM((2 * width, 2 * width), F32),
            pltpu.VMEM((held, width), F32),
            pltpu.VMEM((held, width), F32),
            pltpu.SemaphoreType.DMA((2,)),
        ],
        compiler_params=LARGE,
    )(got, vectors, w_qkv, w_out, early)
    back, token = pl.pallas_call(
        functools.partial(rows_kernel, devs if flip else 1),
        out_shape=(shape(held, 2 * width), shape(8, 128, dtype=F32)),
        in_specs=[VMEM] * 5,
        out_specs=(VMEM,) * 2,
        compiler_params=SMALL,
        cost_estimate=pl.CostEstimate(
            flops=64 * held * width * width, bytes_accessed=16 * held * width, transcendentals=0
        ),
    )(got, attn, d_normed, vectors, w_out)

    def give_back(back):
        return pl.pallas_call(
            return_kernel,
            out_shape=(shape(rows, width), shape(rows, width), shape(8, 128, dtype=F32)),
            in_specs=[VMEM] * 2,
            out_specs=(VMEM,) * 3,
            compiler_params=SMALL,
        )(pick, back)

    if near > 1:
        mine, theirs = parts

        def add(*pieces, after=(), flops=0):
            return pl.pallas_call(
                functools.partial(sum_kernel, len(pieces)),
                out_shape=half,
                in_specs=[VMEM] * (len(pieces) + len(after)),
                out_specs=VMEM,
                compiler_params=SMALL,
                cost_estimate=pl.CostEstimate(flops=flops, bytes_accessed=0, transcendentals=0),
            )(*pieces, *after)

        total = add(mine, swap(theirs, 1, devs), after=(token,))
        back = pl.pallas_call(
            tie_kernel,
            out_shape=back,
            in_specs=[ANY, VMEM],
            out_specs=ANY,
            input_output_aliases={0: 0},
            compiler_params=SMALL,
        )(back, total)
        back = exchange(back.reshape(devs, block_rows, 2 * width)).reshape(held, 2 * width)
        mixed, grad_points, token = give_back(back)
        total = add(total, swap(total, devs // 2, devs), flops=40_000_000_000)
        steps = [step for step in range(2, devs // 2, 2)]
        total = add(total, *(swap(total, step, devs) for step in steps))
        parts = [total, swap(total, 1, devs)]
        grad_gain, grad_wq, grad_bq, grad_wo, grad_bo = pl.pallas_call(
            weights_kernel,
            out_shape=tuple(
                shape(*dims, dtype=F32)
                for dims in ((width,), (width, 3 * width), (3 * width,), (width, width), (width,))
            ),
            in_specs=[VMEM] * 3,
            out_specs=(VMEM,) * 5,
            scratch_shapes=[pltpu.VMEM((2 * width, 2 * width), F32)],
            compiler_params=SMALL,
        )(*parts, token)
    else:
        left, right, sums = parts
        message = jnp.concatenate(
            [
                back.reshape(devs, block_rows, 2 * width),
                left.reshape(devs, share, 2 * width),
                right.reshape(devs, share, 2 * width),
                jnp.broadcast_to(sums[None], (devs, 8, 2 * width)),
            ],
            axis=1,
        )
        message = exchange(message)
        total = jnp.sum(message[:, block_rows:].astype(F32), axis=0)
        mine = total[: 2 * share].astype(BF16)
        both = exchange(jnp.broadcast_to(mine[None], (devs, 2 * share, 2 * width))).astype(F32)
        mixed, grad_points, _ = give_back(message[:, :block_rows].reshape(held, 2 * width))
        left = both[:, :share].reshape(width, 2 * width)
        right = both[:, share:].reshape(width, 2 * width)
        grad_wq = jnp.concatenate([left, right[:, :width]], axis=1)
        grad_wo = right[:, width:]
        flat = total[2 * share :].reshape(-1)
        grad_bq = flat[: 3 * width]
        grad_bo = flat[3 * width : 4 * width]
        grad_gain = flat[4 * width : 5 * width]

    return (mixed, grad_points, grad_gain, grad_wq, grad_bq, grad_wo, grad_bo)


def solution(mesh):
    placed = (
        P(("parts", "seq"), None),
        P(None, ("parts", "seq")),
        P(("parts", "seq")),
        P(("parts", "seq"), None),
        P(),
        P(),
        P(),
        P(),
        P(),
    )
    return jax.shard_map(
        local,
        mesh=mesh,
        in_specs=placed,
        out_specs=(
            P(("parts", "seq"), None),
            P(("parts", "seq"), None),
            P("parts"),
            P("parts", None),
            P("parts"),
            P("parts", None),
            P("parts"),
        ),
        check_vma=False,
    )
```
